32 devices in a mesh: seq: 2 (over core), kax: 4 (over y, x), vax: 4 (over z).
Axes of the slice: x: 2, y: 2, z: 4, core: 2. Of those that a mesh axis runs over, the one named last changes fastest.
Arguments:
- tokens: bfloat16 [2048, 1024], P('seq'), may hold values from -6 to 6
- norm_gain: bfloat16 [1024], replicated, may hold values from 0.5 to 1.5
- query_weight: bfloat16 [1024, 4, 128], P(None, None, 'kax'), may hold values from -0.1875 to 0.1875
- key_weight: bfloat16 [1024, 4, 128], P(None, None, 'kax'), may hold values from -0.1875 to 0.1875
- value_weight: bfloat16 [1024, 4, 256], P(None, None, 'vax'), may hold values from -0.1875 to 0.1875
- gate_weight: bfloat16 [1024, 4, 256], P(None, None, 'vax'), may hold values from -0.1875 to 0.1875
- decay_down: bfloat16 [1024, 16], replicated, may hold values from -0.1875 to 0.1875
- decay_up: bfloat16 [16, 4, 128], P(None, None, 'kax'), may hold values from -1.5 to 1.5
- decay_bias: bfloat16 [4, 128], P(None, 'kax'), may hold values from 0 to 12
- group_gain: bfloat16 [256], P('vax'), may hold values from 0.5 to 1.5
- out_weight: bfloat16 [4, 256, 1024], P('kax', 'vax'), may hold values from -0.25 to 0.25
- ffn_gain: bfloat16 [1024], replicated, may hold values from 0.5 to 1.5
- ffn_gate: bfloat16 [1024, 2816], P(None, ('kax', 'vax')), may hold values from -0.1875 to 0.1875
- ffn_up: bfloat16 [1024, 2816], P(None, ('kax', 'vax')), may hold values from -0.1875 to 0.1875
- ffn_down: bfloat16 [2816, 1024], P(('kax', 'vax')), may hold values from -0.109375 to 0.109375
- cotangent: bfloat16 [2048, 1024], P('seq'), may hold values from -6 to 6
Outputs:
- output: bfloat16 [2048, 1024], P('seq', ('kax', 'vax'))
- input_grad: bfloat16 [2048, 1024], P('seq', ('kax', 'vax'))
- norm_gain_grad: float32 [1024], P(('kax', 'vax'))
- query_weight_grad: float32 [1024, 4, 128], P(None, 'vax', 'kax')
- key_weight_grad: float32 [1024, 4, 128], P(None, 'vax', 'kax')
- value_weight_grad: float32 [1024, 4, 256], P(None, 'kax', 'vax')
- gate_weight_grad: float32 [1024, 4, 256], P(None, 'kax', 'vax')
- decay_down_grad: float32 [1024, 16], P(None, ('kax', 'vax'))
- decay_up_grad: float32 [16, 4, 128], P(None, 'vax', 'kax')
- decay_bias_grad: float32 [4, 128], P('vax', 'kax')
- group_gain_grad: float32 [256], P('vax')
- out_weight_grad: float32 [4, 256, 1024], P('kax', 'vax')
- ffn_gain_grad: float32 [1024], P(('kax', 'vax'))
- ffn_gate_grad: float32 [1024, 2816], P(None, ('kax', 'vax'))
- ffn_up_grad: float32 [1024, 2816], P(None, ('kax', 'vax'))
- ffn_down_grad: float32 [2816, 1024], P(('kax', 'vax'))
The draws below stay inside these ranges and needn't reach their ends.
All inputs are finite; a program needn't handle non-finite values.
Results may differ from the reference program's by a relative error of at most 0.03.
Values may be sent and summed in bfloat16 or wider, within the bound.
A program may use at most 128 MiB of HBM per device.

```python
import jax
import jax.numpy as jnp
from jax import lax

D = 1024
H = 4
DKH = 128
DVH = 256
GR = 16
FF = 2816
CH = 64
TOKENS = 2048


def level_of(key, dims, cuts, smallest, high):
    loudness, own = 1.0, jax.random.fold_in(key, 6)
    for position, parts in cuts:
        steps = jnp.exp(jax.random.uniform(jax.random.fold_in(own, position), (parts,), jnp.float32, smallest / len(cuts), high / len(cuts)))
        loudness = loudness * jnp.repeat(steps, dims[position] // parts).reshape([-1 if axis == position else 1 for axis in range(len(dims))])
    return loudness


def scatter_about(stream_key, dims, scale, limit, split=(), kind=jnp.bfloat16):
    gain = level_of(stream_key, dims, split, -0.22, 0.18) if split else 1.0
    result = jax.random.normal(stream_key, dims, jnp.float32) * scale * gain
    return jnp.minimum(jnp.maximum(result, -limit), limit).astype(kind)


def setup_inputs(seed: int = 0) -> dict:
    splits = jax.random.split(jax.random.key(seed), 17)
    return {
        "tokens": scatter_about(splits[0], (TOKENS, D), 1.0, 6.0, ((0, 2),)),
        "norm_gain": jnp.clip(1.0 + 0.1 * jax.random.normal(splits[1], (D,), jnp.float32), 0.5, 1.5).astype(jnp.bfloat16),
        "query_weight": scatter_about(splits[2], (D, H, DKH), D ** -0.5, 0.1875, ((2, 4),)),
        "key_weight": scatter_about(splits[3], (D, H, DKH), D ** -0.5, 0.1875, ((2, 4),)),
        "value_weight": scatter_about(splits[4], (D, H, DVH), D ** -0.5, 0.1875, ((2, 4),)),
        "gate_weight": scatter_about(splits[5], (D, H, DVH), D ** -0.5, 0.1875, ((2, 4),)),
        "decay_down": scatter_about(splits[6], (D, GR), D ** -0.5, 0.1875),
        "decay_up": scatter_about(splits[7], (GR, H, DKH), GR ** -0.5, 1.5, ((2, 4),)),
        "decay_bias": jnp.clip(12.0 * jax.random.uniform(splits[8], (H, DKH), jnp.float32) ** level_of(splits[8], (H, DKH), ((1, 4),), -0.2, 0.2), 0.0, 12.0).astype(jnp.bfloat16),
        "group_gain": jnp.clip(1.0 + 0.1 * jax.random.normal(splits[9], (DVH,), jnp.float32), 0.5, 1.5).astype(jnp.bfloat16),
        "out_weight": scatter_about(splits[10], (H, DVH, D), (H * DVH // 2) ** -0.5, 0.25, ((0, 4), (1, 4))),
        "ffn_gain": jnp.clip(1.0 + 0.1 * jax.random.normal(splits[11], (D,), jnp.float32), 0.5, 1.5).astype(jnp.bfloat16),
        "ffn_gate": scatter_about(splits[12], (D, FF), D ** -0.5, 0.1875, ((1, 16),)),
        "ffn_up": scatter_about(splits[13], (D, FF), D ** -0.5, 0.1875, ((1, 16),)),
        "ffn_down": scatter_about(splits[14], (FF, D), FF ** -0.5, 0.109375, ((0, 16),)),
        "cotangent": scatter_about(splits[15], (TOKENS, D), 1.0, 6.0, ((0, 2),)),
    }


@jax.custom_vjp
def low(v):
    return lax.optimization_barrier(v.astype(jnp.bfloat16)).astype(jnp.float32)

@jax.custom_vjp
def low_back(v):
    return v

def low_keep(v):
    return (low(v), None)

def low_pass(kept, grad):
    return (grad,)

def back_keep(v):
    return (v, None)

def back_low(kept, grad):
    return (low(grad),)
low.defvjp(low_keep, low_pass)
low_back.defvjp(back_keep, back_low)
epsilon = 1e-06

def matmul(left, right):
    return jnp.dot(left, right, precision=lax.Precision.HIGHEST)

def block_step(recurrent_state, inputs):
    query_rows, key_matrix_rows, value_matrix_rows, rates = inputs
    running_total = jnp.cumsum(rates, axis=0)
    causal = (jnp.arange(CH)[:, None] >= jnp.arange(CH)[None, :])[:, :, None, None]
    spread = running_total[:, None] - running_total[None, :]
    weights = jnp.where(causal, jnp.exp(jnp.where(causal, spread, 0.0)), 0.0)
    scores = jnp.einsum('thk,shk,tshk->hts', query_rows, key_matrix_rows, weights, precision=lax.Precision.HIGHEST)
    block_output = jnp.einsum('hts,shv->thv', scores, value_matrix_rows, precision=lax.Precision.HIGHEST)
    block_output = block_output + jnp.einsum('dey,eyf->def', query_rows * jnp.exp(running_total), recurrent_state, precision=lax.Precision.HIGHEST)
    final_sum_decay = running_total[-1]
    state_update = jnp.einsum('ntp,ntr->tpr', key_matrix_rows * jnp.exp(final_sum_decay[None] - running_total), value_matrix_rows, precision=lax.Precision.HIGHEST)
    recurrent_state = jnp.exp(final_sum_decay)[:, :, None] * recurrent_state + state_update
    return (recurrent_state, block_output)

def mixer(query_rows, key_matrix_rows, value_matrix_rows, rates):
    length = query_rows.shape[0]
    blocks = length // CH
    inputs = (query_rows.reshape(blocks, CH, H, DKH), key_matrix_rows.reshape(blocks, CH, H, DKH), value_matrix_rows.reshape(blocks, CH, H, DVH), rates.reshape(blocks, CH, H, DKH))
    start = jnp.zeros((H, DKH, DVH), query_rows.dtype)
    final_state, results = lax.scan(jax.checkpoint(block_step), start, inputs)
    return results.reshape(length, H, DVH)

def rms_scale(values):
    return lax.rsqrt(lax.optimization_barrier(jnp.mean(values * values, axis=-1, keepdims=True)) + epsilon)

def forward(tokens, norm_gain, query_weight, key_weight, value_weight, gate_weight, decay_down, decay_up, decay_bias, group_gain, out_weight, ffn_gain, ffn_gate, ffn_up, ffn_down):
    length = tokens.shape[0]
    normed = low(tokens * rms_scale(tokens) * norm_gain)
    query_rows = low_back(matmul(normed, query_weight.reshape(D, -1))).reshape(length, H, DKH) * DKH ** (-0.5)
    key_matrix_rows = low_back(matmul(normed, key_weight.reshape(D, -1))).reshape(length, H, DKH)
    value_matrix_rows = low_back(matmul(normed, value_weight.reshape(D, -1))).reshape(length, H, DVH)
    gate_pre = low_back(matmul(normed, gate_weight.reshape(D, -1))).reshape(length, H, DVH)
    low_rank = matmul(normed, decay_down)
    decay_arg = matmul(low_rank, decay_up.reshape(GR, -1)).reshape(length, H, DKH) + decay_bias
    rates = jax.nn.log_sigmoid(decay_arg) / 16.0
    mixed = mixer(query_rows, key_matrix_rows, value_matrix_rows, rates)
    gated = low(mixed * rms_scale(mixed) * group_gain * jax.nn.silu(gate_pre))
    attention = low_back(matmul(gated.reshape(length, -1), out_weight.reshape(-1, D)))
    resid = tokens + attention
    ffn_in = low(resid * rms_scale(resid) * ffn_gain)
    gate_val = low_back(matmul(ffn_in, ffn_gate))
    up_val = low_back(matmul(ffn_in, ffn_up))
    hidden = low(jax.nn.silu(gate_val) * up_val)
    return resid + low_back(matmul(hidden, ffn_down))

def reference(tokens, norm_gain, query_weight, key_weight, value_weight, gate_weight, decay_down, decay_up, decay_bias, group_gain, out_weight, ffn_gain, ffn_gate, ffn_up, ffn_down, cotangent):
    params = tuple((item.astype(jnp.float32) for item in (tokens, norm_gain, query_weight, key_weight, value_weight, gate_weight, decay_down, decay_up, decay_bias, group_gain, out_weight, ffn_gain, ffn_gate, ffn_up, ffn_down)))
    block_output, pullback = jax.vjp(forward, *params)
    grads = pullback(cotangent.astype(jnp.float32))
    return (block_output.astype(jnp.bfloat16), grads[0].astype(jnp.bfloat16), grads[1], grads[2], grads[3], grads[4], grads[5], grads[6], grads[7], grads[8], grads[9], grads[10], grads[11], grads[12], grads[13], grads[14])
```

```python
import functools

import jax
import jax.numpy as jnp
from jax import lax
from jax.experimental import pallas as pl
from jax.experimental.pallas import tpu as pltpu
from jax.sharding import PartitionSpec as P

MESH = pl.DeviceIdType.MESH
BF = jnp.bfloat16
F32 = jnp.float32
CB = 128
WAYS = 4
EPS = 1e-06
HIGH = lax.Precision.HIGHEST


def nn(a, b, precision=None):
    return lax.dot_general(
        a, b, (((1,), (0,)), ((), ())), precision=precision, preferred_element_type=F32
    )


def nt(a, b, precision=None):
    return lax.dot_general(
        a, b, (((1,), (1,)), ((), ())), precision=precision, preferred_element_type=F32
    )


def tn(a, b, precision=None):
    return lax.dot_general(
        a, b, (((0,), (0,)), ((), ())), precision=precision, preferred_element_type=F32
    )


def xor(index, d):
    if d == 1:
        return index + 1 - 2 * lax.rem(index, 2)
    if d == 2:
        return lax.rem(index + 2, 4)
    return 3 - index


def as_row(column):
    return jnp.broadcast_to(column, (column.shape[0], 128)).T[:8]


def as_column(row):
    return jnp.broadcast_to(row[:1], (128, row.shape[1])).T[:, :1]


def layer_kernel(
    n_seq,
    tok,
    cot,
    gains,
    wq,
    wk,
    ext,
    wv,
    wg,
    gge,
    dd,
    wo,
    fg,
    fu,
    fd,
    o_out,
    o_in,
    o_f,
    o_vg,
    o_qk,
    o_ext,
    o_ow,
    o_small,
    x_v,
    c_v,
    n_v,
    xr_v,
    dd_v,
    gain_v,
    qk_v,
    ext_v,
    v_v,
    g_v,
    gge_v,
    o_v,
    f_v,
    st_v,
    tt_v,
    bst_v,
    btt_v,
    ga_v,
    sgg,
    rgg,
    sst,
    rst,
    so,
    ro,
    sgf,
    rgf,
    sgn,
    rgn,
    snt,
    rnt,
    ao,
    oseg,
    ai,
    iseg,
    gw,
    pre,
    pres,
    rfw,
    fin_f,
    gv,
    prev,
    presv,
    rvg,
    mid_vg,
    perm_vg,
    fin_vg,
    gq,
    preq,
    presq,
    rqk,
    fin_qk,
    ge,
    preg,
    rge,
    fin_e,
    gow,
    preo,
    preso,
    row_,
    mid_ow,
    fin_ow,
    sm0,
    sm1,
    sm2,
    sm3,
    pick,
    gh_v,
    act_v,
    p_v,
    ss,
    rs,
    ls,
):
    s = lax.axis_index("seq")
    i = lax.axis_index("kax")
    j = lax.axis_index("vax")
    par = lax.rem(s, 2)
    oth = 1 - par
    T = x_v.shape[0]
    D = x_v.shape[1]
    half = D // 2
    W = WAYS
    mine = pl.ds(pl.multiple_of(par * half, half), half)
    other = pl.ds(pl.multiple_of(oth * half, half), half)
    partner = {"seq": s + 1 - 2 * par}
    kdev = [None] + [{"kax": xor(i, d)} for d in (1, 2, 3)]
    vdev = [None] + [{"vax": xor(j, d)} for d in (1, 2, 3)]
    ki = [None] + [xor(i, d) for d in (1, 2, 3)]
    vj = [None] + [xor(j, d) for d in (1, 2, 3)]
    seqdev = [{"seq": lax.rem(s + e, n_seq)} for e in range(1, n_seq)]
    flip = {"kax": j, "vax": i}

    count = [0, 0]
    sent = []

    def remote(src, dst, dev):
        n = count[0]
        count[0] += 1
        return pltpu.make_async_remote_copy(
            src_ref=src,
            dst_ref=dst,
            send_sem=ss.at[n],
            recv_sem=rs.at[n],
            device_id=dev,
            device_id_type=MESH,
        )

    def send(src, dst, dev):
        cp = remote(src, dst, dev)
        cp.start()
        sent.append(cp)
        return cp

    def load(src, dst):
        n = count[1]
        count[1] += 1
        cp = pltpu.make_async_copy(src, dst, ls.at[n])
        cp.start()
        return cp

    l_qk = [load(wq.at[j], qk_v.at[i, 0]), load(wk.at[j], qk_v.at[i, 1]), load(ext, ext_v.at[i])]
    l_x = [load(tok.at[pl.ds(pl.multiple_of(i * T, T), T)], x_v), load(gains, gain_v)]
    dd_v[16:, :] = jnp.zeros((dd_v.shape[0] - 16, D), BF)
    l_dd = load(dd, dd_v.at[pl.ds(0, 16)])
    l_v = load(wv.at[j], v_v.at[j])
    l_g = [load(wg.at[j], g_v.at[j]), load(gge, gge_v.at[j])]
    l_c = load(cot.at[pl.ds(pl.multiple_of(i * T, T), T)], c_v)
    l_f = [load(fg, f_v.at[0, i]), load(fu, f_v.at[1, i]), load(fd, f_v.at[2, i])]
    l_o = load(wo, o_v.at[i, j])

    barrier = pltpu.get_barrier_semaphore()
    for dev in kdev[1:] + vdev[1:] + seqdev:
        pl.semaphore_signal(barrier, inc=1, device_id=dev, device_id_type=MESH)

    others = 6 + len(seqdev)

    @pl.when(i != j)
    def _():
        pl.semaphore_signal(barrier, inc=1, device_id=flip, device_id_type=MESH)
        pl.semaphore_wait(barrier, others + 1)

    @pl.when(i == j)
    def _():
        pl.semaphore_wait(barrier, others)

    for cp in l_qk:
        cp.wait()
    t_qk = [None] + [send(qk_v.at[i, par], qk_v.at[i, par], kdev[d]) for d in (1, 2, 3)]
    t_ext = [None] + [send(ext_v.at[i], ext_v.at[i], kdev[d]) for d in (1, 2, 3)]
    t_v = [None] + [
        send(wv.at[vj[d], :, mine], v_v.at[j, :, mine], vdev[d]) for d in (1, 2, 3)
    ]

    for cp in l_x:
        cp.wait()
    x = x_v[...].astype(F32)
    g1 = gain_v[0:1, :]
    g3 = gain_v[1:2, :]
    r1 = lax.rsqrt(jnp.sum(x * x, axis=1, keepdims=True) / D + EPS)
    n_v[...] = (x * r1 * g1).astype(BF)
    l_dd.wait()
    lane = lax.broadcasted_iota(jnp.int32, (T, 128), 1)
    lrp = jnp.where(lane == 16, 1.0, nt(n_v[...], dd_v[...]))
    xr_v[...] = (x * (r1 * r1 * r1)).astype(BF).T

    f_qk = []
    for d in (1, 2, 3):
        t_qk[d].wait_recv()
        f_qk.append(send(qk_v.at[ki[d], par], qk_v.at[ki[d], par], partner))
    t_f = []
    for d in (1, 2, 3):
        t_f.append(
            [
                send(w.at[:, mine], f_v.at[n, i, :, mine], kdev[d])
                for n, w in enumerate((fg, fu, fd))
            ]
        )
    for d in (1, 2, 3):
        t_ext[d].wait_recv()
    for cp in f_qk:
        cp.wait_recv()
    normed = n_v[...]
    wq_all = qk_v[:, 0].reshape(W * 32, D)
    wk_all = qk_v[:, 1].reshape(W * 32, D)
    ext_all = ext_v[...].reshape(W * 32, 128)
    scale = 128.0 ** (-0.5)
    q = nt(normed, wq_all) * scale
    k = nt(normed, wk_all)
    arg = nt(lrp, ext_all.astype(F32), HIGH)
    rates = (jnp.minimum(arg, 0.0) - jnp.log1p(jnp.exp(-jnp.abs(arg)))) / 16.0
    row_id = lax.broadcasted_iota(jnp.int32, (CB, CB), 0)
    col_id = lax.broadcasted_iota(jnp.int32, (CB, CB), 1)
    causal = row_id >= col_id
    tri = jnp.where(causal, 1.0, 0.0)
    nblk = T // CB
    blk = [slice(c * CB, (c + 1) * CB) for c in range(nblk)]
    e1, e2, em, el, dec, qd, kd, qi, ke, score = [], [], [], [], [], [], [], [], [], []
    for c in range(nblk):
        cum = nn(tri, rates[blk[c]], HIGH)
        mid = cum[CB // 2 - 1 : CB // 2]
        last = cum[CB - 1 : CB]
        e1.append(jnp.exp(cum - mid))
        e2.append(jnp.exp(mid - cum))
        em.append(jnp.exp(mid))
        el.append(jnp.exp(last - mid))
        dec.append(jnp.exp(last))
        a = q[blk[c]] * e1[c]
        b = k[blk[c]] * e2[c]
        qd.append(a.astype(BF))
        kd.append(b.astype(BF))
        qi.append((a * em[c]).astype(BF))
        ke.append((b * el[c]).astype(BF))
        score.append(jnp.where(causal, nt(qd[c], kd[c]), 0.0).astype(BF))

    l_v.wait()
    f_vv = []
    for d in (1, 2, 3):
        t_v[d].wait_recv()
        f_vv.append(send(v_v.at[vj[d], :, mine], v_v.at[vj[d], :, mine], partner))
    t_g = [None] + [
        send(wg.at[vj[d], :, mine], g_v.at[j, :, mine], vdev[d]) for d in (1, 2, 3)
    ]
    t_gge = [None] + [send(gge, gge_v.at[j], vdev[d]) for d in (1, 2, 3)]
    t_o = [None] + [
        send(wo.at[:, mine], o_v.at[i, j, :, mine], vdev[d]) for d in (1, 2, 3)
    ]
    for cp in f_vv:
        cp.wait_recv()
    wv_all = v_v[...].reshape(W * 64, D)
    v = nt(normed, wv_all).astype(BF)
    up = [tn(v[blk[c]], ke[c]) for c in range(nblk)]
    loc = up[0]
    locd = dec[0]
    for c in range(1, nblk):
        loc = loc * dec[c] + up[c]
        locd = locd * dec[c]
    VC = loc.shape[0]
    st_v[i, :VC] = loc.astype(BF)
    st_v[i, VC:] = jnp.broadcast_to(locd, (16, 128)).astype(BF)
    t_st = [send(st_v.at[i], st_v.at[i], kdev[d]) for d in (1, 2, 3)]
    mixed = [nn(score[c], v[blk[c]]) for c in range(nblk)]

    f_g = []
    for cp in l_g:
        cp.wait()
    for d in (1, 2, 3):
        t_g[d].wait_recv()
        f_g.append(send(g_v.at[vj[d], :, mine], g_v.at[vj[d], :, mine], partner))

    def entering(slots, totals, back):
        order = range(W - 1, -1, -1) if back else range(W)
        pre_s = jnp.zeros((VC, 128), F32)
        pre_d = jnp.ones((1, 128), F32)
        tot_s = jnp.zeros((VC, 128), F32)
        tot_d = jnp.ones((1, 128), F32)
        for other_i in order:
            one_s = slots[other_i, :VC].astype(F32)
            one_d = slots[other_i, VC : VC + 1].astype(F32)
            use = (other_i > i) if back else (other_i < i)
            pre_s = jnp.where(use, pre_s * one_d + one_s, pre_s)
            pre_d = jnp.where(use, pre_d * one_d, pre_d)
            tot_s = tot_s * one_d + one_s
            tot_d = tot_d * one_d
        totals[s, :VC] = tot_s.astype(BF)
        totals[s, VC:] = jnp.broadcast_to(tot_d, (16, 128)).astype(BF)
        moves = [send(totals.at[s], totals.at[s], dev) for dev in seqdev]
        for cp in moves:
            cp.wait_recv()
        order = range(n_seq - 1, -1, -1) if back else range(n_seq)
        far = jnp.zeros((VC, 128), F32)
        for other_s in order:
            one_s = totals[other_s, :VC].astype(F32)
            one_d = totals[other_s, VC : VC + 1].astype(F32)
            use = (other_s > s) if back else (other_s < s)
            far = jnp.where(use, far * one_d + one_s, far)
        return pre_s + pre_d * far

    for cp in t_st:
        cp.wait_recv()
    start = [entering(st_v, tt_v, False)]
    for c in range(nblk):
        start.append(start[c] * dec[c] + up[c])
    start_low = [a.astype(BF) for a in start]
    for c in range(nblk):
        mixed[c] = mixed[c] + nt(qi[c], start_low[c])
    mix = jnp.concatenate(mixed, axis=0)
    r2 = lax.rsqrt(jnp.sum(mix * mix, axis=1, keepdims=True) / VC + EPS)
    normal = mix * r2
    for cp in f_g:
        cp.wait_recv()
    for d in (1, 2, 3):
        t_gge[d].wait_recv()
    wg_all = g_v[...].reshape(W * 64, D)
    gate = nt(normed, wg_all)
    gg = gge_v[...].astype(F32).reshape(W * 64, 128).T[:1]
    sig = 1.0 / (1.0 + jnp.exp(-gate))
    act = gate * sig
    dact = sig + act * (1.0 - sig)
    ga_v[j] = (normal * gg * act).astype(BF)
    t_ga = [send(ga_v.at[j], ga_v.at[j], vdev[d]) for d in (1, 2, 3)]
    act_v[0] = act
    act_v[1] = dact
    act_v[2] = normal

    l_o.wait()
    for d in (1, 2, 3):
        t_o[d].wait_recv()
    t_o2 = [None] + [
        send(o_v.at[i, :, :, mine], o_v.at[i, :, :, mine], kdev[d]) for d in (1, 2, 3)
    ]
    f_o = [
        send(o_v.at[i, vj[d], :, mine], o_v.at[i, vj[d], :, mine], partner) for d in (1, 2, 3)
    ]
    for cp in l_f:
        cp.wait()
    f_f = []
    for d in (1, 2, 3):
        for cp in t_f[d - 1]:
            cp.wait_recv()
        f_f.append(send(f_v.at[:, ki[d], :, mine], f_v.at[:, ki[d], :, mine], partner))
    l_c.wait()
    for cp in f_f:
        cp.wait_recv()
    FB = f_v.shape[2]
    gT = f_v[0].reshape(W * FB, D)
    uT = f_v[1].reshape(W * FB, D)
    dn = f_v[2].reshape(W * FB, D)
    gh_v[...] = nt(c_v[...], dn)
    for d in (1, 2, 3):
        t_o2[d].wait_recv()
        f_o.append(
            send(o_v.at[ki[d], :, :, mine], o_v.at[ki[d], :, :, mine], partner)
        )
    for cp in t_ga:
        cp.wait_recv()
    for cp in f_o:
        cp.wait_recv()
    att = nn(ga_v[0], o_v[0].reshape(W * 64, D))
    for h in range(1, W):
        att = att + nn(ga_v[h], o_v[h].reshape(W * 64, D))
    resid = x_v[...].astype(F32) + att
    r3 = lax.rsqrt(jnp.sum(resid * resid, axis=1, keepdims=True) / D + EPS)
    fin = (resid * r3 * g3).astype(BF)

    gval = nt(fin, gT)
    uval = nt(fin, uT)
    fsig = 1.0 / (1.0 + jnp.exp(-gval))
    fact = gval * fsig
    hid = (fact * uval).astype(BF)
    gh = gh_v[...]
    gup = (gh * fact).astype(BF)
    ggate = (gh * uval * (fsig + fact * (1.0 - fsig))).astype(BF)
    part = nn(ggate, gT) + nn(gup, uT)
    p_v[...] = part
    ow_flat = o_v[...].reshape(W * W * 64, D)
    ggp = nt((part * g3).astype(BF), ow_flat)
    for h in range(W):
        sgg[h] = ggp[:, h * VC : (h + 1) * VC].astype(BF)
    t_gg = [send(sgg.at[vj[d]], rgg.at[d], vdev[d]) for d in (1, 2, 3)]
    m3p = jnp.sum(resid * g3 * part, axis=1, keepdims=True)
    sst[...] = as_row(m3p)
    t_m3 = [send(sst, rst.at[d], vdev[d]) for d in (1, 2, 3)]

    feature = lax.broadcasted_iota(jnp.int32, (1, D), 1)
    own_slab = jnp.where(lax.rem(feature // 64, W) == j, 1.0, 0.0)
    own_run = jnp.where(feature // (D // W) == j, 1.0, 0.0)
    outp = nn(hid, dn) + own_slab * resid
    so[...] = outp.astype(BF).T.reshape(W, W, 64, T)
    t_out = [send(so.at[:, vj[d]], ro.at[d], vdev[d]) for d in (1, 2, 3)]
    ffn_gain = jnp.sum(part * resid * r3, axis=0, keepdims=True)

    gw[0] = tn(ggate, fin).astype(BF).reshape(W, FB, D)
    gw[1] = tn(gup, fin).astype(BF).reshape(W, FB, D)
    gw[2] = tn(hid, c_v[...]).astype(BF).reshape(W, FB, D)
    t_pre = send(gw.at[:, :, :, other], pre, partner)

    for cp in t_m3:
        cp.wait_recv()
    m3 = as_column(sst[...] + rst[1] + rst[2] + rst[3]) / D
    base = c_v[...].astype(F32) - resid * (r3 * r3 * r3 * m3)
    direct = nt(base.astype(BF), o_v[j].reshape(W * 64, D))
    for cp in t_gg:
        cp.wait_recv()
    ggs = sgg[j].astype(F32) + rgg[1].astype(F32) + rgg[2].astype(F32) + rgg[3].astype(F32)
    ggrad = direct + r3 * ggs
    act = act_v[0]
    normal = act_v[2]
    dgate = (ggrad * normal * gg * act_v[1]).astype(BF)
    gs = ggrad * act
    group = jnp.sum(gs * normal, axis=0, keepdims=True)
    gnm = gs * gg
    gmix = (r2 * (gnm - normal * (jnp.sum(normal * gnm, axis=1, keepdims=True) / VC))).astype(BF)

    qst = [tn(gmix[blk[c]], qi[c]) for c in range(nblk)]
    bloc = qst[nblk - 1]
    for c in range(nblk - 2, -1, -1):
        bloc = bloc * dec[c] + qst[c]
    bst_v[i, :VC] = bloc.astype(BF)
    bst_v[i, VC:] = jnp.broadcast_to(locd, (16, 128)).astype(BF)
    t_bst = [send(bst_v.at[i], bst_v.at[i], kdev[d]) for d in (1, 2, 3)]

    full = p_v[...] * (g3 * r3)
    mixed_in = full + own_run * base
    for h in range(W):
        sgf[h] = mixed_in[:, h * (D // W) : (h + 1) * (D // W)].astype(BF)
    t_gf = [send(sgf.at[vj[d]], rgf.at[d], vdev[d]) for d in (1, 2, 3)]
    gv[1] = tn(dgate, normed).astype(BF).reshape(W, 64, D)
    dscore, dq_in, dk_in, dv_in = [], [], [], []
    for c in range(nblk):
        ds = jnp.where(causal, nt(gmix[blk[c]], v[blk[c]]), 0.0).astype(BF)
        dq_in.append(nn(ds, kd[c]) + em[c] * nn(gmix[blk[c]], start_low[c]))
        dk_in.append(tn(ds, qd[c]))
        dv_in.append(tn(score[c], gmix[blk[c]]))
    t_pre.wait_recv()
    for n in range(3):
        pres[n] = (gw[n, :, :, mine].astype(F32) + pre[n].astype(F32)).astype(BF)
    for cp in t_bst:
        cp.wait_recv()
    after = [None] * nblk
    after[nblk - 1] = entering(bst_v, btt_v, True)
    for c in range(nblk - 2, -1, -1):
        after[c] = after[c + 1] * dec[c + 1] + qst[c + 1]
    t_fw = [send(pres.at[:, ki[d]], rfw.at[d], kdev[d]) for d in (1, 2, 3)]

    ql, kl, vl, ga = [], [], [], []
    for c in range(nblk):
        low_after = after[c].astype(BF)
        dq = e1[c] * dq_in[c]
        dk = e2[c] * (dk_in[c] + el[c] * nn(v[blk[c]], low_after))
        dv = dv_in[c] + nt(ke[c], low_after)
        gc = q[blk[c]] * dq - k[blk[c]] * dk
        extra = jnp.sum(after[c] * start[c + 1], axis=0, keepdims=True)
        gc = jnp.where(row_id == CB - 1, gc + extra, gc)
        gr = tn(tri, gc, HIGH)
        a = arg[blk[c]]
        ga.append(gr / (1.0 + jnp.exp(a)) / 16.0)
        ql.append((dq * scale).astype(BF))
        kl.append(dk.astype(BF))
        vl.append(dv.astype(BF))
    ql = jnp.concatenate(ql, axis=0)
    kl = jnp.concatenate(kl, axis=0)
    vl = jnp.concatenate(vl, axis=0)
    ga = jnp.concatenate(ga, axis=0).astype(BF)
    glr = nn(ga, ext_all).astype(BF)
    gn = nn(ql, wq_all) + nn(kl, wk_all) + nn(vl, wv_all) + nn(dgate, wg_all) + nn(glr, dd_v[...])
    x = x_v[...].astype(F32)
    gnx = gn * x
    snt[...] = as_row(jnp.sum(gnx * g1, axis=1, keepdims=True))
    t_m1 = [send(snt, rnt.at[d], vdev[d]) for d in (1, 2, 3)]
    whole = gn * (r1 * g1) + full + own_slab * base
    sgn[...] = whole.astype(BF).T.reshape(W, W, 64, T)
    t_gn = [send(sgn.at[:, vj[d]], rgn.at[d], vdev[d]) for d in (1, 2, 3)]

    norm_gain = jnp.sum(gnx * r1, axis=0, keepdims=True)
    small = tn(glr, normed)[:16]
    rid = lax.broadcasted_iota(jnp.int32, (16, D), 0)
    wide = jnp.concatenate([group, jnp.zeros((1, D - VC), F32)], axis=1)
    rest = jnp.where(rid == 0, norm_gain, jnp.where(rid == 1, ffn_gain, jnp.where(rid == 2, wide, 0.0)))
    sm0[:16] = small.astype(BF)
    sm0[16:] = rest.astype(BF)
    t_s0 = [send(sm0, sm1.at[d], vdev[d]) for d in (1, 2, 3)]

    gv[0] = tn(vl, normed).astype(BF).reshape(W, 64, D)
    gq[:, 0] = tn(ql, normed).astype(BF).reshape(W, 32, D)
    gq[:, 1] = tn(kl, normed).astype(BF).reshape(W, 32, D)
    ge[...] = tn(ga, lrp.astype(BF)).reshape(W, 32, 128)
    t_pv = send(gv.at[:, :, :, other], prev, partner)
    t_pq = send(gq.at[:, oth], preq, partner)
    t_ge = send(ge, preg, partner)
    t_pv.wait_recv()
    for n in range(2):
        presv[n] = (gv[n, :, :, mine].astype(F32) + prev[n].astype(F32)).astype(BF)
    t_vg = [send(presv.at[:, ki[d]], rvg.at[d], kdev[d]) for d in (1, 2, 3)]
    t_pq.wait_recv()
    presq[...] = (gq[:, par].astype(F32) + preq[...].astype(F32)).astype(BF)
    t_qk2 = [send(presq.at[ki[d]], rqk.at[d], kdev[d]) for d in (1, 2, 3)]
    t_ge.wait_recv()
    preg[...] = ge[...] + preg[...]
    t_ge2 = [send(preg.at[ki[d]], rge.at[d], kdev[d]) for d in (1, 2, 3)]

    for cp in t_gf:
        cp.wait_recv()
    gatt = (
        sgf[j].astype(F32) + rgf[1].astype(F32) + rgf[2].astype(F32) + rgf[3].astype(F32)
    ).astype(BF)
    for h in range(W):
        gow[h] = tn(ga_v[h], gatt).astype(BF).reshape(W, 64, D // W)
    qtr = D // W // 2
    t_po = send(
        gow.at[:, :, :, pl.ds(pl.multiple_of(oth * qtr, qtr), qtr)], preo, partner
    )

    for cp in t_out:
        cp.wait_recv()
    ao[...] = (
        so[:, j].astype(F32) + ro[1].astype(F32) + ro[2].astype(F32) + ro[3].astype(F32)
    ).astype(BF)
    oseg[i] = ao[i]
    t_ao = [send(ao.at[ki[d]], oseg.at[i], kdev[d]) for d in (1, 2, 3)]
    t_po.wait_recv()
    preso[...] = (
        gow[:, :, :, pl.ds(pl.multiple_of(par * qtr, qtr), qtr)].astype(F32)
        + preo[...].astype(F32)
    ).astype(BF)
    t_ow = [send(preso.at[ki[d]], row_.at[d], kdev[d]) for d in (1, 2, 3)]

    for cp in t_m1:
        cp.wait_recv()
    m1 = (snt[:1] + rnt[1, :1] + rnt[2, :1] + rnt[3, :1]) / D
    for cp in t_gn:
        cp.wait_recv()
    xr = xr_v[...].reshape(W, W, 64, T)
    for h in range(W):
        here = (
            sgn[h, j].astype(F32)
            + rgn[1, h].astype(F32)
            + rgn[2, h].astype(F32)
            + rgn[3, h].astype(F32)
        )
        at = pl.ds(pl.multiple_of((h * W + j) * 64, 64), 64)
        ai[h] = (here - xr_v[at, :].astype(F32) * m1).astype(BF)
    iseg[i] = ai[i]
    t_ai = [send(ai.at[ki[d]], iseg.at[i], kdev[d]) for d in (1, 2, 3)]

    for cp in t_vg:
        cp.wait_recv()
    mid_vg[...] = (
        presv[:, i].astype(F32)
        + rvg[1].astype(F32)
        + rvg[2].astype(F32)
        + rvg[3].astype(F32)
    ).astype(BF)
    t_flip = remote(mid_vg, perm_vg, flip)

    @pl.when(i != j)
    def _():
        t_flip.start()

    for cp in t_qk2 + t_ge2:
        cp.wait_recv()
    fin_qk[par] = (
        presq[i].astype(F32)
        + rqk[1].astype(F32)
        + rqk[2].astype(F32)
        + rqk[3].astype(F32)
    ).astype(BF)
    t_fq = send(fin_qk.at[par], fin_qk.at[par], partner)
    fin_e[...] = preg[i] + rge[1] + rge[2] + rge[3]

    for cp in t_ow:
        cp.wait_recv()
    mid_ow[...] = (
        preso[i].astype(F32)
        + row_[1].astype(F32)
        + row_[2].astype(F32)
        + row_[3].astype(F32)
    ).astype(BF)
    fin_ow[par, j] = mid_ow[j]
    t_mo = [send(mid_ow.at[vj[d]], fin_ow.at[par, j], vdev[d]) for d in (1, 2, 3)]

    for cp in t_s0:
        cp.wait_recv()
    sm2[0] = (
        sm0[...].astype(F32)
        + sm1[1].astype(F32)
        + sm1[2].astype(F32)
        + sm1[3].astype(F32)
    ).astype(BF)
    t_s1 = [send(sm2.at[0], sm2.at[d], kdev[d]) for d in (1, 2, 3)]

    for cp in t_fw:
        cp.wait_recv()
    for n in range(3):
        fin_f[par, n] = (
            pres[n, i].astype(F32)
            + rfw[1, n].astype(F32)
            + rfw[2, n].astype(F32)
            + rfw[3, n].astype(F32)
        ).astype(BF)
    t_ff = send(fin_f.at[par], fin_f.at[par], partner)

    for cp in t_s1:
        cp.wait_recv()
    sm3[0] = (
        sm2[0].astype(F32)
        + sm2[1].astype(F32)
        + sm2[2].astype(F32)
        + sm2[3].astype(F32)
    ).astype(BF)
    t_s2 = send(sm3.at[0], sm3.at[1], partner)

    @pl.when(i != j)
    def _():
        t_flip.wait_recv()
        fin_vg[par] = perm_vg[...]

    @pl.when(i == j)
    def _():
        fin_vg[par] = mid_vg[...]

    t_fv = send(fin_vg.at[par], fin_vg.at[par], partner)
    for cp in t_mo:
        cp.wait_recv()
    t_fo = send(fin_ow.at[par], fin_ow.at[par], partner)

    outs = []
    for cp in t_ao:
        cp.wait_recv()
    outs.append(load(oseg, o_out))
    t_fq.wait_recv()
    outs.append(load(fin_qk, o_qk))
    outs.append(load(fin_e, o_ext))
    t_ff.wait_recv()
    outs.append(load(fin_f, o_f))
    t_s2.wait_recv()
    tot = sm3[0].astype(F32) + sm3[1].astype(F32)
    pick[...] = tot
    outs.append(load(pick, o_small))
    for cp in t_ai:
        cp.wait_recv()
    outs.append(load(iseg, o_in))
    t_fv.wait_recv()
    outs.append(load(fin_vg, o_vg))
    t_fo.wait_recv()
    outs.append(load(fin_ow, o_ow))
    for cp in outs:
        cp.wait()
    for cp in sent:
        cp.wait_send()

    @pl.when(i != j)
    def _():
        t_flip.wait_send()


N_REMOTE = 200
N_LOCAL = 40


def layer(n_seq, args):
    tok = args[0]
    rows, D = tok.shape
    T = rows // WAYS
    FB = args[11].shape[0]
    W = WAYS
    VC = W * 64
    half = D // 2
    qtr = D // W // 2

    def sds(shape, dtype=BF):
        return jax.ShapeDtypeStruct(shape, dtype)

    def vm(shape, dtype=BF):
        return pltpu.VMEM(shape, dtype)

    outs = [
        sds((W, 64, T)),
        sds((W, 64, T)),
        sds((2, 3, FB, half)),
        sds((2, 2, 64, half)),
        sds((2, 32, D)),
        sds((32, 128), F32),
        sds((2, W, 64, qtr)),
        sds((32, D), F32),
    ]
    scratch = [
        vm((T, D)),
        vm((T, D)),
        vm((T, D)),
        vm((D, T)),
        vm((128, D)),
        vm((8, D), F32),
        vm((W, 2, 32, D)),
        vm((W, 32, 128)),
        vm((W, 64, D)),
        vm((W, 64, D)),
        vm((W, 64, 128)),
        vm((W, W, 64, D)),
        vm((3, W, FB, D)),
        vm((W, VC + 16, 128)),
        vm((n_seq, VC + 16, 128)),
        vm((W, VC + 16, 128)),
        vm((n_seq, VC + 16, 128)),
        vm((W, T, VC)),
        vm((W, T, VC)),
        vm((W, T, VC)),
        vm((8, T), F32),
        vm((W, 8, T), F32),
        vm((W, W, 64, T)),
        vm((W, W, 64, T)),
        vm((W, T, D // W)),
        vm((W, T, D // W)),
        vm((W, W, 64, T)),
        vm((W, W, 64, T)),
        vm((8, T), F32),
        vm((W, 8, T), F32),
        vm((W, 64, T)),
        vm((W, 64, T)),
        vm((W, 64, T)),
        vm((W, 64, T)),
        vm((3, W, FB, D)),
        vm((3, W, FB, half)),
        vm((3, W, FB, half)),
        vm((W, 3, FB, half)),
        vm((2, 3, FB, half)),
        vm((2, W, 64, D)),
        vm((2, W, 64, half)),
        vm((2, W, 64, half)),
        vm((W, 2, 64, half)),
        vm((2, 64, half)),
        vm((2, 64, half)),
        vm((2, 2, 64, half)),
        vm((W, 2, 32, D)),
        vm((W, 32, D)),
        vm((W, 32, D)),
        vm((W, 32, D)),
        vm((2, 32, D)),
        vm((W, 32, 128), F32),
        vm((W, 32, 128), F32),
        vm((W, 32, 128), F32),
        vm((32, 128), F32),
        vm((W, W, 64, D // W)),
        vm((W, W, 64, qtr)),
        vm((W, W, 64, qtr)),
        vm((W, W, 64, qtr)),
        vm((W, 64, qtr)),
        vm((2, W, 64, qtr)),
        vm((32, D)),
        vm((W, 32, D)),
        vm((W, 32, D)),
        vm((2, 32, D)),
        vm((32, D), F32),
        vm((T, W * FB), F32),
        vm((3, T, VC), F32),
        vm((T, D), F32),
        pltpu.SemaphoreType.DMA((N_REMOTE,)),
        pltpu.SemaphoreType.DMA((N_REMOTE,)),
        pltpu.SemaphoreType.DMA((N_LOCAL,)),
    ]
    return pl.pallas_call(
        functools.partial(layer_kernel, n_seq),
        out_shape=outs,
        in_specs=[pl.BlockSpec(memory_space=pl.ANY)] * len(args),
        out_specs=[pl.BlockSpec(memory_space=pl.ANY)] * len(outs),
        scratch_shapes=scratch,
        compiler_params=pltpu.CompilerParams(
            collective_id=0, has_side_effects=True, vmem_limit_bytes=60 * 2**20
        ),
        name="layer",
    )(*args)


def finish_kernel(
    o_out, o_in, o_f, o_vg, o_qk, o_ow, r_out, r_in, r_fg, r_fu, r_fd, r_v, r_g, r_q, r_k, r_o
):
    T = o_out.shape[2]
    for h in range(WAYS):
        r_out[:, h * T : (h + 1) * T] = o_out[h]
        r_in[:, h * T : (h + 1) * T] = o_in[h]
    half = o_f.shape[3]
    for h in range(2):
        at = slice(h * half, (h + 1) * half)
        for n, r in enumerate((r_fg, r_fu, r_fd)):
            r[:, at] = o_f[h, n].astype(F32)
        for n, r in enumerate((r_v, r_g)):
            r[:, at] = o_vg[h, n].astype(F32)
    r_q[...] = o_qk[0].astype(F32)
    r_k[...] = o_qk[1].astype(F32)
    qtr = o_ow.shape[3]
    for z in range(WAYS):
        for h in range(2):
            at = (2 * z + h) * qtr
            r_o[:, at : at + qtr] = o_ow[h, z].astype(F32)


def finish(parts):
    rows = parts[0].shape[0] * parts[0].shape[2]
    D = 2 * parts[2].shape[3]
    FB = parts[2].shape[2]

    def sds(shape, dtype=F32):
        return jax.ShapeDtypeStruct(shape, dtype)

    outs = [
        sds((64, rows), BF),
        sds((64, rows), BF),
        sds((FB, D)),
        sds((FB, D)),
        sds((FB, D)),
        sds((64, D)),
        sds((64, D)),
        sds((32, D)),
        sds((32, D)),
        sds((64, D)),
    ]
    return pl.pallas_call(
        finish_kernel,
        out_shape=outs,
        in_specs=[pl.BlockSpec(memory_space=pltpu.VMEM)] * len(parts),
        out_specs=[pl.BlockSpec(memory_space=pltpu.VMEM)] * len(outs),
        compiler_params=pltpu.CompilerParams(vmem_limit_bytes=32 * 2**20),
        name="finish",
    )(*parts)


def shards(
    n_seq,
    tokens,
    norm_gain,
    query_weight,
    key_weight,
    value_weight,
    gate_weight,
    decay_down,
    decay_up,
    decay_bias,
    group_gain,
    out_weight,
    ffn_gain,
    ffn_gate,
    ffn_up,
    ffn_down,
    cotangent,
):
    D = tokens.shape[1]
    i = lax.axis_index("kax")
    j = lax.axis_index("vax")
    pair = i * WAYS + j
    gains = jnp.concatenate(
        [norm_gain[None], ffn_gain[None], jnp.zeros((6, D), BF)], axis=0
    ).astype(F32)
    up_here = lax.dynamic_index_in_dim(decay_up, j, 1, False).T
    bias_here = lax.dynamic_index_in_dim(decay_bias, j, 0, False)[:, None]
    ext = jnp.concatenate(
        [up_here, bias_here, jnp.zeros((32, 128 - up_here.shape[1] - 1), BF)], axis=1
    )
    gge = jnp.broadcast_to(group_gain[:, None], (64, 128))
    parts = layer(
        n_seq,
        (
            tokens,
            cotangent,
            gains,
            query_weight.transpose(1, 2, 0),
            key_weight.transpose(1, 2, 0),
            ext,
            value_weight.transpose(1, 2, 0),
            gate_weight.transpose(1, 2, 0),
            gge,
            decay_down.T,
            out_weight[0],
            ffn_gate.T,
            ffn_up.T,
            ffn_down,
        ),
    )
    o_out, o_in, o_f, o_vg, o_qk, o_ext, o_ow, o_small = parts
    if n_seq > 2:

        def over_pairs(a):
            return jnp.sum(lax.all_gather(a, "seq")[::2].astype(F32), axis=0).astype(a.dtype)

        o_f, o_vg, o_qk, o_ext, o_ow, o_small = (
            over_pairs(a) for a in (o_f, o_vg, o_qk, o_ext, o_ow, o_small)
        )
    r_out, r_in, r_fg, r_fu, r_fd, r_v, r_g, r_q, r_k, r_o = finish(
        (o_out, o_in, o_f, o_vg, o_qk, o_ow)
    )
    slab = D // (WAYS * WAYS)
    norm_gain_grad = lax.dynamic_slice(o_small, (16, pair * slab), (1, slab))[0]
    ffn_gain_grad = lax.dynamic_slice(o_small, (17, pair * slab), (1, slab))[0]
    group_gain_grad = lax.dynamic_slice(o_small, (18, j * 64), (1, 64))[0]
    decay_down_grad = lax.dynamic_slice(o_small, (pair, 0), (1, D)).T
    decay_up_grad = o_ext[:, :16].T[:, None, :]
    decay_bias_grad = o_ext[:, 16][None, :]
    return (
        r_out.T,
        r_in.T,
        norm_gain_grad,
        r_q.T[:, None, :],
        r_k.T[:, None, :],
        r_v.T[:, None, :],
        r_g.T[:, None, :],
        decay_down_grad,
        decay_up_grad,
        decay_bias_grad,
        group_gain_grad,
        r_o[None],
        ffn_gain_grad,
        r_fg.T,
        r_fu.T,
        r_fd,
    )


def solution(mesh):
    in_specs = (
        P("seq", None),
        P(),
        P(None, None, "kax"),
        P(None, None, "kax"),
        P(None, None, "vax"),
        P(None, None, "vax"),
        P(),
        P(None, None, "kax"),
        P(None, "kax"),
        P("vax"),
        P("kax", "vax", None),
        P(),
        P(None, ("kax", "vax")),
        P(None, ("kax", "vax")),
        P(("kax", "vax"), None),
        P("seq", None),
    )
    out_specs = (
        P("seq", ("kax", "vax")),
        P("seq", ("kax", "vax")),
        P(("kax", "vax")),
        P(None, "vax", "kax"),
        P(None, "vax", "kax"),
        P(None, "kax", "vax"),
        P(None, "kax", "vax"),
        P(None, ("kax", "vax")),
        P(None, "vax", "kax"),
        P("vax", "kax"),
        P("vax"),
        P("kax", "vax", None),
        P(("kax", "vax")),
        P(None, ("kax", "vax")),
        P(None, ("kax", "vax")),
        P(("kax", "vax"), None),
    )
    return jax.shard_map(
        functools.partial(shards, mesh.shape["seq"]),
        mesh=mesh,
        in_specs=in_specs,
        out_specs=out_specs,
        check_vma=False,
    )
```

```python
import functools

import jax
import jax.numpy as jnp
from jax import lax
from jax.experimental import pallas as pl
from jax.experimental.pallas import tpu as pltpu
from jax.sharding import PartitionSpec as P

MESH = pl.DeviceIdType.MESH
BF = jnp.bfloat16
F32 = jnp.float32
CB = 128
WAYS = 4
EPS = 1e-06
HIGH = lax.Precision.HIGHEST


def nn(a, b, precision=None):
    return lax.dot_general(
        a, b, (((1,), (0,)), ((), ())), precision=precision, preferred_element_type=F32
    )


def nt(a, b, precision=None):
    return lax.dot_general(
        a, b, (((1,), (1,)), ((), ())), precision=precision, preferred_element_type=F32
    )


def tn(a, b, precision=None):
    return lax.dot_general(
        a, b, (((0,), (0,)), ((), ())), precision=precision, preferred_element_type=F32
    )


def xor(index, d):
    if d == 1:
        return index + 1 - 2 * lax.rem(index, 2)
    if d == 2:
        return lax.rem(index + 2, 4)
    return 3 - index


def as_row(column):
    return jnp.broadcast_to(column, (column.shape[0], 128)).T[:8]


def as_column(row):
    return jnp.broadcast_to(row[:1], (128, row.shape[1])).T[:, :1]


def flat_row(block):
    return jnp.concatenate([block[r : r + 1] for r in range(block.shape[0])], axis=1)


def lanes(block):
    return jnp.concatenate([block[n] for n in range(block.shape[0])], axis=1)


def total(own, got):
    out = own.astype(F32)
    for d in (1, 2, 3):
        out = out + got[d].astype(F32)
    return out


def layer_kernel(
    n_seq,
    tok,
    cot,
    ng,
    ffg,
    dup,
    dbi,
    ggn,
    wq,
    wk,
    wv,
    wg,
    dd,
    wo,
    fg,
    fu,
    fd,
    o_out,
    o_in,
    o_f,
    o_d,
    o_vg,
    o_qk,
    o_ext,
    o_ow,
    o_small,
    x_v,
    c_v,
    x_all,
    c_all,
    n_all,
    n_v,
    xr_v,
    dd_v,
    ng_v,
    ffg_v,
    dup_v,
    dbi_v,
    ggn_v,
    sq_v,
    gain_v,
    qk_v,
    ext_v,
    v_v,
    g_v,
    gge_v,
    o_v,
    f_v,
    st_v,
    tt_v,
    bst_v,
    btt_v,
    ga_v,
    sgg,
    rgg,
    sst,
    rst,
    so,
    ro,
    sgn,
    rgn,
    ao,
    oseg,
    ai,
    iseg,
    hd,
    hseg,
    gw,
    pre,
    pres,
    rfw,
    fin_f,
    dsum,
    gow,
    preo,
    preso,
    rowk,
    mid_o,
    rowz,
    fin_ow,
    vz,
    zvg,
    kvg,
    vgsum,
    qka,
    kqa,
    qksum,
    esum,
    sm0,
    sm1,
    sm2,
    sm3,
    sm4,
    pick,
    small_v,
    gh_v,
    act_v,
    p_v,
    ss,
    rs,
    ls,
):
    s = lax.axis_index("seq")
    i = lax.axis_index("kax")
    j = lax.axis_index("vax")
    par = lax.rem(s, 2)
    oth = 1 - par
    T, D = x_v.shape
    rows = x_all.shape[0]
    FB = f_v.shape[2]
    half = D // 2
    W = WAYS
    DIRS = (1, 2, 3)
    mine = pl.ds(pl.multiple_of(par * half, half), half)
    other = pl.ds(pl.multiple_of(oth * half, half), half)
    partner = {"seq": s + 1 - 2 * par}
    kdev = [None] + [{"kax": xor(i, d)} for d in DIRS]
    vdev = [None] + [{"vax": xor(j, d)} for d in DIRS]
    ki = [None] + [xor(i, d) for d in DIRS]
    vj = [None] + [xor(j, d) for d in DIRS]
    seqdev = [{"seq": lax.rem(s + e, n_seq)} for e in range(1, n_seq)]

    count = [0, 0]
    sent = []

    def remote(src, dst, dev):
        n = count[0]
        count[0] += 1
        return pltpu.make_async_remote_copy(
            src_ref=src,
            dst_ref=dst,
            send_sem=ss.at[n],
            recv_sem=rs.at[n],
            device_id=dev,
            device_id_type=MESH,
        )

    def send(src, dst, dev):
        cp = remote(src, dst, dev)
        cp.start()
        sent.append(cp)
        return cp

    def load(src, dst):
        n = count[1]
        count[1] += 1
        cp = pltpu.make_async_copy(src, dst, ls.at[n])
        cp.start()
        return cp

    def left(cp):
        cp.wait_send()
        sent[:] = [one for one in sent if one is not cp]

    def arrived(copies):
        for cp in copies:
            cp.wait_recv()

    def here(copies):
        for cp in copies:
            cp.wait()

    l_small = [load(dup, dup_v), load(dbi, dbi_v), load(ggn, ggn_v)]
    l_qk = [load(wq.at[j], qk_v.at[i, 0]), load(wk.at[j], qk_v.at[i, 1])]
    segment = pl.ds(pl.multiple_of(i * T, T), T)
    l_x = [load(tok.at[segment], x_v), load(ng, ng_v), load(ffg, ffg_v)]
    l_dd = load(dd, dd_v.at[pl.ds(0, 16)])
    l_v = load(wv.at[j], v_v.at[j])
    l_g = load(wg.at[j], g_v.at[j])
    l_c = load(cot.at[segment], c_v)
    l_f = [load(fg, f_v.at[0, i]), load(fu, f_v.at[1, i]), load(fd, f_v.at[2, i])]
    l_o = load(wo, o_v.at[i, j])
    l_xa = load(tok, x_all)
    l_ca = load(cot, c_all)

    barrier = pltpu.get_barrier_semaphore()
    for dev in kdev[1:] + vdev[1:] + seqdev:
        pl.semaphore_signal(barrier, inc=1, device_id=dev, device_id_type=MESH)

    dd_v[16:, :] = jnp.zeros((dd_v.shape[0] - 16, D), BF)
    here(l_small)
    head3 = lax.broadcasted_iota(jnp.int32, (16, W, 32), 1)
    head2 = lax.broadcasted_iota(jnp.int32, (W, 32), 0)
    sq_v[...] = jnp.zeros_like(sq_v)
    sq_v[0:16, 0:32] = jnp.sum(jnp.where(head3 == j, dup_v[...].astype(F32), 0.0), axis=1)
    sq_v[16:17, 0:32] = jnp.sum(
        jnp.where(head2 == j, dbi_v[...].astype(F32), 0.0), axis=0, keepdims=True
    )
    ext_v[i] = sq_v[...].T[:32].astype(BF)
    sq_v[...] = jnp.zeros_like(sq_v)
    sq_v[0:8, 0:64] = jnp.broadcast_to(ggn_v[...].astype(F32), (8, 64))
    gge_v[j] = sq_v[...].T[:64].astype(BF)

    pl.semaphore_wait(barrier, 6 + len(seqdev))

    here(l_qk)
    t_qk = [None] + [send(qk_v.at[i, par], qk_v.at[i, par], kdev[d]) for d in DIRS]
    t_v = [None] + [send(wv.at[vj[d], :, mine], v_v.at[j, :, mine], vdev[d]) for d in DIRS]
    t_ext = [send(ext_v.at[i], ext_v.at[i], kdev[d]) for d in DIRS]
    low = pl.ds(0, 32)
    high = pl.ds(32, 32)
    t_oa = [None] + [
        send(wo.at[low, mine], o_v.at[i, j, low, mine], vdev[d]) for d in DIRS
    ]
    t_ob = [None] + [
        send(wo.at[high, mine], o_v.at[i, j, high, mine], kdev[d]) for d in DIRS
    ]
    cut = FB // 32 * 16
    weights = (fg, fu, fd)
    pieces = [(2, 0, cut), (2, cut, FB - cut), (0, 0, FB), (1, 0, FB)]

    def send_piece(piece):
        n, first, size = piece
        at = pl.ds(first, size)
        return [None] + [
            send(weights[n].at[at, mine], f_v.at[n, i, at, mine], kdev[d]) for d in DIRS
        ]

    def pass_piece(piece, copies):
        n, first, size = piece
        at = pl.ds(first, size)
        moves = []
        for d in DIRS:
            copies[d].wait_recv()
            view = f_v.at[n, ki[d], at, mine]
            moves.append(send(view, view, partner))
        return moves

    t_f = [send_piece(pieces[0])]
    t_g = [None] + [send(wg.at[vj[d], :, mine], g_v.at[j, :, mine], vdev[d]) for d in DIRS]
    t_gge = [send(gge_v.at[j], gge_v.at[j], vdev[d]) for d in DIRS]

    here(l_x)
    x = x_v[...].astype(F32)
    g1 = flat_row(ng_v[...].astype(F32))
    g3 = flat_row(ffg_v[...].astype(F32))
    r1 = lax.rsqrt(jnp.sum(x * x, axis=1, keepdims=True) / D + EPS)
    n_v[...] = (x * r1 * g1).astype(BF)
    l_dd.wait()
    lane = lax.broadcasted_iota(jnp.int32, (T, 128), 1)
    lrp = jnp.where(lane == 16, 1.0, nt(n_v[...], dd_v[...]))

    f_qk = []
    for d in DIRS:
        t_qk[d].wait_recv()
        f_qk.append(send(qk_v.at[ki[d], par], qk_v.at[ki[d], par], partner))
    arrived(t_ext)
    arrived(f_qk)
    normed = n_v[...]
    wq_all = qk_v[:, 0].reshape(W * 32, D)
    wk_all = qk_v[:, 1].reshape(W * 32, D)
    ext_all = ext_v[...].reshape(W * 32, 128)
    scale = 128.0 ** (-0.5)
    q = nt(normed, wq_all) * scale
    k = nt(normed, wk_all)
    arg = nt(lrp, ext_all.astype(F32), HIGH)
    rates = (jnp.minimum(arg, 0.0) - jnp.log1p(jnp.exp(-jnp.abs(arg)))) / 16.0
    row_id = lax.broadcasted_iota(jnp.int32, (CB, CB), 0)
    col_id = lax.broadcasted_iota(jnp.int32, (CB, CB), 1)
    causal = row_id >= col_id
    tri = jnp.where(causal, 1.0, 0.0)
    nblk = T // CB
    blk = [slice(c * CB, (c + 1) * CB) for c in range(nblk)]
    e1, e2, em, el, dec, qd, kd, qi, ke, score = [], [], [], [], [], [], [], [], [], []
    for c in range(nblk):
        cum = nn(tri, rates[blk[c]], HIGH)
        mid = cum[CB // 2 - 1 : CB // 2]
        last = cum[CB - 1 : CB]
        e1.append(jnp.exp(cum - mid))
        e2.append(jnp.exp(mid - cum))
        em.append(jnp.exp(mid))
        el.append(jnp.exp(last - mid))
        dec.append(jnp.exp(last))
        a = q[blk[c]] * e1[c]
        b = k[blk[c]] * e2[c]
        qd.append(a.astype(BF))
        kd.append(b.astype(BF))
        qi.append((a * em[c]).astype(BF))
        ke.append((b * el[c]).astype(BF))
        score.append(jnp.where(causal, nt(qd[c], kd[c]), 0.0).astype(BF))

    l_v.wait()
    f_vv = []
    for d in DIRS:
        t_v[d].wait_recv()
        f_vv.append(send(v_v.at[vj[d], :, mine], v_v.at[vj[d], :, mine], partner))
    arrived(f_vv)
    wv_all = v_v[...].reshape(W * 64, D)
    v = nt(normed, wv_all).astype(BF)
    up = [tn(v[blk[c]], ke[c]) for c in range(nblk)]
    loc = up[0]
    locd = dec[0]
    for c in range(1, nblk):
        loc = loc * dec[c] + up[c]
        locd = locd * dec[c]
    VC = loc.shape[0]
    st_v[i, :VC] = loc.astype(BF)
    st_v[i, VC:] = jnp.broadcast_to(locd, (16, 128)).astype(BF)
    t_st = [send(st_v.at[i], st_v.at[i], kdev[d]) for d in DIRS]
    for piece in pieces[1:]:
        t_f.append(send_piece(piece))
    mixed = [nn(score[c], v[blk[c]]) for c in range(nblk)]

    f_o = []
    l_o.wait()
    for d in DIRS:
        t_oa[d].wait_recv()
        view = o_v.at[i, vj[d], low, mine]
        f_o.append(send(view, view, partner))
    t_oa2 = [None] + [
        send(o_v.at[i, :, low, mine], o_v.at[i, :, low, mine], kdev[d]) for d in DIRS
    ]
    for d in DIRS:
        t_ob[d].wait_recv()
        view = o_v.at[ki[d], j, high, mine]
        f_o.append(send(view, view, partner))
    f_g = []
    l_g.wait()
    for d in DIRS:
        t_g[d].wait_recv()
        f_g.append(send(g_v.at[vj[d], :, mine], g_v.at[vj[d], :, mine], partner))
    arrived(f_g)
    arrived(t_gge)
    wg_all = g_v[...].reshape(W * 64, D)
    gate = nt(normed, wg_all)
    gg = gge_v[...].astype(F32).reshape(W * 64, 128).T[:1]
    sig = 1.0 / (1.0 + jnp.exp(-gate))
    act = gate * sig
    act_v[0] = act
    act_v[1] = sig + act * (1.0 - sig)

    def entering(slots, totals, back):
        order = range(W - 1, -1, -1) if back else range(W)
        pre_s = jnp.zeros((VC, 128), F32)
        pre_d = jnp.ones((1, 128), F32)
        tot_s = jnp.zeros((VC, 128), F32)
        tot_d = jnp.ones((1, 128), F32)
        for other_i in order:
            one_s = slots[other_i, :VC].astype(F32)
            one_d = slots[other_i, VC : VC + 1].astype(F32)
            use = (other_i > i) if back else (other_i < i)
            pre_s = jnp.where(use, pre_s * one_d + one_s, pre_s)
            pre_d = jnp.where(use, pre_d * one_d, pre_d)
            tot_s = tot_s * one_d + one_s
            tot_d = tot_d * one_d
        totals[s, :VC] = tot_s.astype(BF)
        totals[s, VC:] = jnp.broadcast_to(tot_d, (16, 128)).astype(BF)
        arrived([send(totals.at[s], totals.at[s], dev) for dev in seqdev])
        order = range(n_seq - 1, -1, -1) if back else range(n_seq)
        far = jnp.zeros((VC, 128), F32)
        for other_s in order:
            one_s = totals[other_s, :VC].astype(F32)
            one_d = totals[other_s, VC : VC + 1].astype(F32)
            use = (other_s > s) if back else (other_s < s)
            far = jnp.where(use, far * one_d + one_s, far)
        return pre_s + pre_d * far

    arrived(t_st)
    start = [entering(st_v, tt_v, False)]
    for c in range(nblk):
        start.append(start[c] * dec[c] + up[c])
    start_low = [a.astype(BF) for a in start]
    for c in range(nblk):
        mixed[c] = mixed[c] + nt(qi[c], start_low[c])
    mix = jnp.concatenate(mixed, axis=0)
    r2 = lax.rsqrt(jnp.sum(mix * mix, axis=1, keepdims=True) / VC + EPS)
    normal = mix * r2
    ga_v[j] = (normal * gg * act_v[0]).astype(BF)
    act_v[2] = normal
    t_ga = [send(ga_v.at[j], ga_v.at[j], vdev[d]) for d in DIRS]
    t_ob2 = [None] + [
        send(o_v.at[:, j, high, mine], o_v.at[:, j, high, mine], vdev[d]) for d in DIRS
    ]

    here([l_xa, l_ca])
    for part in range(rows // T):
        at = pl.ds(part * T, T)
        xa = x_all[at, :].astype(F32)
        ra = lax.rsqrt(jnp.sum(xa * xa, axis=1, keepdims=True) / D + EPS)
        n_all[at, :] = (xa * ra * g1).astype(BF)
    xr_v[...] = (x * (r1 * r1 * r1)).astype(BF).T
    here(l_f + [l_c])
    f_f = []
    for piece, copies in zip(pieces[:2], t_f[:2]):
        f_f += pass_piece(piece, copies)
    arrived(f_f)
    dn = f_v[2].reshape(W * FB, D)
    gh_v[...] = nt(c_v[...], dn)
    f_f = []
    for piece, copies in zip(pieces[2:], t_f[2:]):
        f_f += pass_piece(piece, copies)
    for d in DIRS:
        t_oa2[d].wait_recv()
        view = o_v.at[ki[d], :, low, mine]
        f_o.append(send(view, view, partner))
    arrived(t_ga)
    for d in DIRS:
        t_ob2[d].wait_recv()
        view = o_v.at[:, vj[d], high, mine]
        f_o.append(send(view, view, partner))
    arrived(f_o)
    att = nn(ga_v[0], o_v[0].reshape(W * 64, D))
    for h in range(1, W):
        att = att + nn(ga_v[h], o_v[h].reshape(W * 64, D))
    resid = x_v[...].astype(F32) + att
    r3 = lax.rsqrt(jnp.sum(resid * resid, axis=1, keepdims=True) / D + EPS)
    fin = (resid * r3 * g3).astype(BF)
    arrived(f_f)

    gT = f_v[0].reshape(W * FB, D)
    uT = f_v[1].reshape(W * FB, D)
    gval = nt(fin, gT)
    uval = nt(fin, uT)
    fsig = 1.0 / (1.0 + jnp.exp(-gval))
    fact = gval * fsig
    hid = (fact * uval).astype(BF)
    gh = gh_v[...]
    gup = (gh * fact).astype(BF)
    ggate = (gh * uval * (fsig + fact * (1.0 - fsig))).astype(BF)
    part = nn(ggate, gT) + nn(gup, uT)
    p_v[...] = part
    sst[...] = as_row(jnp.sum(resid * g3 * part, axis=1, keepdims=True))
    t_m3 = [send(sst, rst.at[d], vdev[d]) for d in DIRS]
    ggp = nt((part * g3).astype(BF), o_v[...].reshape(W * W * 64, D))
    for h in range(W):
        sgg[h] = ggp[:, h * VC : (h + 1) * VC].astype(BF)
    t_gg = [send(sgg.at[vj[d]], rgg.at[d], vdev[d]) for d in DIRS]
    hd[...] = hid.T.reshape(W, FB, T)
    t_hd = [send(hd.at[ki[d]], hseg.at[i], kdev[d]) for d in DIRS]
    hseg[i] = hd[i]

    t_pre = []
    for n, grad in enumerate((ggate, gup)):
        gw[n] = tn(grad, fin).astype(BF).reshape(W, FB, D)
        t_pre.append(send(gw.at[n, :, :, other], pre.at[n], partner))

    feature = lax.broadcasted_iota(jnp.int32, (1, D), 1)
    own_slab = jnp.where(lax.rem(feature // 64, W) == j, 1.0, 0.0)
    own_run = jnp.where(feature // (D // W) == j, 1.0, 0.0)
    so[...] = (nn(hid, dn) + own_slab * resid).astype(BF).T.reshape(W, W, 64, T)
    pair01 = pl.ds(0, W // 2)
    pair23 = pl.ds(W // 2, W // 2)
    t_out = [send(so.at[pair01, vj[d]], ro.at[d, pair01], vdev[d]) for d in DIRS]
    ffn_gain = jnp.sum(part * resid * r3, axis=0, keepdims=True)

    def settle(n):
        t_pre[n].wait_recv()
        pres[n] = (gw[n, :, :, mine].astype(F32) + pre[n].astype(F32)).astype(BF)
        return [send(pres.at[n, ki[d]], rfw.at[n, d], kdev[d]) for d in DIRS]

    t_fw = settle(0)

    arrived(t_m3)
    m3 = as_column(sst[...] + rst[1] + rst[2] + rst[3]) / D
    base = c_v[...].astype(F32) - resid * (r3 * r3 * r3 * m3)
    direct = nt(base.astype(BF), o_v[j].reshape(W * 64, D))
    full = p_v[...] * (g3 * r3)
    mixed_in = (full + own_run * base).astype(BF)
    for h in range(W):
        gow[h] = tn(ga_v[h], mixed_in).astype(BF)
    t_po = send(gow.at[:, :, other], preo, partner)
    arrived(t_gg)

    ggs = total(sgg[j], rgg)
    ggrad = direct + r3 * ggs
    act = act_v[0]
    normal = act_v[2]
    dgate = (ggrad * normal * gg * act_v[1]).astype(BF)
    gs = ggrad * act
    group = jnp.sum(gs * normal, axis=0, keepdims=True)
    gnm = gs * gg
    gmix = (r2 * (gnm - normal * (jnp.sum(normal * gnm, axis=1, keepdims=True) / VC))).astype(BF)

    qst = [tn(gmix[blk[c]], qi[c]) for c in range(nblk)]
    bloc = qst[nblk - 1]
    for c in range(nblk - 2, -1, -1):
        bloc = bloc * dec[c] + qst[c]
    bst_v[i, :VC] = bloc.astype(BF)
    bst_v[i, VC:] = jnp.broadcast_to(locd, (16, 128)).astype(BF)
    t_bst = [send(bst_v.at[i], bst_v.at[i], kdev[d]) for d in DIRS]
    vz[1] = dgate.T.reshape(W, 64, T)
    t_gz = [send(vz.at[1, vj[d]], zvg.at[1, j], vdev[d]) for d in DIRS]
    t_fw += settle(1)
    dscore, dq_in, dk_in, dv_in = [], [], [], []
    for c in range(nblk):
        ds = jnp.where(causal, nt(gmix[blk[c]], v[blk[c]]), 0.0).astype(BF)
        dq_in.append(nn(ds, kd[c]) + em[c] * nn(gmix[blk[c]], start_low[c]))
        dk_in.append(tn(ds, qd[c]))
        dv_in.append(tn(score[c], gmix[blk[c]]))
    t_po.wait_recv()
    preso[...] = (gow[:, :, mine].astype(F32) + preo[...].astype(F32)).astype(BF)
    arrived(t_bst)
    after = [None] * nblk
    after[nblk - 1] = entering(bst_v, btt_v, True)
    for c in range(nblk - 2, -1, -1):
        after[c] = after[c + 1] * dec[c + 1] + qst[c + 1]

    ql, kl, vl, ga = [], [], [], []
    for c in range(nblk):
        low_after = after[c].astype(BF)
        dq = e1[c] * dq_in[c]
        dk = e2[c] * (dk_in[c] + el[c] * nn(v[blk[c]], low_after))
        dv = dv_in[c] + nt(ke[c], low_after)
        gc = q[blk[c]] * dq - k[blk[c]] * dk
        extra = jnp.sum(after[c] * start[c + 1], axis=0, keepdims=True)
        gc = jnp.where(row_id == CB - 1, gc + extra, gc)
        gr = tn(tri, gc, HIGH)
        ga.append(gr / (1.0 + jnp.exp(arg[blk[c]])) / 16.0)
        ql.append((dq * scale).astype(BF))
        kl.append(dk.astype(BF))
        vl.append(dv.astype(BF))
    ql = jnp.concatenate(ql, axis=0)
    kl = jnp.concatenate(kl, axis=0)
    vl = jnp.concatenate(vl, axis=0)
    ga = jnp.concatenate(ga, axis=0).astype(BF)
    vz[0] = vl.T.reshape(W, 64, T)
    t_vz = [send(vz.at[0, vj[d]], zvg.at[0, j], vdev[d]) for d in DIRS]
    qka[:, 0] = ql.T.reshape(W, 32, T)
    qka[:, 1] = kl.T.reshape(W, 32, T)
    qka[:, 2] = ga.T.reshape(W, 32, T)
    t_qa = [send(qka.at[ki[d]], kqa.at[i], kdev[d]) for d in DIRS]
    glr = nn(ga, ext_all).astype(BF)
    gn = nn(ql, wq_all) + nn(kl, wk_all) + nn(vl, wv_all) + nn(dgate, wg_all) + nn(glr, dd_v[...])
    x = x_v[...].astype(F32)
    gnx = gn * x
    norm_gain = jnp.sum(gnx * r1, axis=0, keepdims=True)
    m1p = as_row(jnp.sum(gnx * g1, axis=1, keepdims=True))[:1]
    small = tn(glr, normed)[:16]
    rid = lax.broadcasted_iota(jnp.int32, (16, T), 0)
    for h in range(W):
        at = slice(h * T, (h + 1) * T)
        sm0[h, 0:16] = small[:, at].astype(BF)
        rest = jnp.where(rid == 0, norm_gain[:, at], 0.0)
        rest = jnp.where(rid == 1, ffn_gain[:, at], rest)
        rest = jnp.where(rid == 3, m1p, rest)
        if h == 0:
            rest = jnp.where(rid == 2, group, rest)
        sm0[h, 16:32] = rest.astype(BF)
    t_s0 = [send(sm0.at[vj[d]], sm1.at[d], vdev[d]) for d in DIRS]
    whole = gn * (r1 * g1) + full + own_slab * base
    sgn[...] = whole.astype(BF).T.reshape(W, W, 64, T)
    t_gn = [send(sgn.at[:, vj[d]], rgn.at[d], vdev[d]) for d in DIRS]
    t_out2 = [send(so.at[pair23, vj[d]], ro.at[d, pair23], vdev[d]) for d in DIRS]
    t_ow = [send(preso.at[ki[d]], rowk.at[d], kdev[d]) for d in DIRS]

    arrived(t_hd)
    dsum[0] = nn(lanes(hseg[...]), c_all[...]).astype(BF)
    t_ds = send(dsum.at[0], dsum.at[1], partner)

    arrived(t_gz)
    zvg[1, j] = vz[1, j]
    t_gk = [send(zvg.at[1, ki[d]], kvg.at[1, i], kdev[d]) for d in DIRS]
    kvg[1, i] = zvg[1, i]

    arrived(t_s0)
    sm2[0] = total(sm0[j], sm1).astype(BF)
    m1 = (
        sm0[0, 19:20].astype(F32)
        + sm1[1, 19:20].astype(F32)
        + sm1[2, 19:20].astype(F32)
        + sm1[3, 19:20].astype(F32)
    ) / D
    t_s1 = [send(sm2.at[0], sm2.at[d], kdev[d]) for d in DIRS]
    arrived(t_vz)
    zvg[0, j] = vz[0, j]
    t_vk = [send(zvg.at[0, ki[d]], kvg.at[0, i], kdev[d]) for d in DIRS]
    kvg[0, i] = zvg[0, i]

    arrived(t_qa)
    kqa[i] = qka[i]
    nall = n_all[...]
    for n in range(2):
        qksum[0, n] = nn(lanes(kqa[:, n]), nall).astype(BF)
    low_all = jnp.where(
        lax.broadcasted_iota(jnp.int32, (rows, 128), 1) == 16, 1.0, nt(nall, dd_v[...])
    )
    esum[0] = nn(lanes(kqa[:, 2]), low_all.astype(BF))
    t_qs = send(qksum.at[0], qksum.at[1], partner)
    t_es = send(esum.at[0], esum.at[1], partner)

    arrived(t_fw)
    for n in range(2):
        fin_f[par, n] = total(pres[n, i], rfw.at[n]).astype(BF)
    t_ff = send(fin_f.at[par], fin_f.at[par], partner)
    arrived(t_s1)
    sm3[0] = total(sm2[0], sm2).astype(BF)
    t_s2 = send(sm3.at[0], sm3.at[1], partner)

    arrived(t_gk + t_vk)
    for n in range(2):
        vgsum[0, n] = nn(lanes(kvg[n]), nall).astype(BF)
    t_vs = send(vgsum.at[0], vgsum.at[1], partner)
    t_s2.wait_recv()
    sm4[j] = (sm3[0].astype(F32) + sm3[1].astype(F32)).astype(BF)
    t_s3 = [send(sm4.at[j], sm4.at[j], vdev[d]) for d in DIRS]

    arrived(t_ow)
    mid_o[...] = total(preso[i], rowk).astype(BF).reshape(W, 64, half)
    t_oz = [send(mid_o.at[vj[d]], rowz.at[d], vdev[d]) for d in DIRS]

    arrived(t_gn)
    for h in range(W):
        got = sgn[h, j].astype(F32)
        for d in DIRS:
            got = got + rgn[d, h].astype(F32)
        at = pl.ds(pl.multiple_of((h * W + j) * 64, 64), 64)
        ai[h] = (got - xr_v[at, :].astype(F32) * m1).astype(BF)
    t_ai = [send(ai.at[ki[d]], iseg.at[i], kdev[d]) for d in DIRS]
    iseg[i] = ai[i]

    arrived(t_out + t_out2)
    for h in range(W):
        got = so[h, j].astype(F32)
        for d in DIRS:
            got = got + ro[d, h].astype(F32)
        ao[h] = got.astype(BF)
    t_ao = [send(ao.at[ki[d]], oseg.at[i], kdev[d]) for d in DIRS]
    oseg[i] = ao[i]

    outs = []
    t_ds.wait_recv()
    left(t_ds)
    dsum[0] = (dsum[0].astype(F32) + dsum[1].astype(F32)).astype(BF)
    outs.append(load(dsum.at[0], o_d))
    t_qs.wait_recv()
    t_es.wait_recv()
    left(t_qs)
    left(t_es)
    qksum[0] = (qksum[0].astype(F32) + qksum[1].astype(F32)).astype(BF)
    esum[0] = esum[0] + esum[1]
    outs.append(load(qksum.at[0], o_qk))
    outs.append(load(esum.at[0], o_ext))
    t_ff.wait_recv()
    outs.append(load(fin_f, o_f))
    t_vs.wait_recv()
    left(t_vs)
    vgsum[0] = (vgsum[0].astype(F32) + vgsum[1].astype(F32)).astype(BF)
    outs.append(load(vgsum.at[0], o_vg))
    arrived(t_s3)
    for h in range(W):
        pick[:, h * T : (h + 1) * T] = sm4[h].astype(F32)
    pair = i * W + j
    small_v[...] = jnp.zeros_like(small_v)
    small_v[0:1, :] = pick[pl.ds(pair, 1), :]
    wide = pick[16:24, :]
    slab = D // (W * W)
    chosen = jnp.zeros((8, slab), F32)
    for n in range(W * W):
        chosen = jnp.where(pair == n, wide[:, n * slab : (n + 1) * slab], chosen)
    for n in range(W):
        group_slab = jnp.where(j == n, wide[2:3, n * 64 : (n + 1) * 64], 0.0)
        small_v[3:4, 0:64] = small_v[3:4, 0:64] + group_slab
    small_v[1:3, 0:slab] = chosen[0:2]
    outs.append(load(small_v, o_small))
    arrived(t_oz)
    fin_ow[par] = total(mid_o[j], rowz).astype(BF)
    t_fo = send(fin_ow.at[par], fin_ow.at[par], partner)
    arrived(t_ai)
    outs.append(load(iseg, o_in))
    arrived(t_ao)
    outs.append(load(oseg, o_out))
    t_fo.wait_recv()
    outs.append(load(fin_ow, o_ow))
    here(outs)
    for cp in sent:
        cp.wait_send()


N_REMOTE = 260
N_LOCAL = 40


def layer(n_seq, args):
    rows, D = args[0].shape
    W = WAYS
    T = rows // W
    FB = args[-1].shape[0]
    VC = W * 64
    half = D // 2

    def sds(shape, dtype=BF):
        return jax.ShapeDtypeStruct(shape, dtype)

    def vm(shape, dtype=BF):
        return pltpu.VMEM(shape, dtype)

    outs = [
        sds((W, 64, T)),
        sds((W, 64, T)),
        sds((2, 2, FB, half)),
        sds((FB, D)),
        sds((2, 64, D)),
        sds((2, 32, D)),
        sds((32, 128), F32),
        sds((2, 64, half)),
        sds((8, D), F32),
    ]
    scratch = [
        vm((T, D)),
        vm((T, D)),
        vm((rows, D)),
        vm((rows, D)),
        vm((rows, D)),
        vm((T, D)),
        vm((D, T)),
        vm((128, D)),
        vm((8, 128)),
        vm((8, 128)),
        vm((16, W, 32)),
        vm((W, 32)),
        vm((1, 64)),
        vm((128, 128), F32),
        vm((8, D), F32),
        vm((W, 2, 32, D)),
        vm((W, 32, 128)),
        vm((W, 64, D)),
        vm((W, 64, D)),
        vm((W, 64, 128)),
        vm((W, W, 64, D)),
        vm((3, W, FB, D)),
        vm((W, VC + 16, 128)),
        vm((n_seq, VC + 16, 128)),
        vm((W, VC + 16, 128)),
        vm((n_seq, VC + 16, 128)),
        vm((W, T, VC)),
        vm((W, T, VC)),
        vm((W, T, VC)),
        vm((8, T), F32),
        vm((W, 8, T), F32),
        vm((W, W, 64, T)),
        vm((W, W, 64, T)),
        vm((W, W, 64, T)),
        vm((W, W, 64, T)),
        vm((W, 64, T)),
        vm((W, 64, T)),
        vm((W, 64, T)),
        vm((W, 64, T)),
        vm((W, FB, T)),
        vm((W, FB, T)),
        vm((2, W, FB, D)),
        vm((2, W, FB, half)),
        vm((2, W, FB, half)),
        vm((2, W, FB, half)),
        vm((2, 2, FB, half)),
        vm((2, FB, D)),
        vm((W, VC, D)),
        vm((W, VC, half)),
        vm((W, VC, half)),
        vm((W, VC, half)),
        vm((W, 64, half)),
        vm((W, 64, half)),
        vm((2, 64, half)),
        vm((2, W, 64, T)),
        vm((2, W, 64, T)),
        vm((2, W, 64, T)),
        vm((2, 2, 64, D)),
        vm((W, 3, 32, T)),
        vm((W, 3, 32, T)),
        vm((2, 2, 32, D)),
        vm((2, 32, 128), F32),
        vm((W, 32, T)),
        vm((W, 32, T)),
        vm((W, 32, T)),
        vm((2, 32, T)),
        vm((W, 32, T)),
        vm((32, D), F32),
        vm((8, D), F32),
        vm((T, W * FB), F32),
        vm((3, T, VC), F32),
        vm((T, D), F32),
        pltpu.SemaphoreType.DMA((N_REMOTE,)),
        pltpu.SemaphoreType.DMA((N_REMOTE,)),
        pltpu.SemaphoreType.DMA((N_LOCAL,)),
    ]
    return pl.pallas_call(
        functools.partial(layer_kernel, n_seq),
        out_shape=outs,
        in_specs=[pl.BlockSpec(memory_space=pl.ANY)] * len(args),
        out_specs=[pl.BlockSpec(memory_space=pl.ANY)] * len(outs),
        scratch_shapes=scratch,
        compiler_params=pltpu.CompilerParams(
            collective_id=0, has_side_effects=True, vmem_limit_bytes=60 * 2**20
        ),
        name="layer",
    )(*args)


def finish_kernel(*refs):
    n_in = 9
    parts, rest = refs[:n_in], refs[n_in:]
    results, held, sem = rest[:16], rest[16:-1], rest[-1]
    copies = [pltpu.make_async_copy(a, b, sem.at[n]) for n, (a, b) in enumerate(zip(parts, held))]
    for cp in copies:
        cp.start()
    o_out, o_in, o_f, o_d, o_vg, o_qk, o_ext, o_ow, o_small = held
    (r_out, r_in, r_ng, r_q, r_k, r_v, r_g, r_dd, r_du, r_db, r_gg, r_o, r_fn, r_fg, r_fu, r_fd) = results
    T = o_out.shape[2]
    half = o_f.shape[3]
    copies[3].wait()
    r_fd[...] = o_d[...].astype(F32)
    copies[2].wait()
    for h in range(2):
        at = slice(h * half, (h + 1) * half)
        r_fg[:, at] = o_f[h, 0].astype(F32)
        r_fu[:, at] = o_f[h, 1].astype(F32)
    copies[4].wait()
    r_v[...] = o_vg[0].astype(F32)
    r_g[...] = o_vg[1].astype(F32)
    copies[5].wait()
    r_q[...] = o_qk[0].astype(F32)
    r_k[...] = o_qk[1].astype(F32)
    copies[7].wait()
    for h in range(2):
        r_o[:, h * half : (h + 1) * half] = o_ow[h].astype(F32)
    copies[0].wait()
    copies[1].wait()
    for n in range(WAYS):
        r_out[:, n * T : (n + 1) * T] = o_out[n]
        r_in[:, n * T : (n + 1) * T] = o_in[n]
    copies[8].wait()
    r_dd[...] = o_small[0:1, :]
    r_ng[...] = o_small[1:2, 0 : r_ng.shape[1]]
    r_fn[...] = o_small[2:3, 0 : r_fn.shape[1]]
    r_gg[...] = o_small[3:4, 0:64]
    copies[6].wait()
    decay = o_ext[...].T
    r_du[...] = decay[0:16, :].reshape(16, 1, 32)
    r_db[...] = decay[16:17, :]


def finish(parts):
    rows = parts[0].shape[0] * parts[0].shape[2]
    D = parts[3].shape[1]
    FB = parts[3].shape[0]
    slab = D // (WAYS * WAYS)

    def sds(shape, dtype=F32):
        return jax.ShapeDtypeStruct(shape, dtype)

    outs = [
        sds((64, rows), BF),
        sds((64, rows), BF),
        sds((1, slab)),
        sds((32, D)),
        sds((32, D)),
        sds((64, D)),
        sds((64, D)),
        sds((1, D)),
        sds((16, 1, 32)),
        sds((1, 32)),
        sds((1, 64)),
        sds((64, D)),
        sds((1, slab)),
        sds((FB, D)),
        sds((FB, D)),
        sds((FB, D)),
    ]
    return pl.pallas_call(
        finish_kernel,
        out_shape=outs,
        in_specs=[pl.BlockSpec(memory_space=pl.ANY)] * len(parts),
        out_specs=[pl.BlockSpec(memory_space=pltpu.VMEM)] * len(outs),
        scratch_shapes=[pltpu.VMEM(p.shape, p.dtype) for p in parts]
        + [pltpu.SemaphoreType.DMA((len(parts),))],
        compiler_params=pltpu.CompilerParams(vmem_limit_bytes=60 * 2**20),
        name="finish",
    )(*parts)


def shards(
    n_seq,
    tokens,
    norm_gain,
    query_weight,
    key_weight,
    value_weight,
    gate_weight,
    decay_down,
    decay_up,
    decay_bias,
    group_gain,
    out_weight,
    ffn_gain,
    ffn_gate,
    ffn_up,
    ffn_down,
    cotangent,
):
    parts = layer(
        n_seq,
        (
            tokens,
            cotangent,
            norm_gain.reshape(8, -1),
            ffn_gain.reshape(8, -1),
            decay_up,
            decay_bias,
            group_gain[None],
            query_weight.transpose(1, 2, 0),
            key_weight.transpose(1, 2, 0),
            value_weight.transpose(1, 2, 0),
            gate_weight.transpose(1, 2, 0),
            decay_down.T,
            out_weight[0],
            ffn_gate.T,
            ffn_up.T,
            ffn_down,
        ),
    )
    if n_seq > 2:

        def over_pairs(a):
            return jnp.sum(lax.all_gather(a, "seq")[::2].astype(F32), axis=0).astype(a.dtype)

        parts = list(parts[:2]) + [over_pairs(a) for a in parts[2:]]
    (r_out, r_in, r_ng, r_q, r_k, r_v, r_g, r_dd, r_du, r_db, r_gg, r_o, r_fn, r_fg, r_fu, r_fd) = finish(parts)
    return (
        r_out.T,
        r_in.T,
        r_ng[0],
        r_q.T[:, None, :],
        r_k.T[:, None, :],
        r_v.T[:, None, :],
        r_g.T[:, None, :],
        r_dd.T,
        r_du,
        r_db,
        r_gg[0],
        r_o[None],
        r_fn[0],
        r_fg.T,
        r_fu.T,
        r_fd,
    )


def solution(mesh):
    in_specs = (
        P("seq", None),
        P(),
        P(None, None, "kax"),
        P(None, None, "kax"),
        P(None, None, "vax"),
        P(None, None, "vax"),
        P(),
        P(None, None, "kax"),
        P(None, "kax"),
        P("vax"),
        P("kax", "vax", None),
        P(),
        P(None, ("kax", "vax")),
        P(None, ("kax", "vax")),
        P(("kax", "vax"), None),
        P("seq", None),
    )
    out_specs = (
        P("seq", ("kax", "vax")),
        P("seq", ("kax", "vax")),
        P(("kax", "vax")),
        P(None, "vax", "kax"),
        P(None, "vax", "kax"),
        P(None, "kax", "vax"),
        P(None, "kax", "vax"),
        P(None, ("kax", "vax")),
        P(None, "vax", "kax"),
        P("vax", "kax"),
        P("vax"),
        P("kax", "vax", None),
        P(("kax", "vax")),
        P(None, ("kax", "vax")),
        P(None, ("kax", "vax")),
        P(("kax", "vax"), None),
    )
    return jax.shard_map(
        functools.partial(shards, mesh.shape["seq"]),
        mesh=mesh,
        in_specs=in_specs,
        out_specs=out_specs,
        check_vma=False,
    )
```

```python
import functools

import jax
import jax.numpy as jnp
from jax import lax
from jax.experimental import pallas as pl
from jax.experimental.pallas import tpu as pltpu
from jax.sharding import PartitionSpec as P

MESH = pl.DeviceIdType.MESH
BF = jnp.bfloat16
F32 = jnp.float32
CB = 128
WAYS = 4
EPS = 1e-06
HIGH = lax.Precision.HIGHEST


def nn(a, b, precision=None):
    return lax.dot_general(
        a, b, (((1,), (0,)), ((), ())), precision=precision, preferred_element_type=F32
    )


def nt(a, b, precision=None):
    return lax.dot_general(
        a, b, (((1,), (1,)), ((), ())), precision=precision, preferred_element_type=F32
    )


def tn(a, b, precision=None):
    return lax.dot_general(
        a, b, (((0,), (0,)), ((), ())), precision=precision, preferred_element_type=F32
    )


def xor(index, d):
    if d == 1:
        return index + 1 - 2 * lax.rem(index, 2)
    if d == 2:
        return lax.rem(index + 2, 4)
    return 3 - index


def as_row(column):
    return jnp.broadcast_to(column, (column.shape[0], 128)).T[:8]


def as_column(row):
    return jnp.broadcast_to(row[:1], (128, row.shape[1])).T[:, :1]


def flat_row(block):
    return jnp.concatenate([block[r : r + 1] for r in range(block.shape[0])], axis=1)


def lanes(block):
    return jnp.concatenate([block[n] for n in range(block.shape[0])], axis=1)


def total(own, got):
    out = own.astype(F32)
    for d in (1, 2, 3):
        out = out + got[d].astype(F32)
    return out


def layer_kernel(
    n_seq,
    tok,
    cot,
    ng,
    ffg,
    dup,
    dbi,
    ggn,
    wq,
    wk,
    wv,
    wg,
    dd,
    wo,
    fg,
    fu,
    fd,
    o_out,
    o_in,
    o_f,
    o_d,
    o_vg,
    o_qk,
    o_ext,
    o_ow,
    o_small,
    x_v,
    c_v,
    x_all,
    c_all,
    n_all,
    n_v,
    xr_v,
    dd_v,
    ng_v,
    ffg_v,
    dup_v,
    dbi_v,
    ggn_v,
    sq_v,
    gain_v,
    qk_v,
    ext_v,
    v_v,
    g_v,
    gge_v,
    o_v,
    f_v,
    st_v,
    tt_v,
    bst_v,
    btt_v,
    ga_v,
    sgg,
    rgg,
    cgg,
    sst,
    rst,
    so,
    ro,
    co,
    sgn,
    rgn,
    cgn,
    ao,
    oseg,
    ai,
    iseg,
    hd,
    hseg,
    gw,
    pre,
    pres,
    rfw,
    qfw,
    cfw,
    fin_f,
    dsum,
    gow,
    preo,
    preso,
    rowk,
    qow,
    cow,
    mid_o,
    rowz,
    fin_ow,
    vz,
    zvg,
    kvg,
    vgsum,
    qka,
    kqa,
    qksum,
    esum,
    sm0,
    sm1,
    sm2,
    sm3,
    sm4,
    pick,
    small_v,
    gh_v,
    act_v,
    p_v,
    ss,
    rs,
    ls,
):
    s = lax.axis_index("seq")
    i = lax.axis_index("kax")
    j = lax.axis_index("vax")
    par = lax.rem(s, 2)
    oth = 1 - par
    T, D = x_v.shape
    rows = x_all.shape[0]
    FB = f_v.shape[2]
    half = D // 2
    W = WAYS
    DIRS = (1, 2, 3)
    mine = pl.ds(pl.multiple_of(par * half, half), half)
    other = pl.ds(pl.multiple_of(oth * half, half), half)
    partner = {"seq": s + 1 - 2 * par}
    kdev = [None] + [{"kax": xor(i, d)} for d in DIRS]
    vdev = [None] + [{"vax": xor(j, d)} for d in DIRS]
    ki = [None] + [xor(i, d) for d in DIRS]
    vj = [None] + [xor(j, d) for d in DIRS]
    seqdev = [{"seq": lax.rem(s + e, n_seq)} for e in range(1, n_seq)]

    count = [0, 0]
    sent = []

    def slot():
        count[0] += 1
        return count[0] - 1

    def remote(src, dst, dev, to=None):
        n = slot()
        return pltpu.make_async_remote_copy(
            src_ref=src,
            dst_ref=dst,
            send_sem=ss.at[n],
            recv_sem=rs.at[n if to is None else to],
            device_id=dev,
            device_id_type=MESH,
        )

    def send(src, dst, dev):
        cp = remote(src, dst, dev)
        cp.start()
        sent.append(cp)
        return cp

    def load(src, dst):
        n = count[1]
        count[1] += 1
        cp = pltpu.make_async_copy(src, dst, ls.at[n])
        cp.start()
        return cp

    def left(cp):
        cp.wait_send()
        sent[:] = [one for one in sent if one is not cp]

    def arrived(copies):
        for cp in copies:
            cp.wait_recv()

    def here(copies):
        for cp in copies:
            cp.wait()

    inner = lax.rem(j + 1, W) >= 2
    inner_sent = []
    outer_sent = []

    class LineGather:
        def __init__(self, view):
            a, b, c = slot(), slot(), slot()
            self.near = remote(view(j), view(j), vdev[1], a)
            self.near.start()
            sent.append(self.near)
            across = remote(view(j), view(j), vdev[3], c)
            self.got = [
                pltpu.make_async_remote_copy(
                    src_ref=view(vj[d]),
                    dst_ref=view(vj[d]),
                    send_sem=ss.at[n],
                    recv_sem=rs.at[n],
                    device_id=vdev[1],
                    device_id_type=MESH,
                )
                for d, n in zip(DIRS, (a, b, c))
            ]
            self.on = [
                remote(view(vj[1]), view(vj[1]), vdev[3], b),
                remote(view(vj[3]), view(vj[3]), vdev[1], b),
                remote(view(vj[2]), view(vj[2]), vdev[1], c),
            ]
            inner_sent.extend([across] + self.on)

            @pl.when(inner)
            def _():
                across.start()

        def step(self, n):
            @pl.when(inner)
            def _():
                self.got[(0, 2, 1)[n]].wait_recv()
                self.on[n].start()

        def collect(self):
            @pl.when(jnp.logical_not(inner))
            def _():
                arrived(self.got)

    class LineSum:
        def __init__(self, part, near, far, relay, summed):
            self.part, self.near, self.far, self.relay, self.summed = part, near, far, relay, summed
            b = slot()
            self.first = [
                remote(part(vj[3]), relay.at[0], vdev[1]),
                remote(part(vj[2]), relay.at[1], vdev[1]),
            ]
            outer_sent.extend(self.first)

            @pl.when(jnp.logical_not(inner))
            def _():
                for cp in self.first:
                    cp.start()

            self.direct = send(part(vj[1]), near, vdev[1])
            self.second = [
                remote(summed.at[0], far, vdev[2], b),
                remote(summed.at[1], far, vdev[3], b),
            ]
            inner_sent.extend(self.second)
            self.last = pltpu.make_async_remote_copy(
                src_ref=far,
                dst_ref=far,
                send_sem=ss.at[b],
                recv_sem=rs.at[b],
                device_id=vdev[1],
                device_id_type=MESH,
            )

        def step(self, n):
            @pl.when(inner)
            def _():
                self.first[n].wait_recv()
                mine_too = self.part(vj[2 + n])[...].astype(F32)
                self.summed[n] = (mine_too + self.relay[n].astype(F32)).astype(BF)
                self.second[n].start()

        def collect(self):
            self.direct.wait_recv()
            self.last.wait_recv()

        def total(self):
            out = self.part(j)[...].astype(F32)
            return out + self.near[...].astype(F32) + self.far[...].astype(F32)

    class SquareSum:
        def __init__(self, part, got, relay, summed):
            self.part, self.got, self.relay, self.summed = part, got, relay, summed
            q = got.shape[-1] // 2
            self.at = [pl.ds(0, q), pl.ds(q, q)]
            self.first = [
                send(self.half(ki[3], n), relay.at[n], kdev[1 + n]) for n in range(2)
            ]
            self.direct = [
                send(self.half(ki[1 + n], n), self.into(n, n), kdev[1 + n]) for n in range(2)
            ]

        def half(self, target, n):
            return self.part(target, self.at[n])

        def into(self, n, h):
            return self.got.at[n, :, self.at[h]]

        def step(self):
            self.second = []
            for n in range(2):
                self.first[n].wait_recv()
                own = self.half(ki[2 - n], n)[...].astype(F32)
                self.summed[n] = (own + self.relay[n].astype(F32)).astype(BF)
                self.second.append(
                    send(self.summed.at[n], self.into(1 - n, n), kdev[2 - n])
                )

        def collect(self):
            arrived(self.direct + self.second)

        def total(self):
            out = self.part(i, pl.ds(0, self.got.shape[-1]))[...].astype(F32)
            return out + self.got[0].astype(F32) + self.got[1].astype(F32)

    l_small = [load(dup, dup_v), load(dbi, dbi_v), load(ggn, ggn_v)]
    l_qk = [load(wq.at[j], qk_v.at[i, 0]), load(wk.at[j], qk_v.at[i, 1])]
    segment = pl.ds(pl.multiple_of(i * T, T), T)
    l_x = [load(tok.at[segment], x_v), load(ng, ng_v), load(ffg, ffg_v)]
    l_dd = load(dd, dd_v.at[pl.ds(0, 16)])
    l_v = load(wv.at[j], v_v.at[j])
    l_g = load(wg.at[j], g_v.at[j])
    l_c = load(cot.at[segment], c_v)
    l_f = [load(fg, f_v.at[0, i]), load(fu, f_v.at[1, i]), load(fd, f_v.at[2, i])]
    l_o = load(wo, o_v.at[i, j])
    l_xa = load(tok, x_all)
    l_ca = load(cot, c_all)

    barrier = pltpu.get_barrier_semaphore()
    for dev in kdev[1:] + vdev[1:] + seqdev:
        pl.semaphore_signal(barrier, inc=1, device_id=dev, device_id_type=MESH)

    dd_v[16:, :] = jnp.zeros((dd_v.shape[0] - 16, D), BF)
    here(l_small)
    head3 = lax.broadcasted_iota(jnp.int32, (16, W, 32), 1)
    head2 = lax.broadcasted_iota(jnp.int32, (W, 32), 0)
    sq_v[...] = jnp.zeros_like(sq_v)
    sq_v[0:16, 0:32] = jnp.sum(jnp.where(head3 == j, dup_v[...].astype(F32), 0.0), axis=1)
    sq_v[16:17, 0:32] = jnp.sum(
        jnp.where(head2 == j, dbi_v[...].astype(F32), 0.0), axis=0, keepdims=True
    )
    ext_v[i] = sq_v[...].T[:32].astype(BF)
    sq_v[...] = jnp.zeros_like(sq_v)
    sq_v[0:8, 0:64] = jnp.broadcast_to(ggn_v[...].astype(F32), (8, 64))
    gge_v[j] = sq_v[...].T[:64].astype(BF)

    pl.semaphore_wait(barrier, 6 + len(seqdev))

    here(l_qk)
    t_qk = [None] + [send(qk_v.at[i, par], qk_v.at[i, par], kdev[d]) for d in DIRS]
    t_v = [None] + [send(wv.at[vj[d], :, mine], v_v.at[j, :, mine], vdev[d]) for d in DIRS]
    t_ext = [send(ext_v.at[i], ext_v.at[i], kdev[d]) for d in DIRS]
    low = pl.ds(0, 32)
    high = pl.ds(32, 32)
    t_oa = [None] + [
        send(wo.at[low, mine], o_v.at[i, j, low, mine], vdev[d]) for d in DIRS
    ]
    t_ob = [None] + [
        send(wo.at[high, mine], o_v.at[i, j, high, mine], kdev[d]) for d in DIRS
    ]
    quarter = half // 2
    two = [
        pl.ds(pl.multiple_of(par * half + n * quarter, quarter), quarter) for n in range(2)
    ]

    class SquareGather:
        def __init__(self, view, own=None):
            self.view = view
            own = view(i, mine) if own is None else own
            self.near = [send(own, view(i, mine), kdev[d]) for d in (1, 2)]

        def step(self):
            self.far, moves = [], []
            for n in range(2):
                self.near[n].wait_recv()
                view = self.view(ki[1 + n], two[n])
                self.far.append(send(view, view, kdev[2 - n]))
                view = self.view(ki[1 + n], mine)
                moves.append(send(view, view, partner))
            return moves

        def collect(self):
            arrived(self.far)
            view = self.view(ki[3], mine)
            return [send(view, view, partner)]

    weights = (fg, fu, fd)

    def gather_weight(n):
        return SquareGather(lambda src, at: f_v.at[n, src, :, at], weights[n].at[:, mine])

    t_fd = gather_weight(2)
    t_g = [None] + [send(wg.at[vj[d], :, mine], g_v.at[j, :, mine], vdev[d]) for d in DIRS]
    t_gge = [send(gge_v.at[j], gge_v.at[j], vdev[d]) for d in DIRS]

    here(l_x)
    x = x_v[...].astype(F32)
    g1 = flat_row(ng_v[...].astype(F32))
    g3 = flat_row(ffg_v[...].astype(F32))
    r1 = lax.rsqrt(jnp.sum(x * x, axis=1, keepdims=True) / D + EPS)
    n_v[...] = (x * r1 * g1).astype(BF)
    l_dd.wait()
    lane = lax.broadcasted_iota(jnp.int32, (T, 128), 1)
    lrp = jnp.where(lane == 16, 1.0, nt(n_v[...], dd_v[...]))

    f_qk = []
    for d in DIRS:
        t_qk[d].wait_recv()
        f_qk.append(send(qk_v.at[ki[d], par], qk_v.at[ki[d], par], partner))
    arrived(t_ext)
    arrived(f_qk)
    normed = n_v[...]
    wq_all = qk_v[:, 0].reshape(W * 32, D)
    wk_all = qk_v[:, 1].reshape(W * 32, D)
    ext_all = ext_v[...].reshape(W * 32, 128)
    scale = 128.0 ** (-0.5)
    q = nt(normed, wq_all) * scale
    k = nt(normed, wk_all)
    arg = nt(lrp, ext_all.astype(F32), HIGH)
    rates = (jnp.minimum(arg, 0.0) - jnp.log1p(jnp.exp(-jnp.abs(arg)))) / 16.0
    row_id = lax.broadcasted_iota(jnp.int32, (CB, CB), 0)
    col_id = lax.broadcasted_iota(jnp.int32, (CB, CB), 1)
    causal = row_id >= col_id
    tri = jnp.where(causal, 1.0, 0.0)
    nblk = T // CB
    blk = [slice(c * CB, (c + 1) * CB) for c in range(nblk)]
    e1, e2, em, el, dec, qd, kd, qi, ke, score = [], [], [], [], [], [], [], [], [], []
    for c in range(nblk):
        cum = nn(tri, rates[blk[c]], HIGH)
        mid = cum[CB // 2 - 1 : CB // 2]
        last = cum[CB - 1 : CB]
        e1.append(jnp.exp(cum - mid))
        e2.append(jnp.exp(mid - cum))
        em.append(jnp.exp(mid))
        el.append(jnp.exp(last - mid))
        dec.append(jnp.exp(last))
        a = q[blk[c]] * e1[c]
        b = k[blk[c]] * e2[c]
        qd.append(a.astype(BF))
        kd.append(b.astype(BF))
        qi.append((a * em[c]).astype(BF))
        ke.append((b * el[c]).astype(BF))
        score.append(jnp.where(causal, nt(qd[c], kd[c]), 0.0).astype(BF))

    l_v.wait()
    f_vv = []
    for d in DIRS:
        t_v[d].wait_recv()
        f_vv.append(send(v_v.at[vj[d], :, mine], v_v.at[vj[d], :, mine], partner))
    arrived(f_vv)
    wv_all = v_v[...].reshape(W * 64, D)
    v = nt(normed, wv_all).astype(BF)
    up = [tn(v[blk[c]], ke[c]) for c in range(nblk)]
    loc = up[0]
    locd = dec[0]
    for c in range(1, nblk):
        loc = loc * dec[c] + up[c]
        locd = locd * dec[c]
    VC = loc.shape[0]
    st_v[i, :VC] = loc.astype(BF)
    st_v[i, VC:] = jnp.broadcast_to(locd, (16, 128)).astype(BF)
    t_st = [send(st_v.at[i], st_v.at[i], kdev[d]) for d in DIRS]
    t_fg = gather_weight(0)
    t_fu = gather_weight(1)
    mixed = [nn(score[c], v[blk[c]]) for c in range(nblk)]

    f_o = []
    l_o.wait()
    for d in DIRS:
        t_oa[d].wait_recv()
        view = o_v.at[i, vj[d], low, mine]
        f_o.append(send(view, view, partner))
    t_oa2 = SquareGather(lambda src, at: o_v.at[src, :, low, at])
    for d in DIRS:
        t_ob[d].wait_recv()
        view = o_v.at[ki[d], j, high, mine]
        f_o.append(send(view, view, partner))
    t_ob2 = LineGather(lambda src: o_v.at[:, src, high, mine])
    here(l_f)
    f_f = t_fd.step()

    def gather_states(slots, totals, back):
        order = range(W - 1, -1, -1) if back else range(W)
        pre_s = jnp.zeros((VC, 128), F32)
        pre_d = jnp.ones((1, 128), F32)
        tot_s = jnp.zeros((VC, 128), F32)
        tot_d = jnp.ones((1, 128), F32)
        for other_i in order:
            one_s = slots[other_i, :VC].astype(F32)
            one_d = slots[other_i, VC : VC + 1].astype(F32)
            use = (other_i > i) if back else (other_i < i)
            pre_s = jnp.where(use, pre_s * one_d + one_s, pre_s)
            pre_d = jnp.where(use, pre_d * one_d, pre_d)
            tot_s = tot_s * one_d + one_s
            tot_d = tot_d * one_d
        totals[s, :VC] = tot_s.astype(BF)
        totals[s, VC:] = jnp.broadcast_to(tot_d, (16, 128)).astype(BF)
        return pre_s, pre_d, [send(totals.at[s], totals.at[s], dev) for dev in seqdev]

    def entering(totals, back, pre_s, pre_d, moves):
        arrived(moves)
        order = range(n_seq - 1, -1, -1) if back else range(n_seq)
        far = jnp.zeros((VC, 128), F32)
        for other_s in order:
            one_s = totals[other_s, :VC].astype(F32)
            one_d = totals[other_s, VC : VC + 1].astype(F32)
            use = (other_s > s) if back else (other_s < s)
            far = jnp.where(use, far * one_d + one_s, far)
        return pre_s + pre_d * far

    arrived(t_st)
    states = gather_states(st_v, tt_v, False)

    f_g = []
    l_g.wait()
    for d in DIRS:
        t_g[d].wait_recv()
        f_g.append(send(g_v.at[vj[d], :, mine], g_v.at[vj[d], :, mine], partner))
    start = [entering(tt_v, False, *states)]
    for c in range(nblk):
        start.append(start[c] * dec[c] + up[c])
    start_low = [a.astype(BF) for a in start]
    for c in range(nblk):
        mixed[c] = mixed[c] + nt(qi[c], start_low[c])
    mix = jnp.concatenate(mixed, axis=0)
    r2 = lax.rsqrt(jnp.sum(mix * mix, axis=1, keepdims=True) / VC + EPS)
    normal = mix * r2
    arrived(f_g)
    arrived(t_gge)
    wg_all = g_v[...].reshape(W * 64, D)
    gate = nt(normed, wg_all)
    gg = gge_v[...].astype(F32).reshape(W * 64, 128).T[:1]
    sig = 1.0 / (1.0 + jnp.exp(-gate))
    act = gate * sig
    act_v[0] = act
    act_v[1] = sig + act * (1.0 - sig)
    ga_v[j] = (normal * gg * act).astype(BF)
    act_v[2] = normal
    t_ga = LineGather(lambda src: ga_v.at[src])

    here([l_xa, l_ca])
    for part in range(rows // T):
        at = pl.ds(part * T, T)
        xa = x_all[at, :].astype(F32)
        ra = lax.rsqrt(jnp.sum(xa * xa, axis=1, keepdims=True) / D + EPS)
        n_all[at, :] = (xa * ra * g1).astype(BF)
    xr_v[...] = (x * (r1 * r1 * r1)).astype(BF).T
    t_ob2.step(0)
    t_ob2.step(1)
    f_f += t_fg.step()
    t_ob2.step(2)
    t_ga.step(0)
    t_ga.step(1)
    f_f += t_fd.collect()
    f_f += t_fu.step()
    f_o += t_oa2.step()
    t_ga.step(2)
    l_c.wait()
    arrived(f_f)
    dn = f_v[2].reshape(W * FB, D)
    gh_v[...] = nt(c_v[...], dn)
    f_f = t_fg.collect()
    f_f += t_fu.collect()
    f_o += t_oa2.collect()
    t_ob2.collect()
    for d in DIRS:
        view = o_v.at[:, vj[d], high, mine]
        f_o.append(send(view, view, partner))
    t_ga.collect()
    arrived(f_o)
    att = nn(ga_v[0], o_v[0].reshape(W * 64, D))
    for h in range(1, W):
        att = att + nn(ga_v[h], o_v[h].reshape(W * 64, D))
    resid = x_v[...].astype(F32) + att
    r3 = lax.rsqrt(jnp.sum(resid * resid, axis=1, keepdims=True) / D + EPS)
    fin = (resid * r3 * g3).astype(BF)
    arrived(f_f)

    gT = f_v[0].reshape(W * FB, D)
    uT = f_v[1].reshape(W * FB, D)
    gval = nt(fin, gT)
    uval = nt(fin, uT)
    fsig = 1.0 / (1.0 + jnp.exp(-gval))
    fact = gval * fsig
    hid = (fact * uval).astype(BF)
    gh = gh_v[...]
    gup = (gh * fact).astype(BF)
    ggate = (gh * uval * (fsig + fact * (1.0 - fsig))).astype(BF)
    part = nn(ggate, gT) + nn(gup, uT)
    p_v[...] = part
    sst[...] = as_row(jnp.sum(resid * g3 * part, axis=1, keepdims=True))
    t_m3 = [send(sst, rst.at[d], vdev[d]) for d in DIRS]
    ggp = nt((part * g3).astype(BF), o_v[...].reshape(W * W * 64, D))
    for h in range(W):
        sgg[h] = ggp[:, h * VC : (h + 1) * VC].astype(BF)
    t_gg = LineSum(lambda to: sgg.at[to], rgg.at[0], rgg.at[1], rgg.at[pl.ds(2, 2)], cgg)
    hd[...] = hid.T.reshape(W, FB, T)
    t_hd = [send(hd.at[ki[d]], hseg.at[i], kdev[d]) for d in DIRS]
    hseg[i] = hd[i]

    t_gg.step(0)

    t_pre = []
    for n, grad in enumerate((ggate, gup)):
        gw[n] = tn(grad, fin).astype(BF).reshape(W, FB, D)
        t_pre.append(send(gw.at[n, :, :, other], pre.at[n], partner))

    feature = lax.broadcasted_iota(jnp.int32, (1, D), 1)
    own_slab = jnp.where(lax.rem(feature // 64, W) == j, 1.0, 0.0)
    own_run = jnp.where(feature // (D // W) == j, 1.0, 0.0)
    so[...] = (nn(hid, dn) + own_slab * resid).astype(BF).T.reshape(W, W, 64, T)
    t_gg.step(1)
    t_out = LineSum(lambda to: so.at[:, to], ro.at[0], ro.at[1], ro.at[pl.ds(2, 2)], co)
    ffn_gain = jnp.sum(part * resid * r3, axis=0, keepdims=True)

    def settle(n):
        t_pre[n].wait_recv()
        pres[n] = (gw[n, :, :, mine].astype(F32) + pre[n].astype(F32)).astype(BF)
        return SquareSum(
            lambda to, at: pres.at[n, to, :, at], rfw.at[n], qfw.at[n], cfw.at[n]
        )

    t_fw = [settle(0)]

    arrived(t_m3)
    m3 = as_column(sst[...] + rst[1] + rst[2] + rst[3]) / D
    base = c_v[...].astype(F32) - resid * (r3 * r3 * r3 * m3)
    direct = nt(base.astype(BF), o_v[j].reshape(W * 64, D))
    full = p_v[...] * (g3 * r3)
    mixed_in = (full + own_run * base).astype(BF)
    for h in range(W):
        gow[h] = tn(ga_v[h], mixed_in).astype(BF)
    t_po = send(gow.at[:, :, other], preo, partner)
    t_out.step(0)
    t_gg.collect()

    ggs = t_gg.total()
    ggrad = direct + r3 * ggs
    act = act_v[0]
    normal = act_v[2]
    dgate = (ggrad * normal * gg * act_v[1]).astype(BF)
    gs = ggrad * act
    group = jnp.sum(gs * normal, axis=0, keepdims=True)
    gnm = gs * gg
    gmix = (r2 * (gnm - normal * (jnp.sum(normal * gnm, axis=1, keepdims=True) / VC))).astype(BF)

    qst = [tn(gmix[blk[c]], qi[c]) for c in range(nblk)]
    bloc = qst[nblk - 1]
    for c in range(nblk - 2, -1, -1):
        bloc = bloc * dec[c] + qst[c]
    bst_v[i, :VC] = bloc.astype(BF)
    bst_v[i, VC:] = jnp.broadcast_to(locd, (16, 128)).astype(BF)
    t_bst = [send(bst_v.at[i], bst_v.at[i], kdev[d]) for d in DIRS]
    vz[1] = dgate.T.reshape(W, 64, T)
    t_gz = [send(vz.at[1, vj[d]], zvg.at[1, j], vdev[d]) for d in DIRS]
    t_fw.append(settle(1))
    t_out.step(1)
    t_fw[0].step()
    dscore, dq_in, dk_in, dv_in = [], [], [], []
    for c in range(nblk):
        ds = jnp.where(causal, nt(gmix[blk[c]], v[blk[c]]), 0.0).astype(BF)
        dq_in.append(nn(ds, kd[c]) + em[c] * nn(gmix[blk[c]], start_low[c]))
        dk_in.append(tn(ds, qd[c]))
        dv_in.append(tn(score[c], gmix[blk[c]]))
    t_po.wait_recv()
    preso[...] = (gow[:, :, mine].astype(F32) + preo[...].astype(F32)).astype(BF)
    arrived(t_bst)
    after = [None] * nblk
    states = gather_states(bst_v, btt_v, True)
    t_fw[1].step()
    after[nblk - 1] = entering(btt_v, True, *states)
    for c in range(nblk - 2, -1, -1):
        after[c] = after[c + 1] * dec[c + 1] + qst[c + 1]

    ql, kl, vl, ga = [], [], [], []
    for c in range(nblk):
        low_after = after[c].astype(BF)
        dq = e1[c] * dq_in[c]
        dk = e2[c] * (dk_in[c] + el[c] * nn(v[blk[c]], low_after))
        dv = dv_in[c] + nt(ke[c], low_after)
        gc = q[blk[c]] * dq - k[blk[c]] * dk
        extra = jnp.sum(after[c] * start[c + 1], axis=0, keepdims=True)
        gc = jnp.where(row_id == CB - 1, gc + extra, gc)
        gr = tn(tri, gc, HIGH)
        ga.append(gr / (1.0 + jnp.exp(arg[blk[c]])) / 16.0)
        ql.append((dq * scale).astype(BF))
        kl.append(dk.astype(BF))
        vl.append(dv.astype(BF))
    ql = jnp.concatenate(ql, axis=0)
    kl = jnp.concatenate(kl, axis=0)
    vl = jnp.concatenate(vl, axis=0)
    ga = jnp.concatenate(ga, axis=0).astype(BF)
    vz[0] = vl.T.reshape(W, 64, T)
    t_vz = [send(vz.at[0, vj[d]], zvg.at[0, j], vdev[d]) for d in DIRS]
    qka[:, 0] = ql.T.reshape(W, 32, T)
    qka[:, 1] = kl.T.reshape(W, 32, T)
    qka[:, 2] = ga.T.reshape(W, 32, T)
    t_qa = [send(qka.at[ki[d]], kqa.at[i], kdev[d]) for d in DIRS]
    glr = nn(ga, ext_all).astype(BF)
    gn = nn(ql, wq_all) + nn(kl, wk_all) + nn(vl, wv_all) + nn(dgate, wg_all) + nn(glr, dd_v[...])
    x = x_v[...].astype(F32)
    gnx = gn * x
    norm_gain = jnp.sum(gnx * r1, axis=0, keepdims=True)
    m1p = as_row(jnp.sum(gnx * g1, axis=1, keepdims=True))[:1]
    small = tn(glr, normed)[:16]
    rid = lax.broadcasted_iota(jnp.int32, (16, T), 0)
    for h in range(W):
        at = slice(h * T, (h + 1) * T)
        sm0[h, 0:16] = small[:, at].astype(BF)
        rest = jnp.where(rid == 0, norm_gain[:, at], 0.0)
        rest = jnp.where(rid == 1, ffn_gain[:, at], rest)
        rest = jnp.where(rid == 3, m1p, rest)
        if h == 0:
            rest = jnp.where(rid == 2, group, rest)
        sm0[h, 16:32] = rest.astype(BF)
    t_s0 = [send(sm0.at[vj[d]], sm1.at[d], vdev[d]) for d in DIRS]
    whole = gn * (r1 * g1) + full + own_slab * base
    sgn[...] = whole.astype(BF).T.reshape(W, W, 64, T)
    t_gn = LineSum(lambda to: sgn.at[:, to], rgn.at[0], rgn.at[1], rgn.at[pl.ds(2, 2)], cgn)
    t_ow = SquareSum(lambda to, at: preso.at[to, :, at], rowk, qow, cow)

    t_out.collect()
    ao[...] = t_out.total().astype(BF)
    t_ao = [send(ao.at[ki[d]], oseg.at[i], kdev[d]) for d in DIRS]
    oseg[i] = ao[i]

    arrived(t_hd)
    dsum[0] = nn(lanes(hseg[...]), c_all[...]).astype(BF)
    t_ds = send(dsum.at[0], dsum.at[1], partner)

    arrived(t_gz)
    zvg[1, j] = vz[1, j]
    t_gk = [send(zvg.at[1, ki[d]], kvg.at[1, i], kdev[d]) for d in DIRS]
    kvg[1, i] = zvg[1, i]

    arrived(t_s0)
    sm2[0] = total(sm0[j], sm1).astype(BF)
    m1 = (
        sm0[0, 19:20].astype(F32)
        + sm1[1, 19:20].astype(F32)
        + sm1[2, 19:20].astype(F32)
        + sm1[3, 19:20].astype(F32)
    ) / D
    t_s1 = [send(sm2.at[0], sm2.at[d], kdev[d]) for d in DIRS]
    t_gn.step(0)
    arrived(t_vz)
    zvg[0, j] = vz[0, j]
    t_vk = [send(zvg.at[0, ki[d]], kvg.at[0, i], kdev[d]) for d in DIRS]
    kvg[0, i] = zvg[0, i]
    t_gn.step(1)
    t_ow.step()

    arrived(t_qa)
    kqa[i] = qka[i]
    nall = n_all[...]
    for n in range(2):
        qksum[0, n] = nn(lanes(kqa[:, n]), nall).astype(BF)
    low_all = jnp.where(
        lax.broadcasted_iota(jnp.int32, (rows, 128), 1) == 16, 1.0, nt(nall, dd_v[...])
    )
    esum[0] = nn(lanes(kqa[:, 2]), low_all.astype(BF))
    t_qs = send(qksum.at[0], qksum.at[1], partner)
    t_es = send(esum.at[0], esum.at[1], partner)

    for n in range(2):
        t_fw[n].collect()
        fin_f[par, n] = t_fw[n].total().astype(BF)
    t_ff = send(fin_f.at[par], fin_f.at[par], partner)
    arrived(t_s1)
    sm3[0] = total(sm2[0], sm2).astype(BF)
    t_s2 = send(sm3.at[0], sm3.at[1], partner)

    arrived(t_gk + t_vk)
    for n in range(2):
        vgsum[0, n] = nn(lanes(kvg[n]), nall).astype(BF)
    t_vs = send(vgsum.at[0], vgsum.at[1], partner)
    t_s2.wait_recv()
    sm4[j] = (sm3[0].astype(F32) + sm3[1].astype(F32)).astype(BF)
    t_s3 = [send(sm4.at[j], sm4.at[j], vdev[d]) for d in DIRS]

    t_ow.collect()
    mid_o[...] = t_ow.total().astype(BF).reshape(W, 64, half)
    t_oz = [send(mid_o.at[vj[d]], rowz.at[d], vdev[d]) for d in DIRS]

    t_gn.collect()
    summed = t_gn.total()
    for h in range(W):
        at = pl.ds(pl.multiple_of((h * W + j) * 64, 64), 64)
        ai[h] = (summed[h] - xr_v[at, :].astype(F32) * m1).astype(BF)
    t_ai = [send(ai.at[ki[d]], iseg.at[i], kdev[d]) for d in DIRS]
    iseg[i] = ai[i]

    outs = []
    t_ds.wait_recv()
    left(t_ds)
    dsum[0] = (dsum[0].astype(F32) + dsum[1].astype(F32)).astype(BF)
    outs.append(load(dsum.at[0], o_d))
    t_qs.wait_recv()
    t_es.wait_recv()
    left(t_qs)
    left(t_es)
    qksum[0] = (qksum[0].astype(F32) + qksum[1].astype(F32)).astype(BF)
    esum[0] = esum[0] + esum[1]
    outs.append(load(qksum.at[0], o_qk))
    outs.append(load(esum.at[0], o_ext))
    t_ff.wait_recv()
    outs.append(load(fin_f, o_f))
    t_vs.wait_recv()
    left(t_vs)
    vgsum[0] = (vgsum[0].astype(F32) + vgsum[1].astype(F32)).astype(BF)
    outs.append(load(vgsum.at[0], o_vg))
    arrived(t_s3)
    for h in range(W):
        pick[:, h * T : (h + 1) * T] = sm4[h].astype(F32)
    pair = i * W + j
    small_v[...] = jnp.zeros_like(small_v)
    small_v[0:1, :] = pick[pl.ds(pair, 1), :]
    wide = pick[16:24, :]
    slab = D // (W * W)
    chosen = jnp.zeros((8, slab), F32)
    for n in range(W * W):
        chosen = jnp.where(pair == n, wide[:, n * slab : (n + 1) * slab], chosen)
    for n in range(W):
        group_slab = jnp.where(j == n, wide[2:3, n * 64 : (n + 1) * 64], 0.0)
        small_v[3:4, 0:64] = small_v[3:4, 0:64] + group_slab
    small_v[1:3, 0:slab] = chosen[0:2]
    outs.append(load(small_v, o_small))
    arrived(t_oz)
    fin_ow[par] = total(mid_o[j], rowz).astype(BF)
    t_fo = send(fin_ow.at[par], fin_ow.at[par], partner)
    arrived(t_ai)
    outs.append(load(iseg, o_in))
    arrived(t_ao)
    outs.append(load(oseg, o_out))
    t_fo.wait_recv()
    outs.append(load(fin_ow, o_ow))
    here(outs)
    for cp in sent:
        cp.wait_send()

    @pl.when(inner)
    def _():
        for cp in inner_sent:
            cp.wait_send()

    @pl.when(jnp.logical_not(inner))
    def _():
        for cp in outer_sent:
            cp.wait_send()


N_REMOTE = 172
N_LOCAL = 27


def layer(n_seq, args):
    rows, D = args[0].shape
    W = WAYS
    T = rows // W
    FB = args[-1].shape[0]
    VC = W * 64
    half = D // 2

    def sds(shape, dtype=BF):
        return jax.ShapeDtypeStruct(shape, dtype)

    def vm(shape, dtype=BF):
        return pltpu.VMEM(shape, dtype)

    outs = [
        sds((W, 64, T)),
        sds((W, 64, T)),
        sds((2, 2, FB, half)),
        sds((FB, D)),
        sds((2, 64, D)),
        sds((2, 32, D)),
        sds((32, 128), F32),
        sds((2, 64, half)),
        sds((8, D), F32),
    ]
    scratch = [
        vm((T, D)),
        vm((T, D)),
        vm((rows, D)),
        vm((rows, D)),
        vm((rows, D)),
        vm((T, D)),
        vm((D, T)),
        vm((128, D)),
        vm((8, 128)),
        vm((8, 128)),
        vm((16, W, 32)),
        vm((W, 32)),
        vm((1, 64)),
        vm((128, 128), F32),
        vm((8, D), F32),
        vm((W, 2, 32, D)),
        vm((W, 32, 128)),
        vm((W, 64, D)),
        vm((W, 64, D)),
        vm((W, 64, 128)),
        vm((W, W, 64, D)),
        vm((3, W, FB, D)),
        vm((W, VC + 16, 128)),
        vm((n_seq, VC + 16, 128)),
        vm((W, VC + 16, 128)),
        vm((n_seq, VC + 16, 128)),
        vm((W, T, VC)),
        vm((W, T, VC)),
        vm((W, T, VC)),
        vm((2, T, VC)),
        vm((8, T), F32),
        vm((W, 8, T), F32),
        vm((W, W, 64, T)),
        vm((W, W, 64, T)),
        vm((2, W, 64, T)),
        vm((W, W, 64, T)),
        vm((W, W, 64, T)),
        vm((2, W, 64, T)),
        vm((W, 64, T)),
        vm((W, 64, T)),
        vm((W, 64, T)),
        vm((W, 64, T)),
        vm((W, FB, T)),
        vm((W, FB, T)),
        vm((2, W, FB, D)),
        vm((2, W, FB, half)),
        vm((2, W, FB, half)),
        vm((2, 2, FB, half)),
        vm((2, 2, FB, half // 2)),
        vm((2, 2, FB, half // 2)),
        vm((2, 2, FB, half)),
        vm((2, FB, D)),
        vm((W, VC, D)),
        vm((W, VC, half)),
        vm((W, VC, half)),
        vm((2, VC, half)),
        vm((2, VC, half // 2)),
        vm((2, VC, half // 2)),
        vm((W, 64, half)),
        vm((W, 64, half)),
        vm((2, 64, half)),
        vm((2, W, 64, T)),
        vm((2, W, 64, T)),
        vm((2, W, 64, T)),
        vm((2, 2, 64, D)),
        vm((W, 3, 32, T)),
        vm((W, 3, 32, T)),
        vm((2, 2, 32, D)),
        vm((2, 32, 128), F32),
        vm((W, 32, T)),
        vm((W, 32, T)),
        vm((W, 32, T)),
        vm((2, 32, T)),
        vm((W, 32, T)),
        vm((32, D), F32),
        vm((8, D), F32),
        vm((T, W * FB), F32),
        vm((3, T, VC), F32),
        vm((T, D), F32),
        pltpu.SemaphoreType.DMA((N_REMOTE + 2 * n_seq,)),
        pltpu.SemaphoreType.DMA((N_REMOTE + 2 * n_seq,)),
        pltpu.SemaphoreType.DMA((N_LOCAL,)),
    ]
    return pl.pallas_call(
        functools.partial(layer_kernel, n_seq),
        out_shape=outs,
        in_specs=[pl.BlockSpec(memory_space=pl.ANY)] * len(args),
        out_specs=[pl.BlockSpec(memory_space=pl.ANY)] * len(outs),
        scratch_shapes=scratch,
        compiler_params=pltpu.CompilerParams(
            collective_id=0, has_side_effects=True, vmem_limit_bytes=60 * 2**20
        ),
        name="layer",
    )(*args)


def finish_kernel(*refs):
    n_in = 9
    parts, rest = refs[:n_in], refs[n_in:]
    results, held, sem = rest[:16], rest[16:-1], rest[-1]
    copies = [pltpu.make_async_copy(a, b, sem.at[n]) for n, (a, b) in enumerate(zip(parts, held))]
    for cp in copies:
        cp.start()
    o_out, o_in, o_f, o_d, o_vg, o_qk, o_ext, o_ow, o_small = held
    (r_out, r_in, r_ng, r_q, r_k, r_v, r_g, r_dd, r_du, r_db, r_gg, r_o, r_fn, r_fg, r_fu, r_fd) = results
    T = o_out.shape[2]
    half = o_f.shape[3]
    copies[3].wait()
    r_fd[...] = o_d[...].astype(F32)
    copies[2].wait()
    for h in range(2):
        at = slice(h * half, (h + 1) * half)
        r_fg[:, at] = o_f[h, 0].astype(F32)
        r_fu[:, at] = o_f[h, 1].astype(F32)
    copies[4].wait()
    r_v[...] = o_vg[0].astype(F32)
    r_g[...] = o_vg[1].astype(F32)
    copies[5].wait()
    r_q[...] = o_qk[0].astype(F32)
    r_k[...] = o_qk[1].astype(F32)
    copies[7].wait()
    for h in range(2):
        r_o[:, h * half : (h + 1) * half] = o_ow[h].astype(F32)
    copies[0].wait()
    copies[1].wait()
    for n in range(WAYS):
        r_out[:, n * T : (n + 1) * T] = o_out[n]
        r_in[:, n * T : (n + 1) * T] = o_in[n]
    copies[8].wait()
    r_dd[...] = o_small[0:1, :]
    r_ng[...] = o_small[1:2, 0 : r_ng.shape[1]]
    r_fn[...] = o_small[2:3, 0 : r_fn.shape[1]]
    r_gg[...] = o_small[3:4, 0:64]
    copies[6].wait()
    decay = o_ext[...].T
    r_du[...] = decay[0:16, :].reshape(16, 1, 32)
    r_db[...] = decay[16:17, :]


def finish(parts):
    rows = parts[0].shape[0] * parts[0].shape[2]
    D = parts[3].shape[1]
    FB = parts[3].shape[0]
    slab = D // (WAYS * WAYS)

    def sds(shape, dtype=F32):
        return jax.ShapeDtypeStruct(shape, dtype)

    outs = [
        sds((64, rows), BF),
        sds((64, rows), BF),
        sds((1, slab)),
        sds((32, D)),
        sds((32, D)),
        sds((64, D)),
        sds((64, D)),
        sds((1, D)),
        sds((16, 1, 32)),
        sds((1, 32)),
        sds((1, 64)),
        sds((64, D)),
        sds((1, slab)),
        sds((FB, D)),
        sds((FB, D)),
        sds((FB, D)),
    ]
    return pl.pallas_call(
        finish_kernel,
        out_shape=outs,
        in_specs=[pl.BlockSpec(memory_space=pl.ANY)] * len(parts),
        out_specs=[pl.BlockSpec(memory_space=pltpu.VMEM)] * len(outs),
        scratch_shapes=[pltpu.VMEM(p.shape, p.dtype) for p in parts]
        + [pltpu.SemaphoreType.DMA((len(parts),))],
        compiler_params=pltpu.CompilerParams(vmem_limit_bytes=60 * 2**20),
        name="finish",
    )(*parts)


def shards(
    n_seq,
    tokens,
    norm_gain,
    query_weight,
    key_weight,
    value_weight,
    gate_weight,
    decay_down,
    decay_up,
    decay_bias,
    group_gain,
    out_weight,
    ffn_gain,
    ffn_gate,
    ffn_up,
    ffn_down,
    cotangent,
):
    parts = layer(
        n_seq,
        (
            tokens,
            cotangent,
            norm_gain.reshape(8, -1),
            ffn_gain.reshape(8, -1),
            decay_up,
            decay_bias,
            group_gain[None],
            query_weight.transpose(1, 2, 0),
            key_weight.transpose(1, 2, 0),
            value_weight.transpose(1, 2, 0),
            gate_weight.transpose(1, 2, 0),
            decay_down.T,
            out_weight[0],
            ffn_gate.T,
            ffn_up.T,
            ffn_down,
        ),
    )
    if n_seq > 2:

        def over_pairs(a):
            return jnp.sum(lax.all_gather(a, "seq")[::2].astype(F32), axis=0).astype(a.dtype)

        parts = list(parts[:2]) + [over_pairs(a) for a in parts[2:]]
    (r_out, r_in, r_ng, r_q, r_k, r_v, r_g, r_dd, r_du, r_db, r_gg, r_o, r_fn, r_fg, r_fu, r_fd) = finish(parts)
    return (
        r_out.T,
        r_in.T,
        r_ng[0],
        r_q.T[:, None, :],
        r_k.T[:, None, :],
        r_v.T[:, None, :],
        r_g.T[:, None, :],
        r_dd.T,
        r_du,
        r_db,
        r_gg[0],
        r_o[None],
        r_fn[0],
        r_fg.T,
        r_fu.T,
        r_fd,
    )


def solution(mesh):
    in_specs = (
        P("seq", None),
        P(),
        P(None, None, "kax"),
        P(None, None, "kax"),
        P(None, None, "vax"),
        P(None, None, "vax"),
        P(),
        P(None, None, "kax"),
        P(None, "kax"),
        P("vax"),
        P("kax", "vax", None),
        P(),
        P(None, ("kax", "vax")),
        P(None, ("kax", "vax")),
        P(("kax", "vax"), None),
        P("seq", None),
    )
    out_specs = (
        P("seq", ("kax", "vax")),
        P("seq", ("kax", "vax")),
        P(("kax", "vax")),
        P(None, "vax", "kax"),
        P(None, "vax", "kax"),
        P(None, "kax", "vax"),
        P(None, "kax", "vax"),
        P(None, ("kax", "vax")),
        P(None, "vax", "kax"),
        P("vax", "kax"),
        P("vax"),
        P("kax", "vax", None),
        P(("kax", "vax")),
        P(None, ("kax", "vax")),
        P(None, ("kax", "vax")),
        P(("kax", "vax"), None),
    )
    return jax.shard_map(
        functools.partial(shards, mesh.shape["seq"]),
        mesh=mesh,
        in_specs=in_specs,
        out_specs=out_specs,
        check_vma=False,
    )
```

```python
import functools

import jax
import jax.numpy as jnp
from jax import lax
from jax.experimental import pallas as pl
from jax.experimental.pallas import tpu as pltpu
from jax.sharding import PartitionSpec as P

MESH = pl.DeviceIdType.MESH
BF = jnp.bfloat16
F32 = jnp.float32
CB = 128
WAYS = 4
EPS = 1e-06
HIGH = lax.Precision.HIGHEST


def nn(a, b, precision=None):
    return lax.dot_general(
        a, b, (((1,), (0,)), ((), ())), precision=precision, preferred_element_type=F32
    )


def nt(a, b, precision=None):
    return lax.dot_general(
        a, b, (((1,), (1,)), ((), ())), precision=precision, preferred_element_type=F32
    )


def tn(a, b, precision=None):
    return lax.dot_general(
        a, b, (((0,), (0,)), ((), ())), precision=precision, preferred_element_type=F32
    )


def xor(index, d):
    if d == 1:
        return index + 1 - 2 * lax.rem(index, 2)
    if d == 2:
        return lax.rem(index + 2, 4)
    return 3 - index


def as_row(column):
    return jnp.broadcast_to(column, (column.shape[0], 128)).T[:8]


def as_column(row):
    return jnp.broadcast_to(row[:1], (128, row.shape[1])).T[:, :1]


def flat_row(block):
    return jnp.concatenate([block[r : r + 1] for r in range(block.shape[0])], axis=1)


def lanes(block):
    return jnp.concatenate([block[n] for n in range(block.shape[0])], axis=1)


def total(own, got):
    out = own.astype(F32)
    for d in (1, 2, 3):
        out = out + got[d].astype(F32)
    return out


def layer_kernel(
    n_seq,
    tok,
    cot,
    ng,
    ffg,
    dup,
    dbi,
    ggn,
    wq,
    wk,
    wv,
    wg,
    dd,
    wo,
    fg,
    fu,
    fd,
    r_out,
    r_in,
    r_ng,
    r_q,
    r_k,
    r_v,
    r_g,
    r_dd,
    r_du,
    r_db,
    r_gg,
    r_o,
    r_fn,
    r_fg,
    r_fu,
    r_fd,
    x_v,
    c_v,
    x_all,
    c_all,
    n_all,
    n_v,
    xr_v,
    dd_v,
    ng_v,
    ffg_v,
    dup_v,
    dbi_v,
    ggn_v,
    sq_v,
    gain_v,
    qk_v,
    ext_v,
    v_v,
    g_v,
    gge_v,
    o_v,
    f_v,
    st_v,
    tt_v,
    bst_v,
    btt_v,
    ga_v,
    sgg,
    rgg,
    cgg,
    sst,
    rst,
    so,
    ro,
    co,
    sgn,
    rgn,
    cgn,
    ao,
    oseg,
    ai,
    iseg,
    hd,
    hseg,
    gw,
    pre,
    pres,
    rfw,
    qfw,
    cfw,
    fin_f,
    dsum,
    gow,
    preo,
    preso,
    rowk,
    qow,
    cow,
    mid_o,
    rowz,
    coz,
    fin_ow,
    vz,
    zvg,
    kvg,
    vgsum,
    qka,
    kqa,
    qksum,
    esum,
    sm0,
    sm1,
    sm2,
    sm3,
    sm4,
    pick,
    lall_v,
    gh_v,
    act_v,
    p_v,
    ss,
    rs,
    ls,
):
    s = lax.axis_index("seq")
    i = lax.axis_index("kax")
    j = lax.axis_index("vax")
    par = lax.rem(s, 2)
    oth = 1 - par
    T, D = x_v.shape
    rows = x_all.shape[0]
    FB = f_v.shape[2]
    half = D // 2
    W = WAYS
    DIRS = (1, 2, 3)
    mine = pl.ds(pl.multiple_of(par * half, half), half)
    other = pl.ds(pl.multiple_of(oth * half, half), half)
    partner = {"seq": s + 1 - 2 * par}
    kdev = [None] + [{"kax": xor(i, d)} for d in DIRS]
    vdev = [None] + [{"vax": xor(j, d)} for d in DIRS]
    ki = [None] + [xor(i, d) for d in DIRS]
    vj = [None] + [xor(j, d) for d in DIRS]
    seqdev = [{"seq": lax.rem(s + e, n_seq)} for e in range(1, n_seq)]

    count = [0, 0]
    sent = []

    def slot():
        count[0] += 1
        return count[0] - 1

    def remote(src, dst, dev, to=None):
        n = slot()
        return pltpu.make_async_remote_copy(
            src_ref=src,
            dst_ref=dst,
            send_sem=ss.at[n],
            recv_sem=rs.at[n if to is None else to],
            device_id=dev,
            device_id_type=MESH,
        )

    def send(src, dst, dev):
        cp = remote(src, dst, dev)
        cp.start()
        sent.append(cp)
        return cp

    def load(src, dst):
        n = count[1]
        count[1] += 1
        cp = pltpu.make_async_copy(src, dst, ls.at[n])
        cp.start()
        return cp

    class Fan:
        def __init__(self, copies, size):
            n = slot()

            def one(src, dst, dev):
                return pltpu.make_async_remote_copy(
                    src_ref=src,
                    dst_ref=dst,
                    send_sem=ss.at[n],
                    recv_sem=rs.at[n],
                    device_id=dev,
                    device_id_type=MESH,
                )

            for src, dst, dev in copies:
                one(src, dst, dev).start()
            self.all = one(size, size, partner)
            sent.append(self)

        def wait_recv(self):
            self.all.wait_recv()

        def wait_send(self):
            self.all.wait_send()

    def arrived(copies):
        for cp in copies:
            cp.wait_recv()

    def here(copies):
        for cp in copies:
            cp.wait()

    inner = lax.rem(j + 1, W) >= 2
    inner_sent = []
    outer_sent = []

    class LineGather:
        def __init__(self, view):
            a, b, c = slot(), slot(), slot()
            self.near = remote(view(j), view(j), vdev[1], a)
            self.near.start()
            sent.append(self.near)
            across = remote(view(j), view(j), vdev[3], c)
            self.got = [
                pltpu.make_async_remote_copy(
                    src_ref=view(vj[d]),
                    dst_ref=view(vj[d]),
                    send_sem=ss.at[n],
                    recv_sem=rs.at[n],
                    device_id=vdev[1],
                    device_id_type=MESH,
                )
                for d, n in zip(DIRS, (a, b, c))
            ]
            self.on = [
                remote(view(vj[1]), view(vj[1]), vdev[3], b),
                remote(view(vj[3]), view(vj[3]), vdev[1], b),
                remote(view(vj[2]), view(vj[2]), vdev[1], c),
            ]
            inner_sent.extend([across] + self.on)

            @pl.when(inner)
            def _():
                across.start()

        def step(self, n):
            @pl.when(inner)
            def _():
                self.got[(0, 2, 1)[n]].wait_recv()
                self.on[n].start()

        def collect(self):
            @pl.when(jnp.logical_not(inner))
            def _():
                arrived(self.got)

    class LineSum:
        def __init__(self, part, near, far, relay, summed):
            self.part, self.near, self.far, self.relay, self.summed = part, near, far, relay, summed
            b = slot()
            self.first = [
                remote(part(vj[3]), relay.at[0], vdev[1]),
                remote(part(vj[2]), relay.at[1], vdev[1]),
            ]
            outer_sent.extend(self.first)

            @pl.when(jnp.logical_not(inner))
            def _():
                for cp in self.first:
                    cp.start()

            self.second = [
                remote(summed.at[0], far, vdev[2], b),
                remote(summed.at[1], far, vdev[3], b),
            ]
            inner_sent.extend(self.second)
            self.last = pltpu.make_async_remote_copy(
                src_ref=far,
                dst_ref=far,
                send_sem=ss.at[b],
                recv_sem=rs.at[b],
                device_id=vdev[1],
                device_id_type=MESH,
            )

        def rest(self):
            self.direct = send(self.part(vj[1]), self.near, vdev[1])
            return self

        def step(self, n):
            @pl.when(inner)
            def _():
                self.first[n].wait_recv()
                mine_too = self.part(vj[2 + n])[...].astype(F32)
                self.summed[n] = (mine_too + self.relay[n].astype(F32)).astype(BF)
                self.second[n].start()

        def collect(self):
            self.direct.wait_recv()
            self.last.wait_recv()

        def total(self):
            out = self.part(j)[...].astype(F32)
            return out + self.near[...].astype(F32) + self.far[...].astype(F32)

    class SquareSum:
        def __init__(self, part, got, relay, summed):
            self.part, self.got, self.relay, self.summed = part, got, relay, summed
            q = got.shape[-1] // 2
            self.at = [pl.ds(0, q), pl.ds(q, q)]
            self.first = [
                send(self.half(ki[3], n), relay.at[n], kdev[1 + n]) for n in range(2)
            ]
            self.direct = [
                send(self.half(ki[1 + n], n), self.into(n, n), kdev[1 + n]) for n in range(2)
            ]

        def half(self, target, n):
            return self.part(target, self.at[n])

        def into(self, n, h):
            return self.got.at[n, :, self.at[h]]

        def step(self):
            self.second = []
            for n in range(2):
                self.first[n].wait_recv()
                own = self.half(ki[2 - n], n)[...].astype(F32)
                self.summed[n] = (own + self.relay[n].astype(F32)).astype(BF)
                self.second.append(
                    send(self.summed.at[n], self.into(1 - n, n), kdev[2 - n])
                )

        def collect(self):
            arrived(self.direct + self.second)

        def total(self):
            out = self.part(i, pl.ds(0, self.got.shape[-1]))[...].astype(F32)
            return out + self.got[0].astype(F32) + self.got[1].astype(F32)

    l_small = [load(dup, dup_v), load(dbi, dbi_v), load(ggn, ggn_v)]
    l_qk = [load(wq.at[j], qk_v.at[i, 0]), load(wk.at[j], qk_v.at[i, 1])]
    segment = pl.ds(pl.multiple_of(i * T, T), T)
    l_x = [load(tok.at[segment], x_v), load(ng, ng_v), load(ffg, ffg_v)]
    l_dd = load(dd, dd_v.at[pl.ds(0, 16)])
    l_v = load(wv.at[j], v_v.at[j])
    l_g = load(wg.at[j], g_v.at[j])
    l_c = load(cot.at[segment], c_v)
    l_f = [load(fg, f_v.at[0, i]), load(fu, f_v.at[1, i]), load(fd, f_v.at[2, i])]
    l_o = load(wo, o_v.at[i, j])
    l_xa = load(tok, x_all)
    l_ca = load(cot, c_all)

    barrier = pltpu.get_barrier_semaphore()
    for dev in kdev[1:] + vdev[1:] + seqdev:
        pl.semaphore_signal(barrier, inc=1, device_id=dev, device_id_type=MESH)

    dd_v[16:, :] = jnp.zeros((dd_v.shape[0] - 16, D), BF)
    here(l_small)
    head3 = lax.broadcasted_iota(jnp.int32, (16, W, 32), 1)
    head2 = lax.broadcasted_iota(jnp.int32, (W, 32), 0)
    sq_v[...] = jnp.zeros_like(sq_v)
    sq_v[0:16, 0:32] = jnp.sum(jnp.where(head3 == j, dup_v[...].astype(F32), 0.0), axis=1)
    sq_v[16:17, 0:32] = jnp.sum(
        jnp.where(head2 == j, dbi_v[...].astype(F32), 0.0), axis=0, keepdims=True
    )
    ext_v[i] = sq_v[...].T[:32].astype(BF)
    sq_v[...] = jnp.zeros_like(sq_v)
    sq_v[0:16, 0:64] = jnp.broadcast_to(ggn_v[...].astype(F32), (16, 64))
    gge_v[j] = sq_v[0:16].astype(BF)

    pl.semaphore_wait(barrier, 6 + len(seqdev))

    here(l_qk)
    t_qk = [None] + [send(qk_v.at[i, par], qk_v.at[i, par], kdev[d]) for d in DIRS]
    t_v = [None] + [send(wv.at[vj[d], :, mine], v_v.at[j, :, mine], vdev[d]) for d in DIRS]
    t_ext = Fan([(ext_v.at[i], ext_v.at[i], kdev[d]) for d in DIRS], ext_v.at[pl.ds(0, 3)])
    low = pl.ds(0, 32)
    high = pl.ds(32, 32)
    t_oa = [None] + [
        send(wo.at[low, mine], o_v.at[i, j, low, mine], vdev[d]) for d in DIRS
    ]
    t_ob = [None] + [
        send(wo.at[high, mine], o_v.at[i, j, high, mine], kdev[d]) for d in DIRS
    ]
    quarter = half // 2
    two = [
        pl.ds(pl.multiple_of(par * half + n * quarter, quarter), quarter) for n in range(2)
    ]

    class SquareGather:
        def __init__(self, view, own=None):
            self.view = view
            own = view(i, mine) if own is None else own
            self.near = [send(own, view(i, mine), kdev[d]) for d in (1, 2)]

        def step(self):
            self.far, moves = [], []
            for n in range(2):
                self.near[n].wait_recv()
                view = self.view(ki[1 + n], two[n])
                self.far.append(send(view, view, kdev[2 - n]))
                view = self.view(ki[1 + n], mine)
                moves.append(send(view, view, partner))
            return moves

        def collect(self):
            arrived(self.far)
            view = self.view(ki[3], mine)
            return [send(view, view, partner)]

    weights = (fg, fu, fd)

    def gather_weight(n):
        return SquareGather(lambda src, at: f_v.at[n, src, :, at], weights[n].at[:, mine])

    t_fd = gather_weight(2)
    t_g = [None] + [send(wg.at[vj[d], :, mine], g_v.at[j, :, mine], vdev[d]) for d in DIRS]
    t_gge = Fan([(gge_v.at[j], gge_v.at[j], vdev[d]) for d in DIRS], gge_v.at[pl.ds(0, 3)])

    here(l_x)
    x = x_v[...].astype(F32)
    g1 = flat_row(ng_v[...].astype(F32))
    g3 = flat_row(ffg_v[...].astype(F32))
    r1 = lax.rsqrt(jnp.sum(x * x, axis=1, keepdims=True) / D + EPS)
    n_v[...] = (x * r1 * g1).astype(BF)
    l_dd.wait()
    lane = lax.broadcasted_iota(jnp.int32, (T, 128), 1)
    lrp = jnp.where(lane == 16, 1.0, nt(n_v[...], dd_v[...]))

    for d in DIRS:
        t_qk[d].wait_recv()
    views = [qk_v.at[ki[d], par] for d in DIRS]
    f_qk = Fan([(view, view, partner) for view in views], qk_v.at[pl.ds(0, 3), 0])
    t_ext.wait_recv()
    f_qk.wait_recv()
    normed = n_v[...]
    wq_all = qk_v[:, 0].reshape(W * 32, D)
    wk_all = qk_v[:, 1].reshape(W * 32, D)
    ext_all = ext_v[...].reshape(W * 32, 128)
    scale = 128.0 ** (-0.5)
    q = nt(normed, wq_all) * scale
    k = nt(normed, wk_all)
    arg = nt(lrp, ext_all.astype(F32), HIGH)
    rates = (jnp.minimum(arg, 0.0) - jnp.log1p(jnp.exp(-jnp.abs(arg)))) / 16.0
    row_id = lax.broadcasted_iota(jnp.int32, (CB, CB), 0)
    col_id = lax.broadcasted_iota(jnp.int32, (CB, CB), 1)
    causal = row_id >= col_id
    tri = jnp.where(causal, 1.0, 0.0)
    nblk = T // CB
    blk = [slice(c * CB, (c + 1) * CB) for c in range(nblk)]
    e1, e2, em, el, dec, qd, kd, qi, ke, score = [], [], [], [], [], [], [], [], [], []
    for c in range(nblk):
        cum = nn(tri, rates[blk[c]], HIGH)
        mid = cum[CB // 2 - 1 : CB // 2]
        last = cum[CB - 1 : CB]
        e1.append(jnp.exp(cum - mid))
        e2.append(jnp.exp(mid - cum))
        em.append(jnp.exp(mid))
        el.append(jnp.exp(last - mid))
        dec.append(jnp.exp(last))
        a = q[blk[c]] * e1[c]
        b = k[blk[c]] * e2[c]
        qd.append(a.astype(BF))
        kd.append(b.astype(BF))
        qi.append((a * em[c]).astype(BF))
        ke.append((b * el[c]).astype(BF))
        score.append(jnp.where(causal, nt(qd[c], kd[c]), 0.0).astype(BF))

    l_v.wait()
    for d in DIRS:
        t_v[d].wait_recv()
    first_half = pl.ds(0, half)
    views = [v_v.at[vj[d], :, mine] for d in DIRS]
    f_vv = Fan([(view, view, partner) for view in views], v_v.at[pl.ds(0, 3), :, first_half])
    f_vv.wait_recv()
    wv_all = v_v[...].reshape(W * 64, D)
    v = nt(normed, wv_all).astype(BF)
    up = [tn(v[blk[c]], ke[c]) for c in range(nblk)]
    loc = up[0]
    locd = dec[0]
    for c in range(1, nblk):
        loc = loc * dec[c] + up[c]
        locd = locd * dec[c]
    VC = loc.shape[0]
    st_v[i, :VC] = loc.astype(BF)
    st_v[i, VC:] = jnp.broadcast_to(locd, (16, 128)).astype(BF)
    t_st = Fan([(st_v.at[i], st_v.at[i], kdev[d]) for d in DIRS], st_v.at[pl.ds(0, 3)])
    t_fg = gather_weight(0)
    t_fu = gather_weight(1)
    mixed = [nn(score[c], v[blk[c]]) for c in range(nblk)]

    f_o = []
    l_o.wait()
    for d in DIRS:
        t_oa[d].wait_recv()
        view = o_v.at[i, vj[d], low, mine]
        f_o.append(send(view, view, partner))
    t_oa2 = SquareGather(lambda src, at: o_v.at[src, :, low, at])
    for d in DIRS:
        t_ob[d].wait_recv()
        view = o_v.at[ki[d], j, high, mine]
        f_o.append(send(view, view, partner))
    t_ob2 = LineGather(lambda src: o_v.at[:, src, high, mine])
    here(l_f)
    f_f = t_fd.step()

    def gather_states(slots, totals, back):
        order = range(W - 1, -1, -1) if back else range(W)
        pre_s = jnp.zeros((VC, 128), F32)
        pre_d = jnp.ones((1, 128), F32)
        tot_s = jnp.zeros((VC, 128), F32)
        tot_d = jnp.ones((1, 128), F32)
        for other_i in order:
            one_s = slots[other_i, :VC].astype(F32)
            one_d = slots[other_i, VC : VC + 1].astype(F32)
            use = (other_i > i) if back else (other_i < i)
            pre_s = jnp.where(use, pre_s * one_d + one_s, pre_s)
            pre_d = jnp.where(use, pre_d * one_d, pre_d)
            tot_s = tot_s * one_d + one_s
            tot_d = tot_d * one_d
        totals[s, :VC] = tot_s.astype(BF)
        totals[s, VC:] = jnp.broadcast_to(tot_d, (16, 128)).astype(BF)
        return pre_s, pre_d, [send(totals.at[s], totals.at[s], dev) for dev in seqdev]

    def entering(totals, back, pre_s, pre_d, moves):
        arrived(moves)
        order = range(n_seq - 1, -1, -1) if back else range(n_seq)
        far = jnp.zeros((VC, 128), F32)
        for other_s in order:
            one_s = totals[other_s, :VC].astype(F32)
            one_d = totals[other_s, VC : VC + 1].astype(F32)
            use = (other_s > s) if back else (other_s < s)
            far = jnp.where(use, far * one_d + one_s, far)
        return pre_s + pre_d * far

    t_st.wait_recv()
    states = gather_states(st_v, tt_v, False)

    l_g.wait()
    for d in DIRS:
        t_g[d].wait_recv()
    views = [g_v.at[vj[d], :, mine] for d in DIRS]
    f_g = Fan([(view, view, partner) for view in views], g_v.at[pl.ds(0, 3), :, first_half])
    start = [entering(tt_v, False, *states)]
    for c in range(nblk):
        start.append(start[c] * dec[c] + up[c])
    start_low = [a.astype(BF) for a in start]
    for c in range(nblk):
        mixed[c] = mixed[c] + nt(qi[c], start_low[c])
    mix = jnp.concatenate(mixed, axis=0)
    r2 = lax.rsqrt(jnp.sum(mix * mix, axis=1, keepdims=True) / VC + EPS)
    normal = mix * r2
    f_g.wait_recv()
    t_gge.wait_recv()
    wg_all = g_v[...].reshape(W * 64, D)
    gate = nt(normed, wg_all)
    gg = jnp.concatenate([gge_v[h].astype(F32)[0:1, 0:64] for h in range(W)], axis=1)
    sig = 1.0 / (1.0 + jnp.exp(-gate))
    act = gate * sig
    act_v[0] = act
    act_v[1] = sig + act * (1.0 - sig)
    ga_v[j] = (normal * gg * act).astype(BF)
    act_v[2] = normal
    t_ga = LineGather(lambda src: ga_v.at[src])

    here([l_xa, l_ca])
    for part in range(rows // T):
        at = pl.ds(part * T, T)
        xa = x_all[at, :].astype(F32)
        ra = lax.rsqrt(jnp.sum(xa * xa, axis=1, keepdims=True) / D + EPS)
        n_all[at, :] = (xa * ra * g1).astype(BF)
    xr_v[...] = (x * (r1 * r1 * r1)).astype(BF).T
    low_all = jnp.where(
        lax.broadcasted_iota(jnp.int32, (rows, 128), 1) == 16, 1.0, nt(n_all[...], dd_v[...])
    )
    lall_v[...] = low_all.astype(BF)
    t_ob2.step(0)
    t_ob2.step(1)
    f_f += t_fg.step()
    t_ob2.step(2)
    t_ga.step(0)
    t_ga.step(1)
    f_f += t_fd.collect()
    f_f += t_fu.step()
    f_o += t_oa2.step()
    t_ga.step(2)
    l_c.wait()
    arrived(f_f)
    dn = f_v[2].reshape(W * FB, D)
    gh_v[...] = nt(c_v[...], dn)
    f_f = t_fg.collect()
    f_f += t_fu.collect()
    f_o += t_oa2.collect()
    t_ob2.collect()
    for d in DIRS:
        view = o_v.at[:, vj[d], high, mine]
        f_o.append(send(view, view, partner))
    t_ga.collect()
    arrived(f_o)
    att = nn(ga_v[0], o_v[0].reshape(W * 64, D))
    for h in range(1, W):
        att = att + nn(ga_v[h], o_v[h].reshape(W * 64, D))
    resid = x_v[...].astype(F32) + att
    r3 = lax.rsqrt(jnp.sum(resid * resid, axis=1, keepdims=True) / D + EPS)
    fin = (resid * r3 * g3).astype(BF)
    arrived(f_f)

    gT = f_v[0].reshape(W * FB, D)
    uT = f_v[1].reshape(W * FB, D)
    gval = nt(fin, gT)
    uval = nt(fin, uT)
    fsig = 1.0 / (1.0 + jnp.exp(-gval))
    fact = gval * fsig
    hid = (fact * uval).astype(BF)
    gh = gh_v[...]
    gup = (gh * fact).astype(BF)
    ggate = (gh * uval * (fsig + fact * (1.0 - fsig))).astype(BF)
    part = nn(ggate, gT) + nn(gup, uT)
    p_v[...] = part
    sst[...] = as_row(jnp.sum(resid * g3 * part, axis=1, keepdims=True))
    t_m3 = Fan([(sst, rst.at[d], vdev[d]) for d in DIRS], rst.at[pl.ds(1, 3)])
    ggp = nt((part * g3).astype(BF), o_v[...].reshape(W * W * 64, D))
    for h in range(W):
        sgg[h] = ggp[:, h * VC : (h + 1) * VC].astype(BF)
    halves = [pl.ds(n * T // 2, T // 2) for n in range(2)]
    t_gg = [
        LineSum(
            lambda to, at=at: sgg.at[to, at],
            rgg.at[0, at],
            rgg.at[1, at],
            rgg.at[pl.ds(2, 2), at],
            cgg.at[:, at],
        )
        for at in halves
    ]
    for line in t_gg:
        line.rest()
    hd[...] = hid.T.reshape(W, FB, T)
    t_hd = Fan([(hd.at[ki[d]], hseg.at[i], kdev[d]) for d in DIRS], hseg.at[pl.ds(0, 3)])
    hseg[i] = hd[i]

    def weight_part(n, grad):
        gw[n] = tn(grad, fin).astype(BF).reshape(W, FB, D)
        return send(gw.at[n, :, :, other], pre.at[n], partner)

    def settle(n, move):
        move.wait_recv()
        pres[n] = (gw[n, :, :, mine].astype(F32) + pre[n].astype(F32)).astype(BF)

    def square(n):
        return SquareSum(
            lambda to, at: pres.at[n, to, :, at], rfw.at[n], qfw.at[n], cfw.at[n]
        )

    t_pre0 = weight_part(0, ggate)

    feature = lax.broadcasted_iota(jnp.int32, (1, D), 1)
    own_slab = jnp.where(lax.rem(feature // 64, W) == j, 1.0, 0.0)
    own_run = jnp.where(feature // (D // W) == j, 1.0, 0.0)
    t_m3.wait_recv()
    m3 = as_column(sst[...] + rst[1] + rst[2] + rst[3]) / D
    base = c_v[...].astype(F32) - resid * (r3 * r3 * r3 * m3)
    t_gg[0].step(0)
    direct = nt(base.astype(BF), o_v[j].reshape(W * 64, D))
    full = p_v[...] * (g3 * r3)
    mixed_in = (full + own_run * base).astype(BF)
    for h in range(W):
        gow[h] = tn(ga_v[h], mixed_in).astype(BF)
    t_po = send(gow.at[:, :, other], preo, partner)
    t_gg[0].step(1)
    settle(0, t_pre0)
    t_fw0 = square(0)
    so[...] = (nn(hid, dn) + own_slab * resid).astype(BF).T.reshape(W, W, 64, T)
    t_gg[1].step(0)
    t_out = LineSum(lambda to: so.at[:, to], ro.at[0], ro.at[1], ro.at[pl.ds(2, 2)], co).rest()
    ffn_gain = jnp.sum(part * resid * r3, axis=0, keepdims=True)
    t_gg[1].step(1)
    t_pre1 = weight_part(1, gup)
    t_po.wait_recv()
    preso[...] = (gow[:, :, mine].astype(F32) + preo[...].astype(F32)).astype(BF)
    t_fw0.step()
    for line in t_gg:
        line.collect()

    ggs = jnp.concatenate([line.total() for line in t_gg], axis=0)
    ggrad = direct + r3 * ggs
    act = act_v[0]
    normal = act_v[2]
    dgate = (ggrad * normal * gg * act_v[1]).astype(BF)
    gs = ggrad * act
    group = jnp.sum(gs * normal, axis=0, keepdims=True)
    gnm = gs * gg
    gmix = (r2 * (gnm - normal * (jnp.sum(normal * gnm, axis=1, keepdims=True) / VC))).astype(BF)

    qst = [tn(gmix[blk[c]], qi[c]) for c in range(nblk)]
    bloc = qst[nblk - 1]
    for c in range(nblk - 2, -1, -1):
        bloc = bloc * dec[c] + qst[c]
    bst_v[i, :VC] = bloc.astype(BF)
    bst_v[i, VC:] = jnp.broadcast_to(locd, (16, 128)).astype(BF)
    t_bst = Fan([(bst_v.at[i], bst_v.at[i], kdev[d]) for d in DIRS], bst_v.at[pl.ds(0, 3)])
    t_ow = SquareSum(lambda to, at: preso.at[to, :, at], rowk, qow, cow)
    vz[1] = dgate.T.reshape(W, 64, T)
    t_gz = Fan([(vz.at[1, vj[d]], zvg.at[1, j], vdev[d]) for d in DIRS], zvg.at[1, pl.ds(0, 3)])
    dq_in, dk_in, dv_in = [], [], []
    for c in range(nblk):
        ds = jnp.where(causal, nt(gmix[blk[c]], v[blk[c]]), 0.0).astype(BF)
        dq_in.append(nn(ds, kd[c]) + em[c] * nn(gmix[blk[c]], start_low[c]))
        dk_in.append(tn(ds, qd[c]))
        dv_in.append(tn(score[c], gmix[blk[c]]))
    settle(1, t_pre1)
    t_bst.wait_recv()
    after = [None] * nblk
    states = gather_states(bst_v, btt_v, True)
    t_out.step(0)
    after[nblk - 1] = entering(btt_v, True, *states)
    for c in range(nblk - 2, -1, -1):
        after[c] = after[c + 1] * dec[c + 1] + qst[c + 1]

    ql, kl, vl, ga = [], [], [], []
    for c in range(nblk):
        low_after = after[c].astype(BF)
        dq = e1[c] * dq_in[c]
        dk = e2[c] * (dk_in[c] + el[c] * nn(v[blk[c]], low_after))
        dv = dv_in[c] + nt(ke[c], low_after)
        gc = q[blk[c]] * dq - k[blk[c]] * dk
        extra = jnp.sum(after[c] * start[c + 1], axis=0, keepdims=True)
        gc = jnp.where(row_id == CB - 1, gc + extra, gc)
        gr = tn(tri, gc, HIGH)
        ga.append(gr / (1.0 + jnp.exp(arg[blk[c]])) / 16.0)
        ql.append((dq * scale).astype(BF))
        kl.append(dk.astype(BF))
        vl.append(dv.astype(BF))
    ql = jnp.concatenate(ql, axis=0)
    kl = jnp.concatenate(kl, axis=0)
    vl = jnp.concatenate(vl, axis=0)
    ga = jnp.concatenate(ga, axis=0).astype(BF)
    vz[0] = vl.T.reshape(W, 64, T)
    t_vz = Fan([(vz.at[0, vj[d]], zvg.at[0, j], vdev[d]) for d in DIRS], zvg.at[0, pl.ds(0, 3)])
    qka[:, 0] = ql.T.reshape(W, 32, T)
    qka[:, 1] = kl.T.reshape(W, 32, T)
    qka[:, 2] = ga.T.reshape(W, 32, T)
    t_qa = Fan([(qka.at[ki[d]], kqa.at[i], kdev[d]) for d in DIRS], kqa.at[pl.ds(0, 3)])
    t_out.step(1)
    glr = nn(ga, ext_all).astype(BF)
    gn = nn(ql, wq_all) + nn(kl, wk_all) + nn(vl, wv_all) + nn(dgate, wg_all) + nn(glr, dd_v[...])
    x = x_v[...].astype(F32)
    gnx = gn * x
    norm_gain = jnp.sum(gnx * r1, axis=0, keepdims=True)
    m1p = as_row(jnp.sum(gnx * g1, axis=1, keepdims=True))[:1]
    small = tn(glr, normed)[:16]
    rid = lax.broadcasted_iota(jnp.int32, (16, T), 0)
    for h in range(W):
        at = slice(h * T, (h + 1) * T)
        sm0[h, 0:16] = small[:, at].astype(BF)
        rest = jnp.where(rid == 0, norm_gain[:, at], 0.0)
        rest = jnp.where(rid == 1, ffn_gain[:, at], rest)
        rest = jnp.where(rid == 3, m1p, rest)
        if h == 0:
            rest = jnp.where(rid == 2, group, rest)
        sm0[h, 16:32] = rest.astype(BF)
    t_s0 = Fan([(sm0.at[vj[d]], sm1.at[d], vdev[d]) for d in DIRS], sm1.at[pl.ds(1, 3)])
    whole = gn * (r1 * g1) + full + own_slab * base
    sgn[...] = whole.astype(BF).T.reshape(W, W, 64, T)
    pairs = [pl.ds(n * W // 2, W // 2) for n in range(2)]
    t_gn = [
        LineSum(
            lambda to, at=at: sgn.at[at, to],
            rgn.at[0, at],
            rgn.at[1, at],
            rgn.at[pl.ds(2, 2), at],
            cgn.at[:, at],
        )
        for at in pairs
    ]
    for line in t_gn:
        line.rest()
    t_ow.step()
    t_fw1 = square(1)

    t_out.collect()
    ao[...] = t_out.total().astype(BF)
    t_ao = Fan([(ao.at[ki[d]], oseg.at[i], kdev[d]) for d in DIRS], oseg.at[pl.ds(0, 3)])
    oseg[i] = ao[i]

    t_gz.wait_recv()
    zvg[1, j] = vz[1, j]
    t_gk = Fan([(zvg.at[1, ki[d]], kvg.at[1, i], kdev[d]) for d in DIRS], kvg.at[1, pl.ds(0, 3)])
    kvg[1, i] = zvg[1, i]

    t_hd.wait_recv()
    dsum[0] = nn(lanes(hseg[...]), c_all[...]).astype(BF)
    t_ds = send(dsum.at[0], dsum.at[1], partner)

    t_s0.wait_recv()
    sm2[0] = total(sm0[j], sm1).astype(BF)
    m1 = (
        sm0[0, 19:20].astype(F32)
        + sm1[1, 19:20].astype(F32)
        + sm1[2, 19:20].astype(F32)
        + sm1[3, 19:20].astype(F32)
    ) / D
    t_s1 = Fan([(sm2.at[0], sm2.at[d], kdev[d]) for d in DIRS], sm2.at[pl.ds(1, 3)])
    t_vz.wait_recv()
    zvg[0, j] = vz[0, j]
    t_vk = Fan([(zvg.at[0, ki[d]], kvg.at[0, i], kdev[d]) for d in DIRS], kvg.at[0, pl.ds(0, 3)])
    kvg[0, i] = zvg[0, i]
    t_gn[0].step(0)
    t_gn[0].step(1)
    t_fw1.step()
    t_gn[1].step(0)
    t_gn[1].step(1)

    t_ow.collect()
    mid_o[...] = t_ow.total().astype(BF).reshape(W, 64, half)
    t_oz = LineSum(
        lambda to: mid_o.at[to], rowz.at[0], rowz.at[1], rowz.at[pl.ds(2, 2)], coz
    ).rest()

    t_qa.wait_recv()
    kqa[i] = qka[i]
    nall = n_all[...]
    for n in range(2):
        qksum[0, n] = nn(lanes(kqa[:, n]), nall).astype(BF)
    esum[0] = nn(lanes(kqa[:, 2]), lall_v[...])
    t_qs = send(qksum.at[0], qksum.at[1], partner)
    t_es = send(esum.at[0], esum.at[1], partner)

    t_s1.wait_recv()
    sm3[0] = total(sm2[0], sm2).astype(BF)
    t_s2 = send(sm3.at[0], sm3.at[1], partner)

    def finish_square(n, line):
        line.collect()
        fin_f[par, n] = line.total().astype(BF)
        return send(fin_f.at[par, n], fin_f.at[par, n], partner)

    t_ff = [finish_square(0, t_fw0)]

    t_gk.wait_recv()
    t_vk.wait_recv()
    for n in range(2):
        vgsum[0, n] = nn(lanes(kvg[n]), nall).astype(BF)
    t_vs = send(vgsum.at[0], vgsum.at[1], partner)
    t_s2.wait_recv()
    sm4[j] = (sm3[0].astype(F32) + sm3[1].astype(F32)).astype(BF)
    t_s3 = Fan([(sm4.at[j], sm4.at[j], vdev[d]) for d in DIRS], sm4.at[pl.ds(0, 3)])

    for line in t_gn:
        line.collect()
    summed = jnp.concatenate([line.total() for line in t_gn], axis=0)
    for h in range(W):
        at = pl.ds(pl.multiple_of((h * W + j) * 64, 64), 64)
        ai[h] = (summed[h] - xr_v[at, :].astype(F32) * m1).astype(BF)
    t_ai = Fan([(ai.at[ki[d]], iseg.at[i], kdev[d]) for d in DIRS], iseg.at[pl.ds(0, 3)])
    iseg[i] = ai[i]
    t_oz.step(0)
    t_oz.step(1)
    t_ff.append(finish_square(1, t_fw1))

    t_ds.wait_recv()
    r_fd[...] = dsum[0].astype(F32) + dsum[1].astype(F32)
    t_ao.wait_recv()
    r_out[...] = lanes(oseg[...])
    t_qs.wait_recv()
    r_q[...] = qksum[0, 0].astype(F32) + qksum[1, 0].astype(F32)
    r_k[...] = qksum[0, 1].astype(F32) + qksum[1, 1].astype(F32)
    t_es.wait_recv()
    decay = (esum[0] + esum[1]).T
    r_du[...] = decay[0:16, :].reshape(16, 1, 32)
    r_db[...] = decay[16:17, :]
    t_vs.wait_recv()
    r_v[...] = vgsum[0, 0].astype(F32) + vgsum[1, 0].astype(F32)
    r_g[...] = vgsum[0, 1].astype(F32) + vgsum[1, 1].astype(F32)
    t_ff[0].wait_recv()
    for h in range(2):
        r_fg[:, h * half : (h + 1) * half] = fin_f[h, 0].astype(F32)
    t_oz.collect()
    fin_ow[par] = t_oz.total().astype(BF)
    t_fo = send(fin_ow.at[par], fin_ow.at[par], partner)
    t_ff[1].wait_recv()
    for h in range(2):
        r_fu[:, h * half : (h + 1) * half] = fin_f[h, 1].astype(F32)
    t_s3.wait_recv()
    for h in range(W):
        pick[:, h * T : (h + 1) * T] = sm4[h].astype(F32)
    pair = i * W + j
    r_dd[...] = pick[pl.ds(pair, 1), :]
    wide = pick[16:24, :]
    slab = D // (W * W)
    chosen = jnp.zeros((8, slab), F32)
    for n in range(W * W):
        chosen = jnp.where(pair == n, wide[:, n * slab : (n + 1) * slab], chosen)
    r_ng[...] = chosen[0:1]
    r_fn[...] = chosen[1:2]
    chosen = jnp.zeros((8, 64), F32)
    for n in range(W):
        chosen = jnp.where(j == n, wide[:, n * 64 : (n + 1) * 64], chosen)
    r_gg[...] = chosen[2:3]
    t_ai.wait_recv()
    r_in[...] = lanes(iseg[...])
    t_fo.wait_recv()
    for h in range(2):
        r_o[:, h * half : (h + 1) * half] = fin_ow[h].astype(F32)
    for cp in sent:
        cp.wait_send()

    @pl.when(inner)
    def _():
        for cp in inner_sent:
            cp.wait_send()

    @pl.when(jnp.logical_not(inner))
    def _():
        for cp in outer_sent:
            cp.wait_send()


N_REMOTE = 150
N_LOCAL = 18


def layer(n_seq, args):
    rows, D = args[0].shape
    W = WAYS
    T = rows // W
    FB = args[-1].shape[0]
    VC = W * 64
    half = D // 2

    def sds(shape, dtype=F32):
        return pltpu.VMEM(shape, dtype)

    def vm(shape, dtype=BF):
        return pltpu.VMEM(shape, dtype)

    slab = D // (W * W)
    outs = [
        sds((64, rows), BF),
        sds((64, rows), BF),
        sds((1, slab)),
        sds((32, D)),
        sds((32, D)),
        sds((64, D)),
        sds((64, D)),
        sds((1, D)),
        sds((16, 1, 32)),
        sds((1, 32)),
        sds((1, 64)),
        sds((64, D)),
        sds((1, slab)),
        sds((FB, D)),
        sds((FB, D)),
        sds((FB, D)),
    ]
    scratch = [
        vm((T, D)),
        vm((T, D)),
        vm((rows, D)),
        vm((rows, D)),
        vm((rows, D)),
        vm((T, D)),
        vm((D, T)),
        vm((128, D)),
        vm((8, 128)),
        vm((8, 128)),
        vm((16, W, 32)),
        vm((W, 32)),
        vm((1, 64)),
        vm((128, 128), F32),
        vm((8, D), F32),
        vm((W, 2, 32, D)),
        vm((W, 32, 128)),
        vm((W, 64, D)),
        vm((W, 64, D)),
        vm((W, 16, 128)),
        vm((W, W, 64, D)),
        vm((3, W, FB, D)),
        vm((W, VC + 16, 128)),
        vm((n_seq, VC + 16, 128)),
        vm((W, VC + 16, 128)),
        vm((n_seq, VC + 16, 128)),
        vm((W, T, VC)),
        vm((W, T, VC)),
        vm((W, T, VC)),
        vm((2, T, VC)),
        vm((8, T), F32),
        vm((W, 8, T), F32),
        vm((W, W, 64, T)),
        vm((W, W, 64, T)),
        vm((2, W, 64, T)),
        vm((W, W, 64, T)),
        vm((W, W, 64, T)),
        vm((2, W, 64, T)),
        vm((W, 64, T)),
        vm((W, 64, T)),
        vm((W, 64, T)),
        vm((W, 64, T)),
        vm((W, FB, T)),
        vm((W, FB, T)),
        vm((2, W, FB, D)),
        vm((2, W, FB, half)),
        vm((2, W, FB, half)),
        vm((2, 2, FB, half)),
        vm((2, 2, FB, half // 2)),
        vm((2, 2, FB, half // 2)),
        vm((2, 2, FB, half)),
        vm((2, FB, D)),
        vm((W, VC, D)),
        vm((W, VC, half)),
        vm((W, VC, half)),
        vm((2, VC, half)),
        vm((2, VC, half // 2)),
        vm((2, VC, half // 2)),
        vm((W, 64, half)),
        vm((W, 64, half)),
        vm((2, 64, half)),
        vm((2, 64, half)),
        vm((2, W, 64, T)),
        vm((2, W, 64, T)),
        vm((2, W, 64, T)),
        vm((2, 2, 64, D)),
        vm((W, 3, 32, T)),
        vm((W, 3, 32, T)),
        vm((2, 2, 32, D)),
        vm((2, 32, 128), F32),
        vm((W, 32, T)),
        vm((W, 32, T)),
        vm((W, 32, T)),
        vm((2, 32, T)),
        vm((W, 32, T)),
        vm((32, D), F32),
        vm((rows, 128)),
        vm((T, W * FB), F32),
        vm((3, T, VC), F32),
        vm((T, D), F32),
        pltpu.SemaphoreType.DMA((N_REMOTE + 2 * n_seq,)),
        pltpu.SemaphoreType.DMA((N_REMOTE + 2 * n_seq,)),
        pltpu.SemaphoreType.DMA((N_LOCAL,)),
    ]
    return pl.pallas_call(
        functools.partial(layer_kernel, n_seq),
        out_shape=outs,
        in_specs=[pl.BlockSpec(memory_space=pl.ANY)] * len(args),
        out_specs=[pl.BlockSpec(memory_space=pltpu.VMEM)] * len(outs),
        scratch_shapes=scratch,
        compiler_params=pltpu.CompilerParams(
            collective_id=0, has_side_effects=True, vmem_limit_bytes=60 * 2**20
        ),
        name="layer",
    )(*args)


def finish_kernel(*refs):
    n = len(refs) // 2
    sem = refs[-1]
    copies = [pltpu.make_async_copy(refs[k], refs[n + k], sem.at[k]) for k in range(n)]
    for cp in copies:
        cp.start()
    for cp in copies:
        cp.wait()


def finish(parts):
    return pl.pallas_call(
        finish_kernel,
        out_shape=[jax.ShapeDtypeStruct(p.shape, p.dtype) for p in parts],
        in_specs=[pl.BlockSpec(memory_space=pltpu.VMEM)] * len(parts),
        out_specs=[pl.BlockSpec(memory_space=pl.ANY)] * len(parts),
        scratch_shapes=[pltpu.SemaphoreType.DMA((len(parts),))],
        compiler_params=pltpu.CompilerParams(vmem_limit_bytes=16 * 2**20),
        name="finish",
    )(*parts)


def shards(
    n_seq,
    tokens,
    norm_gain,
    query_weight,
    key_weight,
    value_weight,
    gate_weight,
    decay_down,
    decay_up,
    decay_bias,
    group_gain,
    out_weight,
    ffn_gain,
    ffn_gate,
    ffn_up,
    ffn_down,
    cotangent,
):
    parts = layer(
        n_seq,
        (
            tokens,
            cotangent,
            norm_gain.reshape(8, -1),
            ffn_gain.reshape(8, -1),
            decay_up,
            decay_bias,
            group_gain[None],
            query_weight.transpose(1, 2, 0),
            key_weight.transpose(1, 2, 0),
            value_weight.transpose(1, 2, 0),
            gate_weight.transpose(1, 2, 0),
            decay_down.T,
            out_weight[0],
            ffn_gate.T,
            ffn_up.T,
            ffn_down,
        ),
    )
    if n_seq > 2:

        def over_pairs(a):
            return jnp.sum(lax.all_gather(a, "seq")[::2].astype(F32), axis=0).astype(a.dtype)

        parts = list(parts[:2]) + [over_pairs(a) for a in parts[2:]]
    (r_out, r_in, r_ng, r_q, r_k, r_v, r_g, r_dd, r_du, r_db, r_gg, r_o, r_fn, r_fg, r_fu, r_fd) = finish(parts)
    return (
        r_out.T,
        r_in.T,
        r_ng[0],
        r_q.T[:, None, :],
        r_k.T[:, None, :],
        r_v.T[:, None, :],
        r_g.T[:, None, :],
        r_dd.T,
        r_du,
        r_db,
        r_gg[0],
        r_o[None],
        r_fn[0],
        r_fg.T,
        r_fu.T,
        r_fd,
    )


def solution(mesh):
    in_specs = (
        P("seq", None),
        P(),
        P(None, None, "kax"),
        P(None, None, "kax"),
        P(None, None, "vax"),
        P(None, None, "vax"),
        P(),
        P(None, None, "kax"),
        P(None, "kax"),
        P("vax"),
        P("kax", "vax", None),
        P(),
        P(None, ("kax", "vax")),
        P(None, ("kax", "vax")),
        P(("kax", "vax"), None),
        P("seq", None),
    )
    out_specs = (
        P("seq", ("kax", "vax")),
        P("seq", ("kax", "vax")),
        P(("kax", "vax")),
        P(None, "vax", "kax"),
        P(None, "vax", "kax"),
        P(None, "kax", "vax"),
        P(None, "kax", "vax"),
        P(None, ("kax", "vax")),
        P(None, "vax", "kax"),
        P("vax", "kax"),
        P("vax"),
        P("kax", "vax", None),
        P(("kax", "vax")),
        P(None, ("kax", "vax")),
        P(None, ("kax", "vax")),
        P(("kax", "vax"), None),
    )
    return jax.shard_map(
        functools.partial(shards, mesh.shape["seq"]),
        mesh=mesh,
        in_specs=in_specs,
        out_specs=out_specs,
        check_vma=False,
    )
```

```python
import functools

import jax
import jax.numpy as jnp
from jax import lax
from jax.experimental import pallas as pl
from jax.experimental.pallas import tpu as pltpu
from jax.sharding import PartitionSpec as P

MESH = pl.DeviceIdType.MESH
BF = jnp.bfloat16
F32 = jnp.float32
CB = 128
WAYS = 4
EPS = 1e-06
HIGH = lax.Precision.HIGHEST


def nn(a, b, precision=None):
    return lax.dot_general(
        a, b, (((1,), (0,)), ((), ())), precision=precision, preferred_element_type=F32
    )


def nt(a, b, precision=None):
    return lax.dot_general(
        a, b, (((1,), (1,)), ((), ())), precision=precision, preferred_element_type=F32
    )


def tn(a, b, precision=None):
    return lax.dot_general(
        a, b, (((0,), (0,)), ((), ())), precision=precision, preferred_element_type=F32
    )


def xor(index, d):
    if d == 1:
        return index + 1 - 2 * lax.rem(index, 2)
    if d == 2:
        return lax.rem(index + 2, 4)
    return 3 - index


def as_row(column):
    return jnp.broadcast_to(column, (column.shape[0], 128)).T[:8]


def as_column(row):
    return jnp.broadcast_to(row[:1], (128, row.shape[1])).T[:, :1]


def flat_row(block):
    return jnp.concatenate([block[r : r + 1] for r in range(block.shape[0])], axis=1)


def lanes(block):
    return jnp.concatenate([block[n] for n in range(block.shape[0])], axis=1)


def total(own, got):
    out = own.astype(F32)
    for d in (1, 2, 3):
        out = out + got[d].astype(F32)
    return out


def layer_kernel(
    n_seq,
    tok,
    cot,
    ng,
    ffg,
    dup,
    dbi,
    ggn,
    wq,
    wk,
    wv,
    wg,
    dd,
    wo,
    fg,
    fu,
    fd,
    r_out,
    r_in,
    r_ng,
    r_q,
    r_k,
    r_v,
    r_g,
    r_dd,
    r_du,
    r_db,
    r_gg,
    r_o,
    r_fn,
    r_fg,
    r_fu,
    r_fd,
    x_v,
    c_v,
    x_all,
    c_all,
    n_all,
    n_v,
    xr_v,
    dd_v,
    ng_v,
    ffg_v,
    dup_v,
    dbi_v,
    ggn_v,
    sq_v,
    gain_v,
    qk_v,
    ext_v,
    v_v,
    g_v,
    gge_v,
    o_v,
    f_v,
    st_v,
    tt_v,
    bst_v,
    btt_v,
    ga_v,
    sgg,
    rgg,
    cgg,
    sst,
    rst,
    so,
    ro,
    co,
    sgn,
    rgn,
    cgn,
    ao,
    oseg,
    ai,
    iseg,
    hd,
    hseg,
    gw,
    pre,
    pres,
    rfw,
    qfw,
    cfw,
    fin_f,
    dsum,
    gow,
    preo,
    preso,
    rowk,
    qow,
    cow,
    mid_o,
    rowz,
    coz,
    fin_ow,
    vz,
    zvg,
    kvg,
    vgsum,
    qka,
    kqa,
    qksum,
    esum,
    sm0,
    sm1,
    sm2,
    sm3,
    lall_v,
    gh_v,
    act_v,
    p_v,
    ss,
    rs,
    ls,
):
    s = lax.axis_index("seq")
    i = lax.axis_index("kax")
    j = lax.axis_index("vax")
    par = lax.rem(s, 2)
    oth = 1 - par
    T, D = x_v.shape
    rows = x_all.shape[0]
    FB = f_v.shape[2]
    half = D // 2
    W = WAYS
    DIRS = (1, 2, 3)
    mine = pl.ds(pl.multiple_of(par * half, half), half)
    other = pl.ds(pl.multiple_of(oth * half, half), half)
    partner = {"seq": s + 1 - 2 * par}
    kdev = [None] + [{"kax": xor(i, d)} for d in DIRS]
    vdev = [None] + [{"vax": xor(j, d)} for d in DIRS]
    ki = [None] + [xor(i, d) for d in DIRS]
    vj = [None] + [xor(j, d) for d in DIRS]
    seqdev = [{"seq": lax.rem(s + e, n_seq)} for e in range(1, n_seq)]

    count = [0, 0, 0]
    sent, inner_sent, outer_sent = [], [], []

    def slot(kind):
        count[kind] += 1
        return count[kind] - 1

    def out_slot():
        return slot(0)

    def in_slot():
        return slot(1)

    def copy(src, dst, dev, n, m):
        return pltpu.make_async_remote_copy(
            src_ref=src,
            dst_ref=dst,
            send_sem=ss.at[n],
            recv_sem=rs.at[m],
            device_id=dev,
            device_id_type=MESH,
        )

    def send(src, dst, dev):
        cp = copy(src, dst, dev, out_slot(), in_slot())
        cp.start()
        sent.append(cp)
        return cp

    def load(src, dst):
        cp = pltpu.make_async_copy(src, dst, ls.at[slot(2)])
        cp.start()
        return cp

    class Fan:
        def __init__(self, copies, size):
            n, m = out_slot(), in_slot()
            for src, dst, dev in copies:
                copy(src, dst, dev, n, m).start()
            self.all = copy(size, size, partner, n, m)
            sent.append(self.all)

        def wait_recv(self):
            self.all.wait_recv()

    def arrived(copies):
        for cp in copies:
            cp.wait_recv()

    def here(copies):
        for cp in copies:
            cp.wait()

    inner = lax.rem(j + 1, W) >= 2

    class LineGather:
        def __init__(self, view, four):
            a, b, c = in_slot(), in_slot(), in_slot()
            n, m = out_slot(), out_slot()
            near = copy(view(j), view(j), vdev[1], n, a)
            near.start()
            sent.append(near)
            across = copy(view(j), view(j), vdev[3], m, c)
            self.got = [
                copy(view(vj[d]), view(vj[d]), vdev[1], n, at) for d, at in zip(DIRS, (a, b, c))
            ]
            self.on = [
                copy(view(vj[1]), view(vj[1]), vdev[3], m, b),
                copy(view(vj[3]), view(vj[3]), vdev[1], m, b),
                copy(view(vj[2]), view(vj[2]), vdev[1], m, c),
            ]
            inner_sent.append(copy(four, four, vdev[1], m, a))

            @pl.when(inner)
            def _():
                across.start()

        def step(self, n):
            @pl.when(inner)
            def _():
                self.got[(0, 2, 1)[n]].wait_recv()
                self.on[n].start()

        def collect(self):
            @pl.when(jnp.logical_not(inner))
            def _():
                arrived(self.got)

    class LineSum:
        def __init__(self, part, both, relay, summed):
            self.part, self.both, self.relay, self.summed = part, both, relay, summed
            a, b, c = in_slot(), in_slot(), in_slot()
            n, m, o = out_slot(), out_slot(), out_slot()
            self.first = [
                copy(part(vj[3]), relay.at[0], vdev[1], n, a),
                copy(part(vj[2]), relay.at[1], vdev[1], n, b),
            ]
            self.direct = copy(part(vj[1]), both.at[0], vdev[1], m, c)
            self.second = [copy(summed.at[k], both.at[1], vdev[2 + k], o, c) for k in range(2)]
            self.all = copy(both, both, vdev[1], m, c)
            outer_sent.append(copy(relay, relay, vdev[1], n, a))
            sent.append(self.direct)
            inner_sent.append(copy(summed, summed, vdev[1], o, a))

        def go(self, n):
            if n < 2:

                @pl.when(jnp.logical_not(inner))
                def _():
                    self.first[n].start()

            elif n == 2:
                self.direct.start()

        def rest(self):
            for n in range(3):
                self.go(n)
            return self

        def step(self, n):
            @pl.when(inner)
            def _():
                self.first[n].wait_recv()
                mine_too = self.part(vj[2 + n])[...].astype(F32)
                self.summed[n] = (mine_too + self.relay[n].astype(F32)).astype(BF)
                self.second[n].start()

        def collect(self):
            self.all.wait_recv()

        def total(self):
            out = self.part(j)[...].astype(F32)
            return out + self.both[0].astype(F32) + self.both[1].astype(F32)

    class SquareSum:
        def __init__(self, part, got, relay, summed):
            self.part, self.got, self.relay, self.summed = part, got, relay, summed
            q = got.shape[-1] // 2
            self.at = [pl.ds(0, q), pl.ds(q, q)]
            a, self.into_slot = in_slot(), in_slot()
            n, self.out = out_slot(), out_slot()
            for k in range(2):
                copy(self.half(ki[3], k), relay.at[k], kdev[1 + k], n, a).start()
            for k in range(2):
                copy(self.half(ki[1 + k], k), self.into(k, k), kdev[1 + k], n, self.into_slot).start()
            self.relayed = copy(relay, relay, kdev[1], n, a)
            sent.append(copy(got, got, kdev[1], n, a))

        def half(self, target, n):
            return self.part(target, self.at[n])

        def into(self, n, h):
            return self.got.at[n, :, self.at[h]]

        def step(self):
            self.relayed.wait_recv()
            for k in range(2):
                own = self.half(ki[2 - k], k)[...].astype(F32)
                self.summed[k] = (own + self.relay[k].astype(F32)).astype(BF)
                copy(
                    self.summed.at[k], self.into(1 - k, k), kdev[2 - k], self.out, self.into_slot
                ).start()
            sent.append(copy(self.summed, self.summed, kdev[1], self.out, self.into_slot))

        def collect(self):
            copy(self.got, self.got, kdev[1], self.out, self.into_slot).wait_recv()

        def total(self):
            out = self.part(i, pl.ds(0, self.got.shape[-1]))[...].astype(F32)
            return out + self.got[0].astype(F32) + self.got[1].astype(F32)

    quarter = half // 2
    mine_parts = [
        pl.ds(pl.multiple_of(par * half + n * quarter, quarter), quarter) for n in range(2)
    ]

    class SquareGather:
        def __init__(self, view, many, whole=mine, parts=mine_parts, own=None, pass_on=True):
            self.view, self.many, self.whole, self.parts = view, many, whole, parts
            self.pass_on = pass_on
            own = view(i, whole) if own is None else own
            into = view(i, whole)
            self.near = Fan([(own, into, kdev[d]) for d in (1, 2)], many(2))

        def forward(self, sources):
            if not self.pass_on:
                return []
            views = [self.view(src, self.whole) for src in sources]
            return [Fan([(one, one, partner) for one in views], self.many(len(views)))]

        def step(self):
            self.near.wait_recv()
            views = [self.view(ki[1 + n], self.parts[n]) for n in range(2)]
            self.far = Fan([(views[n], views[n], kdev[2 - n]) for n in range(2)], self.many(1))
            return self.forward((ki[1], ki[2]))

        def collect(self):
            self.far.wait_recv()
            return self.forward((ki[3],))

    barrier = pltpu.get_barrier_semaphore()
    for dev in kdev[1:] + vdev[1:] + seqdev:
        pl.semaphore_signal(barrier, inc=1, device_id=dev, device_id_type=MESH)

    l_small = [load(dup, dup_v), load(dbi, dbi_v), load(ggn, ggn_v)]
    l_qk = [load(wq.at[j], qk_v.at[i, 0]), load(wk.at[j], qk_v.at[i, 1])]
    segment = pl.ds(pl.multiple_of(i * T, T), T)
    l_x = [load(tok.at[segment], x_v), load(ng, ng_v), load(ffg, ffg_v)]
    l_dd = load(dd, dd_v.at[pl.ds(0, 16)])
    l_v = load(wv.at[j], v_v.at[j])
    l_g = load(wg.at[j], g_v.at[j])
    l_c = load(cot.at[segment], c_v)
    l_f = [load(fg, f_v.at[0, i]), load(fu, f_v.at[1, i]), load(fd, f_v.at[2, i])]
    l_o = load(wo, o_v.at[i, j])
    l_xa = load(tok, x_all)
    l_ca = load(cot, c_all)

    dd_v[16:, :] = jnp.zeros((dd_v.shape[0] - 16, D), BF)
    here(l_small)
    head3 = lax.broadcasted_iota(jnp.int32, (16, W, 32), 1)
    head2 = lax.broadcasted_iota(jnp.int32, (W, 32), 0)
    sq_v[...] = jnp.zeros_like(sq_v)
    sq_v[0:16, 0:32] = jnp.sum(jnp.where(head3 == j, dup_v[...].astype(F32), 0.0), axis=1)
    sq_v[16:17, 0:32] = jnp.sum(
        jnp.where(head2 == j, dbi_v[...].astype(F32), 0.0), axis=0, keepdims=True
    )
    ext_v[i] = sq_v[...].T[:32].astype(BF)
    sq_v[...] = jnp.zeros_like(sq_v)
    sq_v[0:16, 0:64] = jnp.broadcast_to(ggn_v[...].astype(F32), (16, 64))
    gge_v[j] = sq_v[0:16].astype(BF)

    pl.semaphore_wait(barrier, 6 + len(seqdev))

    here(l_qk)
    t_qk = Fan(
        [(qk_v.at[i, par], qk_v.at[i, par], kdev[d]) for d in DIRS], qk_v.at[pl.ds(0, 3), 0]
    )
    left = pl.ds(0, half)
    t_v = Fan(
        [(wv.at[vj[d], :, mine], v_v.at[j, :, mine], vdev[d]) for d in DIRS],
        v_v.at[pl.ds(0, 3), :, left],
    )
    t_ext = Fan([(ext_v.at[i], ext_v.at[i], kdev[d]) for d in DIRS], ext_v.at[pl.ds(0, 3)])
    low = pl.ds(0, 32)
    high = pl.ds(32, 32)
    t_ob = Fan(
        [(wo.at[high, mine], o_v.at[i, j, high, mine], kdev[d]) for d in DIRS],
        o_v.at[pl.ds(0, 3), 0, high, mine],
    )
    weights = (fg, fu, fd)

    def gather_weight(n, rows_at):
        return SquareGather(
            lambda src, at: f_v.at[n, src, rows_at, at],
            lambda count: f_v.at[n, pl.ds(0, count), rows_at, mine],
            own=weights[n].at[rows_at, mine],
        )

    cut = FB // 32 * 16
    top = pl.ds(0, cut)
    bottom = pl.ds(cut, FB - cut)
    every = pl.ds(0, FB)
    t_fd = gather_weight(2, every)
    l_o.wait()
    t_oa = LineGather(lambda src: o_v.at[i, src, low, mine], o_v.at[0, :, low, mine])
    t_g = Fan(
        [(wg.at[vj[d], :, mine], g_v.at[j, :, mine], vdev[d]) for d in DIRS],
        g_v.at[pl.ds(0, 3), :, left],
    )
    t_gge = Fan([(gge_v.at[j], gge_v.at[j], vdev[d]) for d in DIRS], gge_v.at[pl.ds(0, 3)])

    here(l_x)
    x = x_v[...].astype(F32)
    g1 = flat_row(ng_v[...].astype(F32))
    g3 = flat_row(ffg_v[...].astype(F32))
    r1 = lax.rsqrt(jnp.sum(x * x, axis=1, keepdims=True) / D + EPS)
    n_v[...] = (x * r1 * g1).astype(BF)
    l_dd.wait()
    lane = lax.broadcasted_iota(jnp.int32, (T, 128), 1)
    lrp = jnp.where(lane == 16, 1.0, nt(n_v[...], dd_v[...]))

    t_qk.wait_recv()
    views = [qk_v.at[ki[d], par] for d in DIRS]
    f_qk = Fan([(one, one, partner) for one in views], qk_v.at[pl.ds(0, 3), 0])
    t_fg = [gather_weight(0, top)]
    f_qk.wait_recv()
    t_ext.wait_recv()
    normed = n_v[...]
    wq_all = qk_v[:, 0].reshape(W * 32, D)
    wk_all = qk_v[:, 1].reshape(W * 32, D)
    ext_all = ext_v[...].reshape(W * 32, 128)
    scale = 128.0 ** (-0.5)
    q = nt(normed, wq_all) * scale
    k = nt(normed, wk_all)
    arg = nt(lrp, ext_all.astype(F32), HIGH)
    rates = (jnp.minimum(arg, 0.0) - jnp.log1p(jnp.exp(-jnp.abs(arg)))) / 16.0
    row_id = lax.broadcasted_iota(jnp.int32, (CB, CB), 0)
    col_id = lax.broadcasted_iota(jnp.int32, (CB, CB), 1)
    causal = row_id >= col_id
    tri = jnp.where(causal, 1.0, 0.0)
    nblk = T // CB
    blk = [slice(c * CB, (c + 1) * CB) for c in range(nblk)]
    e1, e2, em, el, dec, qd, kd, qi, ke, score = [], [], [], [], [], [], [], [], [], []
    for c in range(nblk):
        cum = nn(tri, rates[blk[c]], HIGH)
        mid = cum[CB // 2 - 1 : CB // 2]
        last = cum[CB - 1 : CB]
        e1.append(jnp.exp(cum - mid))
        e2.append(jnp.exp(mid - cum))
        em.append(jnp.exp(mid))
        el.append(jnp.exp(last - mid))
        dec.append(jnp.exp(last))
        a = q[blk[c]] * e1[c]
        b = k[blk[c]] * e2[c]
        qd.append(a.astype(BF))
        kd.append(b.astype(BF))
        qi.append((a * em[c]).astype(BF))
        ke.append((b * el[c]).astype(BF))
        score.append(jnp.where(causal, nt(qd[c], kd[c]), 0.0).astype(BF))

    l_v.wait()
    t_v.wait_recv()
    views = [v_v.at[vj[d], :, mine] for d in DIRS]
    f_vv = Fan([(one, one, partner) for one in views], v_v.at[pl.ds(0, 3), :, left])
    f_vv.wait_recv()
    wv_all = v_v[...].reshape(W * 64, D)
    v = nt(normed, wv_all).astype(BF)
    up = [tn(v[blk[c]], ke[c]) for c in range(nblk)]
    loc = up[0]
    locd = dec[0]
    for c in range(1, nblk):
        loc = loc * dec[c] + up[c]
        locd = locd * dec[c]
    VC = loc.shape[0]
    st_v[i, :VC] = loc.astype(BF)
    st_v[i, VC:] = jnp.broadcast_to(locd, (16, 128)).astype(BF)
    t_st = Fan([(st_v.at[i], st_v.at[i], kdev[d]) for d in DIRS], st_v.at[pl.ds(0, 3)])
    t_fg.append(gather_weight(0, bottom))
    t_fu = gather_weight(1, every)
    t_oa.step(0)
    t_oa.step(1)
    mixed = [nn(score[c], v[blk[c]]) for c in range(nblk)]

    t_ob.wait_recv()
    views = [o_v.at[ki[d], j, high, mine] for d in DIRS]
    f_o = [Fan([(one, one, partner) for one in views], o_v.at[pl.ds(0, 3), 0, high, mine])]
    t_ob2 = LineGather(lambda src: o_v.at[:, src, high, mine], o_v.at[:, :, high, mine])
    here(l_f)
    f_f = t_fd.step()
    t_oa.step(2)

    def gather_states(slots, totals, back):
        order = range(W - 1, -1, -1) if back else range(W)
        pre_s = jnp.zeros((VC, 128), F32)
        pre_d = jnp.ones((1, 128), F32)
        tot_s = jnp.zeros((VC, 128), F32)
        tot_d = jnp.ones((1, 128), F32)
        for other_i in order:
            one_s = slots[other_i, :VC].astype(F32)
            one_d = slots[other_i, VC : VC + 1].astype(F32)
            use = (other_i > i) if back else (other_i < i)
            pre_s = jnp.where(use, pre_s * one_d + one_s, pre_s)
            pre_d = jnp.where(use, pre_d * one_d, pre_d)
            tot_s = tot_s * one_d + one_s
            tot_d = tot_d * one_d
        totals[s, :VC] = tot_s.astype(BF)
        totals[s, VC:] = jnp.broadcast_to(tot_d, (16, 128)).astype(BF)
        return pre_s, pre_d, [send(totals.at[s], totals.at[s], dev) for dev in seqdev]

    def entering(totals, back, pre_s, pre_d, moves):
        arrived(moves)
        order = range(n_seq - 1, -1, -1) if back else range(n_seq)
        far = jnp.zeros((VC, 128), F32)
        for other_s in order:
            one_s = totals[other_s, :VC].astype(F32)
            one_d = totals[other_s, VC : VC + 1].astype(F32)
            use = (other_s > s) if back else (other_s < s)
            far = jnp.where(use, far * one_d + one_s, far)
        return pre_s + pre_d * far

    t_st.wait_recv()
    states = gather_states(st_v, tt_v, False)

    l_g.wait()
    t_g.wait_recv()
    views = [g_v.at[vj[d], :, mine] for d in DIRS]
    f_g = Fan([(one, one, partner) for one in views], g_v.at[pl.ds(0, 3), :, left])
    t_ob2.step(0)
    t_ob2.step(1)
    start = [entering(tt_v, False, *states)]
    for c in range(nblk):
        start.append(start[c] * dec[c] + up[c])
    start_low = [a.astype(BF) for a in start]
    for c in range(nblk):
        mixed[c] = mixed[c] + nt(qi[c], start_low[c])
    mix = jnp.concatenate(mixed, axis=0)
    r2 = lax.rsqrt(jnp.sum(mix * mix, axis=1, keepdims=True) / VC + EPS)
    normal = mix * r2
    f_g.wait_recv()
    t_gge.wait_recv()
    wg_all = g_v[...].reshape(W * 64, D)
    gate = nt(normed, wg_all)
    gg = jnp.concatenate([gge_v[h].astype(F32)[0:1, 0:64] for h in range(W)], axis=1)
    sig = 1.0 / (1.0 + jnp.exp(-gate))
    act = gate * sig
    act_v[0] = act
    act_v[1] = sig + act * (1.0 - sig)
    ga_v[j] = (normal * gg * act).astype(BF)
    act_v[2] = normal
    halves = [pl.ds(n * T // 2, T // 2) for n in range(2)]
    t_ga = [LineGather(lambda src, at=at: ga_v.at[src, at], ga_v.at[:, at]) for at in halves]

    t_oa.collect()
    views = [o_v.at[i, vj[d], low, mine] for d in DIRS]
    f_o.append(Fan([(one, one, partner) for one in views], o_v.at[0, pl.ds(0, 3), low, mine]))
    t_oa2 = SquareGather(
        lambda src, at: o_v.at[src, :, low, at], lambda count: o_v.at[pl.ds(0, count), :, low, mine]
    )

    here([l_xa, l_ca])
    for part in range(rows // T):
        at = pl.ds(part * T, T)
        xa = x_all[at, :].astype(F32)
        ra = lax.rsqrt(jnp.sum(xa * xa, axis=1, keepdims=True) / D + EPS)
        n_all[at, :] = (xa * ra * g1).astype(BF)
    xr_v[...] = (x * (r1 * r1 * r1)).astype(BF).T
    low_all = jnp.where(
        lax.broadcasted_iota(jnp.int32, (rows, 128), 1) == 16, 1.0, nt(n_all[...], dd_v[...])
    )
    lall_v[...] = low_all.astype(BF)
    for line in t_fg:
        f_f += line.step()
    t_ob2.step(2)
    t_ga[0].step(0)
    t_ga[0].step(1)
    t_ga[1].step(0)
    t_ga[1].step(1)
    f_f += t_fu.step()
    t_ga[0].step(2)
    t_ga[1].step(2)
    f_o += t_oa2.step()
    f_f += t_fd.collect()
    l_c.wait()
    arrived(f_f)
    dn = f_v[2].reshape(W * FB, D)
    gh_v[...] = nt(c_v[...], dn)
    f_f = t_fg[0].collect() + t_fg[1].collect()
    f_f += t_fu.collect()
    f_o += t_oa2.collect()
    t_ob2.collect()
    views = [o_v.at[:, vj[d], high, mine] for d in DIRS]
    f_o.append(Fan([(one, one, partner) for one in views], o_v.at[:, pl.ds(0, 3), high, mine]))
    for line in t_ga:
        line.collect()
    arrived(f_o)
    arrived(f_f)

    gT = f_v[0].reshape(W * FB, D)
    uT = f_v[1].reshape(W * FB, D)
    att = nn(ga_v[0], o_v[0].reshape(W * 64, D))
    for h in range(1, W):
        att = att + nn(ga_v[h], o_v[h].reshape(W * 64, D))
    resid = x_v[...].astype(F32) + att
    r3 = lax.rsqrt(jnp.sum(resid * resid, axis=1, keepdims=True) / D + EPS)
    fin = (resid * r3 * g3).astype(BF)
    gval = nt(fin, gT)
    uval = nt(fin, uT)
    fsig = 1.0 / (1.0 + jnp.exp(-gval))
    fact = gval * fsig
    hid = (fact * uval).astype(BF)
    gh = gh_v[...]
    gup = (gh * fact).astype(BF)
    ggate = (gh * uval * (fsig + fact * (1.0 - fsig))).astype(BF)
    hd[...] = hid.T.reshape(W, FB, T)
    t_hd = Fan([(hd.at[ki[d]], hseg.at[i], kdev[d]) for d in DIRS], hseg.at[pl.ds(0, 3)])
    hseg[i] = hd[i]
    part = nn(ggate, gT) + nn(gup, uT)
    p_v[...] = part
    sst[...] = as_row(jnp.sum(resid * g3 * part, axis=1, keepdims=True))
    t_m3 = Fan([(sst, rst.at[d], vdev[d]) for d in DIRS], rst.at[pl.ds(1, 3)])
    part_low = (part * g3).astype(BF)
    t_gg = [
        LineSum(
            lambda to, at=at: sgg.at[to, at],
            rgg.at[pl.ds(0, 2), at],
            rgg.at[pl.ds(2, 2), at],
            cgg.at[:, at],
        )
        for at in halves
    ]
    ggp = nt(part_low, o_v[...].reshape(W * W * 64, D))
    for h in range(W):
        sgg[h] = ggp[:, h * VC : (h + 1) * VC].astype(BF)
    for n in range(3):
        for line in t_gg:
            line.go(n)

    def weight_part(n, grad):
        gw[n] = tn(grad, fin).astype(BF).reshape(W, FB, D)
        return send(gw.at[n, :, :, other], pre.at[n], partner)

    def settle(n, move):
        move.wait_recv()
        pres[n] = (gw[n, :, :, mine].astype(F32) + pre[n].astype(F32)).astype(BF)

    def square(n):
        return SquareSum(
            lambda to, at: pres.at[n, to, :, at], rfw.at[n], qfw.at[n], cfw.at[n]
        )

    t_pre0 = weight_part(0, ggate)

    feature = lax.broadcasted_iota(jnp.int32, (1, D), 1)
    own_slab = jnp.where(lax.rem(feature // 64, W) == j, 1.0, 0.0)
    own_run = jnp.where(feature // (D // W) == j, 1.0, 0.0)
    t_m3.wait_recv()
    m3 = as_column(sst[...] + rst[1] + rst[2] + rst[3]) / D
    base = c_v[...].astype(F32) - resid * (r3 * r3 * r3 * m3)
    t_gg[0].step(0)
    settle(0, t_pre0)
    t_fw0 = square(0)
    direct = nt(base.astype(BF), o_v[j].reshape(W * 64, D))
    full = p_v[...] * (g3 * r3)
    mixed_in = (full + own_run * base).astype(BF)
    for h in range(W):
        gow[h] = tn(ga_v[h], mixed_in).astype(BF)
    t_po = send(gow.at[:, :, other], preo, partner)
    t_gg[0].step(1)
    so[...] = (nn(hid, dn) + own_slab * resid).astype(BF).T.reshape(W, W, 64, T)
    t_gg[1].step(0)
    t_out = LineSum(lambda to: so.at[:, to], ro.at[pl.ds(0, 2)], ro.at[pl.ds(2, 2)], co).rest()
    ffn_gain = jnp.sum(part * resid * r3, axis=0, keepdims=True)
    t_gg[1].step(1)
    t_pre1 = weight_part(1, gup)
    t_po.wait_recv()
    preso[...] = (gow[:, :, mine].astype(F32) + preo[...].astype(F32)).astype(BF)
    t_fw0.step()
    settle(1, t_pre1)
    t_fw1 = square(1)
    for line in t_gg:
        line.collect()

    ggs = jnp.concatenate([line.total() for line in t_gg], axis=0)
    ggrad = direct + r3 * ggs
    act = act_v[0]
    normal = act_v[2]
    dgate = (ggrad * normal * gg * act_v[1]).astype(BF)
    gs = ggrad * act
    group = jnp.sum(gs * normal, axis=0, keepdims=True)
    group_rows = [
        jnp.concatenate(
            [group[:, h * 64 : (h + 1) * 64], jnp.zeros((1, T - 64), F32)], axis=1
        )
        for h in range(W)
    ]
    gnm = gs * gg
    gmix = (r2 * (gnm - normal * (jnp.sum(normal * gnm, axis=1, keepdims=True) / VC))).astype(BF)

    qst = [tn(gmix[blk[c]], qi[c]) for c in range(nblk)]
    bloc = qst[nblk - 1]
    for c in range(nblk - 2, -1, -1):
        bloc = bloc * dec[c] + qst[c]
    bst_v[i, :VC] = bloc.astype(BF)
    bst_v[i, VC:] = jnp.broadcast_to(locd, (16, 128)).astype(BF)
    t_bst = Fan([(bst_v.at[i], bst_v.at[i], kdev[d]) for d in DIRS], bst_v.at[pl.ds(0, 3)])
    t_ow = SquareSum(lambda to, at: preso.at[to, :, at], rowk, qow, cow)
    vz[1] = dgate.T.reshape(W, 64, T)
    t_gz = Fan([(vz.at[1, vj[d]], zvg.at[1, j], vdev[d]) for d in DIRS], zvg.at[1, pl.ds(0, 3)])
    dq_in, dk_in, dv_in = [], [], []
    for c in range(nblk):
        ds = jnp.where(causal, nt(gmix[blk[c]], v[blk[c]]), 0.0).astype(BF)
        dq_in.append(nn(ds, kd[c]) + em[c] * nn(gmix[blk[c]], start_low[c]))
        dk_in.append(tn(ds, qd[c]))
        dv_in.append(tn(score[c], gmix[blk[c]]))
    t_out.step(0)
    t_hd.wait_recv()
    dsum[0] = nn(lanes(hseg[...]), c_all[...]).astype(BF)
    t_ds = send(dsum.at[0], dsum.at[1], partner)
    t_bst.wait_recv()
    after = [None] * nblk
    states = gather_states(bst_v, btt_v, True)
    after[nblk - 1] = entering(btt_v, True, *states)
    for c in range(nblk - 2, -1, -1):
        after[c] = after[c + 1] * dec[c + 1] + qst[c + 1]
    t_out.step(1)
    t_fw1.step()

    ql, kl, vl, ga = [], [], [], []
    for c in range(nblk):
        low_after = after[c].astype(BF)
        dq = e1[c] * dq_in[c]
        dk = e2[c] * (dk_in[c] + el[c] * nn(v[blk[c]], low_after))
        dv = dv_in[c] + nt(ke[c], low_after)
        gc = q[blk[c]] * dq - k[blk[c]] * dk
        extra = jnp.sum(after[c] * start[c + 1], axis=0, keepdims=True)
        gc = jnp.where(row_id == CB - 1, gc + extra, gc)
        gr = tn(tri, gc, HIGH)
        ga.append(gr / (1.0 + jnp.exp(arg[blk[c]])) / 16.0)
        ql.append((dq * scale).astype(BF))
        kl.append(dk.astype(BF))
        vl.append(dv.astype(BF))
    ql = jnp.concatenate(ql, axis=0)
    kl = jnp.concatenate(kl, axis=0)
    vl = jnp.concatenate(vl, axis=0)
    ga = jnp.concatenate(ga, axis=0).astype(BF)
    vz[0] = vl.T.reshape(W, 64, T)
    qka[:, 0] = ql.T.reshape(W, 32, T)
    qka[:, 1] = kl.T.reshape(W, 32, T)
    qka[:, 2] = ga.T.reshape(W, 32, T)
    t_qa = Fan([(qka.at[ki[d]], kqa.at[i], kdev[d]) for d in DIRS], kqa.at[pl.ds(0, 3)])
    glr = nn(ga, ext_all).astype(BF)
    gn = nn(ql, wq_all) + nn(kl, wk_all) + nn(vl, wv_all) + nn(dgate, wg_all) + nn(glr, dd_v[...])
    x = x_v[...].astype(F32)
    gnx = gn * x
    norm_gain = jnp.sum(gnx * r1, axis=0, keepdims=True)
    m1p = as_row(jnp.sum(gnx * g1, axis=1, keepdims=True))[:1]
    rank_row = lax.broadcasted_iota(jnp.int32, (16, 128), 0)
    rank_col = lax.broadcasted_iota(jnp.int32, (16, 128), 1)
    by_owner = jnp.where(rank_col == lax.rem(rank_row, W) * W + rank_row // W, 1.0, 0.0)
    small = nn(by_owner.astype(BF), tn(glr, normed).astype(BF))
    slab = D // (W * W)
    rid = lax.broadcasted_iota(jnp.int32, (16, T), 0)
    for h in range(W):
        ranks = small[h * W : (h + 1) * W]
        sm0[h, 0:16] = jnp.concatenate(
            [ranks[:, n * T : (n + 1) * T] for n in range(W)], axis=0
        ).astype(BF)

        def slabs(row):
            return jnp.concatenate(
                [row[:, (W * n + h) * slab : (W * n + h + 1) * slab] for n in range(W)], axis=1
            )

        rest = jnp.where(rid == 0, slabs(norm_gain), 0.0)
        rest = jnp.where(rid == 1, slabs(ffn_gain), rest)
        rest = jnp.where(rid == 2, group_rows[h], rest)
        rest = jnp.where(rid == 3, m1p, rest)
        sm0[h, 16:32] = rest.astype(BF)
    t_s0 = Fan([(sm0.at[vj[d]], sm1.at[d], vdev[d]) for d in DIRS], sm1.at[pl.ds(1, 3)])
    whole = gn * (r1 * g1) + full + own_slab * base
    sgn[...] = whole.astype(BF).T.reshape(W, W, 64, T)
    pairs = [pl.ds(n * W // 2, W // 2) for n in range(2)]
    t_gn = [
        LineSum(
            lambda to, at=at: sgn.at[at, to],
            rgn.at[pl.ds(0, 2), at],
            rgn.at[pl.ds(2, 2), at],
            cgn.at[:, at],
        )
        for at in pairs
    ]
    for n in range(3):
        for line in t_gn:
            line.go(n)
    t_vz = Fan([(vz.at[0, vj[d]], zvg.at[0, j], vdev[d]) for d in DIRS], zvg.at[0, pl.ds(0, 3)])

    t_ow.step()

    t_gz.wait_recv()
    zvg[1, j] = vz[1, j]
    t_gk = Fan([(zvg.at[1, ki[d]], kvg.at[1, i], kdev[d]) for d in DIRS], kvg.at[1, pl.ds(0, 3)])
    kvg[1, i] = zvg[1, i]

    def finish_square(n, line):
        line.collect()
        fin_f[par, n] = line.total().astype(BF)
        return send(fin_f.at[par, n], fin_f.at[par, n], partner)

    t_ff = [finish_square(0, t_fw0)]

    t_s0.wait_recv()
    sm2[0] = total(sm0[j], sm1).astype(BF)
    m1 = (
        sm0[0, 19:20].astype(F32)
        + sm1[1, 19:20].astype(F32)
        + sm1[2, 19:20].astype(F32)
        + sm1[3, 19:20].astype(F32)
    ) / D
    t_s1 = Fan([(sm2.at[0], sm2.at[d], kdev[d]) for d in DIRS], sm2.at[pl.ds(1, 3)])

    t_out.collect()
    ao[...] = t_out.total().astype(BF)
    t_ao = Fan([(ao.at[ki[d]], oseg.at[i], kdev[d]) for d in DIRS], oseg.at[pl.ds(0, 3)])
    oseg[i] = ao[i]

    t_gn[0].step(0)
    t_gn[1].step(0)
    t_gn[0].step(1)
    t_gn[1].step(1)
    t_ff.append(finish_square(1, t_fw1))

    t_ow.collect()
    mid_o[...] = t_ow.total().astype(BF).reshape(W, 64, half)
    t_oz = LineSum(
        lambda to: mid_o.at[to], rowz.at[pl.ds(0, 2)], rowz.at[pl.ds(2, 2)], coz
    ).rest()

    t_qa.wait_recv()
    kqa[i] = qka[i]
    nall = n_all[...]
    for n in range(2):
        qksum[0, n] = nn(lanes(kqa[:, n]), nall).astype(BF)
    esum[0] = nn(lanes(kqa[:, 2]), lall_v[...])
    t_qs = send(qksum.at[0], qksum.at[1], partner)
    t_es = send(esum.at[0], esum.at[1], partner)

    t_gk.wait_recv()
    vgsum[0, 1] = nn(lanes(kvg[1]), nall).astype(BF)
    t_vs = [send(vgsum.at[0, 1], vgsum.at[1, 1], partner)]

    for line in t_gn:
        line.collect()
    summed = jnp.concatenate([line.total() for line in t_gn], axis=0)
    for h in range(W):
        at = pl.ds(pl.multiple_of((h * W + j) * 64, 64), 64)
        ai[h] = (summed[h] - xr_v[at, :].astype(F32) * m1).astype(BF)
    t_ai = Fan([(ai.at[ki[d]], iseg.at[i], kdev[d]) for d in DIRS], iseg.at[pl.ds(0, 3)])
    iseg[i] = ai[i]

    t_vz.wait_recv()
    zvg[0, j] = vz[0, j]
    t_vk = Fan([(zvg.at[0, ki[d]], kvg.at[0, i], kdev[d]) for d in DIRS], kvg.at[0, pl.ds(0, 3)])
    kvg[0, i] = zvg[0, i]

    t_s1.wait_recv()
    sm3[0] = total(sm2[0], sm2).astype(BF)
    t_s2 = send(sm3.at[0], sm3.at[1], partner)
    t_oz.step(0)
    t_oz.step(1)
    t_vk.wait_recv()
    vgsum[0, 0] = nn(lanes(kvg[0]), nall).astype(BF)
    t_vs.append(send(vgsum.at[0, 0], vgsum.at[1, 0], partner))

    t_ds.wait_recv()
    r_fd[...] = dsum[0].astype(F32) + dsum[1].astype(F32)
    t_ao.wait_recv()
    r_out[...] = lanes(oseg[...])
    t_qs.wait_recv()
    r_q[...] = qksum[0, 0].astype(F32) + qksum[1, 0].astype(F32)
    r_k[...] = qksum[0, 1].astype(F32) + qksum[1, 1].astype(F32)
    t_es.wait_recv()
    decay = (esum[0] + esum[1]).T
    r_du[...] = decay[0:16, :].reshape(16, 1, 32)
    r_db[...] = decay[16:17, :]
    t_ff[0].wait_recv()
    for h in range(2):
        r_fg[:, h * half : (h + 1) * half] = fin_f[h, 0].astype(F32)
    t_oz.collect()
    fin_ow[par] = t_oz.total().astype(BF)
    t_fo = send(fin_ow.at[par], fin_ow.at[par], partner)
    t_ff[1].wait_recv()
    for h in range(2):
        r_fu[:, h * half : (h + 1) * half] = fin_f[h, 1].astype(F32)
    arrived(t_vs)
    r_v[...] = vgsum[0, 0].astype(F32) + vgsum[1, 0].astype(F32)
    r_g[...] = vgsum[0, 1].astype(F32) + vgsum[1, 1].astype(F32)
    t_s2.wait_recv()
    tot = sm3[0].astype(F32) + sm3[1].astype(F32)
    own_ranks, own_slabs = [], jnp.zeros((2, slab), F32)
    for n in range(W):
        own_ranks.append(jnp.zeros((1, T), F32))
        for h in range(W):
            row = tot[n * W + h : n * W + h + 1]
            own_ranks[n] = jnp.where(i == h, row, own_ranks[n])
        own_slabs = jnp.where(i == n, tot[16:18, n * slab : (n + 1) * slab], own_slabs)
    r_dd[...] = jnp.concatenate(own_ranks, axis=1)
    r_ng[...] = own_slabs[0:1]
    r_fn[...] = own_slabs[1:2]
    r_gg[...] = tot[18:19, 0:64]
    t_ai.wait_recv()
    r_in[...] = lanes(iseg[...])
    t_fo.wait_recv()
    for h in range(2):
        r_o[:, h * half : (h + 1) * half] = fin_ow[h].astype(F32)
    for cp in sent:
        cp.wait_send()

    @pl.when(inner)
    def _():
        for cp in inner_sent:
            cp.wait_send()

    @pl.when(jnp.logical_not(inner))
    def _():
        for cp in outer_sent:
            cp.wait_send()


N_OUT = 88
N_IN = 92
N_LOCAL = 18


def layer(n_seq, args):
    rows, D = args[0].shape
    W = WAYS
    T = rows // W
    FB = args[-1].shape[0]
    VC = W * 64
    half = D // 2

    def sds(shape, dtype=F32):
        return pltpu.VMEM(shape, dtype)

    def vm(shape, dtype=BF):
        return pltpu.VMEM(shape, dtype)

    slab = D // (W * W)
    outs = [
        sds((64, rows), BF),
        sds((64, rows), BF),
        sds((1, slab)),
        sds((32, D)),
        sds((32, D)),
        sds((64, D)),
        sds((64, D)),
        sds((1, D)),
        sds((16, 1, 32)),
        sds((1, 32)),
        sds((1, 64)),
        sds((64, D)),
        sds((1, slab)),
        sds((FB, D)),
        sds((FB, D)),
        sds((FB, D)),
    ]
    scratch = [
        vm((T, D)),
        vm((T, D)),
        vm((rows, D)),
        vm((rows, D)),
        vm((rows, D)),
        vm((T, D)),
        vm((D, T)),
        vm((128, D)),
        vm((8, 128)),
        vm((8, 128)),
        vm((16, W, 32)),
        vm((W, 32)),
        vm((1, 64)),
        vm((128, 128), F32),
        vm((8, D), F32),
        vm((W, 2, 32, D)),
        vm((W, 32, 128)),
        vm((W, 64, D)),
        vm((W, 64, D)),
        vm((W, 16, 128)),
        vm((W, W, 64, D)),
        vm((3, W, FB, D)),
        vm((W, VC + 16, 128)),
        vm((n_seq, VC + 16, 128)),
        vm((W, VC + 16, 128)),
        vm((n_seq, VC + 16, 128)),
        vm((W, T, VC)),
        vm((W, T, VC)),
        vm((W, T, VC)),
        vm((2, T, VC)),
        vm((8, T), F32),
        vm((W, 8, T), F32),
        vm((W, W, 64, T)),
        vm((W, W, 64, T)),
        vm((2, W, 64, T)),
        vm((W, W, 64, T)),
        vm((W, W, 64, T)),
        vm((2, W, 64, T)),
        vm((W, 64, T)),
        vm((W, 64, T)),
        vm((W, 64, T)),
        vm((W, 64, T)),
        vm((W, FB, T)),
        vm((W, FB, T)),
        vm((2, W, FB, D)),
        vm((2, W, FB, half)),
        vm((2, W, FB, half)),
        vm((2, 2, FB, half)),
        vm((2, 2, FB, half // 2)),
        vm((2, 2, FB, half // 2)),
        vm((2, 2, FB, half)),
        vm((2, FB, D)),
        vm((W, VC, D)),
        vm((W, VC, half)),
        vm((W, VC, half)),
        vm((2, VC, half)),
        vm((2, VC, half // 2)),
        vm((2, VC, half // 2)),
        vm((W, 64, half)),
        vm((W, 64, half)),
        vm((2, 64, half)),
        vm((2, 64, half)),
        vm((2, W, 64, T)),
        vm((2, W, 64, T)),
        vm((2, W, 64, T)),
        vm((2, 2, 64, D)),
        vm((W, 3, 32, T)),
        vm((W, 3, 32, T)),
        vm((2, 2, 32, D)),
        vm((2, 32, 128), F32),
        vm((W, 32, T)),
        vm((W, 32, T)),
        vm((W, 32, T)),
        vm((2, 32, T)),
        vm((rows, 128)),
        vm((T, W * FB), F32),
        vm((3, T, VC), F32),
        vm((T, D), F32),
        pltpu.SemaphoreType.DMA((N_OUT + 2 * n_seq,)),
        pltpu.SemaphoreType.DMA((N_IN + 2 * n_seq,)),
        pltpu.SemaphoreType.DMA((N_LOCAL,)),
    ]
    return pl.pallas_call(
        functools.partial(layer_kernel, n_seq),
        out_shape=outs,
        in_specs=[pl.BlockSpec(memory_space=pl.ANY)] * len(args),
        out_specs=[pl.BlockSpec(memory_space=pltpu.VMEM)] * len(outs),
        scratch_shapes=scratch,
        compiler_params=pltpu.CompilerParams(
            collective_id=0, has_side_effects=True, vmem_limit_bytes=60 * 2**20
        ),
        name="layer",
    )(*args)


def finish_kernel(*refs):
    n = len(refs) // 2
    sem = refs[-1]
    copies = [pltpu.make_async_copy(refs[k], refs[n + k], sem.at[k]) for k in range(n)]
    for cp in copies:
        cp.start()
    for cp in copies:
        cp.wait()


def finish(parts):
    return pl.pallas_call(
        finish_kernel,
        out_shape=[jax.ShapeDtypeStruct(p.shape, p.dtype) for p in parts],
        in_specs=[pl.BlockSpec(memory_space=pltpu.VMEM)] * len(parts),
        out_specs=[pl.BlockSpec(memory_space=pl.ANY)] * len(parts),
        scratch_shapes=[pltpu.SemaphoreType.DMA((len(parts),))],
        compiler_params=pltpu.CompilerParams(vmem_limit_bytes=16 * 2**20),
        name="finish",
    )(*parts)


def shards(
    n_seq,
    tokens,
    norm_gain,
    query_weight,
    key_weight,
    value_weight,
    gate_weight,
    decay_down,
    decay_up,
    decay_bias,
    group_gain,
    out_weight,
    ffn_gain,
    ffn_gate,
    ffn_up,
    ffn_down,
    cotangent,
):
    parts = layer(
        n_seq,
        (
            tokens,
            cotangent,
            norm_gain.reshape(8, -1),
            ffn_gain.reshape(8, -1),
            decay_up,
            decay_bias,
            group_gain[None],
            query_weight.transpose(1, 2, 0),
            key_weight.transpose(1, 2, 0),
            value_weight.transpose(1, 2, 0),
            gate_weight.transpose(1, 2, 0),
            decay_down.T,
            out_weight[0],
            ffn_gate.T,
            ffn_up.T,
            ffn_down,
        ),
    )
    if n_seq > 2:

        def over_pairs(a):
            return jnp.sum(lax.all_gather(a, "seq")[::2].astype(F32), axis=0).astype(a.dtype)

        parts = list(parts[:2]) + [over_pairs(a) for a in parts[2:]]
    (r_out, r_in, r_ng, r_q, r_k, r_v, r_g, r_dd, r_du, r_db, r_gg, r_o, r_fn, r_fg, r_fu, r_fd) = finish(parts)
    return (
        r_out.T,
        r_in.T,
        r_ng[0],
        r_q.T[:, None, :],
        r_k.T[:, None, :],
        r_v.T[:, None, :],
        r_g.T[:, None, :],
        r_dd.T,
        r_du,
        r_db,
        r_gg[0],
        r_o[None],
        r_fn[0],
        r_fg.T,
        r_fu.T,
        r_fd,
    )


def solution(mesh):
    in_specs = (
        P("seq", None),
        P(),
        P(None, None, "kax"),
        P(None, None, "kax"),
        P(None, None, "vax"),
        P(None, None, "vax"),
        P(),
        P(None, None, "kax"),
        P(None, "kax"),
        P("vax"),
        P("kax", "vax", None),
        P(),
        P(None, ("kax", "vax")),
        P(None, ("kax", "vax")),
        P(("kax", "vax"), None),
        P("seq", None),
    )
    out_specs = (
        P("seq", ("kax", "vax")),
        P("seq", ("kax", "vax")),
        P(("kax", "vax")),
        P(None, "vax", "kax"),
        P(None, "vax", "kax"),
        P(None, "kax", "vax"),
        P(None, "kax", "vax"),
        P(None, ("kax", "vax")),
        P(None, "vax", "kax"),
        P("vax", "kax"),
        P("vax"),
        P("kax", "vax", None),
        P(("kax", "vax")),
        P(None, ("kax", "vax")),
        P(None, ("kax", "vax")),
        P(("kax", "vax"), None),
    )
    return jax.shard_map(
        functools.partial(shards, mesh.shape["seq"]),
        mesh=mesh,
        in_specs=in_specs,
        out_specs=out_specs,
        check_vma=False,
    )
```

```python
import functools

import jax
import jax.numpy as jnp
from jax import lax
from jax.experimental import pallas as pl
from jax.experimental.pallas import tpu as pltpu
from jax.sharding import PartitionSpec as P

MESH = pl.DeviceIdType.MESH
BF = jnp.bfloat16
F32 = jnp.float32
CB = 128
WAYS = 4
EPS = 1e-06
HIGH = lax.Precision.HIGHEST


def nn(a, b, precision=None):
    return lax.dot_general(
        a, b, (((1,), (0,)), ((), ())), precision=precision, preferred_element_type=F32
    )


def nt(a, b, precision=None):
    return lax.dot_general(
        a, b, (((1,), (1,)), ((), ())), precision=precision, preferred_element_type=F32
    )


def tn(a, b, precision=None):
    return lax.dot_general(
        a, b, (((0,), (0,)), ((), ())), precision=precision, preferred_element_type=F32
    )


def xor(index, d):
    if d == 1:
        return index + 1 - 2 * lax.rem(index, 2)
    if d == 2:
        return lax.rem(index + 2, 4)
    return 3 - index


def as_row(column):
    return jnp.broadcast_to(column, (column.shape[0], 128)).T[:8]


def as_column(row):
    return jnp.broadcast_to(row[:1], (128, row.shape[1])).T[:, :1]


def flat_row(block):
    return jnp.concatenate([block[r : r + 1] for r in range(block.shape[0])], axis=1)


def lanes(block):
    return jnp.concatenate([block[n] for n in range(block.shape[0])], axis=1)


def total(own, got):
    out = own.astype(F32)
    for d in (1, 2, 3):
        out = out + got[d].astype(F32)
    return out


def layer_kernel(
    n_seq,
    tok,
    cot,
    ng,
    ffg,
    dup,
    dbi,
    ggn,
    wq,
    wk,
    wv,
    wg,
    dd,
    wo,
    fg,
    fu,
    fd,
    r_out,
    r_in,
    r_ng,
    r_q,
    r_k,
    r_v,
    r_g,
    r_dd,
    r_du,
    r_db,
    r_gg,
    r_o,
    r_fn,
    r_fg,
    r_fu,
    r_fd,
    x_v,
    c_v,
    x_all,
    c_all,
    n_all,
    n_v,
    xr_v,
    dd_v,
    ng_v,
    ffg_v,
    dup_v,
    dbi_v,
    ggn_v,
    sq_v,
    gain_v,
    qk_v,
    ext_v,
    v_v,
    g_v,
    gge_v,
    o_v,
    f_v,
    st_v,
    tt_v,
    bst_v,
    btt_v,
    ga_v,
    sgg,
    rgg,
    cgg,
    sst,
    rst,
    so,
    ro,
    co,
    sgn,
    rgn,
    cgn,
    ao,
    oseg,
    ai,
    iseg,
    hd,
    hseg,
    gw,
    pre,
    pres,
    rfw,
    qfw,
    cfw,
    fin_f,
    dsum,
    gow,
    preo,
    preso,
    rowk,
    qow,
    cow,
    mid_o,
    rowz,
    coz,
    fin_ow,
    vz,
    zvg,
    kvg,
    vgsum,
    qka,
    kqa,
    qksum,
    esum,
    sm0,
    sm1,
    sm2,
    sm3,
    lall_v,
    gh_v,
    act_v,
    p_v,
    ss,
    rs,
    ls,
):
    s = lax.axis_index("seq")
    i = lax.axis_index("kax")
    j = lax.axis_index("vax")
    par = lax.rem(s, 2)
    oth = 1 - par
    T, D = x_v.shape
    rows = x_all.shape[0]
    FB = f_v.shape[2]
    half = D // 2
    W = WAYS
    DIRS = (1, 2, 3)
    mine = pl.ds(pl.multiple_of(par * half, half), half)
    other = pl.ds(pl.multiple_of(oth * half, half), half)
    partner = {"seq": s + 1 - 2 * par}
    kdev = [None] + [{"kax": xor(i, d)} for d in DIRS]
    vdev = [None] + [{"vax": xor(j, d)} for d in DIRS]
    ki = [None] + [xor(i, d) for d in DIRS]
    vj = [None] + [xor(j, d) for d in DIRS]
    seqdev = [{"seq": lax.rem(s + e, n_seq)} for e in range(1, n_seq)]

    count = [0, 0, 0]
    sent, inner_sent, outer_sent = [], [], []

    def slot(kind):
        count[kind] += 1
        return count[kind] - 1

    def out_slot():
        return slot(0)

    def in_slot():
        return slot(1)

    def copy(src, dst, dev, n, m):
        return pltpu.make_async_remote_copy(
            src_ref=src,
            dst_ref=dst,
            send_sem=ss.at[n],
            recv_sem=rs.at[m],
            device_id=dev,
            device_id_type=MESH,
        )

    ring = []

    def ring_slot():
        if len(ring) < 28:
            return out_slot()
        n, cp = ring.pop(0)
        cp.wait_send()
        return n

    def send(src, dst, dev):
        n = ring_slot()
        cp = copy(src, dst, dev, n, in_slot())
        cp.start()
        ring.append((n, cp))
        return cp

    def load(src, dst):
        cp = pltpu.make_async_copy(src, dst, ls.at[slot(2)])
        cp.start()
        return cp

    class Fan:
        def __init__(self, copies, size):
            n, m = ring_slot(), in_slot()
            for src, dst, dev in copies:
                copy(src, dst, dev, n, m).start()
            self.all = copy(size, size, partner, n, m)
            ring.append((n, self.all))

        def wait_recv(self):
            self.all.wait_recv()

    def arrived(copies):
        for cp in copies:
            cp.wait_recv()

    def here(copies):
        for cp in copies:
            cp.wait()

    inner = lax.rem(j + 1, W) >= 2

    class LineGather:
        def __init__(self, view, four):
            a, b, c = in_slot(), in_slot(), in_slot()
            n, m = out_slot(), out_slot()
            near = copy(view(j), view(j), vdev[1], n, a)
            near.start()
            sent.append(near)
            across = copy(view(j), view(j), vdev[3], m, c)
            self.got = [
                copy(view(vj[d]), view(vj[d]), vdev[1], n, at) for d, at in zip(DIRS, (a, b, c))
            ]
            self.on = [
                copy(view(vj[1]), view(vj[1]), vdev[3], m, b),
                copy(view(vj[3]), view(vj[3]), vdev[1], m, b),
                copy(view(vj[2]), view(vj[2]), vdev[1], m, c),
            ]
            inner_sent.append(copy(four, four, vdev[1], m, a))

            @pl.when(inner)
            def _():
                across.start()

        def step(self, n):
            @pl.when(inner)
            def _():
                self.got[(0, 2, 1)[n]].wait_recv()
                self.on[n].start()

        def collect(self):
            @pl.when(jnp.logical_not(inner))
            def _():
                arrived(self.got)

    class LineSum:
        def __init__(self, part, both, relay, summed):
            self.part, self.both, self.relay, self.summed = part, both, relay, summed
            a, b, c = in_slot(), in_slot(), in_slot()
            n, m, o = out_slot(), out_slot(), out_slot()
            self.first = [
                copy(part(vj[3]), relay.at[0], vdev[1], n, a),
                copy(part(vj[2]), relay.at[1], vdev[1], n, b),
            ]
            self.direct = copy(part(vj[1]), both.at[0], vdev[1], m, c)
            self.second = [copy(summed.at[k], both.at[1], vdev[2 + k], o, c) for k in range(2)]
            self.all = copy(both, both, vdev[1], m, c)
            outer_sent.append(copy(relay, relay, vdev[1], n, a))
            sent.append(self.direct)
            inner_sent.append(copy(summed, summed, vdev[1], o, a))

        def go(self, n):
            if n < 2:

                @pl.when(jnp.logical_not(inner))
                def _():
                    self.first[n].start()

            elif n == 2:
                self.direct.start()

        def rest(self):
            for n in range(3):
                self.go(n)
            return self

        def step(self, n):
            @pl.when(inner)
            def _():
                self.first[n].wait_recv()
                mine_too = self.part(vj[2 + n])[...].astype(F32)
                self.summed[n] = (mine_too + self.relay[n].astype(F32)).astype(BF)
                self.second[n].start()

        def collect(self):
            self.all.wait_recv()

        def total(self):
            out = self.part(j)[...].astype(F32)
            return out + self.both[0].astype(F32) + self.both[1].astype(F32)

    class SquareSum:
        def __init__(self, part, got, relay, summed):
            self.part, self.got, self.relay, self.summed = part, got, relay, summed
            q = got.shape[-1] // 2
            self.at = [pl.ds(0, q), pl.ds(q, q)]
            a, self.into_slot = in_slot(), in_slot()
            n, self.out = out_slot(), out_slot()
            for k in range(2):
                copy(self.half(ki[3], k), relay.at[k], kdev[1 + k], n, a).start()
            for k in range(2):
                copy(self.half(ki[1 + k], k), self.into(k, k), kdev[1 + k], n, self.into_slot).start()
            self.relayed = copy(relay, relay, kdev[1], n, a)
            sent.append(copy(got, got, kdev[1], n, a))

        def half(self, target, n):
            return self.part(target, self.at[n])

        def into(self, n, h):
            return self.got.at[n, :, self.at[h]]

        def step(self):
            self.relayed.wait_recv()
            for k in range(2):
                own = self.half(ki[2 - k], k)[...].astype(F32)
                self.summed[k] = (own + self.relay[k].astype(F32)).astype(BF)
                copy(
                    self.summed.at[k], self.into(1 - k, k), kdev[2 - k], self.out, self.into_slot
                ).start()
            sent.append(copy(self.summed, self.summed, kdev[1], self.out, self.into_slot))

        def collect(self):
            copy(self.got, self.got, kdev[1], self.out, self.into_slot).wait_recv()

        def total(self):
            out = self.part(i, pl.ds(0, self.got.shape[-1]))[...].astype(F32)
            return out + self.got[0].astype(F32) + self.got[1].astype(F32)

    quarter = half // 2
    mine_parts = [
        pl.ds(pl.multiple_of(par * half + n * quarter, quarter), quarter) for n in range(2)
    ]

    class SquareGather:
        def __init__(self, view, many, whole=mine, parts=mine_parts, own=None, pass_on=True):
            self.view, self.many, self.whole, self.parts = view, many, whole, parts
            self.pass_on = pass_on
            own = view(i, whole) if own is None else own
            into = view(i, whole)
            self.near = Fan([(own, into, kdev[d]) for d in (1, 2)], many(2))

        def forward(self, sources):
            if not self.pass_on:
                return []
            views = [self.view(src, self.whole) for src in sources]
            return [Fan([(one, one, partner) for one in views], self.many(len(views)))]

        def step(self):
            self.near.wait_recv()
            views = [self.view(ki[1 + n], self.parts[n]) for n in range(2)]
            self.far = Fan([(views[n], views[n], kdev[2 - n]) for n in range(2)], self.many(1))
            return self.forward((ki[1], ki[2]))

        def collect(self):
            self.far.wait_recv()
            return self.forward((ki[3],))

    barrier = pltpu.get_barrier_semaphore()
    for dev in kdev[1:] + vdev[1:] + seqdev:
        pl.semaphore_signal(barrier, inc=1, device_id=dev, device_id_type=MESH)

    l_small = [load(dup, dup_v), load(dbi, dbi_v), load(ggn, ggn_v)]
    l_qk = [load(wq.at[j], qk_v.at[i, 0]), load(wk.at[j], qk_v.at[i, 1])]
    segment = pl.ds(pl.multiple_of(i * T, T), T)
    l_x = [load(tok.at[segment], x_v), load(ng, ng_v), load(ffg, ffg_v)]
    l_dd = load(dd, dd_v.at[pl.ds(0, 16)])
    l_v = load(wv.at[j], v_v.at[j])
    l_g = load(wg.at[j], g_v.at[j])
    l_c = load(cot.at[segment], c_v)
    l_f = [load(fg, f_v.at[0, i]), load(fu, f_v.at[1, i]), load(fd, f_v.at[2, i])]
    l_o = load(wo, o_v.at[i, j])
    l_xa = load(tok, x_all)
    l_ca = load(cot, c_all)

    dd_v[16:, :] = jnp.zeros((dd_v.shape[0] - 16, D), BF)
    here(l_small)
    head3 = lax.broadcasted_iota(jnp.int32, (16, W, 32), 1)
    head2 = lax.broadcasted_iota(jnp.int32, (W, 32), 0)
    sq_v[...] = jnp.zeros_like(sq_v)
    sq_v[0:16, 0:32] = jnp.sum(jnp.where(head3 == j, dup_v[...].astype(F32), 0.0), axis=1)
    sq_v[16:17, 0:32] = jnp.sum(
        jnp.where(head2 == j, dbi_v[...].astype(F32), 0.0), axis=0, keepdims=True
    )
    ext_v[i] = sq_v[...].T[:32].astype(BF)
    sq_v[...] = jnp.zeros_like(sq_v)
    sq_v[0:16, 0:64] = jnp.broadcast_to(ggn_v[...].astype(F32), (16, 64))
    gge_v[j] = sq_v[0:16].astype(BF)

    pl.semaphore_wait(barrier, 6 + len(seqdev))

    here(l_qk)
    t_qk = Fan(
        [(qk_v.at[i, par], qk_v.at[i, par], kdev[d]) for d in DIRS], qk_v.at[pl.ds(0, 3), 0]
    )
    left = pl.ds(0, half)
    t_v = Fan(
        [(wv.at[vj[d], :, mine], v_v.at[j, :, mine], vdev[d]) for d in DIRS],
        v_v.at[pl.ds(0, 3), :, left],
    )
    t_ext = Fan([(ext_v.at[i], ext_v.at[i], kdev[d]) for d in DIRS], ext_v.at[pl.ds(0, 3)])
    low = pl.ds(0, 32)
    high = pl.ds(32, 32)
    t_ob = Fan(
        [(wo.at[high, mine], o_v.at[i, j, high, mine], kdev[d]) for d in DIRS],
        o_v.at[pl.ds(0, 3), 0, high, mine],
    )
    weights = (fg, fu, fd)

    def gather_weight(n, rows_at):
        return SquareGather(
            lambda src, at: f_v.at[n, src, rows_at, at],
            lambda count: f_v.at[n, pl.ds(0, count), rows_at, mine],
            own=weights[n].at[rows_at, mine],
        )

    cut = FB // 32 * 16
    top = pl.ds(0, cut)
    bottom = pl.ds(cut, FB - cut)
    every = pl.ds(0, FB)
    t_fd = gather_weight(2, every)
    l_o.wait()
    t_oa = LineGather(lambda src: o_v.at[i, src, low, mine], o_v.at[0, :, low, mine])
    t_g = Fan(
        [(wg.at[vj[d], :, mine], g_v.at[j, :, mine], vdev[d]) for d in DIRS],
        g_v.at[pl.ds(0, 3), :, left],
    )
    t_gge = Fan([(gge_v.at[j], gge_v.at[j], vdev[d]) for d in DIRS], gge_v.at[pl.ds(0, 3)])

    here(l_x)
    x = x_v[...].astype(F32)
    g1 = flat_row(ng_v[...].astype(F32))
    g3 = flat_row(ffg_v[...].astype(F32))
    r1 = lax.rsqrt(jnp.sum(x * x, axis=1, keepdims=True) / D + EPS)
    n_v[...] = (x * r1 * g1).astype(BF)
    l_dd.wait()
    lane = lax.broadcasted_iota(jnp.int32, (T, 128), 1)
    lrp = jnp.where(lane == 16, 1.0, nt(n_v[...], dd_v[...]))

    t_qk.wait_recv()
    views = [qk_v.at[ki[d], par] for d in DIRS]
    f_qk = Fan([(one, one, partner) for one in views], qk_v.at[pl.ds(0, 3), 0])
    t_fg = [gather_weight(0, top)]
    f_qk.wait_recv()
    t_ext.wait_recv()
    normed = n_v[...]
    wq_all = qk_v[:, 0].reshape(W * 32, D)
    wk_all = qk_v[:, 1].reshape(W * 32, D)
    ext_all = ext_v[...].reshape(W * 32, 128)
    scale = 128.0 ** (-0.5)
    q = nt(normed, wq_all) * scale
    k = nt(normed, wk_all)
    arg = nt(lrp, ext_all.astype(F32), HIGH)
    rates = (jnp.minimum(arg, 0.0) - jnp.log1p(jnp.exp(-jnp.abs(arg)))) / 16.0
    row_id = lax.broadcasted_iota(jnp.int32, (CB, CB), 0)
    col_id = lax.broadcasted_iota(jnp.int32, (CB, CB), 1)
    causal = row_id >= col_id
    tri = jnp.where(causal, 1.0, 0.0)
    nblk = T // CB
    blk = [slice(c * CB, (c + 1) * CB) for c in range(nblk)]
    e1, e2, em, el, dec, qd, kd, qi, ke, score = [], [], [], [], [], [], [], [], [], []
    for c in range(nblk):
        cum = nn(tri, rates[blk[c]], HIGH)
        mid = cum[CB // 2 - 1 : CB // 2]
        last = cum[CB - 1 : CB]
        e1.append(jnp.exp(cum - mid))
        e2.append(jnp.exp(mid - cum))
        em.append(jnp.exp(mid))
        el.append(jnp.exp(last - mid))
        dec.append(jnp.exp(last))
        a = q[blk[c]] * e1[c]
        b = k[blk[c]] * e2[c]
        qd.append(a.astype(BF))
        kd.append(b.astype(BF))
        qi.append((a * em[c]).astype(BF))
        ke.append((b * el[c]).astype(BF))
        score.append(jnp.where(causal, nt(qd[c], kd[c]), 0.0).astype(BF))

    l_v.wait()
    t_v.wait_recv()
    views = [v_v.at[vj[d], :, mine] for d in DIRS]
    f_vv = Fan([(one, one, partner) for one in views], v_v.at[pl.ds(0, 3), :, left])
    f_vv.wait_recv()
    wv_all = v_v[...].reshape(W * 64, D)
    v = nt(normed, wv_all).astype(BF)
    up = [tn(v[blk[c]], ke[c]) for c in range(nblk)]
    loc = up[0]
    locd = dec[0]
    for c in range(1, nblk):
        loc = loc * dec[c] + up[c]
        locd = locd * dec[c]
    VC = loc.shape[0]
    st_v[i, :VC] = loc.astype(BF)
    st_v[i, VC:] = jnp.broadcast_to(locd, (16, 128)).astype(BF)
    t_st = Fan([(st_v.at[i], st_v.at[i], kdev[d]) for d in DIRS], st_v.at[pl.ds(0, 3)])
    t_fg.append(gather_weight(0, bottom))
    t_fu = gather_weight(1, every)
    t_oa.step(0)
    t_oa.step(1)
    mixed = [nn(score[c], v[blk[c]]) for c in range(nblk)]

    t_ob.wait_recv()
    views = [o_v.at[ki[d], j, high, mine] for d in DIRS]
    f_o = [Fan([(one, one, partner) for one in views], o_v.at[pl.ds(0, 3), 0, high, mine])]
    t_ob2 = LineGather(lambda src: o_v.at[:, src, high, mine], o_v.at[:, :, high, mine])
    here(l_f)
    f_f = t_fd.step()
    t_oa.step(2)

    def gather_states(slots, totals, back):
        order = range(W - 1, -1, -1) if back else range(W)
        pre_s = jnp.zeros((VC, 128), F32)
        pre_d = jnp.ones((1, 128), F32)
        tot_s = jnp.zeros((VC, 128), F32)
        tot_d = jnp.ones((1, 128), F32)
        for other_i in order:
            one_s = slots[other_i, :VC].astype(F32)
            one_d = slots[other_i, VC : VC + 1].astype(F32)
            use = (other_i > i) if back else (other_i < i)
            pre_s = jnp.where(use, pre_s * one_d + one_s, pre_s)
            pre_d = jnp.where(use, pre_d * one_d, pre_d)
            tot_s = tot_s * one_d + one_s
            tot_d = tot_d * one_d
        totals[s, :VC] = tot_s.astype(BF)
        totals[s, VC:] = jnp.broadcast_to(tot_d, (16, 128)).astype(BF)
        return pre_s, pre_d, [send(totals.at[s], totals.at[s], dev) for dev in seqdev]

    def entering(totals, back, pre_s, pre_d, moves):
        arrived(moves)
        order = range(n_seq - 1, -1, -1) if back else range(n_seq)
        far = jnp.zeros((VC, 128), F32)
        for other_s in order:
            one_s = totals[other_s, :VC].astype(F32)
            one_d = totals[other_s, VC : VC + 1].astype(F32)
            use = (other_s > s) if back else (other_s < s)
            far = jnp.where(use, far * one_d + one_s, far)
        return pre_s + pre_d * far

    t_st.wait_recv()
    states = gather_states(st_v, tt_v, False)

    l_g.wait()
    t_g.wait_recv()
    views = [g_v.at[vj[d], :, mine] for d in DIRS]
    f_g = Fan([(one, one, partner) for one in views], g_v.at[pl.ds(0, 3), :, left])
    t_ob2.step(0)
    t_ob2.step(1)
    start = [entering(tt_v, False, *states)]
    for c in range(nblk):
        start.append(start[c] * dec[c] + up[c])
    start_low = [a.astype(BF) for a in start]
    for c in range(nblk):
        mixed[c] = mixed[c] + nt(qi[c], start_low[c])
    mix = jnp.concatenate(mixed, axis=0)
    r2 = lax.rsqrt(jnp.sum(mix * mix, axis=1, keepdims=True) / VC + EPS)
    normal = mix * r2
    f_g.wait_recv()
    t_gge.wait_recv()
    wg_all = g_v[...].reshape(W * 64, D)
    gate = nt(normed, wg_all)
    gg = jnp.concatenate([gge_v[h].astype(F32)[0:1, 0:64] for h in range(W)], axis=1)
    sig = 1.0 / (1.0 + jnp.exp(-gate))
    act = gate * sig
    act_v[0] = act
    act_v[1] = sig + act * (1.0 - sig)
    ga_v[j] = (normal * gg * act).astype(BF)
    act_v[2] = normal
    halves = [pl.ds(n * T // 2, T // 2) for n in range(2)]
    t_ga = [LineGather(lambda src, at=at: ga_v.at[src, at], ga_v.at[:, at]) for at in halves]

    t_oa.collect()
    views = [o_v.at[i, vj[d], low, mine] for d in DIRS]
    f_o.append(Fan([(one, one, partner) for one in views], o_v.at[0, pl.ds(0, 3), low, mine]))
    t_oa2 = SquareGather(
        lambda src, at: o_v.at[src, :, low, at], lambda count: o_v.at[pl.ds(0, count), :, low, mine]
    )

    here([l_xa, l_ca])
    for part in range(rows // T):
        at = pl.ds(part * T, T)
        xa = x_all[at, :].astype(F32)
        ra = lax.rsqrt(jnp.sum(xa * xa, axis=1, keepdims=True) / D + EPS)
        n_all[at, :] = (xa * ra * g1).astype(BF)
    xr_v[...] = (x * (r1 * r1 * r1)).astype(BF).T
    low_all = jnp.where(
        lax.broadcasted_iota(jnp.int32, (rows, 128), 1) == 16, 1.0, nt(n_all[...], dd_v[...])
    )
    lall_v[...] = low_all.astype(BF)
    for line in t_fg:
        f_f += line.step()
    t_ob2.step(2)
    t_ga[0].step(0)
    t_ga[0].step(1)
    t_ga[1].step(0)
    t_ga[1].step(1)
    f_f += t_fu.step()
    t_ga[0].step(2)
    t_ga[1].step(2)
    f_o += t_oa2.step()
    t_ob2.collect()
    views = [o_v.at[:, vj[d], high, mine] for d in DIRS]
    f_o.append(Fan([(one, one, partner) for one in views], o_v.at[:, pl.ds(0, 3), high, mine]))
    f_f += t_fd.collect()
    l_c.wait()
    arrived(f_f)
    dn = f_v[2].reshape(W * FB, D)
    gh_v[...] = nt(c_v[...], dn)
    f_f = t_fg[0].collect() + t_fg[1].collect()
    f_f += t_fu.collect()
    f_far = t_oa2.collect()
    for line in t_ga:
        line.collect()
    arrived(f_o)


    def attention(head):
        return nn(ga_v[head], o_v[head].reshape(W * 64, D))

    att = attention(i) + attention(ki[1]) + attention(ki[2])
    p_v[...] = att
    arrived(f_far)
    arrived(f_f)
    gT = f_v[0].reshape(W * FB, D)
    uT = f_v[1].reshape(W * FB, D)
    att = p_v[...] + attention(ki[3])
    resid = x_v[...].astype(F32) + att
    r3 = lax.rsqrt(jnp.sum(resid * resid, axis=1, keepdims=True) / D + EPS)
    fin = (resid * r3 * g3).astype(BF)
    gval = nt(fin, gT)
    uval = nt(fin, uT)
    fsig = 1.0 / (1.0 + jnp.exp(-gval))
    fact = gval * fsig
    hid = (fact * uval).astype(BF)
    gh = gh_v[...]
    gup = (gh * fact).astype(BF)
    ggate = (gh * uval * (fsig + fact * (1.0 - fsig))).astype(BF)
    hd[...] = hid.T.reshape(W, FB, T)
    t_hd = Fan([(hd.at[ki[d]], hseg.at[i], kdev[d]) for d in DIRS], hseg.at[pl.ds(0, 3)])
    hseg[i] = hd[i]
    part = nn(ggate, gT) + nn(gup, uT)
    p_v[...] = part
    sst[...] = as_row(jnp.sum(resid * g3 * part, axis=1, keepdims=True))
    t_m3 = Fan([(sst, rst.at[d], vdev[d]) for d in DIRS], rst.at[pl.ds(1, 3)])
    part_low = (part * g3).astype(BF)
    t_gg = [
        LineSum(
            lambda to, at=at: sgg.at[to, at],
            rgg.at[pl.ds(0, 2), at],
            rgg.at[pl.ds(2, 2), at],
            cgg.at[:, at],
        )
        for at in halves
    ]
    ggp = nt(part_low, o_v[...].reshape(W * W * 64, D))
    for h in range(W):
        sgg[h] = ggp[:, h * VC : (h + 1) * VC].astype(BF)
    for n in range(3):
        for line in t_gg:
            line.go(n)

    def weight_part(n, grad):
        gw[n] = tn(grad, fin).astype(BF).reshape(W, FB, D)
        return send(gw.at[n, :, :, other], pre.at[n], partner)

    def settle(n, move):
        move.wait_recv()
        pres[n] = (gw[n, :, :, mine].astype(F32) + pre[n].astype(F32)).astype(BF)

    def square(n, rows_at):
        return SquareSum(
            lambda to, at: pres.at[n, to, rows_at, at],
            rfw.at[n, :, rows_at],
            qfw.at[n, :, rows_at],
            cfw.at[n, :, rows_at],
        )

    t_pre0 = weight_part(0, ggate)
    t_pre1 = weight_part(1, gup)

    feature = lax.broadcasted_iota(jnp.int32, (1, D), 1)
    own_slab = jnp.where(lax.rem(feature // 64, W) == j, 1.0, 0.0)
    own_run = jnp.where(feature // (D // W) == j, 1.0, 0.0)
    so[...] = (nn(hid, dn) + own_slab * resid).astype(BF).T.reshape(W, W, 64, T)
    t_out = LineSum(lambda to: so.at[:, to], ro.at[pl.ds(0, 2)], ro.at[pl.ds(2, 2)], co).rest()
    ffn_gain = jnp.sum(part * resid * r3, axis=0, keepdims=True)
    t_gg[0].step(0)
    t_m3.wait_recv()
    m3 = as_column(sst[...] + rst[1] + rst[2] + rst[3]) / D
    base = c_v[...].astype(F32) - resid * (r3 * r3 * r3 * m3)
    settle(0, t_pre0)
    t_fw0 = square(0, every)
    direct = nt(base.astype(BF), o_v[j].reshape(W * 64, D))
    full = p_v[...] * (g3 * r3)
    mixed_in = (full + own_run * base).astype(BF)
    for h in range(W):
        gow[h] = tn(ga_v[h], mixed_in).astype(BF)
    t_po = send(gow.at[:, :, other], preo, partner)
    t_gg[0].step(1)
    t_gg[1].step(0)
    t_gg[1].step(1)
    t_po.wait_recv()
    preso[...] = (gow[:, :, mine].astype(F32) + preo[...].astype(F32)).astype(BF)
    t_fw0.step()
    settle(1, t_pre1)
    t_fw1 = [square(1, top)]
    for line in t_gg:
        line.collect()

    ggs = jnp.concatenate([line.total() for line in t_gg], axis=0)
    ggrad = direct + r3 * ggs
    act = act_v[0]
    normal = act_v[2]
    dgate = (ggrad * normal * gg * act_v[1]).astype(BF)
    gs = ggrad * act
    group = jnp.sum(gs * normal, axis=0, keepdims=True)
    group_rows = [
        jnp.concatenate(
            [group[:, h * 64 : (h + 1) * 64], jnp.zeros((1, T - 64), F32)], axis=1
        )
        for h in range(W)
    ]
    gnm = gs * gg
    gmix = (r2 * (gnm - normal * (jnp.sum(normal * gnm, axis=1, keepdims=True) / VC))).astype(BF)

    qst = [tn(gmix[blk[c]], qi[c]) for c in range(nblk)]
    bloc = qst[nblk - 1]
    for c in range(nblk - 2, -1, -1):
        bloc = bloc * dec[c] + qst[c]
    bst_v[i, :VC] = bloc.astype(BF)
    bst_v[i, VC:] = jnp.broadcast_to(locd, (16, 128)).astype(BF)
    t_bst = Fan([(bst_v.at[i], bst_v.at[i], kdev[d]) for d in DIRS], bst_v.at[pl.ds(0, 3)])
    t_ow = SquareSum(lambda to, at: preso.at[to, :, at], rowk, qow, cow)
    t_fw1.append(square(1, bottom))
    vz[1] = dgate.T.reshape(W, 64, T)
    t_gz = Fan([(vz.at[1, vj[d]], zvg.at[1, j], vdev[d]) for d in DIRS], zvg.at[1, pl.ds(0, 3)])
    dq_in, dk_in, dv_in = [], [], []
    for c in range(nblk):
        ds = jnp.where(causal, nt(gmix[blk[c]], v[blk[c]]), 0.0).astype(BF)
        dq_in.append(nn(ds, kd[c]) + em[c] * nn(gmix[blk[c]], start_low[c]))
        dk_in.append(tn(ds, qd[c]))
        dv_in.append(tn(score[c], gmix[blk[c]]))
    t_out.step(0)
    t_hd.wait_recv()
    dsum[0] = nn(lanes(hseg[...]), c_all[...]).astype(BF)
    t_ds = send(dsum.at[0], dsum.at[1], partner)
    t_bst.wait_recv()
    after = [None] * nblk
    states = gather_states(bst_v, btt_v, True)
    after[nblk - 1] = entering(btt_v, True, *states)
    for c in range(nblk - 2, -1, -1):
        after[c] = after[c + 1] * dec[c + 1] + qst[c + 1]
    t_out.step(1)
    t_fw1[0].step()

    ql, kl, vl, ga = [], [], [], []
    for c in range(nblk):
        low_after = after[c].astype(BF)
        dq = e1[c] * dq_in[c]
        dk = e2[c] * (dk_in[c] + el[c] * nn(v[blk[c]], low_after))
        dv = dv_in[c] + nt(ke[c], low_after)
        gc = q[blk[c]] * dq - k[blk[c]] * dk
        extra = jnp.sum(after[c] * start[c + 1], axis=0, keepdims=True)
        gc = jnp.where(row_id == CB - 1, gc + extra, gc)
        gr = tn(tri, gc, HIGH)
        ga.append(gr / (1.0 + jnp.exp(arg[blk[c]])) / 16.0)
        ql.append((dq * scale).astype(BF))
        kl.append(dk.astype(BF))
        vl.append(dv.astype(BF))
    ql = jnp.concatenate(ql, axis=0)
    kl = jnp.concatenate(kl, axis=0)
    vl = jnp.concatenate(vl, axis=0)
    ga = jnp.concatenate(ga, axis=0).astype(BF)
    vz[0] = vl.T.reshape(W, 64, T)
    qka[:, 0] = ql.T.reshape(W, 32, T)
    qka[:, 1] = kl.T.reshape(W, 32, T)
    qka[:, 2] = ga.T.reshape(W, 32, T)
    t_qa = Fan([(qka.at[ki[d]], kqa.at[i], kdev[d]) for d in DIRS], kqa.at[pl.ds(0, 3)])
    glr = nn(ga, ext_all).astype(BF)
    gn = nn(ql, wq_all) + nn(kl, wk_all) + nn(vl, wv_all) + nn(dgate, wg_all) + nn(glr, dd_v[...])
    x = x_v[...].astype(F32)
    gnx = gn * x
    norm_gain = jnp.sum(gnx * r1, axis=0, keepdims=True)
    m1p = as_row(jnp.sum(gnx * g1, axis=1, keepdims=True))[:1]
    rank_row = lax.broadcasted_iota(jnp.int32, (16, 128), 0)
    rank_col = lax.broadcasted_iota(jnp.int32, (16, 128), 1)
    by_owner = jnp.where(rank_col == lax.rem(rank_row, W) * W + rank_row // W, 1.0, 0.0)
    small = nn(by_owner.astype(BF), tn(glr, normed).astype(BF))
    slab = D // (W * W)
    rid = lax.broadcasted_iota(jnp.int32, (16, T), 0)
    for h in range(W):
        ranks = small[h * W : (h + 1) * W]
        sm0[h, 0:16] = jnp.concatenate(
            [ranks[:, n * T : (n + 1) * T] for n in range(W)], axis=0
        ).astype(BF)

        def slabs(row):
            return jnp.concatenate(
                [row[:, (W * n + h) * slab : (W * n + h + 1) * slab] for n in range(W)], axis=1
            )

        rest = jnp.where(rid == 0, slabs(norm_gain), 0.0)
        rest = jnp.where(rid == 1, slabs(ffn_gain), rest)
        rest = jnp.where(rid == 2, group_rows[h], rest)
        rest = jnp.where(rid == 3, m1p, rest)
        sm0[h, 16:32] = rest.astype(BF)
    t_s0 = Fan([(sm0.at[vj[d]], sm1.at[d], vdev[d]) for d in DIRS], sm1.at[pl.ds(1, 3)])
    whole = gn * (r1 * g1) + full + own_slab * base
    sgn[...] = whole.astype(BF).T.reshape(W, W, 64, T)
    pairs = [pl.ds(n * W // 2, W // 2) for n in range(2)]
    t_gn = [
        LineSum(
            lambda to, at=at: sgn.at[at, to],
            rgn.at[pl.ds(0, 2), at],
            rgn.at[pl.ds(2, 2), at],
            cgn.at[:, at],
        )
        for at in pairs
    ]
    for n in range(3):
        for line in t_gn:
            line.go(n)
    t_vz = Fan([(vz.at[0, vj[d]], zvg.at[0, j], vdev[d]) for d in DIRS], zvg.at[0, pl.ds(0, 3)])


    t_gz.wait_recv()
    zvg[1, j] = vz[1, j]
    t_gk = Fan([(zvg.at[1, ki[d]], kvg.at[1, i], kdev[d]) for d in DIRS], kvg.at[1, pl.ds(0, 3)])
    kvg[1, i] = zvg[1, i]

    def finish_square(n, lines):
        for line, rows_at in lines:
            line.collect()
            fin_f[par, n, rows_at] = line.total().astype(BF)
        return send(fin_f.at[par, n], fin_f.at[par, n], partner)

    t_ff = [finish_square(0, [(t_fw0, every)])]
    t_ow.step()
    t_fw1[1].step()

    t_s0.wait_recv()
    sm2[0] = total(sm0[j], sm1).astype(BF)
    m1 = (
        sm0[0, 19:20].astype(F32)
        + sm1[1, 19:20].astype(F32)
        + sm1[2, 19:20].astype(F32)
        + sm1[3, 19:20].astype(F32)
    ) / D
    t_s1 = Fan([(sm2.at[0], sm2.at[d], kdev[d]) for d in DIRS], sm2.at[pl.ds(1, 3)])

    t_out.collect()
    ao[...] = t_out.total().astype(BF)
    t_ao = Fan([(ao.at[ki[d]], oseg.at[i], kdev[d]) for d in DIRS], oseg.at[pl.ds(0, 3)])
    oseg[i] = ao[i]

    t_gn[0].step(0)
    t_gn[1].step(0)
    t_gn[0].step(1)
    t_gn[1].step(1)

    t_ow.collect()
    mid_o[...] = t_ow.total().astype(BF).reshape(W, 64, half)
    t_oz = LineSum(
        lambda to: mid_o.at[to], rowz.at[pl.ds(0, 2)], rowz.at[pl.ds(2, 2)], coz
    ).rest()

    t_qa.wait_recv()
    kqa[i] = qka[i]
    nall = n_all[...]
    for n in range(2):
        qksum[0, n] = nn(lanes(kqa[:, n]), nall).astype(BF)
    esum[0] = nn(lanes(kqa[:, 2]), lall_v[...])
    t_qs = send(qksum.at[0], qksum.at[1], partner)
    t_es = send(esum.at[0], esum.at[1], partner)
    t_ff.append(finish_square(1, list(zip(t_fw1, (top, bottom)))))

    t_gk.wait_recv()
    vgsum[0, 1] = nn(lanes(kvg[1]), nall).astype(BF)
    t_vs = [send(vgsum.at[0, 1], vgsum.at[1, 1], partner)]

    for line in t_gn:
        line.collect()
    summed = jnp.concatenate([line.total() for line in t_gn], axis=0)
    for h in range(W):
        at = pl.ds(pl.multiple_of((h * W + j) * 64, 64), 64)
        ai[h] = (summed[h] - xr_v[at, :].astype(F32) * m1).astype(BF)
    t_ai = Fan([(ai.at[ki[d]], iseg.at[i], kdev[d]) for d in DIRS], iseg.at[pl.ds(0, 3)])
    iseg[i] = ai[i]

    t_vz.wait_recv()
    zvg[0, j] = vz[0, j]
    t_vk = Fan([(zvg.at[0, ki[d]], kvg.at[0, i], kdev[d]) for d in DIRS], kvg.at[0, pl.ds(0, 3)])
    kvg[0, i] = zvg[0, i]

    t_s1.wait_recv()
    sm3[0] = total(sm2[0], sm2).astype(BF)
    t_s2 = send(sm3.at[0], sm3.at[1], partner)
    t_oz.step(0)
    t_oz.step(1)
    t_vk.wait_recv()
    vgsum[0, 0] = nn(lanes(kvg[0]), nall).astype(BF)
    t_vs.append(send(vgsum.at[0, 0], vgsum.at[1, 0], partner))

    t_ds.wait_recv()
    r_fd[...] = dsum[0].astype(F32) + dsum[1].astype(F32)
    t_ao.wait_recv()
    r_out[...] = lanes(oseg[...])
    t_qs.wait_recv()
    r_q[...] = qksum[0, 0].astype(F32) + qksum[1, 0].astype(F32)
    r_k[...] = qksum[0, 1].astype(F32) + qksum[1, 1].astype(F32)
    t_es.wait_recv()
    decay = (esum[0] + esum[1]).T
    r_du[...] = decay[0:16, :].reshape(16, 1, 32)
    r_db[...] = decay[16:17, :]
    t_ff[0].wait_recv()
    for h in range(2):
        r_fg[:, h * half : (h + 1) * half] = fin_f[h, 0].astype(F32)
    t_oz.collect()
    fin_ow[par] = t_oz.total().astype(BF)
    t_fo = send(fin_ow.at[par], fin_ow.at[par], partner)
    t_ff[1].wait_recv()
    for h in range(2):
        r_fu[:, h * half : (h + 1) * half] = fin_f[h, 1].astype(F32)
    arrived(t_vs)
    r_v[...] = vgsum[0, 0].astype(F32) + vgsum[1, 0].astype(F32)
    r_g[...] = vgsum[0, 1].astype(F32) + vgsum[1, 1].astype(F32)
    t_s2.wait_recv()
    tot = sm3[0].astype(F32) + sm3[1].astype(F32)
    own_ranks, own_slabs = [], jnp.zeros((2, slab), F32)
    for n in range(W):
        own_ranks.append(jnp.zeros((1, T), F32))
        for h in range(W):
            row = tot[n * W + h : n * W + h + 1]
            own_ranks[n] = jnp.where(i == h, row, own_ranks[n])
        own_slabs = jnp.where(i == n, tot[16:18, n * slab : (n + 1) * slab], own_slabs)
    r_dd[...] = jnp.concatenate(own_ranks, axis=1)
    r_ng[...] = own_slabs[0:1]
    r_fn[...] = own_slabs[1:2]
    r_gg[...] = tot[18:19, 0:64]
    t_ai.wait_recv()
    r_in[...] = lanes(iseg[...])
    t_fo.wait_recv()
    for h in range(2):
        r_o[:, h * half : (h + 1) * half] = fin_ow[h].astype(F32)
    for cp in sent + [cp for _, cp in ring]:
        cp.wait_send()

    @pl.when(inner)
    def _():
        for cp in inner_sent:
            cp.wait_send()

    @pl.when(jnp.logical_not(inner))
    def _():
        for cp in outer_sent:
            cp.wait_send()


N_OUT = 62
N_IN = 93
N_LOCAL = 18


def layer(n_seq, args):
    rows, D = args[0].shape
    W = WAYS
    T = rows // W
    FB = args[-1].shape[0]
    VC = W * 64
    half = D // 2

    def sds(shape, dtype=F32):
        return pltpu.VMEM(shape, dtype)

    def vm(shape, dtype=BF):
        return pltpu.VMEM(shape, dtype)

    slab = D // (W * W)
    outs = [
        sds((64, rows), BF),
        sds((64, rows), BF),
        sds((1, slab)),
        sds((32, D)),
        sds((32, D)),
        sds((64, D)),
        sds((64, D)),
        sds((1, D)),
        sds((16, 1, 32)),
        sds((1, 32)),
        sds((1, 64)),
        sds((64, D)),
        sds((1, slab)),
        sds((FB, D)),
        sds((FB, D)),
        sds((FB, D)),
    ]
    scratch = [
        vm((T, D)),
        vm((T, D)),
        vm((rows, D)),
        vm((rows, D)),
        vm((rows, D)),
        vm((T, D)),
        vm((D, T)),
        vm((128, D)),
        vm((8, 128)),
        vm((8, 128)),
        vm((16, W, 32)),
        vm((W, 32)),
        vm((1, 64)),
        vm((128, 128), F32),
        vm((8, D), F32),
        vm((W, 2, 32, D)),
        vm((W, 32, 128)),
        vm((W, 64, D)),
        vm((W, 64, D)),
        vm((W, 16, 128)),
        vm((W, W, 64, D)),
        vm((3, W, FB, D)),
        vm((W, VC + 16, 128)),
        vm((n_seq, VC + 16, 128)),
        vm((W, VC + 16, 128)),
        vm((n_seq, VC + 16, 128)),
        vm((W, T, VC)),
        vm((W, T, VC)),
        vm((W, T, VC)),
        vm((2, T, VC)),
        vm((8, T), F32),
        vm((W, 8, T), F32),
        vm((W, W, 64, T)),
        vm((W, W, 64, T)),
        vm((2, W, 64, T)),
        vm((W, W, 64, T)),
        vm((W, W, 64, T)),
        vm((2, W, 64, T)),
        vm((W, 64, T)),
        vm((W, 64, T)),
        vm((W, 64, T)),
        vm((W, 64, T)),
        vm((W, FB, T)),
        vm((W, FB, T)),
        vm((2, W, FB, D)),
        vm((2, W, FB, half)),
        vm((2, W, FB, half)),
        vm((2, 2, FB, half)),
        vm((2, 2, FB, half // 2)),
        vm((2, 2, FB, half // 2)),
        vm((2, 2, FB, half)),
        vm((2, FB, D)),
        vm((W, VC, D)),
        vm((W, VC, half)),
        vm((W, VC, half)),
        vm((2, VC, half)),
        vm((2, VC, half // 2)),
        vm((2, VC, half // 2)),
        vm((W, 64, half)),
        vm((W, 64, half)),
        vm((2, 64, half)),
        vm((2, 64, half)),
        vm((2, W, 64, T)),
        vm((2, W, 64, T)),
        vm((2, W, 64, T)),
        vm((2, 2, 64, D)),
        vm((W, 3, 32, T)),
        vm((W, 3, 32, T)),
        vm((2, 2, 32, D)),
        vm((2, 32, 128), F32),
        vm((W, 32, T)),
        vm((W, 32, T)),
        vm((W, 32, T)),
        vm((2, 32, T)),
        vm((rows, 128)),
        vm((T, W * FB), F32),
        vm((3, T, VC), F32),
        vm((T, D), F32),
        pltpu.SemaphoreType.DMA((N_OUT,)),
        pltpu.SemaphoreType.DMA((N_IN + 2 * n_seq,)),
        pltpu.SemaphoreType.DMA((N_LOCAL,)),
    ]
    return pl.pallas_call(
        functools.partial(layer_kernel, n_seq),
        out_shape=outs,
        in_specs=[pl.BlockSpec(memory_space=pl.ANY)] * len(args),
        out_specs=[pl.BlockSpec(memory_space=pltpu.VMEM)] * len(outs),
        scratch_shapes=scratch,
        compiler_params=pltpu.CompilerParams(
            collective_id=0, has_side_effects=True, vmem_limit_bytes=60 * 2**20
        ),
        name="layer",
    )(*args)


def finish_kernel(*refs):
    n = len(refs) // 2
    sem = refs[-1]
    copies = [pltpu.make_async_copy(refs[k], refs[n + k], sem.at[k]) for k in range(n)]
    for cp in copies:
        cp.start()
    for cp in copies:
        cp.wait()


def finish(parts):
    return pl.pallas_call(
        finish_kernel,
        out_shape=[jax.ShapeDtypeStruct(p.shape, p.dtype) for p in parts],
        in_specs=[pl.BlockSpec(memory_space=pltpu.VMEM)] * len(parts),
        out_specs=[pl.BlockSpec(memory_space=pl.ANY)] * len(parts),
        scratch_shapes=[pltpu.SemaphoreType.DMA((len(parts),))],
        compiler_params=pltpu.CompilerParams(vmem_limit_bytes=16 * 2**20),
        name="finish",
    )(*parts)


def shards(
    n_seq,
    tokens,
    norm_gain,
    query_weight,
    key_weight,
    value_weight,
    gate_weight,
    decay_down,
    decay_up,
    decay_bias,
    group_gain,
    out_weight,
    ffn_gain,
    ffn_gate,
    ffn_up,
    ffn_down,
    cotangent,
):
    parts = layer(
        n_seq,
        (
            tokens,
            cotangent,
            norm_gain.reshape(8, -1),
            ffn_gain.reshape(8, -1),
            decay_up,
            decay_bias,
            group_gain[None],
            query_weight.transpose(1, 2, 0),
            key_weight.transpose(1, 2, 0),
            value_weight.transpose(1, 2, 0),
            gate_weight.transpose(1, 2, 0),
            decay_down.T,
            out_weight[0],
            ffn_gate.T,
            ffn_up.T,
            ffn_down,
        ),
    )
    if n_seq > 2:

        def over_pairs(a):
            return jnp.sum(lax.all_gather(a, "seq")[::2].astype(F32), axis=0).astype(a.dtype)

        parts = list(parts[:2]) + [over_pairs(a) for a in parts[2:]]
    (r_out, r_in, r_ng, r_q, r_k, r_v, r_g, r_dd, r_du, r_db, r_gg, r_o, r_fn, r_fg, r_fu, r_fd) = finish(parts)
    return (
        r_out.T,
        r_in.T,
        r_ng[0],
        r_q.T[:, None, :],
        r_k.T[:, None, :],
        r_v.T[:, None, :],
        r_g.T[:, None, :],
        r_dd.T,
        r_du,
        r_db,
        r_gg[0],
        r_o[None],
        r_fn[0],
        r_fg.T,
        r_fu.T,
        r_fd,
    )


def solution(mesh):
    in_specs = (
        P("seq", None),
        P(),
        P(None, None, "kax"),
        P(None, None, "kax"),
        P(None, None, "vax"),
        P(None, None, "vax"),
        P(),
        P(None, None, "kax"),
        P(None, "kax"),
        P("vax"),
        P("kax", "vax", None),
        P(),
        P(None, ("kax", "vax")),
        P(None, ("kax", "vax")),
        P(("kax", "vax"), None),
        P("seq", None),
    )
    out_specs = (
        P("seq", ("kax", "vax")),
        P("seq", ("kax", "vax")),
        P(("kax", "vax")),
        P(None, "vax", "kax"),
        P(None, "vax", "kax"),
        P(None, "kax", "vax"),
        P(None, "kax", "vax"),
        P(None, ("kax", "vax")),
        P(None, "vax", "kax"),
        P("vax", "kax"),
        P("vax"),
        P("kax", "vax", None),
        P(("kax", "vax")),
        P(None, ("kax", "vax")),
        P(None, ("kax", "vax")),
        P(("kax", "vax"), None),
    )
    return jax.shard_map(
        functools.partial(shards, mesh.shape["seq"]),
        mesh=mesh,
        in_specs=in_specs,
        out_specs=out_specs,
        check_vma=False,
    )
```

```python
import functools

import jax
import jax.numpy as jnp
from jax import lax
from jax.experimental import pallas as pl
from jax.experimental.pallas import tpu as pltpu
from jax.sharding import PartitionSpec as P

MESH = pl.DeviceIdType.MESH
BF = jnp.bfloat16
F32 = jnp.float32
CB = 128
WAYS = 4
EPS = 1e-06
HIGH = lax.Precision.HIGHEST


def nn(a, b, precision=None):
    return lax.dot_general(
        a, b, (((1,), (0,)), ((), ())), precision=precision, preferred_element_type=F32
    )


def nt(a, b, precision=None):
    return lax.dot_general(
        a, b, (((1,), (1,)), ((), ())), precision=precision, preferred_element_type=F32
    )


def tn(a, b, precision=None):
    return lax.dot_general(
        a, b, (((0,), (0,)), ((), ())), precision=precision, preferred_element_type=F32
    )


def xor(index, d):
    if d == 1:
        return index + 1 - 2 * lax.rem(index, 2)
    if d == 2:
        return lax.rem(index + 2, 4)
    return 3 - index


def as_row(column):
    return jnp.broadcast_to(column, (column.shape[0], 128)).T[:8]


def as_column(row):
    return jnp.broadcast_to(row[:1], (128, row.shape[1])).T[:, :1]


def flat_row(block):
    return jnp.concatenate([block[r : r + 1] for r in range(block.shape[0])], axis=1)


def lanes(block):
    return jnp.concatenate([block[n] for n in range(block.shape[0])], axis=1)


def total(own, got):
    out = own.astype(F32)
    for d in (1, 2, 3):
        out = out + got[d].astype(F32)
    return out


def layer_kernel(
    n_seq,
    tok,
    cot,
    ng,
    ffg,
    dup,
    dbi,
    ggn,
    wq,
    wk,
    wv,
    wg,
    dd,
    wo,
    fg,
    fu,
    fd,
    r_out,
    r_in,
    r_ng,
    r_q,
    r_k,
    r_v,
    r_g,
    r_dd,
    r_du,
    r_db,
    r_gg,
    r_o,
    r_fn,
    r_fg,
    r_fu,
    r_fd,
    x_v,
    c_v,
    x_all,
    c_all,
    n_all,
    n_v,
    xr_v,
    dd_v,
    ng_v,
    ffg_v,
    dup_v,
    dbi_v,
    ggn_v,
    sq_v,
    gain_v,
    qk_v,
    ext_v,
    v_v,
    g_v,
    gge_v,
    o_v,
    f_v,
    st_v,
    tt_v,
    bst_v,
    btt_v,
    ga_v,
    sgg,
    rgg,
    cgg,
    sst,
    rst,
    so,
    ro,
    co,
    sgn,
    rgn,
    cgn,
    ao,
    oseg,
    ai,
    iseg,
    hd,
    hseg,
    gw,
    pre,
    pres,
    rfw,
    qfw,
    cfw,
    fin_f,
    dsum,
    gow,
    preo,
    preso,
    rowk,
    qow,
    cow,
    mid_o,
    rowz,
    coz,
    fin_ow,
    vz,
    zvg,
    kvg,
    vgsum,
    qka,
    kqa,
    qksum,
    esum,
    sm0,
    sm1,
    sm2,
    sm3,
    lall_v,
    gh_v,
    act_v,
    p_v,
    ss,
    rs,
    ls,
):
    s = lax.axis_index("seq")
    i = lax.axis_index("kax")
    j = lax.axis_index("vax")
    par = lax.rem(s, 2)
    oth = 1 - par
    T, D = x_v.shape
    rows = x_all.shape[0]
    FB = f_v.shape[2]
    half = D // 2
    W = WAYS
    DIRS = (1, 2, 3)
    mine = pl.ds(pl.multiple_of(par * half, half), half)
    other = pl.ds(pl.multiple_of(oth * half, half), half)
    partner = {"seq": s + 1 - 2 * par}
    kdev = [None] + [{"kax": xor(i, d)} for d in DIRS]
    vdev = [None] + [{"vax": xor(j, d)} for d in DIRS]
    ki = [None] + [xor(i, d) for d in DIRS]
    vj = [None] + [xor(j, d) for d in DIRS]
    seqdev = [{"seq": lax.rem(s + e, n_seq)} for e in range(1, n_seq)]

    count = [0, 0, 0]
    inner_sent, outer_sent = [], []

    def slot(kind):
        count[kind] += 1
        return count[kind] - 1

    def out_slot():
        return slot(0)

    def in_slot():
        return slot(1)

    def copy(src, dst, dev, n, m):
        return pltpu.make_async_remote_copy(
            src_ref=src,
            dst_ref=dst,
            send_sem=ss.at[n],
            recv_sem=rs.at[m],
            device_id=dev,
            device_id_type=MESH,
        )

    ring = []

    def ring_slot():
        if len(ring) < 28:
            return out_slot()
        n, cp = ring.pop(0)
        cp.wait_send()
        return n

    def send(src, dst, dev):
        n = ring_slot()
        cp = copy(src, dst, dev, n, in_slot())
        cp.start()
        ring.append((n, cp))
        return cp

    def load(src, dst):
        cp = pltpu.make_async_copy(src, dst, ls.at[slot(2)])
        cp.start()
        return cp

    class Fan:
        def __init__(self, copies, size):
            n, m = ring_slot(), in_slot()
            for src, dst, dev in copies:
                copy(src, dst, dev, n, m).start()
            self.all = copy(size, size, partner, n, m)
            ring.append((n, self.all))

        def wait_recv(self):
            self.all.wait_recv()

    def arrived(copies):
        for cp in copies:
            cp.wait_recv()

    def here(copies):
        for cp in copies:
            cp.wait()

    inner = lax.rem(j + 1, W) >= 2

    class LineGather:
        def __init__(self, view, four):
            a, b, c = in_slot(), in_slot(), in_slot()
            n, m = ring_slot(), out_slot()
            near = copy(view(j), view(j), vdev[1], n, a)
            near.start()
            ring.append((n, near))
            across = copy(view(j), view(j), vdev[3], m, c)
            self.got = [
                copy(view(vj[d]), view(vj[d]), vdev[1], n, at) for d, at in zip(DIRS, (a, b, c))
            ]
            self.on = [
                copy(view(vj[1]), view(vj[1]), vdev[3], m, b),
                copy(view(vj[3]), view(vj[3]), vdev[1], m, b),
                copy(view(vj[2]), view(vj[2]), vdev[1], m, c),
            ]
            inner_sent.append(copy(four, four, vdev[1], m, a))

            @pl.when(inner)
            def _():
                across.start()

        def step(self, n):
            @pl.when(inner)
            def _():
                self.got[(0, 2, 1)[n]].wait_recv()
                self.on[n].start()

        def collect(self):
            @pl.when(jnp.logical_not(inner))
            def _():
                arrived(self.got)

    class LineSum:
        def __init__(self, part, both, relay, summed):
            self.part, self.both, self.relay, self.summed = part, both, relay, summed
            a, b, c = in_slot(), in_slot(), in_slot()
            n, o = out_slot(), out_slot()
            self.into_slot = c
            self.first = [
                copy(part(vj[3]), relay.at[0], vdev[1], n, a),
                copy(part(vj[2]), relay.at[1], vdev[1], n, b),
            ]
            self.second = [copy(summed.at[k], both.at[1], vdev[2 + k], o, c) for k in range(2)]
            self.all = copy(both, both, vdev[1], o, c)
            outer_sent.append(copy(relay, relay, vdev[1], n, a))
            inner_sent.append(copy(summed, summed, vdev[1], o, a))

        def go(self, n):
            if n < 2:

                @pl.when(jnp.logical_not(inner))
                def _():
                    self.first[n].start()

            elif n == 2:
                m = ring_slot()
                direct = copy(self.part(vj[1]), self.both.at[0], vdev[1], m, self.into_slot)
                direct.start()
                ring.append((m, direct))

        def rest(self):
            for n in range(3):
                self.go(n)
            return self

        def step(self, n):
            @pl.when(inner)
            def _():
                self.first[n].wait_recv()
                mine_too = self.part(vj[2 + n])[...].astype(F32)
                self.summed[n] = (mine_too + self.relay[n].astype(F32)).astype(BF)
                self.second[n].start()

        def collect(self):
            self.all.wait_recv()

        def total(self):
            out = self.part(j)[...].astype(F32)
            return out + self.both[0].astype(F32) + self.both[1].astype(F32)

    class SquareSum:
        def __init__(self, part, got, relay, summed):
            self.part, self.got, self.relay, self.summed = part, got, relay, summed
            q = got.shape[-1] // 2
            self.at = [pl.ds(0, q), pl.ds(q, q)]
            a, self.into_slot = in_slot(), in_slot()
            n = ring_slot()
            for k in range(2):
                copy(self.half(ki[3], k), relay.at[k], kdev[1 + k], n, a).start()
            for k in range(2):
                copy(self.half(ki[1 + k], k), self.into(k, k), kdev[1 + k], n, self.into_slot).start()
            self.relayed = copy(relay, relay, kdev[1], n, a)
            ring.append((n, copy(got, got, kdev[1], n, a)))

        def half(self, target, n):
            return self.part(target, self.at[n])

        def into(self, n, h):
            return self.got.at[n, :, self.at[h]]

        def step(self):
            self.relayed.wait_recv()
            n = ring_slot()
            for k in range(2):
                own = self.half(ki[2 - k], k)[...].astype(F32)
                self.summed[k] = (own + self.relay[k].astype(F32)).astype(BF)
                copy(
                    self.summed.at[k], self.into(1 - k, k), kdev[2 - k], n, self.into_slot
                ).start()
            ring.append((n, copy(self.summed, self.summed, kdev[1], n, self.into_slot)))

        def collect(self):
            copy(self.got, self.got, kdev[1], 0, self.into_slot).wait_recv()

        def total(self):
            out = self.part(i, pl.ds(0, self.got.shape[-1]))[...].astype(F32)
            return out + self.got[0].astype(F32) + self.got[1].astype(F32)

    quarter = half // 2
    mine_parts = [
        pl.ds(pl.multiple_of(par * half + n * quarter, quarter), quarter) for n in range(2)
    ]

    class SquareGather:
        def __init__(self, view, many, whole=mine, parts=mine_parts, own=None, pass_on=True):
            self.view, self.many, self.whole, self.parts = view, many, whole, parts
            self.pass_on = pass_on
            own = view(i, whole) if own is None else own
            into = view(i, whole)
            self.near = Fan([(own, into, kdev[d]) for d in (1, 2)], many(2))

        def forward(self, sources):
            if not self.pass_on:
                return []
            views = [self.view(src, self.whole) for src in sources]
            return [Fan([(one, one, partner) for one in views], self.many(len(views)))]

        def step(self):
            self.near.wait_recv()
            views = [self.view(ki[1 + n], self.parts[n]) for n in range(2)]
            self.far = Fan([(views[n], views[n], kdev[2 - n]) for n in range(2)], self.many(1))
            return self.forward((ki[1], ki[2]))

        def collect(self):
            self.far.wait_recv()
            return self.forward((ki[3],))

    barrier = pltpu.get_barrier_semaphore()
    for dev in kdev[1:] + vdev[1:] + seqdev:
        pl.semaphore_signal(barrier, inc=1, device_id=dev, device_id_type=MESH)

    l_small = [load(dup, dup_v), load(dbi, dbi_v), load(ggn, ggn_v)]
    l_qk = [load(wq.at[j], qk_v.at[i, 0]), load(wk.at[j], qk_v.at[i, 1])]
    segment = pl.ds(pl.multiple_of(i * T, T), T)
    l_x = [load(tok.at[segment], x_v), load(ng, ng_v), load(ffg, ffg_v)]
    l_dd = load(dd, dd_v.at[pl.ds(0, 16)])
    l_v = load(wv.at[j], v_v.at[j])
    l_g = load(wg.at[j], g_v.at[j])
    l_c = load(cot.at[segment], c_v)
    l_f = [load(fg, f_v.at[0, i]), load(fu, f_v.at[1, i]), load(fd, f_v.at[2, i])]
    l_o = load(wo, o_v.at[i, j])
    l_xa = load(tok, x_all)
    l_ca = load(cot, c_all)

    pl.semaphore_wait(barrier, 6 + len(seqdev))

    here(l_qk)
    t_qk = Fan(
        [(qk_v.at[i, par], qk_v.at[i, par], kdev[d]) for d in DIRS], qk_v.at[pl.ds(0, 3), 0]
    )
    left = pl.ds(0, half)
    t_v = Fan(
        [(wv.at[vj[d], :, mine], v_v.at[j, :, mine], vdev[d]) for d in DIRS],
        v_v.at[pl.ds(0, 3), :, left],
    )
    dd_v[16:, :] = jnp.zeros((dd_v.shape[0] - 16, D), BF)
    here(l_small)
    head3 = lax.broadcasted_iota(jnp.int32, (16, W, 32), 1)
    head2 = lax.broadcasted_iota(jnp.int32, (W, 32), 0)
    sq_v[...] = jnp.zeros_like(sq_v)
    sq_v[0:16, 0:32] = jnp.sum(jnp.where(head3 == j, dup_v[...].astype(F32), 0.0), axis=1)
    sq_v[16:17, 0:32] = jnp.sum(
        jnp.where(head2 == j, dbi_v[...].astype(F32), 0.0), axis=0, keepdims=True
    )
    ext_v[i] = sq_v[...].T[:32].astype(BF)
    sq_v[...] = jnp.zeros_like(sq_v)
    sq_v[0:16, 0:64] = jnp.broadcast_to(ggn_v[...].astype(F32), (16, 64))
    gge_v[j] = sq_v[0:16].astype(BF)

    t_ext = Fan([(ext_v.at[i], ext_v.at[i], kdev[d]) for d in DIRS], ext_v.at[pl.ds(0, 3)])
    low = pl.ds(0, 32)
    high = pl.ds(32, 32)
    t_ob = Fan(
        [(wo.at[high, mine], o_v.at[i, j, high, mine], kdev[d]) for d in DIRS],
        o_v.at[pl.ds(0, 3), 0, high, mine],
    )
    weights = (fg, fu, fd)

    def gather_weight(n, rows_at):
        return SquareGather(
            lambda src, at: f_v.at[n, src, rows_at, at],
            lambda count: f_v.at[n, pl.ds(0, count), rows_at, mine],
            own=weights[n].at[rows_at, mine],
        )

    cut = FB // 32 * 16
    top = pl.ds(0, cut)
    bottom = pl.ds(cut, FB - cut)
    every = pl.ds(0, FB)
    t_fd = gather_weight(2, every)
    l_o.wait()
    t_oa = LineGather(lambda src: o_v.at[i, src, low, mine], o_v.at[0, :, low, mine])
    t_g = Fan(
        [(wg.at[vj[d], :, mine], g_v.at[j, :, mine], vdev[d]) for d in DIRS],
        g_v.at[pl.ds(0, 3), :, left],
    )
    t_gge = Fan([(gge_v.at[j], gge_v.at[j], vdev[d]) for d in DIRS], gge_v.at[pl.ds(0, 3)])

    here(l_x)
    x = x_v[...].astype(F32)
    g1 = flat_row(ng_v[...].astype(F32))
    g3 = flat_row(ffg_v[...].astype(F32))
    r1 = lax.rsqrt(jnp.sum(x * x, axis=1, keepdims=True) / D + EPS)
    n_v[...] = (x * r1 * g1).astype(BF)
    l_dd.wait()
    lane = lax.broadcasted_iota(jnp.int32, (T, 128), 1)
    lrp = jnp.where(lane == 16, 1.0, nt(n_v[...], dd_v[...]))

    t_qk.wait_recv()
    views = [qk_v.at[ki[d], par] for d in DIRS]
    f_qk = Fan([(one, one, partner) for one in views], qk_v.at[pl.ds(0, 3), 0])
    t_fg = [gather_weight(0, top)]
    f_qk.wait_recv()
    t_ext.wait_recv()
    normed = n_v[...]
    wq_all = qk_v[:, 0].reshape(W * 32, D)
    wk_all = qk_v[:, 1].reshape(W * 32, D)
    ext_all = ext_v[...].reshape(W * 32, 128)
    scale = 128.0 ** (-0.5)
    q = nt(normed, wq_all) * scale
    k = nt(normed, wk_all)
    arg = nt(lrp, ext_all.astype(F32), HIGH)
    rates = (jnp.minimum(arg, 0.0) - jnp.log1p(jnp.exp(-jnp.abs(arg)))) / 16.0
    row_id = lax.broadcasted_iota(jnp.int32, (CB, CB), 0)
    col_id = lax.broadcasted_iota(jnp.int32, (CB, CB), 1)
    causal = row_id >= col_id
    tri = jnp.where(causal, 1.0, 0.0)
    nblk = T // CB
    blk = [slice(c * CB, (c + 1) * CB) for c in range(nblk)]
    e1, e2, em, el, dec, qd, kd, qi, ke, score = [], [], [], [], [], [], [], [], [], []
    for c in range(nblk):
        cum = nn(tri, rates[blk[c]], HIGH)
        mid = cum[CB // 2 - 1 : CB // 2]
        last = cum[CB - 1 : CB]
        e1.append(jnp.exp(cum - mid))
        e2.append(jnp.exp(mid - cum))
        em.append(jnp.exp(mid))
        el.append(jnp.exp(last - mid))
        dec.append(jnp.exp(last))
        a = q[blk[c]] * e1[c]
        b = k[blk[c]] * e2[c]
        qd.append(a.astype(BF))
        kd.append(b.astype(BF))
        qi.append((a * em[c]).astype(BF))
        ke.append((b * el[c]).astype(BF))
        score.append(jnp.where(causal, nt(qd[c], kd[c]), 0.0).astype(BF))

    l_v.wait()
    t_v.wait_recv()
    views = [v_v.at[vj[d], :, mine] for d in DIRS]
    f_vv = Fan([(one, one, partner) for one in views], v_v.at[pl.ds(0, 3), :, left])
    f_vv.wait_recv()
    wv_all = v_v[...].reshape(W * 64, D)
    v = nt(normed, wv_all).astype(BF)
    up = [tn(v[blk[c]], ke[c]) for c in range(nblk)]
    loc = up[0]
    locd = dec[0]
    for c in range(1, nblk):
        loc = loc * dec[c] + up[c]
        locd = locd * dec[c]
    VC = loc.shape[0]
    st_v[i, :VC] = loc.astype(BF)
    st_v[i, VC:] = jnp.broadcast_to(locd, (16, 128)).astype(BF)
    t_st = Fan([(st_v.at[i], st_v.at[i], kdev[d]) for d in DIRS], st_v.at[pl.ds(0, 3)])
    t_fg.append(gather_weight(0, bottom))
    t_fu = gather_weight(1, every)
    t_oa.step(0)
    t_oa.step(1)
    mixed = [nn(score[c], v[blk[c]]) for c in range(nblk)]

    t_ob.wait_recv()
    views = [o_v.at[ki[d], j, high, mine] for d in DIRS]
    f_o = [Fan([(one, one, partner) for one in views], o_v.at[pl.ds(0, 3), 0, high, mine])]
    t_ob2 = LineGather(lambda src: o_v.at[:, src, high, mine], o_v.at[:, :, high, mine])
    here(l_f)
    f_f = t_fd.step()
    t_oa.step(2)

    def gather_states(slots, totals, back):
        order = range(W - 1, -1, -1) if back else range(W)
        pre_s = jnp.zeros((VC, 128), F32)
        pre_d = jnp.ones((1, 128), F32)
        tot_s = jnp.zeros((VC, 128), F32)
        tot_d = jnp.ones((1, 128), F32)
        for other_i in order:
            one_s = slots[other_i, :VC].astype(F32)
            one_d = slots[other_i, VC : VC + 1].astype(F32)
            use = (other_i > i) if back else (other_i < i)
            pre_s = jnp.where(use, pre_s * one_d + one_s, pre_s)
            pre_d = jnp.where(use, pre_d * one_d, pre_d)
            tot_s = tot_s * one_d + one_s
            tot_d = tot_d * one_d
        totals[s, :VC] = tot_s.astype(BF)
        totals[s, VC:] = jnp.broadcast_to(tot_d, (16, 128)).astype(BF)
        return pre_s, pre_d, [send(totals.at[s], totals.at[s], dev) for dev in seqdev]

    def entering(totals, back, pre_s, pre_d, moves):
        arrived(moves)
        order = range(n_seq - 1, -1, -1) if back else range(n_seq)
        far = jnp.zeros((VC, 128), F32)
        for other_s in order:
            one_s = totals[other_s, :VC].astype(F32)
            one_d = totals[other_s, VC : VC + 1].astype(F32)
            use = (other_s > s) if back else (other_s < s)
            far = jnp.where(use, far * one_d + one_s, far)
        return pre_s + pre_d * far

    t_st.wait_recv()
    states = gather_states(st_v, tt_v, False)

    l_g.wait()
    t_g.wait_recv()
    views = [g_v.at[vj[d], :, mine] for d in DIRS]
    f_g = Fan([(one, one, partner) for one in views], g_v.at[pl.ds(0, 3), :, left])
    t_ob2.step(0)
    t_ob2.step(1)
    start = [entering(tt_v, False, *states)]
    for c in range(nblk):
        start.append(start[c] * dec[c] + up[c])
    start_low = [a.astype(BF) for a in start]
    for c in range(nblk):
        mixed[c] = mixed[c] + nt(qi[c], start_low[c])
    mix = jnp.concatenate(mixed, axis=0)
    r2 = lax.rsqrt(jnp.sum(mix * mix, axis=1, keepdims=True) / VC + EPS)
    normal = mix * r2
    f_g.wait_recv()
    t_gge.wait_recv()
    wg_all = g_v[...].reshape(W * 64, D)
    gate = nt(normed, wg_all)
    gg = jnp.concatenate([gge_v[h].astype(F32)[0:1, 0:64] for h in range(W)], axis=1)
    sig = 1.0 / (1.0 + jnp.exp(-gate))
    act = gate * sig
    act_v[0] = act
    act_v[1] = sig + act * (1.0 - sig)
    ga_v[j] = (normal * gg * act).astype(BF)
    act_v[2] = normal
    halves = [pl.ds(n * T // 2, T // 2) for n in range(2)]
    t_ga = [LineGather(lambda src, at=at: ga_v.at[src, at], ga_v.at[:, at]) for at in halves]

    t_oa.collect()
    views = [o_v.at[i, vj[d], low, mine] for d in DIRS]
    f_o.append(Fan([(one, one, partner) for one in views], o_v.at[0, pl.ds(0, 3), low, mine]))
    t_oa2 = SquareGather(
        lambda src, at: o_v.at[src, :, low, at], lambda count: o_v.at[pl.ds(0, count), :, low, mine]
    )

    here([l_xa, l_ca])
    for part in range(rows // T):
        at = pl.ds(part * T, T)
        xa = x_all[at, :].astype(F32)
        ra = lax.rsqrt(jnp.sum(xa * xa, axis=1, keepdims=True) / D + EPS)
        n_all[at, :] = (xa * ra * g1).astype(BF)
    xr_v[...] = (x * (r1 * r1 * r1)).astype(BF).T
    low_all = jnp.where(
        lax.broadcasted_iota(jnp.int32, (rows, 128), 1) == 16, 1.0, nt(n_all[...], dd_v[...])
    )
    lall_v[...] = low_all.astype(BF)
    for line in t_fg:
        f_f += line.step()
    t_ob2.step(2)
    t_ga[0].step(0)
    t_ga[0].step(1)
    t_ga[1].step(0)
    t_ga[1].step(1)
    f_f += t_fu.step()
    t_ga[0].step(2)
    t_ga[1].step(2)
    f_o += t_oa2.step()
    t_ob2.collect()
    views = [o_v.at[:, vj[d], high, mine] for d in DIRS]
    f_o.append(Fan([(one, one, partner) for one in views], o_v.at[:, pl.ds(0, 3), high, mine]))
    f_f += t_fd.collect()
    l_c.wait()
    arrived(f_f)
    dn = f_v[2].reshape(W * FB, D)
    gh_v[...] = nt(c_v[...], dn)
    f_f = t_fg[0].collect() + t_fg[1].collect()
    f_f += t_fu.collect()
    f_far = t_oa2.collect()
    for line in t_ga:
        line.collect()
    arrived(f_o)


    def attention(head):
        return nn(ga_v[head], o_v[head].reshape(W * 64, D))

    att = attention(i) + attention(ki[1]) + attention(ki[2])
    p_v[...] = att
    arrived(f_far)
    arrived(f_f)
    gT = f_v[0].reshape(W * FB, D)
    uT = f_v[1].reshape(W * FB, D)
    att = p_v[...] + attention(ki[3])
    resid = x_v[...].astype(F32) + att
    r3 = lax.rsqrt(jnp.sum(resid * resid, axis=1, keepdims=True) / D + EPS)
    fin = (resid * r3 * g3).astype(BF)
    gval = nt(fin, gT)
    uval = nt(fin, uT)
    fsig = 1.0 / (1.0 + jnp.exp(-gval))
    fact = gval * fsig
    hid = (fact * uval).astype(BF)
    gh = gh_v[...]
    gup = (gh * fact).astype(BF)
    ggate = (gh * uval * (fsig + fact * (1.0 - fsig))).astype(BF)
    hd[...] = hid.T.reshape(W, FB, T)
    t_hd = Fan([(hd.at[ki[d]], hseg.at[i], kdev[d]) for d in DIRS], hseg.at[pl.ds(0, 3)])
    hseg[i] = hd[i]
    part = nn(ggate, gT) + nn(gup, uT)
    p_v[...] = part
    sst[...] = as_row(jnp.sum(resid * g3 * part, axis=1, keepdims=True))
    t_m3 = Fan([(sst, rst.at[d], vdev[d]) for d in DIRS], rst.at[pl.ds(1, 3)])
    part_low = (part * g3).astype(BF)
    t_gg = [
        LineSum(
            lambda to, at=at: sgg.at[to, at],
            rgg.at[pl.ds(0, 2), at],
            rgg.at[pl.ds(2, 2), at],
            cgg.at[:, at],
        )
        for at in halves
    ]
    ggp = nt(part_low, o_v[...].reshape(W * W * 64, D))
    for h in range(W):
        sgg[h] = ggp[:, h * VC : (h + 1) * VC].astype(BF)
    for n in range(3):
        for line in t_gg:
            line.go(n)

    def weight_part(n, grad):
        gw[n] = tn(grad, fin).astype(BF).reshape(W, FB, D)
        return send(gw.at[n, :, :, other], pre.at[n], partner)

    def settle(n, move):
        move.wait_recv()
        pres[n] = (gw[n, :, :, mine].astype(F32) + pre[n].astype(F32)).astype(BF)

    def square(n, rows_at):
        return SquareSum(
            lambda to, at: pres.at[n, to, rows_at, at],
            rfw.at[n, :, rows_at],
            qfw.at[n, :, rows_at],
            cfw.at[n, :, rows_at],
        )

    t_pre0 = weight_part(0, ggate)
    t_pre1 = weight_part(1, gup)

    feature = lax.broadcasted_iota(jnp.int32, (1, D), 1)
    own_slab = jnp.where(lax.rem(feature // 64, W) == j, 1.0, 0.0)
    own_run = jnp.where(feature // (D // W) == j, 1.0, 0.0)
    so[...] = (nn(hid, dn) + own_slab * resid).astype(BF).T.reshape(W, W, 64, T)
    t_out = LineSum(lambda to: so.at[:, to], ro.at[pl.ds(0, 2)], ro.at[pl.ds(2, 2)], co).rest()
    ffn_gain = jnp.sum(part * resid * r3, axis=0, keepdims=True)
    settle(0, t_pre0)
    t_fw0 = square(0, every)
    t_gg[0].step(0)
    t_m3.wait_recv()
    m3 = as_column(sst[...] + rst[1] + rst[2] + rst[3]) / D
    base = c_v[...].astype(F32) - resid * (r3 * r3 * r3 * m3)
    t_gg[0].step(1)
    direct = nt(base.astype(BF), o_v[j].reshape(W * 64, D))
    full = p_v[...] * (g3 * r3)
    mixed_in = (full + own_run * base).astype(BF)
    for h in range(W):
        gow[h] = tn(ga_v[h], mixed_in).astype(BF)
    t_po = send(gow.at[:, :, other], preo, partner)
    t_gg[1].step(0)
    t_fw0.step()
    settle(1, t_pre1)
    t_fw1 = [square(1, top)]
    t_gg[1].step(1)
    t_po.wait_recv()
    preso[...] = (gow[:, :, mine].astype(F32) + preo[...].astype(F32)).astype(BF)
    for line in t_gg:
        line.collect()

    ggs = jnp.concatenate([line.total() for line in t_gg], axis=0)
    ggrad = direct + r3 * ggs
    act = act_v[0]
    normal = act_v[2]
    dgate = (ggrad * normal * gg * act_v[1]).astype(BF)
    gs = ggrad * act
    group = jnp.sum(gs * normal, axis=0, keepdims=True)
    group_rows = [
        jnp.concatenate(
            [group[:, h * 64 : (h + 1) * 64], jnp.zeros((1, T - 64), F32)], axis=1
        )
        for h in range(W)
    ]
    gnm = gs * gg
    gmix = (r2 * (gnm - normal * (jnp.sum(normal * gnm, axis=1, keepdims=True) / VC))).astype(BF)

    qst = [tn(gmix[blk[c]], qi[c]) for c in range(nblk)]
    bloc = qst[nblk - 1]
    for c in range(nblk - 2, -1, -1):
        bloc = bloc * dec[c] + qst[c]
    bst_v[i, :VC] = bloc.astype(BF)
    bst_v[i, VC:] = jnp.broadcast_to(locd, (16, 128)).astype(BF)
    t_bst = Fan([(bst_v.at[i], bst_v.at[i], kdev[d]) for d in DIRS], bst_v.at[pl.ds(0, 3)])
    t_ow = SquareSum(lambda to, at: preso.at[to, :, at], rowk, qow, cow)
    t_fw1.append(square(1, bottom))
    vz[1] = dgate.T.reshape(W, 64, T)
    t_gz = Fan([(vz.at[1, vj[d]], zvg.at[1, j], vdev[d]) for d in DIRS], zvg.at[1, pl.ds(0, 3)])
    dq_all, dk_in, dv_in = [], [], []
    for c in range(nblk):
        ds = jnp.where(causal, nt(gmix[blk[c]], v[blk[c]]), 0.0).astype(BF)
        dq_all.append(e1[c] * (nn(ds, kd[c]) + em[c] * nn(gmix[blk[c]], start_low[c])))
        dk_in.append(tn(ds, qd[c]))
        dv_in.append(tn(score[c], gmix[blk[c]]))
    ql = jnp.concatenate([(dq * scale).astype(BF) for dq in dq_all], axis=0)
    known = nn(dgate, wg_all) + nn(ql, wq_all)
    rest_in = full + own_slab * base
    t_out.step(0)
    t_hd.wait_recv()
    dsum[0] = nn(lanes(hseg[...]), c_all[...]).astype(BF)
    t_ds = send(dsum.at[0], dsum.at[1], partner)
    t_fw1[0].step()
    t_bst.wait_recv()
    after = [None] * nblk
    states = gather_states(bst_v, btt_v, True)
    t_out.step(1)
    after[nblk - 1] = entering(btt_v, True, *states)
    for c in range(nblk - 2, -1, -1):
        after[c] = after[c + 1] * dec[c + 1] + qst[c + 1]

    kl, vl, ga = [], [], []
    for c in range(nblk):
        low_after = after[c].astype(BF)
        dk = e2[c] * (dk_in[c] + el[c] * nn(v[blk[c]], low_after))
        dv = dv_in[c] + nt(ke[c], low_after)
        gc = q[blk[c]] * dq_all[c] - k[blk[c]] * dk
        extra = jnp.sum(after[c] * start[c + 1], axis=0, keepdims=True)
        gc = jnp.where(row_id == CB - 1, gc + extra, gc)
        gr = tn(tri, gc, HIGH)
        ga.append(gr / (1.0 + jnp.exp(arg[blk[c]])) / 16.0)
        kl.append(dk.astype(BF))
        vl.append(dv.astype(BF))
    kl = jnp.concatenate(kl, axis=0)
    vl = jnp.concatenate(vl, axis=0)
    ga = jnp.concatenate(ga, axis=0).astype(BF)
    glr = nn(ga, ext_all).astype(BF)
    gn = known + nn(kl, wk_all) + nn(vl, wv_all) + nn(glr, dd_v[...])
    whole = gn * (r1 * g1) + rest_in
    sgn[...] = whole.astype(BF).T.reshape(W, W, 64, T)
    pairs = [pl.ds(n * W // 2, W // 2) for n in range(2)]
    t_gn = [
        LineSum(
            lambda to, at=at: sgn.at[at, to],
            rgn.at[pl.ds(0, 2), at],
            rgn.at[pl.ds(2, 2), at],
            cgn.at[:, at],
        )
        for at in pairs
    ]
    for n in range(3):
        for line in t_gn:
            line.go(n)
    vz[0] = vl.T.reshape(W, 64, T)
    t_vz = Fan([(vz.at[0, vj[d]], zvg.at[0, j], vdev[d]) for d in DIRS], zvg.at[0, pl.ds(0, 3)])

    gnx = gn * x_v[...].astype(F32)
    norm_gain = jnp.sum(gnx * r1, axis=0, keepdims=True)
    m1p = as_row(jnp.sum(gnx * g1, axis=1, keepdims=True))[:1]
    rank_row = lax.broadcasted_iota(jnp.int32, (16, 128), 0)
    rank_col = lax.broadcasted_iota(jnp.int32, (16, 128), 1)
    by_owner = jnp.where(rank_col == lax.rem(rank_row, W) * W + rank_row // W, 1.0, 0.0)
    small = nn(by_owner.astype(BF), tn(glr, normed).astype(BF))
    slab = D // (W * W)
    rid = lax.broadcasted_iota(jnp.int32, (16, T), 0)
    for h in range(W):
        ranks = small[h * W : (h + 1) * W]
        sm0[h, 0:16] = jnp.concatenate(
            [ranks[:, n * T : (n + 1) * T] for n in range(W)], axis=0
        ).astype(BF)

        def slabs(row):
            return jnp.concatenate(
                [row[:, (W * n + h) * slab : (W * n + h + 1) * slab] for n in range(W)], axis=1
            )

        rest = jnp.where(rid == 0, slabs(norm_gain), 0.0)
        rest = jnp.where(rid == 1, slabs(ffn_gain), rest)
        rest = jnp.where(rid == 2, group_rows[h], rest)
        rest = jnp.where(rid == 3, m1p, rest)
        sm0[h, 16:32] = rest.astype(BF)
    t_s0 = Fan([(sm0.at[vj[d]], sm1.at[d], vdev[d]) for d in DIRS], sm1.at[pl.ds(1, 3)])


    def finish_square(n, lines):
        for line, rows_at in lines:
            line.collect()
            fin_f[par, n, rows_at] = line.total().astype(BF)
        return send(fin_f.at[par, n], fin_f.at[par, n], partner)

    t_ff = [finish_square(0, [(t_fw0, every)])]
    t_ow.step()
    t_fw1[1].step()
    qka[:, 0] = ql.T.reshape(W, 32, T)
    qka[:, 1] = kl.T.reshape(W, 32, T)
    qka[:, 2] = ga.T.reshape(W, 32, T)
    t_qa = Fan([(qka.at[ki[d]], kqa.at[i], kdev[d]) for d in DIRS], kqa.at[pl.ds(0, 3)])
    t_gz.wait_recv()
    zvg[1, j] = vz[1, j]
    t_gk = Fan([(zvg.at[1, ki[d]], kvg.at[1, i], kdev[d]) for d in DIRS], kvg.at[1, pl.ds(0, 3)])
    kvg[1, i] = zvg[1, i]

    t_out.collect()
    ao[...] = t_out.total().astype(BF)
    t_ao = Fan([(ao.at[ki[d]], oseg.at[i], kdev[d]) for d in DIRS], oseg.at[pl.ds(0, 3)])
    oseg[i] = ao[i]

    t_gn[0].step(0)
    t_gn[1].step(0)
    t_gn[0].step(1)
    t_gn[1].step(1)

    t_ow.collect()
    mid_o[...] = t_ow.total().astype(BF).reshape(W, 64, half)
    t_oz = LineSum(
        lambda to: mid_o.at[to], rowz.at[pl.ds(0, 2)], rowz.at[pl.ds(2, 2)], coz
    ).rest()

    t_qa.wait_recv()
    kqa[i] = qka[i]
    nall = n_all[...]
    for n in range(2):
        qksum[0, n] = nn(lanes(kqa[:, n]), nall).astype(BF)
    esum[0] = nn(lanes(kqa[:, 2]), lall_v[...])
    t_qs = send(qksum.at[0], qksum.at[1], partner)
    t_es = send(esum.at[0], esum.at[1], partner)
    for line in t_gn:
        line.collect()
    t_vz.wait_recv()
    zvg[0, j] = vz[0, j]
    t_vk = Fan([(zvg.at[0, ki[d]], kvg.at[0, i], kdev[d]) for d in DIRS], kvg.at[0, pl.ds(0, 3)])
    kvg[0, i] = zvg[0, i]
    t_s0.wait_recv()
    sm2[0] = total(sm0[j], sm1).astype(BF)
    m1 = (
        sm0[0, 19:20].astype(F32)
        + sm1[1, 19:20].astype(F32)
        + sm1[2, 19:20].astype(F32)
        + sm1[3, 19:20].astype(F32)
    ) / D

    summed = jnp.concatenate([line.total() for line in t_gn], axis=0)
    for h in range(W):
        at = pl.ds(pl.multiple_of((h * W + j) * 64, 64), 64)
        ai[h] = (summed[h] - xr_v[at, :].astype(F32) * m1).astype(BF)
    t_ai = Fan([(ai.at[ki[d]], iseg.at[i], kdev[d]) for d in DIRS], iseg.at[pl.ds(0, 3)])
    iseg[i] = ai[i]

    t_s1 = Fan([(sm2.at[0], sm2.at[d], kdev[d]) for d in DIRS], sm2.at[pl.ds(1, 3)])
    t_ff.append(finish_square(1, list(zip(t_fw1, (top, bottom)))))

    t_gk.wait_recv()
    vgsum[0, 1] = nn(lanes(kvg[1]), nall).astype(BF)
    t_vs = [send(vgsum.at[0, 1], vgsum.at[1, 1], partner)]

    t_oz.step(0)
    t_oz.step(1)

    t_vk.wait_recv()
    vgsum[0, 0] = nn(lanes(kvg[0]), nall).astype(BF)
    t_vs.append(send(vgsum.at[0, 0], vgsum.at[1, 0], partner))
    t_s1.wait_recv()
    sm3[0] = total(sm2[0], sm2).astype(BF)
    t_s2 = send(sm3.at[0], sm3.at[1], partner)

    t_ds.wait_recv()
    r_fd[...] = dsum[0].astype(F32) + dsum[1].astype(F32)
    t_ao.wait_recv()
    r_out[...] = lanes(oseg[...])
    t_qs.wait_recv()
    r_q[...] = qksum[0, 0].astype(F32) + qksum[1, 0].astype(F32)
    r_k[...] = qksum[0, 1].astype(F32) + qksum[1, 1].astype(F32)
    t_es.wait_recv()
    decay = (esum[0] + esum[1]).T
    r_du[...] = decay[0:16, :].reshape(16, 1, 32)
    r_db[...] = decay[16:17, :]
    t_ff[0].wait_recv()
    for h in range(2):
        r_fg[:, h * half : (h + 1) * half] = fin_f[h, 0].astype(F32)
    t_oz.collect()
    fin_ow[par] = t_oz.total().astype(BF)
    t_fo = send(fin_ow.at[par], fin_ow.at[par], partner)
    t_ff[1].wait_recv()
    for h in range(2):
        r_fu[:, h * half : (h + 1) * half] = fin_f[h, 1].astype(F32)
    arrived(t_vs)
    r_v[...] = vgsum[0, 0].astype(F32) + vgsum[1, 0].astype(F32)
    r_g[...] = vgsum[0, 1].astype(F32) + vgsum[1, 1].astype(F32)
    t_s2.wait_recv()
    tot = sm3[0].astype(F32) + sm3[1].astype(F32)
    own_ranks, own_slabs = [], jnp.zeros((2, slab), F32)
    for n in range(W):
        own_ranks.append(jnp.zeros((1, T), F32))
        for h in range(W):
            row = tot[n * W + h : n * W + h + 1]
            own_ranks[n] = jnp.where(i == h, row, own_ranks[n])
        own_slabs = jnp.where(i == n, tot[16:18, n * slab : (n + 1) * slab], own_slabs)
    r_dd[...] = jnp.concatenate(own_ranks, axis=1)
    r_ng[...] = own_slabs[0:1]
    r_fn[...] = own_slabs[1:2]
    r_gg[...] = tot[18:19, 0:64]
    t_ai.wait_recv()
    r_in[...] = lanes(iseg[...])
    t_fo.wait_recv()
    for h in range(2):
        r_o[:, h * half : (h + 1) * half] = fin_ow[h].astype(F32)
    for _, cp in ring:
        cp.wait_send()

    @pl.when(inner)
    def _():
        for cp in inner_sent:
            cp.wait_send()

    @pl.when(jnp.logical_not(inner))
    def _():
        for cp in outer_sent:
            cp.wait_send()


N_OUT = 44
N_IN = 93
N_LOCAL = 18


def layer(n_seq, args):
    rows, D = args[0].shape
    W = WAYS
    T = rows // W
    FB = args[-1].shape[0]
    VC = W * 64
    half = D // 2

    def sds(shape, dtype=F32):
        return pltpu.VMEM(shape, dtype)

    def vm(shape, dtype=BF):
        return pltpu.VMEM(shape, dtype)

    slab = D // (W * W)
    outs = [
        sds((64, rows), BF),
        sds((64, rows), BF),
        sds((1, slab)),
        sds((32, D)),
        sds((32, D)),
        sds((64, D)),
        sds((64, D)),
        sds((1, D)),
        sds((16, 1, 32)),
        sds((1, 32)),
        sds((1, 64)),
        sds((64, D)),
        sds((1, slab)),
        sds((FB, D)),
        sds((FB, D)),
        sds((FB, D)),
    ]
    scratch = [
        vm((T, D)),
        vm((T, D)),
        vm((rows, D)),
        vm((rows, D)),
        vm((rows, D)),
        vm((T, D)),
        vm((D, T)),
        vm((128, D)),
        vm((8, 128)),
        vm((8, 128)),
        vm((16, W, 32)),
        vm((W, 32)),
        vm((1, 64)),
        vm((128, 128), F32),
        vm((8, D), F32),
        vm((W, 2, 32, D)),
        vm((W, 32, 128)),
        vm((W, 64, D)),
        vm((W, 64, D)),
        vm((W, 16, 128)),
        vm((W, W, 64, D)),
        vm((3, W, FB, D)),
        vm((W, VC + 16, 128)),
        vm((n_seq, VC + 16, 128)),
        vm((W, VC + 16, 128)),
        vm((n_seq, VC + 16, 128)),
        vm((W, T, VC)),
        vm((W, T, VC)),
        vm((W, T, VC)),
        vm((2, T, VC)),
        vm((8, T), F32),
        vm((W, 8, T), F32),
        vm((W, W, 64, T)),
        vm((W, W, 64, T)),
        vm((2, W, 64, T)),
        vm((W, W, 64, T)),
        vm((W, W, 64, T)),
        vm((2, W, 64, T)),
        vm((W, 64, T)),
        vm((W, 64, T)),
        vm((W, 64, T)),
        vm((W, 64, T)),
        vm((W, FB, T)),
        vm((W, FB, T)),
        vm((2, W, FB, D)),
        vm((2, W, FB, half)),
        vm((2, W, FB, half)),
        vm((2, 2, FB, half)),
        vm((2, 2, FB, half // 2)),
        vm((2, 2, FB, half // 2)),
        vm((2, 2, FB, half)),
        vm((2, FB, D)),
        vm((W, VC, D)),
        vm((W, VC, half)),
        vm((W, VC, half)),
        vm((2, VC, half)),
        vm((2, VC, half // 2)),
        vm((2, VC, half // 2)),
        vm((W, 64, half)),
        vm((W, 64, half)),
        vm((2, 64, half)),
        vm((2, 64, half)),
        vm((2, W, 64, T)),
        vm((2, W, 64, T)),
        vm((2, W, 64, T)),
        vm((2, 2, 64, D)),
        vm((W, 3, 32, T)),
        vm((W, 3, 32, T)),
        vm((2, 2, 32, D)),
        vm((2, 32, 128), F32),
        vm((W, 32, T)),
        vm((W, 32, T)),
        vm((W, 32, T)),
        vm((2, 32, T)),
        vm((rows, 128)),
        vm((T, W * FB), F32),
        vm((3, T, VC), F32),
        vm((T, D), F32),
        pltpu.SemaphoreType.DMA((N_OUT,)),
        pltpu.SemaphoreType.DMA((N_IN + 2 * n_seq,)),
        pltpu.SemaphoreType.DMA((N_LOCAL,)),
    ]
    return pl.pallas_call(
        functools.partial(layer_kernel, n_seq),
        out_shape=outs,
        in_specs=[pl.BlockSpec(memory_space=pl.ANY)] * len(args),
        out_specs=[pl.BlockSpec(memory_space=pltpu.VMEM)] * len(outs),
        scratch_shapes=scratch,
        compiler_params=pltpu.CompilerParams(
            collective_id=0, has_side_effects=True, vmem_limit_bytes=60 * 2**20
        ),
        name="layer",
    )(*args)


def finish_kernel(*refs):
    n = len(refs) // 2
    sem = refs[-1]
    copies = [pltpu.make_async_copy(refs[k], refs[n + k], sem.at[k]) for k in range(n)]
    for cp in copies:
        cp.start()
    for cp in copies:
        cp.wait()


def finish(parts):
    return pl.pallas_call(
        finish_kernel,
        out_shape=[jax.ShapeDtypeStruct(p.shape, p.dtype) for p in parts],
        in_specs=[pl.BlockSpec(memory_space=pltpu.VMEM)] * len(parts),
        out_specs=[pl.BlockSpec(memory_space=pl.ANY)] * len(parts),
        scratch_shapes=[pltpu.SemaphoreType.DMA((len(parts),))],
        compiler_params=pltpu.CompilerParams(vmem_limit_bytes=16 * 2**20),
        name="finish",
    )(*parts)


def shards(
    n_seq,
    tokens,
    norm_gain,
    query_weight,
    key_weight,
    value_weight,
    gate_weight,
    decay_down,
    decay_up,
    decay_bias,
    group_gain,
    out_weight,
    ffn_gain,
    ffn_gate,
    ffn_up,
    ffn_down,
    cotangent,
):
    parts = layer(
        n_seq,
        (
            tokens,
            cotangent,
            norm_gain.reshape(8, -1),
            ffn_gain.reshape(8, -1),
            decay_up,
            decay_bias,
            group_gain[None],
            query_weight.transpose(1, 2, 0),
            key_weight.transpose(1, 2, 0),
            value_weight.transpose(1, 2, 0),
            gate_weight.transpose(1, 2, 0),
            decay_down.T,
            out_weight[0],
            ffn_gate.T,
            ffn_up.T,
            ffn_down,
        ),
    )
    if n_seq > 2:

        def over_pairs(a):
            return jnp.sum(lax.all_gather(a, "seq")[::2].astype(F32), axis=0).astype(a.dtype)

        parts = list(parts[:2]) + [over_pairs(a) for a in parts[2:]]
    (r_out, r_in, r_ng, r_q, r_k, r_v, r_g, r_dd, r_du, r_db, r_gg, r_o, r_fn, r_fg, r_fu, r_fd) = finish(parts)
    return (
        r_out.T,
        r_in.T,
        r_ng[0],
        r_q.T[:, None, :],
        r_k.T[:, None, :],
        r_v.T[:, None, :],
        r_g.T[:, None, :],
        r_dd.T,
        r_du,
        r_db,
        r_gg[0],
        r_o[None],
        r_fn[0],
        r_fg.T,
        r_fu.T,
        r_fd,
    )


def solution(mesh):
    in_specs = (
        P("seq", None),
        P(),
        P(None, None, "kax"),
        P(None, None, "kax"),
        P(None, None, "vax"),
        P(None, None, "vax"),
        P(),
        P(None, None, "kax"),
        P(None, "kax"),
        P("vax"),
        P("kax", "vax", None),
        P(),
        P(None, ("kax", "vax")),
        P(None, ("kax", "vax")),
        P(("kax", "vax"), None),
        P("seq", None),
    )
    out_specs = (
        P("seq", ("kax", "vax")),
        P("seq", ("kax", "vax")),
        P(("kax", "vax")),
        P(None, "vax", "kax"),
        P(None, "vax", "kax"),
        P(None, "kax", "vax"),
        P(None, "kax", "vax"),
        P(None, ("kax", "vax")),
        P(None, "vax", "kax"),
        P("vax", "kax"),
        P("vax"),
        P("kax", "vax", None),
        P(("kax", "vax")),
        P(None, ("kax", "vax")),
        P(None, ("kax", "vax")),
        P(("kax", "vax"), None),
    )
    return jax.shard_map(
        functools.partial(shards, mesh.shape["seq"]),
        mesh=mesh,
        in_specs=in_specs,
        out_specs=out_specs,
        check_vma=False,
    )
```

```python
import functools

import jax
import jax.numpy as jnp
from jax import lax
from jax.experimental import pallas as pl
from jax.experimental.pallas import tpu as pltpu
from jax.sharding import PartitionSpec as P

MESH = pl.DeviceIdType.MESH
BF = jnp.bfloat16
F32 = jnp.float32
CB = 128
WAYS = 4
EPS = 1e-06
HIGH = lax.Precision.HIGHEST


def nn(a, b, precision=None):
    return lax.dot_general(
        a, b, (((1,), (0,)), ((), ())), precision=precision, preferred_element_type=F32
    )


def nt(a, b, precision=None):
    return lax.dot_general(
        a, b, (((1,), (1,)), ((), ())), precision=precision, preferred_element_type=F32
    )


def tn(a, b, precision=None):
    return lax.dot_general(
        a, b, (((0,), (0,)), ((), ())), precision=precision, preferred_element_type=F32
    )


def xor(index, d):
    if d == 1:
        return index + 1 - 2 * lax.rem(index, 2)
    if d == 2:
        return lax.rem(index + 2, 4)
    return 3 - index


def as_row(column):
    return jnp.broadcast_to(column, (column.shape[0], 128)).T[:8]


def as_column(row):
    return jnp.broadcast_to(row[:1], (128, row.shape[1])).T[:, :1]


def flat_row(block):
    return jnp.concatenate([block[r : r + 1] for r in range(block.shape[0])], axis=1)


def lanes(block):
    return jnp.concatenate([block[n] for n in range(block.shape[0])], axis=1)


def total(own, got):
    out = own.astype(F32)
    for d in (1, 2, 3):
        out = out + got[d].astype(F32)
    return out


def layer_kernel(
    n_seq,
    tok,
    cot,
    ng,
    ffg,
    dup,
    dbi,
    ggn,
    wq,
    wk,
    wv,
    wg,
    dd,
    wo,
    fg,
    fu,
    fd,
    r_out,
    r_in,
    r_ng,
    r_q,
    r_k,
    r_v,
    r_g,
    r_dd,
    r_du,
    r_db,
    r_gg,
    r_o,
    r_fn,
    r_fg,
    r_fu,
    r_fd,
    x_v,
    c_v,
    x_all,
    c_all,
    n_all,
    n_v,
    xr_v,
    dd_v,
    ng_v,
    ffg_v,
    dup_v,
    dbi_v,
    ggn_v,
    sq_v,
    gain_v,
    qk_v,
    ext_v,
    v_v,
    g_v,
    gge_v,
    o_v,
    f_v,
    st_v,
    tt_v,
    bst_v,
    btt_v,
    ga_v,
    sgg,
    rgg,
    cgg,
    sst,
    rst,
    so,
    ro,
    co,
    sgn,
    rgn,
    cgn,
    ao,
    oseg,
    ai,
    iseg,
    hd,
    hseg,
    gw,
    pre,
    pres,
    rfw,
    qfw,
    cfw,
    fin_f,
    dsum,
    gow,
    preo,
    preso,
    rowk,
    qow,
    cow,
    mid_o,
    rowz,
    coz,
    fin_ow,
    vz,
    zvg,
    kvg,
    vgsum,
    qka,
    kqa,
    qksum,
    esum,
    sm0,
    sm1,
    sm2,
    sm3,
    lall_v,
    gh_v,
    act_v,
    p_v,
    ss,
    rs,
    ls,
):
    s = lax.axis_index("seq")
    i = lax.axis_index("kax")
    j = lax.axis_index("vax")
    par = lax.rem(s, 2)
    oth = 1 - par
    T, D = x_v.shape
    rows = x_all.shape[0]
    FB = f_v.shape[2]
    half = D // 2
    W = WAYS
    DIRS = (1, 2, 3)
    mine = pl.ds(pl.multiple_of(par * half, half), half)
    other = pl.ds(pl.multiple_of(oth * half, half), half)
    partner = {"seq": s + 1 - 2 * par}
    kdev = [None] + [{"kax": xor(i, d)} for d in DIRS]
    vdev = [None] + [{"vax": xor(j, d)} for d in DIRS]
    ki = [None] + [xor(i, d) for d in DIRS]
    vj = [None] + [xor(j, d) for d in DIRS]
    seqdev = [{"seq": lax.rem(s + e, n_seq)} for e in range(1, n_seq)]

    count = [0, 0, 0]
    inner_sent, outer_sent = [], []

    def slot(kind):
        count[kind] += 1
        return count[kind] - 1

    def out_slot():
        return slot(0)

    def in_slot():
        return slot(1)

    def copy(src, dst, dev, n, m):
        return pltpu.make_async_remote_copy(
            src_ref=src,
            dst_ref=dst,
            send_sem=ss.at[n],
            recv_sem=rs.at[m],
            device_id=dev,
            device_id_type=MESH,
        )

    ring = []

    def ring_slot():
        if len(ring) < 28:
            return out_slot()
        n, cp = ring.pop(0)
        cp.wait_send()
        return n

    def send(src, dst, dev):
        n = ring_slot()
        cp = copy(src, dst, dev, n, in_slot())
        cp.start()
        ring.append((n, cp))
        return cp

    def load(src, dst):
        cp = pltpu.make_async_copy(src, dst, ls.at[slot(2)])
        cp.start()
        return cp

    class Fan:
        def __init__(self, copies, size):
            n, m = ring_slot(), in_slot()
            for src, dst, dev in copies:
                copy(src, dst, dev, n, m).start()
            self.all = copy(size, size, partner, n, m)
            ring.append((n, self.all))

        def wait_recv(self):
            self.all.wait_recv()

    def arrived(copies):
        for cp in copies:
            cp.wait_recv()

    def here(copies):
        for cp in copies:
            cp.wait()

    inner = lax.rem(j + 1, W) >= 2

    class LineGather:
        def __init__(self, view, four):
            a, b, c = in_slot(), in_slot(), in_slot()
            n, m = ring_slot(), out_slot()
            near = copy(view(j), view(j), vdev[1], n, a)
            near.start()
            ring.append((n, near))
            across = copy(view(j), view(j), vdev[3], m, c)
            self.got = [
                copy(view(vj[d]), view(vj[d]), vdev[1], n, at) for d, at in zip(DIRS, (a, b, c))
            ]
            self.on = [
                copy(view(vj[1]), view(vj[1]), vdev[3], m, b),
                copy(view(vj[3]), view(vj[3]), vdev[1], m, b),
                copy(view(vj[2]), view(vj[2]), vdev[1], m, c),
            ]
            inner_sent.append(copy(four, four, vdev[1], m, a))

            @pl.when(inner)
            def _():
                across.start()

        def step(self, n):
            @pl.when(inner)
            def _():
                self.got[(0, 2, 1)[n]].wait_recv()
                self.on[n].start()

        def collect(self):
            @pl.when(jnp.logical_not(inner))
            def _():
                arrived(self.got)

    class LineSum:
        def __init__(self, part, both, relay, summed):
            self.part, self.both, self.relay, self.summed = part, both, relay, summed
            a, b, c = in_slot(), in_slot(), in_slot()
            n, o = out_slot(), out_slot()
            self.into_slot = c
            self.first = [
                copy(part(vj[3]), relay.at[0], vdev[1], n, a),
                copy(part(vj[2]), relay.at[1], vdev[1], n, b),
            ]
            self.second = [copy(summed.at[k], both.at[1], vdev[2 + k], o, c) for k in range(2)]
            self.all = copy(both, both, vdev[1], o, c)
            outer_sent.append(copy(relay, relay, vdev[1], n, a))
            inner_sent.append(copy(summed, summed, vdev[1], o, a))

        def go(self, n):
            if n < 2:

                @pl.when(jnp.logical_not(inner))
                def _():
                    self.first[n].start()

            elif n == 2:
                m = ring_slot()
                direct = copy(self.part(vj[1]), self.both.at[0], vdev[1], m, self.into_slot)
                direct.start()
                ring.append((m, direct))

        def rest(self):
            for n in range(3):
                self.go(n)
            return self

        def step(self, n):
            @pl.when(inner)
            def _():
                self.first[n].wait_recv()
                mine_too = self.part(vj[2 + n])[...].astype(F32)
                self.summed[n] = (mine_too + self.relay[n].astype(F32)).astype(BF)
                self.second[n].start()

        def collect(self):
            self.all.wait_recv()

        def total(self):
            out = self.part(j)[...].astype(F32)
            return out + self.both[0].astype(F32) + self.both[1].astype(F32)

    class SquareSum:
        def __init__(self, part, got, relay, summed):
            self.part, self.got, self.relay, self.summed = part, got, relay, summed
            q = got.shape[-1] // 2
            self.at = [pl.ds(0, q), pl.ds(q, q)]
            a, self.into_slot = in_slot(), in_slot()
            n = ring_slot()
            for k in range(2):
                copy(self.half(ki[3], k), relay.at[k], kdev[1 + k], n, a).start()
            for k in range(2):
                copy(self.half(ki[1 + k], k), self.into(k, k), kdev[1 + k], n, self.into_slot).start()
            self.relayed = copy(relay, relay, kdev[1], n, a)
            ring.append((n, copy(got, got, kdev[1], n, a)))

        def half(self, target, n):
            return self.part(target, self.at[n])

        def into(self, n, h):
            return self.got.at[n, :, self.at[h]]

        def step(self):
            self.relayed.wait_recv()
            n = ring_slot()
            for k in range(2):
                own = self.half(ki[2 - k], k)[...].astype(F32)
                self.summed[k] = (own + self.relay[k].astype(F32)).astype(BF)
                copy(
                    self.summed.at[k], self.into(1 - k, k), kdev[2 - k], n, self.into_slot
                ).start()
            ring.append((n, copy(self.summed, self.summed, kdev[1], n, self.into_slot)))

        def collect(self):
            copy(self.got, self.got, kdev[1], 0, self.into_slot).wait_recv()

        def total(self):
            out = self.part(i, pl.ds(0, self.got.shape[-1]))[...].astype(F32)
            return out + self.got[0].astype(F32) + self.got[1].astype(F32)

    quarter = half // 2
    mine_parts = [
        pl.ds(pl.multiple_of(par * half + n * quarter, quarter), quarter) for n in range(2)
    ]

    class SquareGather:
        def __init__(self, view, many, whole=mine, parts=mine_parts, own=None, pass_on=True):
            self.view, self.many, self.whole, self.parts = view, many, whole, parts
            self.pass_on = pass_on
            own = view(i, whole) if own is None else own
            into = view(i, whole)
            self.near = Fan([(own, into, kdev[d]) for d in (1, 2)], many(2))

        def forward(self, sources):
            if not self.pass_on:
                return []
            views = [self.view(src, self.whole) for src in sources]
            return [Fan([(one, one, partner) for one in views], self.many(len(views)))]

        def step(self):
            self.near.wait_recv()
            views = [self.view(ki[1 + n], self.parts[n]) for n in range(2)]
            self.far = Fan([(views[n], views[n], kdev[2 - n]) for n in range(2)], self.many(1))
            return self.forward((ki[1], ki[2]))

        def collect(self):
            self.far.wait_recv()
            return self.forward((ki[3],))

    barrier = pltpu.get_barrier_semaphore()
    for dev in kdev[1:] + vdev[1:] + seqdev:
        pl.semaphore_signal(barrier, inc=1, device_id=dev, device_id_type=MESH)

    l_small = [load(dup, dup_v), load(dbi, dbi_v), load(ggn, ggn_v)]
    l_qk = [load(wq.at[j], qk_v.at[i, 0]), load(wk.at[j], qk_v.at[i, 1])]
    segment = pl.ds(pl.multiple_of(i * T, T), T)
    l_x = [load(tok.at[segment], x_v), load(ng, ng_v), load(ffg, ffg_v)]
    l_dd = load(dd, dd_v.at[pl.ds(0, 16)])
    l_v = load(wv.at[j], v_v.at[j])
    l_g = load(wg.at[j], g_v.at[j])
    l_c = load(cot.at[segment], c_v)
    l_f = [load(fg, f_v.at[0, i]), load(fu, f_v.at[1, i]), load(fd, f_v.at[2, i])]
    l_o = load(wo, o_v.at[i, j])
    l_xa = load(tok, x_all)
    l_ca = load(cot, c_all)

    pl.semaphore_wait(barrier, 6 + len(seqdev))

    here(l_qk)
    t_qk = Fan(
        [(qk_v.at[i, par], qk_v.at[i, par], kdev[d]) for d in DIRS], qk_v.at[pl.ds(0, 3), 0]
    )
    left = pl.ds(0, half)
    t_v = Fan(
        [(wv.at[vj[d], :, mine], v_v.at[j, :, mine], vdev[d]) for d in DIRS],
        v_v.at[pl.ds(0, 3), :, left],
    )
    dd_v[16:, :] = jnp.zeros((dd_v.shape[0] - 16, D), BF)
    here(l_small)
    head3 = lax.broadcasted_iota(jnp.int32, (16, W, 32), 1)
    head2 = lax.broadcasted_iota(jnp.int32, (W, 32), 0)
    sq_v[...] = jnp.zeros_like(sq_v)
    sq_v[0:16, 0:32] = jnp.sum(jnp.where(head3 == j, dup_v[...].astype(F32), 0.0), axis=1)
    sq_v[16:17, 0:32] = jnp.sum(
        jnp.where(head2 == j, dbi_v[...].astype(F32), 0.0), axis=0, keepdims=True
    )
    ext_v[i] = sq_v[...].T[:32].astype(BF)
    sq_v[...] = jnp.zeros_like(sq_v)
    sq_v[0:16, 0:64] = jnp.broadcast_to(ggn_v[...].astype(F32), (16, 64))
    gge_v[j] = sq_v[0:16].astype(BF)

    t_ext = Fan([(ext_v.at[i], ext_v.at[i], kdev[d]) for d in DIRS], ext_v.at[pl.ds(0, 3)])
    low = pl.ds(0, 32)
    high = pl.ds(32, 32)
    t_ob = Fan(
        [(wo.at[high, mine], o_v.at[i, j, high, mine], kdev[d]) for d in DIRS],
        o_v.at[pl.ds(0, 3), 0, high, mine],
    )
    weights = (fg, fu, fd)

    def gather_weight(n, rows_at):
        return SquareGather(
            lambda src, at: f_v.at[n, src, rows_at, at],
            lambda count: f_v.at[n, pl.ds(0, count), rows_at, mine],
            own=weights[n].at[rows_at, mine],
        )

    cut = FB // 32 * 16
    top = pl.ds(0, cut)
    bottom = pl.ds(cut, FB - cut)
    every = pl.ds(0, FB)
    t_fd = gather_weight(2, every)
    l_o.wait()
    t_oa = LineGather(lambda src: o_v.at[i, src, low, mine], o_v.at[0, :, low, mine])
    t_g = Fan(
        [(wg.at[vj[d], :, mine], g_v.at[j, :, mine], vdev[d]) for d in DIRS],
        g_v.at[pl.ds(0, 3), :, left],
    )
    t_gge = Fan([(gge_v.at[j], gge_v.at[j], vdev[d]) for d in DIRS], gge_v.at[pl.ds(0, 3)])

    here(l_x)
    x = x_v[...].astype(F32)
    g1 = flat_row(ng_v[...].astype(F32))
    g3 = flat_row(ffg_v[...].astype(F32))
    r1 = lax.rsqrt(jnp.sum(x * x, axis=1, keepdims=True) / D + EPS)
    n_v[...] = (x * r1 * g1).astype(BF)
    l_dd.wait()
    lane = lax.broadcasted_iota(jnp.int32, (T, 128), 1)
    lrp = jnp.where(lane == 16, 1.0, nt(n_v[...], dd_v[...]))

    t_qk.wait_recv()
    views = [qk_v.at[ki[d], par] for d in DIRS]
    f_qk = Fan([(one, one, partner) for one in views], qk_v.at[pl.ds(0, 3), 0])
    t_fg = [gather_weight(0, top)]
    f_qk.wait_recv()
    t_ext.wait_recv()
    normed = n_v[...]
    wq_all = qk_v[:, 0].reshape(W * 32, D)
    wk_all = qk_v[:, 1].reshape(W * 32, D)
    ext_all = ext_v[...].reshape(W * 32, 128)
    scale = 128.0 ** (-0.5)
    q = nt(normed, wq_all) * scale
    k = nt(normed, wk_all)
    arg = nt(lrp, ext_all.astype(F32), HIGH)
    rates = (jnp.minimum(arg, 0.0) - jnp.log1p(jnp.exp(-jnp.abs(arg)))) / 16.0
    row_id = lax.broadcasted_iota(jnp.int32, (CB, CB), 0)
    col_id = lax.broadcasted_iota(jnp.int32, (CB, CB), 1)
    causal = row_id >= col_id
    tri = jnp.where(causal, 1.0, 0.0)
    nblk = T // CB
    blk = [slice(c * CB, (c + 1) * CB) for c in range(nblk)]
    e1, e2, em, el, dec, qd, kd, qi, ke, score = [], [], [], [], [], [], [], [], [], []
    for c in range(nblk):
        cum = nn(tri, rates[blk[c]], HIGH)
        mid = cum[CB // 2 - 1 : CB // 2]
        last = cum[CB - 1 : CB]
        e1.append(jnp.exp(cum - mid))
        e2.append(jnp.exp(mid - cum))
        em.append(jnp.exp(mid))
        el.append(jnp.exp(last - mid))
        dec.append(jnp.exp(last))
        a = q[blk[c]] * e1[c]
        b = k[blk[c]] * e2[c]
        qd.append(a.astype(BF))
        kd.append(b.astype(BF))
        qi.append((a * em[c]).astype(BF))
        ke.append((b * el[c]).astype(BF))
        score.append(jnp.where(causal, nt(qd[c], kd[c]), 0.0).astype(BF))

    l_v.wait()
    t_v.wait_recv()
    views = [v_v.at[vj[d], :, mine] for d in DIRS]
    f_vv = Fan([(one, one, partner) for one in views], v_v.at[pl.ds(0, 3), :, left])
    f_vv.wait_recv()
    wv_all = v_v[...].reshape(W * 64, D)
    v = nt(normed, wv_all).astype(BF)
    up = [tn(v[blk[c]], ke[c]) for c in range(nblk)]
    loc = up[0]
    locd = dec[0]
    for c in range(1, nblk):
        loc = loc * dec[c] + up[c]
        locd = locd * dec[c]
    VC = loc.shape[0]
    st_v[i, :VC] = loc.astype(BF)
    st_v[i, VC:] = jnp.broadcast_to(locd, (16, 128)).astype(BF)
    t_st = Fan([(st_v.at[i], st_v.at[i], kdev[d]) for d in DIRS], st_v.at[pl.ds(0, 3)])
    t_fg.append(gather_weight(0, bottom))
    t_fu = gather_weight(1, every)
    t_oa.step(0)
    t_oa.step(1)
    mixed = [nn(score[c], v[blk[c]]) for c in range(nblk)]

    t_ob.wait_recv()
    views = [o_v.at[ki[d], j, high, mine] for d in DIRS]
    f_o = [Fan([(one, one, partner) for one in views], o_v.at[pl.ds(0, 3), 0, high, mine])]
    t_ob2 = LineGather(lambda src: o_v.at[:, src, high, mine], o_v.at[:, :, high, mine])
    here(l_f)
    f_f = t_fd.step()
    t_oa.step(2)

    def gather_states(slots, totals, back):
        order = range(W - 1, -1, -1) if back else range(W)
        tot_s, tot_d = jnp.zeros((VC, 128), F32), jnp.ones((1, 128), F32)
        for other_i in order:
            one_d = slots[other_i, VC : VC + 1].astype(F32)
            tot_s = tot_s * one_d + slots[other_i, :VC].astype(F32)
            tot_d = tot_d * one_d
        totals[s, :VC] = tot_s.astype(BF)
        totals[s, VC:] = jnp.broadcast_to(tot_d, (16, 128)).astype(BF)
        moves = [send(totals.at[s], totals.at[s], dev) for dev in seqdev]
        pre_s, pre_d = jnp.zeros((VC, 128), F32), jnp.ones((1, 128), F32)
        for other_i in order[:-1]:
            one_d = slots[other_i, VC : VC + 1].astype(F32)
            use = (other_i > i) if back else (other_i < i)
            pre_s = jnp.where(use, pre_s * one_d + slots[other_i, :VC].astype(F32), pre_s)
            pre_d = jnp.where(use, pre_d * one_d, pre_d)
        return pre_s, pre_d, moves

    def entering(totals, back, pre_s, pre_d, moves):
        arrived(moves)
        order = range(n_seq - 1, -1, -1) if back else range(n_seq)
        far = jnp.zeros((VC, 128), F32)
        for other_s in order:
            one_s = totals[other_s, :VC].astype(F32)
            one_d = totals[other_s, VC : VC + 1].astype(F32)
            use = (other_s > s) if back else (other_s < s)
            far = jnp.where(use, far * one_d + one_s, far)
        return pre_s + pre_d * far

    t_st.wait_recv()
    states = gather_states(st_v, tt_v, False)

    l_g.wait()
    t_g.wait_recv()
    views = [g_v.at[vj[d], :, mine] for d in DIRS]
    f_g = Fan([(one, one, partner) for one in views], g_v.at[pl.ds(0, 3), :, left])
    t_ob2.step(0)
    t_ob2.step(1)
    start = [entering(tt_v, False, *states)]
    for c in range(nblk):
        start.append(start[c] * dec[c] + up[c])
    start_low = [a.astype(BF) for a in start]
    for c in range(nblk):
        mixed[c] = mixed[c] + nt(qi[c], start_low[c])
    mix = jnp.concatenate(mixed, axis=0)
    r2 = lax.rsqrt(jnp.sum(mix * mix, axis=1, keepdims=True) / VC + EPS)
    normal = mix * r2
    f_g.wait_recv()
    t_gge.wait_recv()
    wg_all = g_v[...].reshape(W * 64, D)
    gate = nt(normed, wg_all)
    gg = jnp.concatenate([gge_v[h].astype(F32)[0:1, 0:64] for h in range(W)], axis=1)
    sig = 1.0 / (1.0 + jnp.exp(-gate))
    act = gate * sig
    act_v[0] = act
    act_v[1] = sig + act * (1.0 - sig)
    ga_v[j] = (normal * gg * act).astype(BF)
    act_v[2] = normal
    halves = [pl.ds(n * T // 2, T // 2) for n in range(2)]
    t_ga = [LineGather(lambda src, at=at: ga_v.at[src, at], ga_v.at[:, at]) for at in halves]

    t_oa.collect()
    views = [o_v.at[i, vj[d], low, mine] for d in DIRS]
    f_o.append(Fan([(one, one, partner) for one in views], o_v.at[0, pl.ds(0, 3), low, mine]))
    t_oa2 = SquareGather(
        lambda src, at: o_v.at[src, :, low, at], lambda count: o_v.at[pl.ds(0, count), :, low, mine]
    )

    here([l_xa, l_ca])
    for part in range(rows // T):
        at = pl.ds(part * T, T)
        xa = x_all[at, :].astype(F32)
        ra = lax.rsqrt(jnp.sum(xa * xa, axis=1, keepdims=True) / D + EPS)
        n_all[at, :] = (xa * ra * g1).astype(BF)
    xr_v[...] = (x * (r1 * r1 * r1)).astype(BF).T
    low_all = jnp.where(
        lax.broadcasted_iota(jnp.int32, (rows, 128), 1) == 16, 1.0, nt(n_all[...], dd_v[...])
    )
    lall_v[...] = low_all.astype(BF)
    for line in t_fg:
        f_f += line.step()
    t_ob2.step(2)
    t_ga[0].step(0)
    t_ga[0].step(1)
    t_ga[1].step(0)
    t_ga[1].step(1)
    f_f += t_fu.step()
    t_ga[0].step(2)
    t_ga[1].step(2)
    f_o += t_oa2.step()
    t_ob2.collect()
    views = [o_v.at[:, vj[d], high, mine] for d in DIRS]
    f_o.append(Fan([(one, one, partner) for one in views], o_v.at[:, pl.ds(0, 3), high, mine]))
    f_f += t_fd.collect()
    l_c.wait()
    arrived(f_f)
    dn = f_v[2].reshape(W * FB, D)
    gh_v[...] = nt(c_v[...], dn)
    f_f = t_fg[0].collect() + t_fg[1].collect()
    f_f += t_fu.collect()
    f_far = t_oa2.collect()
    for line in t_ga:
        line.collect()
    arrived(f_o)


    def attention(head):
        return nn(ga_v[head], o_v[head].reshape(W * 64, D))

    att = attention(i) + attention(ki[1]) + attention(ki[2])
    p_v[...] = att
    arrived(f_far)
    arrived(f_f)
    gT = f_v[0].reshape(W * FB, D)
    uT = f_v[1].reshape(W * FB, D)
    att = p_v[...] + attention(ki[3])
    resid = x_v[...].astype(F32) + att
    r3 = lax.rsqrt(jnp.sum(resid * resid, axis=1, keepdims=True) / D + EPS)
    fin = (resid * r3 * g3).astype(BF)
    gval = nt(fin, gT)
    uval = nt(fin, uT)
    fsig = 1.0 / (1.0 + jnp.exp(-gval))
    fact = gval * fsig
    hid = (fact * uval).astype(BF)
    gh = gh_v[...]
    gup = (gh * fact).astype(BF)
    ggate = (gh * uval * (fsig + fact * (1.0 - fsig))).astype(BF)
    hd[...] = hid.T.reshape(W, FB, T)
    t_hd = Fan([(hd.at[ki[d]], hseg.at[i], kdev[d]) for d in DIRS], hseg.at[pl.ds(0, 3)])
    hseg[i] = hd[i]
    part = nn(ggate, gT) + nn(gup, uT)
    p_v[...] = part
    sst[...] = as_row(jnp.sum(resid * g3 * part, axis=1, keepdims=True))
    t_m3 = Fan([(sst, rst.at[d], vdev[d]) for d in DIRS], rst.at[pl.ds(1, 3)])
    part_low = (part * g3).astype(BF)
    t_gg = [
        LineSum(
            lambda to, at=at: sgg.at[to, at],
            rgg.at[pl.ds(0, 2), at],
            rgg.at[pl.ds(2, 2), at],
            cgg.at[:, at],
        )
        for at in halves
    ]
    ggp = nt(part_low, o_v[...].reshape(W * W * 64, D))
    for h in range(W):
        sgg[h] = ggp[:, h * VC : (h + 1) * VC].astype(BF)
    for n in range(3):
        for line in t_gg:
            line.go(n)

    def weight_part(n, grad):
        gw[n] = tn(grad, fin).astype(BF).reshape(W, FB, D)
        return send(gw.at[n, :, :, other], pre.at[n], partner)

    def settle(n, move):
        move.wait_recv()
        pres[n] = (gw[n, :, :, mine].astype(F32) + pre[n].astype(F32)).astype(BF)

    def square(n, rows_at):
        return SquareSum(
            lambda to, at: pres.at[n, to, rows_at, at],
            rfw.at[n, :, rows_at],
            qfw.at[n, :, rows_at],
            cfw.at[n, :, rows_at],
        )

    t_pre0 = weight_part(0, ggate)
    t_pre1 = weight_part(1, gup)

    feature = lax.broadcasted_iota(jnp.int32, (1, D), 1)
    own_slab = jnp.where(lax.rem(feature // 64, W) == j, 1.0, 0.0)
    own_run = jnp.where(feature // (D // W) == j, 1.0, 0.0)
    so[...] = (nn(hid, dn) + own_slab * resid).astype(BF).T.reshape(W, W, 64, T)
    t_out = LineSum(lambda to: so.at[:, to], ro.at[pl.ds(0, 2)], ro.at[pl.ds(2, 2)], co).rest()
    ffn_gain = jnp.sum(part * resid * r3, axis=0, keepdims=True)
    settle(0, t_pre0)
    t_fw0 = square(0, every)
    t_gg[0].step(0)
    t_m3.wait_recv()
    m3 = as_column(sst[...] + rst[1] + rst[2] + rst[3]) / D
    base = c_v[...].astype(F32) - resid * (r3 * r3 * r3 * m3)
    t_gg[0].step(1)
    direct = nt(base.astype(BF), o_v[j].reshape(W * 64, D))
    full = p_v[...] * (g3 * r3)
    mixed_in = (full + own_run * base).astype(BF)
    for h in range(W):
        gow[h] = tn(ga_v[h], mixed_in).astype(BF)
    t_po = send(gow.at[:, :, other], preo, partner)
    t_gg[1].step(0)
    t_fw0.step()
    settle(1, t_pre1)
    t_fw1 = [square(1, top)]
    t_gg[1].step(1)
    t_po.wait_recv()
    preso[...] = (gow[:, :, mine].astype(F32) + preo[...].astype(F32)).astype(BF)
    for line in t_gg:
        line.collect()

    ggs = jnp.concatenate([line.total() for line in t_gg], axis=0)
    ggrad = direct + r3 * ggs
    act = act_v[0]
    normal = act_v[2]
    dgate = (ggrad * normal * gg * act_v[1]).astype(BF)
    gs = ggrad * act
    group = jnp.sum(gs * normal, axis=0, keepdims=True)
    group_rows = [
        jnp.concatenate(
            [group[:, h * 64 : (h + 1) * 64], jnp.zeros((1, T - 64), F32)], axis=1
        )
        for h in range(W)
    ]
    gnm = gs * gg
    gmix = (r2 * (gnm - normal * (jnp.sum(normal * gnm, axis=1, keepdims=True) / VC))).astype(BF)

    qst = [tn(gmix[blk[c]], qi[c]) for c in range(nblk)]
    bloc = qst[nblk - 1]
    for c in range(nblk - 2, -1, -1):
        bloc = bloc * dec[c] + qst[c]
    bst_v[i, :VC] = bloc.astype(BF)
    bst_v[i, VC:] = jnp.broadcast_to(locd, (16, 128)).astype(BF)
    t_bst = Fan([(bst_v.at[i], bst_v.at[i], kdev[d]) for d in DIRS], bst_v.at[pl.ds(0, 3)])
    t_ow = SquareSum(lambda to, at: preso.at[to, :, at], rowk, qow, cow)
    t_fw1.append(square(1, bottom))
    vz[1] = dgate.T.reshape(W, 64, T)
    t_gz = Fan([(vz.at[1, vj[d]], zvg.at[1, j], vdev[d]) for d in DIRS], zvg.at[1, pl.ds(0, 3)])
    dq_all, dk_in, dv_in = [], [], []
    for c in range(nblk):
        ds = jnp.where(causal, nt(gmix[blk[c]], v[blk[c]]), 0.0).astype(BF)
        dq_all.append(e1[c] * (nn(ds, kd[c]) + em[c] * nn(gmix[blk[c]], start_low[c])))
        dk_in.append(tn(ds, qd[c]))
        dv_in.append(tn(score[c], gmix[blk[c]]))
    ql = jnp.concatenate([(dq * scale).astype(BF) for dq in dq_all], axis=0)
    known = nn(dgate, wg_all) + nn(ql, wq_all)
    rest_in = full + own_slab * base
    t_out.step(0)
    t_hd.wait_recv()
    dsum[0] = nn(lanes(hseg[...]), c_all[...]).astype(BF)
    t_ds = send(dsum.at[0], dsum.at[1], partner)
    t_fw1[0].step()
    t_bst.wait_recv()
    after = [None] * nblk
    states = gather_states(bst_v, btt_v, True)
    t_out.step(1)
    after[nblk - 1] = entering(btt_v, True, *states)
    for c in range(nblk - 2, -1, -1):
        after[c] = after[c + 1] * dec[c + 1] + qst[c + 1]

    kl, vl, ga = [], [], []
    for c in range(nblk):
        low_after = after[c].astype(BF)
        dk = e2[c] * (dk_in[c] + el[c] * nn(v[blk[c]], low_after))
        dv = dv_in[c] + nt(ke[c], low_after)
        gc = q[blk[c]] * dq_all[c] - k[blk[c]] * dk
        extra = jnp.sum(after[c] * start[c + 1], axis=0, keepdims=True)
        gc = jnp.where(row_id == CB - 1, gc + extra, gc)
        gr = tn(tri, gc, HIGH)
        ga.append(gr / (1.0 + jnp.exp(arg[blk[c]])) / 16.0)
        kl.append(dk.astype(BF))
        vl.append(dv.astype(BF))
    kl = jnp.concatenate(kl, axis=0)
    vl = jnp.concatenate(vl, axis=0)
    ga = jnp.concatenate(ga, axis=0).astype(BF)
    glr = nn(ga, ext_all).astype(BF)
    gn = known + nn(kl, wk_all) + nn(vl, wv_all) + nn(glr, dd_v[...])
    whole = gn * (r1 * g1) + rest_in
    sgn[...] = whole.astype(BF).T.reshape(W, W, 64, T)
    pairs = [pl.ds(n * W // 2, W // 2) for n in range(2)]
    t_gn = [
        LineSum(
            lambda to, at=at: sgn.at[at, to],
            rgn.at[pl.ds(0, 2), at],
            rgn.at[pl.ds(2, 2), at],
            cgn.at[:, at],
        )
        for at in pairs
    ]
    for n in range(3):
        for line in t_gn:
            line.go(n)
    vz[0] = vl.T.reshape(W, 64, T)
    t_vz = Fan([(vz.at[0, vj[d]], zvg.at[0, j], vdev[d]) for d in DIRS], zvg.at[0, pl.ds(0, 3)])

    gnx = gn * x_v[...].astype(F32)
    norm_gain = jnp.sum(gnx * r1, axis=0, keepdims=True)
    m1p = as_row(jnp.sum(gnx * g1, axis=1, keepdims=True))[:1]
    rank_row = lax.broadcasted_iota(jnp.int32, (16, 128), 0)
    rank_col = lax.broadcasted_iota(jnp.int32, (16, 128), 1)
    by_owner = jnp.where(rank_col == lax.rem(rank_row, W) * W + rank_row // W, 1.0, 0.0)
    small = nn(by_owner.astype(BF), tn(glr, normed).astype(BF))
    slab = D // (W * W)
    rid = lax.broadcasted_iota(jnp.int32, (16, T), 0)
    for h in range(W):
        ranks = small[h * W : (h + 1) * W]
        sm0[h, 0:16] = jnp.concatenate(
            [ranks[:, n * T : (n + 1) * T] for n in range(W)], axis=0
        ).astype(BF)

        def slabs(row):
            return jnp.concatenate(
                [row[:, (W * n + h) * slab : (W * n + h + 1) * slab] for n in range(W)], axis=1
            )

        rest = jnp.where(rid == 0, slabs(norm_gain), 0.0)
        rest = jnp.where(rid == 1, slabs(ffn_gain), rest)
        rest = jnp.where(rid == 2, group_rows[h], rest)
        rest = jnp.where(rid == 3, m1p, rest)
        sm0[h, 16:32] = rest.astype(BF)
    t_s0 = Fan([(sm0.at[vj[d]], sm1.at[d], vdev[d]) for d in DIRS], sm1.at[pl.ds(1, 3)])


    def finish_square(n, lines):
        for line, rows_at in lines:
            line.collect()
            fin_f[par, n, rows_at] = line.total().astype(BF)
        return send(fin_f.at[par, n], fin_f.at[par, n], partner)

    t_ff = [finish_square(0, [(t_fw0, every)])]
    t_ow.step()
    t_fw1[1].step()
    qka[:, 0] = ql.T.reshape(W, 32, T)
    qka[:, 1] = kl.T.reshape(W, 32, T)
    qka[:, 2] = ga.T.reshape(W, 32, T)
    t_qa = Fan([(qka.at[ki[d]], kqa.at[i], kdev[d]) for d in DIRS], kqa.at[pl.ds(0, 3)])
    t_gz.wait_recv()
    zvg[1, j] = vz[1, j]
    t_gk = Fan([(zvg.at[1, ki[d]], kvg.at[1, i], kdev[d]) for d in DIRS], kvg.at[1, pl.ds(0, 3)])
    kvg[1, i] = zvg[1, i]

    t_out.collect()
    ao[...] = t_out.total().astype(BF)
    t_ao = Fan([(ao.at[ki[d]], oseg.at[i], kdev[d]) for d in DIRS], oseg.at[pl.ds(0, 3)])
    oseg[i] = ao[i]

    t_gn[0].step(0)
    t_gn[1].step(0)
    t_gn[0].step(1)
    t_gn[1].step(1)

    t_ow.collect()
    mid_o[...] = t_ow.total().astype(BF).reshape(W, 64, half)
    t_oz = LineSum(
        lambda to: mid_o.at[to], rowz.at[pl.ds(0, 2)], rowz.at[pl.ds(2, 2)], coz
    ).rest()

    t_qa.wait_recv()
    kqa[i] = qka[i]
    nall = n_all[...]
    for n in range(2):
        qksum[0, n] = nn(lanes(kqa[:, n]), nall).astype(BF)
    esum[0] = nn(lanes(kqa[:, 2]), lall_v[...])
    t_qs = send(qksum.at[0], qksum.at[1], partner)
    t_es = send(esum.at[0], esum.at[1], partner)
    for line in t_gn:
        line.collect()
    t_vz.wait_recv()
    zvg[0, j] = vz[0, j]
    t_vk = Fan([(zvg.at[0, ki[d]], kvg.at[0, i], kdev[d]) for d in DIRS], kvg.at[0, pl.ds(0, 3)])
    kvg[0, i] = zvg[0, i]
    t_s0.wait_recv()
    sm2[0] = total(sm0[j], sm1).astype(BF)
    m1 = (
        sm0[0, 19:20].astype(F32)
        + sm1[1, 19:20].astype(F32)
        + sm1[2, 19:20].astype(F32)
        + sm1[3, 19:20].astype(F32)
    ) / D

    summed = jnp.concatenate([line.total() for line in t_gn], axis=0)
    for h in range(W):
        at = pl.ds(pl.multiple_of((h * W + j) * 64, 64), 64)
        ai[h] = (summed[h] - xr_v[at, :].astype(F32) * m1).astype(BF)
    t_ai = Fan([(ai.at[ki[d]], iseg.at[i], kdev[d]) for d in DIRS], iseg.at[pl.ds(0, 3)])
    iseg[i] = ai[i]

    t_s1 = Fan([(sm2.at[0], sm2.at[d], kdev[d]) for d in DIRS], sm2.at[pl.ds(1, 3)])
    t_ff.append(finish_square(1, list(zip(t_fw1, (top, bottom)))))

    t_gk.wait_recv()
    vgsum[0, 1] = nn(lanes(kvg[1]), nall).astype(BF)
    t_vs = [send(vgsum.at[0, 1], vgsum.at[1, 1], partner)]

    t_oz.step(0)
    t_oz.step(1)

    t_vk.wait_recv()
    vgsum[0, 0] = nn(lanes(kvg[0]), nall).astype(BF)
    t_vs.append(send(vgsum.at[0, 0], vgsum.at[1, 0], partner))
    t_s1.wait_recv()
    sm3[0] = total(sm2[0], sm2).astype(BF)
    t_s2 = send(sm3.at[0], sm3.at[1], partner)

    t_ds.wait_recv()
    r_fd[...] = dsum[0].astype(F32) + dsum[1].astype(F32)
    t_ao.wait_recv()
    r_out[...] = lanes(oseg[...])
    t_qs.wait_recv()
    r_q[...] = qksum[0, 0].astype(F32) + qksum[1, 0].astype(F32)
    r_k[...] = qksum[0, 1].astype(F32) + qksum[1, 1].astype(F32)
    t_es.wait_recv()
    decay = (esum[0] + esum[1]).T
    r_du[...] = decay[0:16, :].reshape(16, 1, 32)
    r_db[...] = decay[16:17, :]
    t_ff[0].wait_recv()
    for h in range(2):
        r_fg[:, h * half : (h + 1) * half] = fin_f[h, 0].astype(F32)
    t_oz.collect()
    fin_ow[par] = t_oz.total().astype(BF)
    t_fo = send(fin_ow.at[par], fin_ow.at[par], partner)
    t_ff[1].wait_recv()
    for h in range(2):
        r_fu[:, h * half : (h + 1) * half] = fin_f[h, 1].astype(F32)
    arrived(t_vs)
    r_v[...] = vgsum[0, 0].astype(F32) + vgsum[1, 0].astype(F32)
    r_g[...] = vgsum[0, 1].astype(F32) + vgsum[1, 1].astype(F32)
    t_s2.wait_recv()
    tot = sm3[0].astype(F32) + sm3[1].astype(F32)
    own_ranks, own_slabs = [], jnp.zeros((2, slab), F32)
    for n in range(W):
        own_ranks.append(jnp.zeros((1, T), F32))
        for h in range(W):
            row = tot[n * W + h : n * W + h + 1]
            own_ranks[n] = jnp.where(i == h, row, own_ranks[n])
        own_slabs = jnp.where(i == n, tot[16:18, n * slab : (n + 1) * slab], own_slabs)
    r_dd[...] = jnp.concatenate(own_ranks, axis=1)
    r_ng[...] = own_slabs[0:1]
    r_fn[...] = own_slabs[1:2]
    r_gg[...] = tot[18:19, 0:64]
    t_ai.wait_recv()
    r_in[...] = lanes(iseg[...])
    t_fo.wait_recv()
    for h in range(2):
        r_o[:, h * half : (h + 1) * half] = fin_ow[h].astype(F32)
    for _, cp in ring:
        cp.wait_send()

    @pl.when(inner)
    def _():
        for cp in inner_sent:
            cp.wait_send()

    @pl.when(jnp.logical_not(inner))
    def _():
        for cp in outer_sent:
            cp.wait_send()


N_OUT = 44
N_IN = 93
N_LOCAL = 18


def layer(n_seq, args):
    rows, D = args[0].shape
    W = WAYS
    T = rows // W
    FB = args[-1].shape[0]
    VC = W * 64
    half = D // 2

    def sds(shape, dtype=F32):
        return pltpu.VMEM(shape, dtype)

    def vm(shape, dtype=BF):
        return pltpu.VMEM(shape, dtype)

    slab = D // (W * W)
    outs = [
        sds((64, rows), BF),
        sds((64, rows), BF),
        sds((1, slab)),
        sds((32, D)),
        sds((32, D)),
        sds((64, D)),
        sds((64, D)),
        sds((1, D)),
        sds((16, 1, 32)),
        sds((1, 32)),
        sds((1, 64)),
        sds((64, D)),
        sds((1, slab)),
        sds((FB, D)),
        sds((FB, D)),
        sds((FB, D)),
    ]
    scratch = [
        vm((T, D)),
        vm((T, D)),
        vm((rows, D)),
        vm((rows, D)),
        vm((rows, D)),
        vm((T, D)),
        vm((D, T)),
        vm((128, D)),
        vm((8, 128)),
        vm((8, 128)),
        vm((16, W, 32)),
        vm((W, 32)),
        vm((1, 64)),
        vm((128, 128), F32),
        vm((8, D), F32),
        vm((W, 2, 32, D)),
        vm((W, 32, 128)),
        vm((W, 64, D)),
        vm((W, 64, D)),
        vm((W, 16, 128)),
        vm((W, W, 64, D)),
        vm((3, W, FB, D)),
        vm((W, VC + 16, 128)),
        vm((n_seq, VC + 16, 128)),
        vm((W, VC + 16, 128)),
        vm((n_seq, VC + 16, 128)),
        vm((W, T, VC)),
        vm((W, T, VC)),
        vm((W, T, VC)),
        vm((2, T, VC)),
        vm((8, T), F32),
        vm((W, 8, T), F32),
        vm((W, W, 64, T)),
        vm((W, W, 64, T)),
        vm((2, W, 64, T)),
        vm((W, W, 64, T)),
        vm((W, W, 64, T)),
        vm((2, W, 64, T)),
        vm((W, 64, T)),
        vm((W, 64, T)),
        vm((W, 64, T)),
        vm((W, 64, T)),
        vm((W, FB, T)),
        vm((W, FB, T)),
        vm((2, W, FB, D)),
        vm((2, W, FB, half)),
        vm((2, W, FB, half)),
        vm((2, 2, FB, half)),
        vm((2, 2, FB, half // 2)),
        vm((2, 2, FB, half // 2)),
        vm((2, 2, FB, half)),
        vm((2, FB, D)),
        vm((W, VC, D)),
        vm((W, VC, half)),
        vm((W, VC, half)),
        vm((2, VC, half)),
        vm((2, VC, half // 2)),
        vm((2, VC, half // 2)),
        vm((W, 64, half)),
        vm((W, 64, half)),
        vm((2, 64, half)),
        vm((2, 64, half)),
        vm((2, W, 64, T)),
        vm((2, W, 64, T)),
        vm((2, W, 64, T)),
        vm((2, 2, 64, D)),
        vm((W, 3, 32, T)),
        vm((W, 3, 32, T)),
        vm((2, 2, 32, D)),
        vm((2, 32, 128), F32),
        vm((W, 32, T)),
        vm((W, 32, T)),
        vm((W, 32, T)),
        vm((2, 32, T)),
        vm((rows, 128)),
        vm((T, W * FB), F32),
        vm((3, T, VC), F32),
        vm((T, D), F32),
        pltpu.SemaphoreType.DMA((N_OUT,)),
        pltpu.SemaphoreType.DMA((N_IN + 2 * n_seq,)),
        pltpu.SemaphoreType.DMA((N_LOCAL,)),
    ]
    return pl.pallas_call(
        functools.partial(layer_kernel, n_seq),
        out_shape=outs,
        in_specs=[pl.BlockSpec(memory_space=pl.ANY)] * len(args),
        out_specs=[pl.BlockSpec(memory_space=pltpu.VMEM)] * len(outs),
        scratch_shapes=scratch,
        compiler_params=pltpu.CompilerParams(
            collective_id=0, has_side_effects=True, vmem_limit_bytes=60 * 2**20
        ),
        name="layer",
    )(*args)


def finish_kernel(*refs):
    n = len(refs) // 2
    sem = refs[-1]
    copies = [pltpu.make_async_copy(refs[k], refs[n + k], sem.at[k]) for k in range(n)]
    for cp in copies:
        cp.start()
    for cp in copies:
        cp.wait()


def finish(parts):
    return pl.pallas_call(
        finish_kernel,
        out_shape=[jax.ShapeDtypeStruct(p.shape, p.dtype) for p in parts],
        in_specs=[pl.BlockSpec(memory_space=pltpu.VMEM)] * len(parts),
        out_specs=[pl.BlockSpec(memory_space=pl.ANY)] * len(parts),
        scratch_shapes=[pltpu.SemaphoreType.DMA((len(parts),))],
        compiler_params=pltpu.CompilerParams(vmem_limit_bytes=16 * 2**20),
        name="finish",
    )(*parts)


def shards(
    n_seq,
    tokens,
    norm_gain,
    query_weight,
    key_weight,
    value_weight,
    gate_weight,
    decay_down,
    decay_up,
    decay_bias,
    group_gain,
    out_weight,
    ffn_gain,
    ffn_gate,
    ffn_up,
    ffn_down,
    cotangent,
):
    parts = layer(
        n_seq,
        (
            tokens,
            cotangent,
            norm_gain.reshape(8, -1),
            ffn_gain.reshape(8, -1),
            decay_up,
            decay_bias,
            group_gain[None],
            query_weight.transpose(1, 2, 0),
            key_weight.transpose(1, 2, 0),
            value_weight.transpose(1, 2, 0),
            gate_weight.transpose(1, 2, 0),
            decay_down.T,
            out_weight[0],
            ffn_gate.T,
            ffn_up.T,
            ffn_down,
        ),
    )
    if n_seq > 2:

        def over_pairs(a):
            return jnp.sum(lax.all_gather(a, "seq")[::2].astype(F32), axis=0).astype(a.dtype)

        parts = list(parts[:2]) + [over_pairs(a) for a in parts[2:]]
    (r_out, r_in, r_ng, r_q, r_k, r_v, r_g, r_dd, r_du, r_db, r_gg, r_o, r_fn, r_fg, r_fu, r_fd) = finish(parts)
    return (
        r_out.T,
        r_in.T,
        r_ng[0],
        r_q.T[:, None, :],
        r_k.T[:, None, :],
        r_v.T[:, None, :],
        r_g.T[:, None, :],
        r_dd.T,
        r_du,
        r_db,
        r_gg[0],
        r_o[None],
        r_fn[0],
        r_fg.T,
        r_fu.T,
        r_fd,
    )


def solution(mesh):
    in_specs = (
        P("seq", None),
        P(),
        P(None, None, "kax"),
        P(None, None, "kax"),
        P(None, None, "vax"),
        P(None, None, "vax"),
        P(),
        P(None, None, "kax"),
        P(None, "kax"),
        P("vax"),
        P("kax", "vax", None),
        P(),
        P(None, ("kax", "vax")),
        P(None, ("kax", "vax")),
        P(("kax", "vax"), None),
        P("seq", None),
    )
    out_specs = (
        P("seq", ("kax", "vax")),
        P("seq", ("kax", "vax")),
        P(("kax", "vax")),
        P(None, "vax", "kax"),
        P(None, "vax", "kax"),
        P(None, "kax", "vax"),
        P(None, "kax", "vax"),
        P(None, ("kax", "vax")),
        P(None, "vax", "kax"),
        P("vax", "kax"),
        P("vax"),
        P("kax", "vax", None),
        P(("kax", "vax")),
        P(None, ("kax", "vax")),
        P(None, ("kax", "vax")),
        P(("kax", "vax"), None),
    )
    return jax.shard_map(
        functools.partial(shards, mesh.shape["seq"]),
        mesh=mesh,
        in_specs=in_specs,
        out_specs=out_specs,
        check_vma=False,
    )
```

```python
import functools

import jax
import jax.numpy as jnp
from jax import lax
from jax.experimental import pallas as pl
from jax.experimental.pallas import tpu as pltpu
from jax.sharding import PartitionSpec as P

MESH = pl.DeviceIdType.MESH
BF = jnp.bfloat16
F32 = jnp.float32
CB = 128
WAYS = 4
EPS = 1e-06
HIGH = lax.Precision.HIGHEST


def nn(a, b, precision=None):
    return lax.dot_general(
        a, b, (((1,), (0,)), ((), ())), precision=precision, preferred_element_type=F32
    )


def nt(a, b, precision=None):
    return lax.dot_general(
        a, b, (((1,), (1,)), ((), ())), precision=precision, preferred_element_type=F32
    )


def tn(a, b, precision=None):
    return lax.dot_general(
        a, b, (((0,), (0,)), ((), ())), precision=precision, preferred_element_type=F32
    )


def xor(index, d):
    if d == 1:
        return index + 1 - 2 * lax.rem(index, 2)
    if d == 2:
        return lax.rem(index + 2, 4)
    return 3 - index


def as_row(column):
    return jnp.broadcast_to(column, (column.shape[0], 128)).T[:8]


def as_column(row):
    return jnp.broadcast_to(row[:1], (128, row.shape[1])).T[:, :1]


def flat_row(block):
    return jnp.concatenate([block[r : r + 1] for r in range(block.shape[0])], axis=1)


def lanes(block):
    return jnp.concatenate([block[n] for n in range(block.shape[0])], axis=1)


def total(own, got):
    out = own.astype(F32)
    for d in (1, 2, 3):
        out = out + got[d].astype(F32)
    return out


def layer_kernel(
    n_seq,
    tok,
    cot,
    ng,
    ffg,
    dup,
    dbi,
    ggn,
    wq,
    wk,
    wv,
    wg,
    dd,
    wo,
    fg,
    fu,
    fd,
    r_out,
    r_in,
    r_ng,
    r_q,
    r_k,
    r_v,
    r_g,
    r_dd,
    r_du,
    r_db,
    r_gg,
    r_o,
    r_fn,
    r_fg,
    r_fu,
    r_fd,
    x_v,
    c_v,
    x_all,
    c_all,
    n_all,
    n_v,
    xr_v,
    dd_v,
    ng_v,
    ffg_v,
    dup_v,
    dbi_v,
    ggn_v,
    sq_v,
    gain_v,
    qk_v,
    ext_v,
    v_v,
    g_v,
    gge_v,
    o_v,
    f_v,
    st_v,
    tt_v,
    bst_v,
    btt_v,
    ga_v,
    sgg,
    rgg,
    cgg,
    sst,
    rst,
    so,
    ro,
    co,
    sgn,
    rgn,
    cgn,
    ao,
    oseg,
    ai,
    iseg,
    hd,
    hseg,
    gw,
    pre,
    pres,
    rfw,
    qfw,
    cfw,
    fin_f,
    dsum,
    gow,
    preo,
    preso,
    rowk,
    qow,
    cow,
    mid_o,
    rowz,
    coz,
    fin_ow,
    vz,
    zvg,
    kvg,
    vgsum,
    qka,
    kqa,
    qksum,
    esum,
    sm0,
    sm1,
    sm2,
    sm3,
    lall_v,
    gh_v,
    act_v,
    p_v,
    ss,
    rs,
    ls,
):
    s = lax.axis_index("seq")
    i = lax.axis_index("kax")
    j = lax.axis_index("vax")
    par = lax.rem(s, 2)
    oth = 1 - par
    T, D = x_v.shape
    rows = x_all.shape[0]
    FB = f_v.shape[2]
    half = D // 2
    W = WAYS
    DIRS = (1, 2, 3)
    mine = pl.ds(pl.multiple_of(par * half, half), half)
    other = pl.ds(pl.multiple_of(oth * half, half), half)
    partner = {"seq": s + 1 - 2 * par}
    kdev = [None] + [{"kax": xor(i, d)} for d in DIRS]
    vdev = [None] + [{"vax": xor(j, d)} for d in DIRS]
    ki = [None] + [xor(i, d) for d in DIRS]
    vj = [None] + [xor(j, d) for d in DIRS]
    seqdev = [{"seq": lax.rem(s + e, n_seq)} for e in range(1, n_seq)]

    count = [0, 0, 0]
    inner_sent, outer_sent = [], []

    def slot(kind):
        count[kind] += 1
        return count[kind] - 1

    def out_slot():
        return slot(0)

    def in_slot():
        return slot(1)

    def copy(src, dst, dev, n, m):
        return pltpu.make_async_remote_copy(
            src_ref=src,
            dst_ref=dst,
            send_sem=ss.at[n],
            recv_sem=rs.at[m],
            device_id=dev,
            device_id_type=MESH,
        )

    ring = []

    def ring_slot():
        if len(ring) < 28:
            return out_slot()
        n, cp = ring.pop(0)
        cp.wait_send()
        return n

    def send(src, dst, dev):
        n = ring_slot()
        cp = copy(src, dst, dev, n, in_slot())
        cp.start()
        ring.append((n, cp))
        return cp

    def load(src, dst):
        cp = pltpu.make_async_copy(src, dst, ls.at[slot(2)])
        cp.start()
        return cp

    class Fan:
        def __init__(self, copies, size):
            n, m = ring_slot(), in_slot()
            for src, dst, dev in copies:
                copy(src, dst, dev, n, m).start()
            self.all = copy(size, size, partner, n, m)
            ring.append((n, self.all))

        def wait_recv(self):
            self.all.wait_recv()

    def arrived(copies):
        for cp in copies:
            cp.wait_recv()

    def here(copies):
        for cp in copies:
            cp.wait()

    inner = lax.rem(j + 1, W) >= 2

    class LineGather:
        def __init__(self, view, four):
            a, b, c = in_slot(), in_slot(), in_slot()
            n, m = ring_slot(), out_slot()
            near = copy(view(j), view(j), vdev[1], n, a)
            near.start()
            ring.append((n, near))
            across = copy(view(j), view(j), vdev[3], m, c)
            self.got = [
                copy(view(vj[d]), view(vj[d]), vdev[1], n, at) for d, at in zip(DIRS, (a, b, c))
            ]
            self.on = [
                copy(view(vj[1]), view(vj[1]), vdev[3], m, b),
                copy(view(vj[3]), view(vj[3]), vdev[1], m, b),
                copy(view(vj[2]), view(vj[2]), vdev[1], m, c),
            ]
            inner_sent.append(copy(four, four, vdev[1], m, a))

            @pl.when(inner)
            def _():
                across.start()

        def step(self, n):
            @pl.when(inner)
            def _():
                self.got[(0, 2, 1)[n]].wait_recv()
                self.on[n].start()

        def collect(self):
            @pl.when(jnp.logical_not(inner))
            def _():
                arrived(self.got)

    class LineSum:
        def __init__(self, part, both, relay, summed):
            self.part, self.both, self.relay, self.summed = part, both, relay, summed
            a, b, c = in_slot(), in_slot(), in_slot()
            n, o = out_slot(), out_slot()
            self.into_slot = c
            self.first = [
                copy(part(vj[3]), relay.at[0], vdev[1], n, a),
                copy(part(vj[2]), relay.at[1], vdev[1], n, b),
            ]
            self.second = [copy(summed.at[k], both.at[1], vdev[2 + k], o, c) for k in range(2)]
            self.all = copy(both, both, vdev[1], o, c)
            outer_sent.append(copy(relay, relay, vdev[1], n, a))
            inner_sent.append(copy(summed, summed, vdev[1], o, a))

        def go(self, n):
            if n < 2:

                @pl.when(jnp.logical_not(inner))
                def _():
                    self.first[n].start()

            elif n == 2:
                m = ring_slot()
                direct = copy(self.part(vj[1]), self.both.at[0], vdev[1], m, self.into_slot)
                direct.start()
                ring.append((m, direct))

        def rest(self):
            for n in range(3):
                self.go(n)
            return self

        def step(self, n):
            @pl.when(inner)
            def _():
                self.first[n].wait_recv()
                mine_too = self.part(vj[2 + n])[...].astype(F32)
                self.summed[n] = (mine_too + self.relay[n].astype(F32)).astype(BF)
                self.second[n].start()

        def collect(self):
            self.all.wait_recv()

        def total(self):
            out = self.part(j)[...].astype(F32)
            return out + self.both[0].astype(F32) + self.both[1].astype(F32)

    class SquareSum:
        def __init__(self, part, got, relay, summed):
            self.part, self.got, self.relay, self.summed = part, got, relay, summed
            q = got.shape[-1] // 2
            self.at = [pl.ds(0, q), pl.ds(q, q)]
            a, self.into_slot = in_slot(), in_slot()
            n = ring_slot()
            for k in range(2):
                copy(self.half(ki[3], k), relay.at[k], kdev[1 + k], n, a).start()
            for k in range(2):
                copy(self.half(ki[1 + k], k), self.into(k, k), kdev[1 + k], n, self.into_slot).start()
            self.relayed = copy(relay, relay, kdev[1], n, a)
            ring.append((n, copy(got, got, kdev[1], n, a)))

        def half(self, target, n):
            return self.part(target, self.at[n])

        def into(self, n, h):
            return self.got.at[n, :, self.at[h]]

        def step(self):
            self.relayed.wait_recv()
            n = ring_slot()
            for k in range(2):
                own = self.half(ki[2 - k], k)[...].astype(F32)
                self.summed[k] = (own + self.relay[k].astype(F32)).astype(BF)
                copy(
                    self.summed.at[k], self.into(1 - k, k), kdev[2 - k], n, self.into_slot
                ).start()
            ring.append((n, copy(self.summed, self.summed, kdev[1], n, self.into_slot)))

        def collect(self):
            copy(self.got, self.got, kdev[1], 0, self.into_slot).wait_recv()

        def total(self):
            out = self.part(i, pl.ds(0, self.got.shape[-1]))[...].astype(F32)
            return out + self.got[0].astype(F32) + self.got[1].astype(F32)

    quarter = half // 2
    mine_parts = [
        pl.ds(pl.multiple_of(par * half + n * quarter, quarter), quarter) for n in range(2)
    ]

    class SquareGather:
        def __init__(self, view, many, whole=mine, parts=mine_parts, own=None, pass_on=True):
            self.view, self.many, self.whole, self.parts = view, many, whole, parts
            self.pass_on = pass_on
            own = view(i, whole) if own is None else own
            into = view(i, whole)
            self.near = Fan([(own, into, kdev[d]) for d in (1, 2)], many(2))

        def forward(self, sources):
            if not self.pass_on:
                return []
            views = [self.view(src, self.whole) for src in sources]
            return [Fan([(one, one, partner) for one in views], self.many(len(views)))]

        def step(self):
            self.near.wait_recv()
            views = [self.view(ki[1 + n], self.parts[n]) for n in range(2)]
            self.far = Fan([(views[n], views[n], kdev[2 - n]) for n in range(2)], self.many(1))
            return self.forward((ki[1], ki[2]))

        def collect(self):
            self.far.wait_recv()
            return self.forward((ki[3],))

    barrier = pltpu.get_barrier_semaphore()
    for dev in kdev[1:] + vdev[1:] + seqdev:
        pl.semaphore_signal(barrier, inc=1, device_id=dev, device_id_type=MESH)

    l_small = [load(dup, dup_v), load(dbi, dbi_v), load(ggn, ggn_v)]
    l_qk = [load(wq.at[j], qk_v.at[i, 0]), load(wk.at[j], qk_v.at[i, 1])]
    segment = pl.ds(pl.multiple_of(i * T, T), T)
    l_x = [load(tok.at[segment], x_v), load(ng, ng_v), load(ffg, ffg_v)]
    l_dd = load(dd, dd_v.at[pl.ds(0, 16)])
    l_v = load(wv.at[j], v_v.at[j])
    l_g = load(wg.at[j], g_v.at[j])
    l_c = load(cot.at[segment], c_v)
    l_f = [load(fg, f_v.at[0, i]), load(fu, f_v.at[1, i]), load(fd, f_v.at[2, i])]
    l_o = load(wo, o_v.at[i, j])
    l_xa = load(tok, x_all)
    l_ca = load(cot, c_all)

    pl.semaphore_wait(barrier, 6 + len(seqdev))

    here(l_qk)
    t_qk = Fan(
        [(qk_v.at[i, par], qk_v.at[i, par], kdev[d]) for d in DIRS], qk_v.at[pl.ds(0, 3), 0]
    )
    left = pl.ds(0, half)
    t_v = Fan(
        [(wv.at[vj[d], :, mine], v_v.at[j, :, mine], vdev[d]) for d in DIRS],
        v_v.at[pl.ds(0, 3), :, left],
    )
    dd_v[16:, :] = jnp.zeros((dd_v.shape[0] - 16, D), BF)
    here(l_small)
    head3 = lax.broadcasted_iota(jnp.int32, (16, W, 32), 1)
    head2 = lax.broadcasted_iota(jnp.int32, (W, 32), 0)
    sq_v[...] = jnp.zeros_like(sq_v)
    sq_v[0:16, 0:32] = jnp.sum(jnp.where(head3 == j, dup_v[...].astype(F32), 0.0), axis=1)
    sq_v[16:17, 0:32] = jnp.sum(
        jnp.where(head2 == j, dbi_v[...].astype(F32), 0.0), axis=0, keepdims=True
    )
    ext_v[i] = sq_v[...].T[:32].astype(BF)
    sq_v[...] = jnp.zeros_like(sq_v)
    sq_v[0:16, 0:64] = jnp.broadcast_to(ggn_v[...].astype(F32), (16, 64))
    gge_v[j] = sq_v[0:16].astype(BF)

    t_ext = Fan([(ext_v.at[i], ext_v.at[i], kdev[d]) for d in DIRS], ext_v.at[pl.ds(0, 3)])
    low = pl.ds(0, 32)
    high = pl.ds(32, 32)
    t_ob = Fan(
        [(wo.at[high, mine], o_v.at[i, j, high, mine], kdev[d]) for d in DIRS],
        o_v.at[pl.ds(0, 3), 0, high, mine],
    )
    weights = (fg, fu, fd)

    def gather_weight(n, rows_at):
        return SquareGather(
            lambda src, at: f_v.at[n, src, rows_at, at],
            lambda count: f_v.at[n, pl.ds(0, count), rows_at, mine],
            own=weights[n].at[rows_at, mine],
        )

    cut = FB // 32 * 16
    top = pl.ds(0, cut)
    bottom = pl.ds(cut, FB - cut)
    every = pl.ds(0, FB)
    t_fd = gather_weight(2, every)
    l_o.wait()
    t_oa = LineGather(lambda src: o_v.at[i, src, low, mine], o_v.at[0, :, low, mine])
    t_g = Fan(
        [(wg.at[vj[d], :, mine], g_v.at[j, :, mine], vdev[d]) for d in DIRS],
        g_v.at[pl.ds(0, 3), :, left],
    )
    t_gge = Fan([(gge_v.at[j], gge_v.at[j], vdev[d]) for d in DIRS], gge_v.at[pl.ds(0, 3)])

    here(l_x)
    x = x_v[...].astype(F32)
    g1 = flat_row(ng_v[...].astype(F32))
    g3 = flat_row(ffg_v[...].astype(F32))
    r1 = lax.rsqrt(jnp.sum(x * x, axis=1, keepdims=True) / D + EPS)
    n_v[...] = (x * r1 * g1).astype(BF)
    l_dd.wait()
    lane = lax.broadcasted_iota(jnp.int32, (T, 128), 1)
    lrp = jnp.where(lane == 16, 1.0, nt(n_v[...], dd_v[...]))

    t_qk.wait_recv()
    views = [qk_v.at[ki[d], par] for d in DIRS]
    f_qk = Fan([(one, one, partner) for one in views], qk_v.at[pl.ds(0, 3), 0])
    t_fg = [gather_weight(0, top)]
    f_qk.wait_recv()
    t_ext.wait_recv()
    normed = n_v[...]
    wq_all = qk_v[:, 0].reshape(W * 32, D)
    wk_all = qk_v[:, 1].reshape(W * 32, D)
    ext_all = ext_v[...].reshape(W * 32, 128)
    scale = 128.0 ** (-0.5)
    q = nt(normed, wq_all) * scale
    k = nt(normed, wk_all)
    arg = nt(lrp, ext_all.astype(F32), HIGH)
    rates = (jnp.minimum(arg, 0.0) - jnp.log1p(jnp.exp(-jnp.abs(arg)))) / 16.0
    row_id = lax.broadcasted_iota(jnp.int32, (CB, CB), 0)
    col_id = lax.broadcasted_iota(jnp.int32, (CB, CB), 1)
    causal = row_id >= col_id
    tri = jnp.where(causal, 1.0, 0.0)
    nblk = T // CB
    blk = [slice(c * CB, (c + 1) * CB) for c in range(nblk)]
    e1, e2, em, el, dec, qd, kd, qi, ke, score = [], [], [], [], [], [], [], [], [], []
    for c in range(nblk):
        cum = nn(tri, rates[blk[c]], HIGH)
        mid = cum[CB // 2 - 1 : CB // 2]
        last = cum[CB - 1 : CB]
        e1.append(jnp.exp(cum - mid))
        e2.append(jnp.exp(mid - cum))
        em.append(jnp.exp(mid))
        el.append(jnp.exp(last - mid))
        dec.append(jnp.exp(last))
        a = q[blk[c]] * e1[c]
        b = k[blk[c]] * e2[c]
        qd.append(a.astype(BF))
        kd.append(b.astype(BF))
        qi.append((a * em[c]).astype(BF))
        ke.append((b * el[c]).astype(BF))
        score.append(jnp.where(causal, nt(qd[c], kd[c]), 0.0).astype(BF))

    l_v.wait()
    t_v.wait_recv()
    views = [v_v.at[vj[d], :, mine] for d in DIRS]
    f_vv = Fan([(one, one, partner) for one in views], v_v.at[pl.ds(0, 3), :, left])
    f_vv.wait_recv()
    wv_all = v_v[...].reshape(W * 64, D)
    v = nt(normed, wv_all).astype(BF)
    up = [tn(v[blk[c]], ke[c]) for c in range(nblk)]
    loc = up[0]
    locd = dec[0]
    for c in range(1, nblk):
        loc = loc * dec[c] + up[c]
        locd = locd * dec[c]
    VC = loc.shape[0]
    st_v[i, :VC] = loc.astype(BF)
    st_v[i, VC:] = jnp.broadcast_to(locd, (16, 128)).astype(BF)
    t_st = Fan([(st_v.at[i], st_v.at[i], kdev[d]) for d in DIRS], st_v.at[pl.ds(0, 3)])
    t_fg.append(gather_weight(0, bottom))
    t_fu = gather_weight(1, every)
    t_oa.step(0)
    t_oa.step(1)
    mixed = [nn(score[c], v[blk[c]]) for c in range(nblk)]

    t_ob.wait_recv()
    views = [o_v.at[ki[d], j, high, mine] for d in DIRS]
    f_o = [Fan([(one, one, partner) for one in views], o_v.at[pl.ds(0, 3), 0, high, mine])]
    t_ob2 = LineGather(lambda src: o_v.at[:, src, high, mine], o_v.at[:, :, high, mine])
    here(l_f)
    f_f = t_fd.step()
    t_oa.step(2)

    def gather_states(slots, totals, back):
        order = range(W - 1, -1, -1) if back else range(W)
        pre_s = jnp.zeros((VC, 128), F32)
        pre_d = jnp.ones((1, 128), F32)
        tot_s = jnp.zeros((VC, 128), F32)
        tot_d = jnp.ones((1, 128), F32)
        for other_i in order:
            one_s = slots[other_i, :VC].astype(F32)
            one_d = slots[other_i, VC : VC + 1].astype(F32)
            use = (other_i > i) if back else (other_i < i)
            pre_s = jnp.where(use, pre_s * one_d + one_s, pre_s)
            pre_d = jnp.where(use, pre_d * one_d, pre_d)
            tot_s = tot_s * one_d + one_s
            tot_d = tot_d * one_d
        totals[s, :VC] = tot_s.astype(BF)
        totals[s, VC:] = jnp.broadcast_to(tot_d, (16, 128)).astype(BF)
        return pre_s, pre_d, [send(totals.at[s], totals.at[s], dev) for dev in seqdev]

    def entering(totals, back, pre_s, pre_d, moves):
        arrived(moves)
        order = range(n_seq - 1, -1, -1) if back else range(n_seq)
        far = jnp.zeros((VC, 128), F32)
        for other_s in order:
            one_s = totals[other_s, :VC].astype(F32)
            one_d = totals[other_s, VC : VC + 1].astype(F32)
            use = (other_s > s) if back else (other_s < s)
            far = jnp.where(use, far * one_d + one_s, far)
        return pre_s + pre_d * far

    t_st.wait_recv()
    states = gather_states(st_v, tt_v, False)

    l_g.wait()
    t_g.wait_recv()
    views = [g_v.at[vj[d], :, mine] for d in DIRS]
    f_g = Fan([(one, one, partner) for one in views], g_v.at[pl.ds(0, 3), :, left])
    t_ob2.step(0)
    t_ob2.step(1)
    start = [entering(tt_v, False, *states)]
    for c in range(nblk):
        start.append(start[c] * dec[c] + up[c])
    start_low = [a.astype(BF) for a in start]
    for c in range(nblk):
        mixed[c] = mixed[c] + nt(qi[c], start_low[c])
    mix = jnp.concatenate(mixed, axis=0)
    r2 = lax.rsqrt(jnp.sum(mix * mix, axis=1, keepdims=True) / VC + EPS)
    normal = mix * r2
    f_g.wait_recv()
    t_gge.wait_recv()
    wg_all = g_v[...].reshape(W * 64, D)
    gate = nt(normed, wg_all)
    gg = jnp.concatenate([gge_v[h].astype(F32)[0:1, 0:64] for h in range(W)], axis=1)
    sig = 1.0 / (1.0 + jnp.exp(-gate))
    act = gate * sig
    act_v[0] = act
    act_v[1] = sig + act * (1.0 - sig)
    ga_v[j] = (normal * gg * act).astype(BF)
    act_v[2] = normal
    halves = [pl.ds(n * T // 2, T // 2) for n in range(2)]
    t_ga = [LineGather(lambda src, at=at: ga_v.at[src, at], ga_v.at[:, at]) for at in halves]

    t_oa.collect()
    views = [o_v.at[i, vj[d], low, mine] for d in DIRS]
    f_o.append(Fan([(one, one, partner) for one in views], o_v.at[0, pl.ds(0, 3), low, mine]))
    t_oa2 = SquareGather(
        lambda src, at: o_v.at[src, :, low, at], lambda count: o_v.at[pl.ds(0, count), :, low, mine]
    )

    here([l_xa, l_ca])
    for part in range(rows // T):
        at = pl.ds(part * T, T)
        xa = x_all[at, :].astype(F32)
        ra = lax.rsqrt(jnp.sum(xa * xa, axis=1, keepdims=True) / D + EPS)
        n_all[at, :] = (xa * ra * g1).astype(BF)
    xr_v[...] = (x * (r1 * r1 * r1)).astype(BF).T
    low_all = jnp.where(
        lax.broadcasted_iota(jnp.int32, (rows, 128), 1) == 16, 1.0, nt(n_all[...], dd_v[...])
    )
    lall_v[...] = low_all.astype(BF)
    for line in t_fg:
        f_f += line.step()
    t_ob2.step(2)
    t_ga[0].step(0)
    t_ga[0].step(1)
    t_ga[1].step(0)
    t_ga[1].step(1)
    f_f += t_fu.step()
    t_ga[0].step(2)
    t_ga[1].step(2)
    f_o += t_oa2.step()
    t_ob2.collect()
    views = [o_v.at[:, vj[d], high, mine] for d in DIRS]
    f_o.append(Fan([(one, one, partner) for one in views], o_v.at[:, pl.ds(0, 3), high, mine]))
    f_f += t_fd.collect()
    l_c.wait()
    arrived(f_f)
    dn = f_v[2].reshape(W * FB, D)
    gh_v[...] = nt(c_v[...], dn)
    f_f = t_fg[0].collect() + t_fg[1].collect()
    f_f += t_fu.collect()
    f_far = t_oa2.collect()
    for line in t_ga:
        line.collect()
    arrived(f_o)


    def attention(head):
        return nn(ga_v[head], o_v[head].reshape(W * 64, D))

    att = attention(i) + attention(ki[1]) + attention(ki[2])
    p_v[...] = att
    arrived(f_far)
    arrived(f_f)
    gT = f_v[0].reshape(W * FB, D)
    uT = f_v[1].reshape(W * FB, D)
    att = p_v[...] + attention(ki[3])
    resid = x_v[...].astype(F32) + att
    r3 = lax.rsqrt(jnp.sum(resid * resid, axis=1, keepdims=True) / D + EPS)
    fin = (resid * r3 * g3).astype(BF)
    gval = nt(fin, gT)
    uval = nt(fin, uT)
    fsig = 1.0 / (1.0 + jnp.exp(-gval))
    fact = gval * fsig
    hid = (fact * uval).astype(BF)
    gh = gh_v[...]
    gup = (gh * fact).astype(BF)
    ggate = (gh * uval * (fsig + fact * (1.0 - fsig))).astype(BF)
    hd[...] = hid.T.reshape(W, FB, T)
    t_hd = Fan([(hd.at[ki[d]], hseg.at[i], kdev[d]) for d in DIRS], hseg.at[pl.ds(0, 3)])
    hseg[i] = hd[i]
    part = nn(ggate, gT) + nn(gup, uT)
    p_v[...] = part
    sst[...] = as_row(jnp.sum(resid * g3 * part, axis=1, keepdims=True))
    t_m3 = Fan([(sst, rst.at[d], vdev[d]) for d in DIRS], rst.at[pl.ds(1, 3)])
    part_low = (part * g3).astype(BF)
    t_gg = [
        LineSum(
            lambda to, at=at: sgg.at[to, at],
            rgg.at[pl.ds(0, 2), at],
            rgg.at[pl.ds(2, 2), at],
            cgg.at[:, at],
        )
        for at in halves
    ]
    ggp = nt(part_low, o_v[...].reshape(W * W * 64, D))
    for h in range(W):
        sgg[h] = ggp[:, h * VC : (h + 1) * VC].astype(BF)
    for n in range(3):
        for line in t_gg:
            line.go(n)

    def weight_part(n, grad):
        gw[n] = tn(grad, fin).astype(BF).reshape(W, FB, D)
        return send(gw.at[n, :, :, other], pre.at[n], partner)

    def settle(n, move):
        move.wait_recv()
        pres[n] = (gw[n, :, :, mine].astype(F32) + pre[n].astype(F32)).astype(BF)

    def square(n, rows_at):
        return SquareSum(
            lambda to, at: pres.at[n, to, rows_at, at],
            rfw.at[n, :, rows_at],
            qfw.at[n, :, rows_at],
            cfw.at[n, :, rows_at],
        )

    t_pre0 = weight_part(0, ggate)
    t_pre1 = weight_part(1, gup)

    feature = lax.broadcasted_iota(jnp.int32, (1, D), 1)
    own_slab = jnp.where(lax.rem(feature // 64, W) == j, 1.0, 0.0)
    own_run = jnp.where(feature // (D // W) == j, 1.0, 0.0)
    so[...] = (nn(hid, dn) + own_slab * resid).astype(BF).T.reshape(W, W, 64, T)
    t_out = LineSum(lambda to: so.at[:, to], ro.at[pl.ds(0, 2)], ro.at[pl.ds(2, 2)], co).rest()
    ffn_gain = jnp.sum(part * resid * r3, axis=0, keepdims=True)
    settle(0, t_pre0)
    t_fw0 = square(0, every)
    t_gg[0].step(0)
    t_m3.wait_recv()
    m3 = as_column(sst[...] + rst[1] + rst[2] + rst[3]) / D
    base = c_v[...].astype(F32) - resid * (r3 * r3 * r3 * m3)
    t_gg[0].step(1)
    direct = nt(base.astype(BF), o_v[j].reshape(W * 64, D))
    full = p_v[...] * (g3 * r3)
    mixed_in = (full + own_run * base).astype(BF)
    for h in range(W):
        gow[h] = tn(ga_v[h], mixed_in).astype(BF)
    t_po = send(gow.at[:, :, other], preo, partner)
    t_gg[1].step(0)
    t_fw0.step()
    settle(1, t_pre1)
    t_fw1 = [square(1, top)]
    t_gg[1].step(1)
    t_po.wait_recv()
    preso[...] = (gow[:, :, mine].astype(F32) + preo[...].astype(F32)).astype(BF)
    for line in t_gg:
        line.collect()

    ggs = jnp.concatenate([line.total() for line in t_gg], axis=0)
    ggrad = direct + r3 * ggs
    act = act_v[0]
    normal = act_v[2]
    dgate = (ggrad * normal * gg * act_v[1]).astype(BF)
    gs = ggrad * act
    group = jnp.sum(gs * normal, axis=0, keepdims=True)
    group_rows = [
        jnp.concatenate(
            [group[:, h * 64 : (h + 1) * 64], jnp.zeros((1, T - 64), F32)], axis=1
        )
        for h in range(W)
    ]
    gnm = gs * gg
    gmix = (r2 * (gnm - normal * (jnp.sum(normal * gnm, axis=1, keepdims=True) / VC))).astype(BF)

    qst = [tn(gmix[blk[c]], qi[c]) for c in range(nblk)]
    bloc = qst[nblk - 1]
    for c in range(nblk - 2, -1, -1):
        bloc = bloc * dec[c] + qst[c]
    bst_v[i, :VC] = bloc.astype(BF)
    bst_v[i, VC:] = jnp.broadcast_to(locd, (16, 128)).astype(BF)
    t_bst = Fan([(bst_v.at[i], bst_v.at[i], kdev[d]) for d in DIRS], bst_v.at[pl.ds(0, 3)])
    t_ow = SquareSum(lambda to, at: preso.at[to, :, at], rowk, qow, cow)
    t_fw1.append(square(1, bottom))
    vz[1] = dgate.T.reshape(W, 64, T)
    t_gz = Fan([(vz.at[1, vj[d]], zvg.at[1, j], vdev[d]) for d in DIRS], zvg.at[1, pl.ds(0, 3)])
    dq_all, dk_in, dv_in = [], [], []
    for c in range(nblk):
        ds = jnp.where(causal, nt(gmix[blk[c]], v[blk[c]]), 0.0).astype(BF)
        dq_all.append(e1[c] * (nn(ds, kd[c]) + em[c] * nn(gmix[blk[c]], start_low[c])))
        dk_in.append(tn(ds, qd[c]))
        dv_in.append(tn(score[c], gmix[blk[c]]))
    ql = jnp.concatenate([(dq * scale).astype(BF) for dq in dq_all], axis=0)
    known = nn(dgate, wg_all) + nn(ql, wq_all)
    rest_in = full + own_slab * base
    t_out.step(0)
    t_hd.wait_recv()
    dsum[0] = nn(lanes(hseg[...]), c_all[...]).astype(BF)
    t_ds = send(dsum.at[0], dsum.at[1], partner)
    t_fw1[0].step()
    t_bst.wait_recv()
    after = [None] * nblk
    states = gather_states(bst_v, btt_v, True)
    t_out.step(1)
    after[nblk - 1] = entering(btt_v, True, *states)
    for c in range(nblk - 2, -1, -1):
        after[c] = after[c + 1] * dec[c + 1] + qst[c + 1]

    kl, vl, ga = [], [], []
    for c in range(nblk):
        low_after = after[c].astype(BF)
        dk = e2[c] * (dk_in[c] + el[c] * nn(v[blk[c]], low_after))
        dv = dv_in[c] + nt(ke[c], low_after)
        gc = q[blk[c]] * dq_all[c] - k[blk[c]] * dk
        extra = jnp.sum(after[c] * start[c + 1], axis=0, keepdims=True)
        gc = jnp.where(row_id == CB - 1, gc + extra, gc)
        gr = tn(tri, gc, HIGH)
        ga.append(gr / (1.0 + jnp.exp(arg[blk[c]])) / 16.0)
        kl.append(dk.astype(BF))
        vl.append(dv.astype(BF))
    kl = jnp.concatenate(kl, axis=0)
    vl = jnp.concatenate(vl, axis=0)
    ga = jnp.concatenate(ga, axis=0).astype(BF)
    glr = nn(ga, ext_all).astype(BF)
    gn = known + nn(kl, wk_all) + nn(vl, wv_all) + nn(glr, dd_v[...])
    whole = gn * (r1 * g1) + rest_in
    sgn[...] = whole.astype(BF).T.reshape(W, W, 64, T)
    pairs = [pl.ds(n * W // 2, W // 2) for n in range(2)]
    t_gn = [
        LineSum(
            lambda to, at=at: sgn.at[at, to],
            rgn.at[pl.ds(0, 2), at],
            rgn.at[pl.ds(2, 2), at],
            cgn.at[:, at],
        )
        for at in pairs
    ]
    for n in range(3):
        for line in t_gn:
            line.go(n)
    vz[0] = vl.T.reshape(W, 64, T)
    t_vz = Fan([(vz.at[0, vj[d]], zvg.at[0, j], vdev[d]) for d in DIRS], zvg.at[0, pl.ds(0, 3)])

    gnx = gn * x_v[...].astype(F32)
    norm_gain = jnp.sum(gnx * r1, axis=0, keepdims=True)
    m1p = as_row(jnp.sum(gnx * g1, axis=1, keepdims=True))[:1]
    rank_row = lax.broadcasted_iota(jnp.int32, (16, 128), 0)
    rank_col = lax.broadcasted_iota(jnp.int32, (16, 128), 1)
    by_owner = jnp.where(rank_col == lax.rem(rank_row, W) * W + rank_row // W, 1.0, 0.0)
    small = nn(by_owner.astype(BF), tn(glr, normed).astype(BF))
    slab = D // (W * W)
    rid = lax.broadcasted_iota(jnp.int32, (16, T), 0)
    for h in range(W):
        ranks = small[h * W : (h + 1) * W]
        sm0[h, 0:16] = jnp.concatenate(
            [ranks[:, n * T : (n + 1) * T] for n in range(W)], axis=0
        ).astype(BF)

        def slabs(row):
            return jnp.concatenate(
                [row[:, (W * n + h) * slab : (W * n + h + 1) * slab] for n in range(W)], axis=1
            )

        rest = jnp.where(rid == 0, slabs(norm_gain), 0.0)
        rest = jnp.where(rid == 1, slabs(ffn_gain), rest)
        rest = jnp.where(rid == 2, group_rows[h], rest)
        rest = jnp.where(rid == 3, m1p, rest)
        sm0[h, 16:32] = rest.astype(BF)
    t_s0 = Fan([(sm0.at[vj[d]], sm1.at[d], vdev[d]) for d in DIRS], sm1.at[pl.ds(1, 3)])


    def finish_square(n, lines):
        for line, rows_at in lines:
            line.collect()
            fin_f[par, n, rows_at] = line.total().astype(BF)
        return send(fin_f.at[par, n], fin_f.at[par, n], partner)

    t_ff = [finish_square(0, [(t_fw0, every)])]
    t_ow.step()
    t_fw1[1].step()
    qka[:, 0] = ql.T.reshape(W, 32, T)
    qka[:, 1] = kl.T.reshape(W, 32, T)
    qka[:, 2] = ga.T.reshape(W, 32, T)
    t_qa = Fan([(qka.at[ki[d]], kqa.at[i], kdev[d]) for d in DIRS], kqa.at[pl.ds(0, 3)])
    t_gz.wait_recv()
    zvg[1, j] = vz[1, j]
    t_gk = Fan([(zvg.at[1, ki[d]], kvg.at[1, i], kdev[d]) for d in DIRS], kvg.at[1, pl.ds(0, 3)])
    kvg[1, i] = zvg[1, i]

    t_out.collect()
    ao[...] = t_out.total().astype(BF)
    t_ao = Fan([(ao.at[ki[d]], oseg.at[i], kdev[d]) for d in DIRS], oseg.at[pl.ds(0, 3)])
    oseg[i] = ao[i]

    t_gn[0].step(0)
    t_gn[1].step(0)
    t_gn[0].step(1)
    t_gn[1].step(1)

    t_ow.collect()
    mid_o[...] = t_ow.total().astype(BF).reshape(W, 64, half)
    t_oz = LineSum(
        lambda to: mid_o.at[to], rowz.at[pl.ds(0, 2)], rowz.at[pl.ds(2, 2)], coz
    ).rest()

    t_qa.wait_recv()
    kqa[i] = qka[i]
    nall = n_all[...]
    for n in range(2):
        qksum[0, n] = nn(lanes(kqa[:, n]), nall).astype(BF)
    esum[0] = nn(lanes(kqa[:, 2]), lall_v[...])
    t_qs = send(qksum.at[0], qksum.at[1], partner)
    t_es = send(esum.at[0], esum.at[1], partner)
    for line in t_gn:
        line.collect()
    t_vz.wait_recv()
    zvg[0, j] = vz[0, j]
    t_vk = Fan([(zvg.at[0, ki[d]], kvg.at[0, i], kdev[d]) for d in DIRS], kvg.at[0, pl.ds(0, 3)])
    kvg[0, i] = zvg[0, i]
    t_s0.wait_recv()
    sm2[0] = total(sm0[j], sm1).astype(BF)
    m1 = (
        sm0[0, 19:20].astype(F32)
        + sm1[1, 19:20].astype(F32)
        + sm1[2, 19:20].astype(F32)
        + sm1[3, 19:20].astype(F32)
    ) / D
    t_s1 = Fan([(sm2.at[0], sm2.at[d], kdev[d]) for d in DIRS], sm2.at[pl.ds(1, 3)])

    summed = jnp.concatenate([line.total() for line in t_gn], axis=0)
    for h in range(W):
        at = pl.ds(pl.multiple_of((h * W + j) * 64, 64), 64)
        ai[h] = (summed[h] - xr_v[at, :].astype(F32) * m1).astype(BF)
    t_ai = Fan([(ai.at[ki[d]], iseg.at[i], kdev[d]) for d in DIRS], iseg.at[pl.ds(0, 3)])
    iseg[i] = ai[i]

    t_ff.append(finish_square(1, list(zip(t_fw1, (top, bottom)))))

    t_gk.wait_recv()
    vgsum[0, 1] = nn(lanes(kvg[1]), nall).astype(BF)
    t_vs = [send(vgsum.at[0, 1], vgsum.at[1, 1], partner)]

    t_oz.step(0)
    t_oz.step(1)

    t_vk.wait_recv()
    vgsum[0, 0] = nn(lanes(kvg[0]), nall).astype(BF)
    t_vs.append(send(vgsum.at[0, 0], vgsum.at[1, 0], partner))
    t_s1.wait_recv()
    sm3[0] = total(sm2[0], sm2).astype(BF)
    t_s2 = send(sm3.at[0], sm3.at[1], partner)

    t_ds.wait_recv()
    r_fd[...] = dsum[0].astype(F32) + dsum[1].astype(F32)
    t_ao.wait_recv()
    r_out[...] = lanes(oseg[...])
    t_qs.wait_recv()
    r_q[...] = qksum[0, 0].astype(F32) + qksum[1, 0].astype(F32)
    r_k[...] = qksum[0, 1].astype(F32) + qksum[1, 1].astype(F32)
    t_es.wait_recv()
    decay = (esum[0] + esum[1]).T
    r_du[...] = decay[0:16, :].reshape(16, 1, 32)
    r_db[...] = decay[16:17, :]
    t_ff[0].wait_recv()
    for h in range(2):
        r_fg[:, h * half : (h + 1) * half] = fin_f[h, 0].astype(F32)
    t_oz.collect()
    fin_ow[par] = t_oz.total().astype(BF)
    t_fo = send(fin_ow.at[par], fin_ow.at[par], partner)
    t_ff[1].wait_recv()
    for h in range(2):
        r_fu[:, h * half : (h + 1) * half] = fin_f[h, 1].astype(F32)
    arrived(t_vs)
    r_v[...] = vgsum[0, 0].astype(F32) + vgsum[1, 0].astype(F32)
    r_g[...] = vgsum[0, 1].astype(F32) + vgsum[1, 1].astype(F32)
    t_s2.wait_recv()
    tot = sm3[0].astype(F32) + sm3[1].astype(F32)
    own_ranks, own_slabs = [], jnp.zeros((2, slab), F32)
    for n in range(W):
        own_ranks.append(jnp.zeros((1, T), F32))
        for h in range(W):
            row = tot[n * W + h : n * W + h + 1]
            own_ranks[n] = jnp.where(i == h, row, own_ranks[n])
        own_slabs = jnp.where(i == n, tot[16:18, n * slab : (n + 1) * slab], own_slabs)
    r_dd[...] = jnp.concatenate(own_ranks, axis=1)
    r_ng[...] = own_slabs[0:1]
    r_fn[...] = own_slabs[1:2]
    r_gg[...] = tot[18:19, 0:64]
    t_ai.wait_recv()
    r_in[...] = lanes(iseg[...])
    t_fo.wait_recv()
    for h in range(2):
        r_o[:, h * half : (h + 1) * half] = fin_ow[h].astype(F32)
    for _, cp in ring:
        cp.wait_send()

    @pl.when(inner)
    def _():
        for cp in inner_sent:
            cp.wait_send()

    @pl.when(jnp.logical_not(inner))
    def _():
        for cp in outer_sent:
            cp.wait_send()


N_OUT = 44
N_IN = 93
N_LOCAL = 18


def layer(n_seq, args):
    rows, D = args[0].shape
    W = WAYS
    T = rows // W
    FB = args[-1].shape[0]
    VC = W * 64
    half = D // 2

    def sds(shape, dtype=F32):
        return pltpu.VMEM(shape, dtype)

    def vm(shape, dtype=BF):
        return pltpu.VMEM(shape, dtype)

    slab = D // (W * W)
    outs = [
        sds((64, rows), BF),
        sds((64, rows), BF),
        sds((1, slab)),
        sds((32, D)),
        sds((32, D)),
        sds((64, D)),
        sds((64, D)),
        sds((1, D)),
        sds((16, 1, 32)),
        sds((1, 32)),
        sds((1, 64)),
        sds((64, D)),
        sds((1, slab)),
        sds((FB, D)),
        sds((FB, D)),
        sds((FB, D)),
    ]
    scratch = [
        vm((T, D)),
        vm((T, D)),
        vm((rows, D)),
        vm((rows, D)),
        vm((rows, D)),
        vm((T, D)),
        vm((D, T)),
        vm((128, D)),
        vm((8, 128)),
        vm((8, 128)),
        vm((16, W, 32)),
        vm((W, 32)),
        vm((1, 64)),
        vm((128, 128), F32),
        vm((8, D), F32),
        vm((W, 2, 32, D)),
        vm((W, 32, 128)),
        vm((W, 64, D)),
        vm((W, 64, D)),
        vm((W, 16, 128)),
        vm((W, W, 64, D)),
        vm((3, W, FB, D)),
        vm((W, VC + 16, 128)),
        vm((n_seq, VC + 16, 128)),
        vm((W, VC + 16, 128)),
        vm((n_seq, VC + 16, 128)),
        vm((W, T, VC)),
        vm((W, T, VC)),
        vm((W, T, VC)),
        vm((2, T, VC)),
        vm((8, T), F32),
        vm((W, 8, T), F32),
        vm((W, W, 64, T)),
        vm((W, W, 64, T)),
        vm((2, W, 64, T)),
        vm((W, W, 64, T)),
        vm((W, W, 64, T)),
        vm((2, W, 64, T)),
        vm((W, 64, T)),
        vm((W, 64, T)),
        vm((W, 64, T)),
        vm((W, 64, T)),
        vm((W, FB, T)),
        vm((W, FB, T)),
        vm((2, W, FB, D)),
        vm((2, W, FB, half)),
        vm((2, W, FB, half)),
        vm((2, 2, FB, half)),
        vm((2, 2, FB, half // 2)),
        vm((2, 2, FB, half // 2)),
        vm((2, 2, FB, half)),
        vm((2, FB, D)),
        vm((W, VC, D)),
        vm((W, VC, half)),
        vm((W, VC, half)),
        vm((2, VC, half)),
        vm((2, VC, half // 2)),
        vm((2, VC, half // 2)),
        vm((W, 64, half)),
        vm((W, 64, half)),
        vm((2, 64, half)),
        vm((2, 64, half)),
        vm((2, W, 64, T)),
        vm((2, W, 64, T)),
        vm((2, W, 64, T)),
        vm((2, 2, 64, D)),
        vm((W, 3, 32, T)),
        vm((W, 3, 32, T)),
        vm((2, 2, 32, D)),
        vm((2, 32, 128), F32),
        vm((W, 32, T)),
        vm((W, 32, T)),
        vm((W, 32, T)),
        vm((2, 32, T)),
        vm((rows, 128)),
        vm((T, W * FB), F32),
        vm((3, T, VC), F32),
        vm((T, D), F32),
        pltpu.SemaphoreType.DMA((N_OUT,)),
        pltpu.SemaphoreType.DMA((N_IN + 2 * n_seq,)),
        pltpu.SemaphoreType.DMA((N_LOCAL,)),
    ]
    return pl.pallas_call(
        functools.partial(layer_kernel, n_seq),
        out_shape=outs,
        in_specs=[pl.BlockSpec(memory_space=pl.ANY)] * len(args),
        out_specs=[pl.BlockSpec(memory_space=pltpu.VMEM)] * len(outs),
        scratch_shapes=scratch,
        compiler_params=pltpu.CompilerParams(
            collective_id=0, has_side_effects=True, vmem_limit_bytes=60 * 2**20
        ),
        name="layer",
    )(*args)


def finish_kernel(*refs):
    n = len(refs) // 2
    sem = refs[-1]
    copies = [pltpu.make_async_copy(refs[k], refs[n + k], sem.at[k]) for k in range(n)]
    for cp in copies:
        cp.start()
    for cp in copies:
        cp.wait()


def finish(parts):
    return pl.pallas_call(
        finish_kernel,
        out_shape=[jax.ShapeDtypeStruct(p.shape, p.dtype) for p in parts],
        in_specs=[pl.BlockSpec(memory_space=pltpu.VMEM)] * len(parts),
        out_specs=[pl.BlockSpec(memory_space=pl.ANY)] * len(parts),
        scratch_shapes=[pltpu.SemaphoreType.DMA((len(parts),))],
        compiler_params=pltpu.CompilerParams(vmem_limit_bytes=16 * 2**20),
        name="finish",
    )(*parts)


def shards(
    n_seq,
    tokens,
    norm_gain,
    query_weight,
    key_weight,
    value_weight,
    gate_weight,
    decay_down,
    decay_up,
    decay_bias,
    group_gain,
    out_weight,
    ffn_gain,
    ffn_gate,
    ffn_up,
    ffn_down,
    cotangent,
):
    parts = layer(
        n_seq,
        (
            tokens,
            cotangent,
            norm_gain.reshape(8, -1),
            ffn_gain.reshape(8, -1),
            decay_up,
            decay_bias,
            group_gain[None],
            query_weight.transpose(1, 2, 0),
            key_weight.transpose(1, 2, 0),
            value_weight.transpose(1, 2, 0),
            gate_weight.transpose(1, 2, 0),
            decay_down.T,
            out_weight[0],
            ffn_gate.T,
            ffn_up.T,
            ffn_down,
        ),
    )
    if n_seq > 2:

        def over_pairs(a):
            return jnp.sum(lax.all_gather(a, "seq")[::2].astype(F32), axis=0).astype(a.dtype)

        parts = list(parts[:2]) + [over_pairs(a) for a in parts[2:]]
    (r_out, r_in, r_ng, r_q, r_k, r_v, r_g, r_dd, r_du, r_db, r_gg, r_o, r_fn, r_fg, r_fu, r_fd) = finish(parts)
    return (
        r_out.T,
        r_in.T,
        r_ng[0],
        r_q.T[:, None, :],
        r_k.T[:, None, :],
        r_v.T[:, None, :],
        r_g.T[:, None, :],
        r_dd.T,
        r_du,
        r_db,
        r_gg[0],
        r_o[None],
        r_fn[0],
        r_fg.T,
        r_fu.T,
        r_fd,
    )


def solution(mesh):
    in_specs = (
        P("seq", None),
        P(),
        P(None, None, "kax"),
        P(None, None, "kax"),
        P(None, None, "vax"),
        P(None, None, "vax"),
        P(),
        P(None, None, "kax"),
        P(None, "kax"),
        P("vax"),
        P("kax", "vax", None),
        P(),
        P(None, ("kax", "vax")),
        P(None, ("kax", "vax")),
        P(("kax", "vax"), None),
        P("seq", None),
    )
    out_specs = (
        P("seq", ("kax", "vax")),
        P("seq", ("kax", "vax")),
        P(("kax", "vax")),
        P(None, "vax", "kax"),
        P(None, "vax", "kax"),
        P(None, "kax", "vax"),
        P(None, "kax", "vax"),
        P(None, ("kax", "vax")),
        P(None, "vax", "kax"),
        P("vax", "kax"),
        P("vax"),
        P("kax", "vax", None),
        P(("kax", "vax")),
        P(None, ("kax", "vax")),
        P(None, ("kax", "vax")),
        P(("kax", "vax"), None),
    )
    return jax.shard_map(
        functools.partial(shards, mesh.shape["seq"]),
        mesh=mesh,
        in_specs=in_specs,
        out_specs=out_specs,
        check_vma=False,
    )
```
